32 devices in a mesh: dp: 8 (over z, y), tensor: 4 (over x, core).
Axes of the slice: x: 2, y: 2, z: 4, core: 2. Of those that a mesh axis runs over, the one named last changes fastest.
Arguments:
- tokens: bfloat16 [4, 8, 1024, 768], P(None, 'dp', 'tensor'), may hold values from -6 to 6
- doc_ids: int32 [4, 8, 1024], P(None, 'dp'), may hold values from 0 to 7, never falling along the last dimension, each value on 1 to 800 neighbouring positions
- w_query: bfloat16 [768, 768], P('dp', 'tensor'), may hold values from -0.21875 to 0.21875
- b_query: float32 [768], P('tensor'), may hold values from -3 to 3
- w_key: bfloat16 [768, 768], P('dp', 'tensor'), may hold values from -0.21875 to 0.21875
- w_value: bfloat16 [768, 768], P('dp', 'tensor'), may hold values from -0.21875 to 0.21875
- b_value: float32 [768], P('tensor'), may hold values from -3 to 3
- w_mixer: bfloat16 [768, 768], P('tensor', 'dp'), may hold values from -1.75 to 1.75
- b_mixer: float32 [768], replicated, may hold values from -2 to 2
- gain_one: float32 [768], replicated, may hold values from 0.25 to 1.75
- bias_one: float32 [768], replicated, may hold values from -2 to 2
- w_inner: bfloat16 [768, 3072], P('dp', 'tensor'), may hold values from -0.21875 to 0.21875
- b_inner: float32 [3072], P('tensor'), may hold values from -3 to 3
- w_outer: bfloat16 [3072, 768], P('tensor', 'dp'), may hold values from -0.109375 to 0.109375
- b_outer: float32 [768], replicated, may hold values from -2 to 2
- gain_two: float32 [768], replicated, may hold values from 0.25 to 1.75
- bias_two: float32 [768], replicated, may hold values from -2 to 2
- cotangent: bfloat16 [4, 8, 1024, 768], P(None, 'dp', 'tensor'), may hold values from -6 to 6
Outputs:
- layer_output: bfloat16 [4, 8, 1024, 768], P(None, 'dp', 'tensor')
- d_tokens: float32 [4, 8, 1024, 768], P(None, 'dp', 'tensor')
- dw_query: float32 [768, 768], P('dp', 'tensor')
- db_query: float32 [768], P('tensor')
- dw_key: float32 [768, 768], P('dp', 'tensor')
- dw_value: float32 [768, 768], P('dp', 'tensor')
- db_value: float32 [768], P('tensor')
- dw_mixer: float32 [768, 768], P('tensor', 'dp')
- db_mixer: float32 [768], replicated
- dgain_one: float32 [768], replicated
- dbias_one: float32 [768], replicated
- dw_inner: float32 [768, 3072], P('dp', 'tensor')
- db_inner: float32 [3072], P('tensor')
- dw_outer: float32 [3072, 768], P('tensor', 'dp')
- db_outer: float32 [768], replicated
- dgain_two: float32 [768], replicated
- dbias_two: float32 [768], replicated
The draws below stay inside these ranges and needn't reach their ends.
Inputs may be any that keep to these rules, and one draw needn't show every extreme that they name: `doc_ids`: within each sequence the numbers never fall; a document is the tokens of one sequence that share a number, and none is longer than 800 tokens.
All inputs are finite; a program needn't handle non-finite values.
Results may differ from the reference program's by a relative error of at most 0.017.
The reference program's roundings to bfloat16 on the way count: a program that leaves them out, or rounds other values in their place, can miss the bound.
Values may be sent and summed in bfloat16 or wider, within the bound.
A program may use at most 256 MiB of HBM per device.

```python
import math
import jax
import jax.numpy as jnp
import numpy as np
from jax import lax

D = 768
HEADS = 12
HEAD = 64
FF = 3072
LEN = 1024
MBATCH = 4
SEQS = 8


def raised(result, stream_key, source, target, parts, factor):
    def block_of(position):
        return (jnp.arange(result.shape[position]) // (result.shape[position] // parts)).reshape((-1,) + (1,) * (result.ndim - 1 - position))

    near = jax.random.permutation(stream_key, parts)[block_of(target)]
    far = (block_of(target) + parts // 2) % parts
    return jnp.where((block_of(source) == near) | (block_of(source) == far), factor * result, result)


def level_of(rng, extent, cuts, smallest, largest):
    loudness = 1.0
    for dim, blocks in cuts:
        draws = jax.random.uniform(jax.random.fold_in(jax.random.fold_in(rng, 6), dim), (blocks,), jnp.float32, smallest / len(cuts), largest / len(cuts))
        loudness = loudness * jnp.repeat(jnp.exp(draws), extent[dim] // blocks).reshape((-1,) + (1,) * (len(extent) - 1 - dim))
    return loudness


def length_profile(number_of, total, limit, slope):
    loads = [(1 << 20) // math.isqrt(rank ** slope) + 1 for rank in range(2, number_of + 1)]
    rest, given = total - limit - (number_of - 1), [1] * (number_of - 1)
    while rest > 0:
        free = [i for i in range(number_of - 1) if given[i] < limit]
        pool, remaining = sum([loads[i] for i in free]), rest
        for i in free:
            extra = min(limit - given[i], max(1, remaining * loads[i] // pool), rest)
            given[i] = given[i] + extra
            rest = rest - extra
    return np.array([limit] + given)


def ragged(stream_key, amount, total, reach, lean):
    if amount == 2:
        one = jax.random.randint(stream_key, (), max(1, total - reach), min(reach, total - 1) + 1)
        return jnp.stack([one, total - one])
    sizes = jnp.asarray(length_profile(amount, total, reach, lean), jnp.int32)
    pairs = (amount - 1) // 2
    source_of, taker = sizes[1:1 + 2 * pairs:2], sizes[2:2 + 2 * pairs:2]
    slack = jnp.minimum(source_of - 1, reach - taker)
    moved = jax.random.randint(jax.random.fold_in(stream_key, 1), (pairs,), 0, 1 << 20) % (slack + 1)
    sizes = sizes.at[1:1 + 2 * pairs:2].set(source_of - moved).at[2:2 + 2 * pairs:2].set(taker + moved)
    return sizes[jax.random.permutation(jax.random.fold_in(stream_key, 2), amount)]


def noise(key, extent, scale, bound, cuts=(), kind=jnp.bfloat16):
    values = scale * jax.random.normal(key, extent, jnp.float32)
    if cuts:
        values = values * level_of(key, extent, cuts, -0.22, 0.18)
    return jnp.clip(values, -bound, bound).astype(kind)


def noise_with(own_key, dims, scale, most, shards, heavy, dtype=jnp.bfloat16):
    result = scale * jax.random.normal(own_key, dims, jnp.float32)
    if shards:
        result = result * level_of(own_key, dims, shards, -0.22, 0.18)
    return jnp.clip(raised(result, jax.random.fold_in(own_key, 3), *heavy), -most, most).astype(dtype)


def setup_inputs(seed: int = 0) -> dict:
    streams_of = jax.random.split(jax.random.key(seed), 19)
    tokens = noise_with(streams_of[0], (MBATCH, SEQS, LEN, D), 1.0, 6.0, ((1, 8), (2, 4)), (1, 3, 8, 2.0))
    doc_ids = jax.vmap(lambda own: jnp.searchsorted(jnp.cumsum(ragged(own, 8, LEN, 25 * LEN // 32, 2)), jnp.arange(LEN), side="right"))(jax.random.split(streams_of[1], MBATCH * SEQS)).reshape((MBATCH, SEQS, LEN)).astype(jnp.int32)
    w_query = noise(streams_of[2], (D, D), D ** -0.5, 0.21875, ((0, 8), (1, 4)))
    b_query = noise(streams_of[3], (D,), 0.5, 3.0, ((0, 4),), jnp.float32)
    w_key = noise(streams_of[4], (D, D), D ** -0.5, 0.21875, ((0, 8), (1, 4)))
    w_value = noise(streams_of[5], (D, D), D ** -0.5, 0.21875, ((0, 8), (1, 4)))
    b_value = noise(streams_of[6], (D,), 0.5, 3.0, ((0, 4),), jnp.float32)
    w_mixer = noise(streams_of[7], (D, D), (max(D // 64, 4)) ** -0.5, 1.75, ((0, 4), (1, 8)))
    b_mixer = noise(streams_of[8], (D,), 0.3, 2.0, (), jnp.float32)
    gain_one = jnp.clip(1.0 + 0.15 * jax.random.normal(streams_of[9], (D,), jnp.float32), 0.25, 1.75)
    bias_one = noise(streams_of[10], (D,), 0.3, 2.0, (), jnp.float32)
    w_inner = noise(streams_of[11], (D, FF), D ** -0.5, 0.21875, ((0, 8), (1, 4)))
    b_inner = noise(streams_of[12], (FF,), 0.5, 3.0, ((0, 4),), jnp.float32)
    w_outer = noise(streams_of[13], (FF, D), FF ** -0.5, 0.109375, ((0, 4), (1, 8)))
    b_outer = noise(streams_of[14], (D,), 0.3, 2.0, (), jnp.float32)
    gain_two = jnp.clip(1.0 + 0.15 * jax.random.normal(streams_of[15], (D,), jnp.float32), 0.25, 1.75)
    bias_two = noise(streams_of[16], (D,), 0.3, 2.0, (), jnp.float32)
    cotangent = noise_with(streams_of[17], (MBATCH, SEQS, LEN, D), 1.0, 6.0, ((1, 8), (2, 4)), (1, 3, 8, 2.0))
    return {"tokens": tokens, "doc_ids": doc_ids, "w_query": w_query, "b_query": b_query, "w_key": w_key, "w_value": w_value, "b_value": b_value, "w_mixer": w_mixer, "b_mixer": b_mixer, "gain_one": gain_one, "bias_one": bias_one, "w_inner": w_inner, "b_inner": b_inner, "w_outer": w_outer, "b_outer": b_outer, "gain_two": gain_two, "bias_two": bias_two, "cotangent": cotangent}


@jax.custom_vjp
def low(v):
    return lax.optimization_barrier(v.astype(jnp.bfloat16)).astype(jnp.float32)

@jax.custom_vjp
def low_back(v):
    return v

def low_keep(v):
    return (low(v), None)

def low_pass(kept, grad):
    return (grad,)

def back_keep(v):
    return (v, None)

def back_low(kept, grad):
    return (low(grad),)
low.defvjp(low_keep, low_pass)
low_back.defvjp(back_keep, back_low)

def matmul(left, right):
    return jnp.dot(left, right, precision=lax.Precision.HIGHEST, preferred_element_type=jnp.float32)

def normalize(values, weights, offsets):
    average = lax.optimization_barrier(jnp.mean(values, axis=-1, keepdims=True))
    centred = values - average
    spread = lax.optimization_barrier(jnp.mean(centred * centred, axis=-1, keepdims=True))
    return centred * lax.rsqrt(spread + 1e-12) * weights + offsets

def attend_one(packed):
    queries, keys_in, values_in, labels = packed
    length = queries.shape[0]
    q_heads = queries.reshape(length, HEADS, HEAD)
    k_heads = keys_in.reshape(length, HEADS, HEAD)
    v_heads = values_in.reshape(length, HEADS, HEAD)
    scores = jnp.einsum('qhd,khd->hqk', q_heads, k_heads, precision=lax.Precision.HIGHEST) * HEAD ** (-0.5)
    same_doc = labels[:, None] == labels[None, :]
    scores = jnp.where(same_doc[None], low_back(scores), -1e+30)
    chances = low(jax.nn.softmax(scores, axis=-1))
    mixed = jnp.einsum('hqk,khd->qhd', chances, v_heads, precision=lax.Precision.HIGHEST)
    return mixed.reshape(length, HEADS * HEAD)

def forward(params, token_block, labels):
    w_query, b_query, w_key, w_value, b_value, w_mixer, b_mixer, gain_one, bias_one, w_inner, b_inner, w_outer, b_outer, gain_two, bias_two = params
    group, length, width = token_block.shape
    token_rows = token_block.reshape(group * length, width)
    queries = low(low_back(matmul(token_rows, w_query) + b_query))
    keys_all = low(low_back(matmul(token_rows, w_key)))
    values_all = low(low_back(matmul(token_rows, w_value) + b_value))
    attended = lax.map(jax.checkpoint(attend_one), (queries.reshape(group, length, width), keys_all.reshape(group, length, width), values_all.reshape(group, length, width), labels))
    attended = low(low_back(attended.reshape(group * length, width)))
    mixed_sum = low_back(matmul(attended, w_mixer))
    first_sum = token_rows + mixed_sum + b_mixer
    normed = normalize(first_sum, gain_one, bias_one)
    inner = low_back(matmul(low(normed), w_inner) + b_inner)
    hidden = low(jax.nn.gelu(inner, approximate=False))
    outer_sum = low_back(matmul(hidden, w_outer))
    second = normed + outer_sum + b_outer
    return normalize(second, gain_two, bias_two)

def reference(tokens, doc_ids, w_query, b_query, w_key, w_value, b_value, w_mixer, b_mixer, gain_one, bias_one, w_inner, b_inner, w_outer, b_outer, gain_two, bias_two, cotangent):
    params = (w_query.astype(jnp.float32), b_query, w_key.astype(jnp.float32), w_value.astype(jnp.float32), b_value, w_mixer.astype(jnp.float32), b_mixer, gain_one, bias_one, w_inner.astype(jnp.float32), b_inner, w_outer.astype(jnp.float32), b_outer, gain_two, bias_two)
    length = tokens.shape[2]
    width = tokens.shape[3]
    token_groups = tokens.astype(jnp.float32).reshape(-1, 4, length, width)
    label_groups = doc_ids.reshape(-1, 4, length)
    cot_groups = cotangent.astype(jnp.float32).reshape(-1, 4, length, width)

    def scan_step(carry, packed):
        token_block, label_block, cot_block = packed

        def apply_layer(params_in, tokens_in):
            return forward(params_in, tokens_in, label_block)
        produced, back_fn = jax.vjp(apply_layer, params, token_block)
        d_params, d_block = back_fn(cot_block.reshape(-1, width))
        carry = jax.tree.map(lambda summed, added: summed + added, carry, d_params)
        return (carry, (produced.reshape(token_block.shape).astype(jnp.bfloat16), d_block))
    start = jax.tree.map(jnp.zeros_like, params)
    totals, (produced_all, d_all) = lax.scan(scan_step, start, (token_groups, label_groups, cot_groups))
    layer_output = produced_all.reshape(tokens.shape)
    d_tokens = d_all.reshape(tokens.shape)
    return (layer_output, d_tokens, totals[0], totals[1], totals[2], totals[3], totals[4], totals[5], totals[6], totals[7], totals[8], totals[9], totals[10], totals[11], totals[12], totals[13], totals[14])
```

```python
from functools import partial

import jax
import jax.numpy as jnp
from jax import lax
from jax.experimental import pallas as pl
from jax.experimental.pallas import tpu as pltpu
from jax.sharding import PartitionSpec as P

HEAD = 64
DOCS = 8
PAD = 256
ROWS = 256
LOG2E = 1.4426950408889634
EPS = 1e-12
F32 = jnp.float32
BF16 = jnp.bfloat16


def dot_nn(left, right):
    return lax.dot_general(left, right, (((1,), (0,)), ((), ())), preferred_element_type=F32)


def dot_nt(left, right):
    return lax.dot_general(left, right, (((1,), (1,)), ((), ())), preferred_element_type=F32)


def rows_of(index, size=ROWS):
    return pl.ds(pl.multiple_of(index * size, size), size)


def lane_index(shape):
    return lax.broadcasted_iota(jnp.int32, shape, 1)


def three_parts(values):
    high = values.astype(BF16)
    rest = values - high.astype(F32)
    middle = rest.astype(BF16)
    low = (rest - middle.astype(F32)).astype(BF16)
    return high, middle, low


def head_only(lanes, head):
    return (lanes >= head * HEAD) & (lanes < (head + 1) * HEAD)


def head_and_extra(lanes, head, width):
    extra = width + DOCS + 3 * head
    return (
        head_only(lanes, head)
        | ((lanes >= width) & (lanes < width + DOCS))
        | ((lanes >= extra) & (lanes < extra + 3))
    )


def unpack(block_ref, slot, width):
    part = block_ref[:, slot * width : (slot + 1) * width]
    return jnp.concatenate([part, jnp.zeros((part.shape[0], PAD - width), part.dtype)], axis=1)


def attend_kernel(
    x_ref, a_ref, bq_ref, bv_ref, qaug_ref, kaug_ref, vaug_ref, bm_ref,
    q_ref, k_ref, v_ref, att_ref, first_ref, w_s,
):
    step = pl.program_id(0)
    length, model = x_ref.shape
    width = a_ref.shape[2] // 4
    heads = width // HEAD
    blocks = length // ROWS
    for slot in range(4):
        w_s[slot] = unpack(a_ref.at[0], slot, width)

    @pl.when(step == 0)
    def _():
        first_ref[...] = x_ref[...].astype(F32) + bm_ref[...]

    @pl.loop(0, blocks)
    def _(index):
        rows = rows_of(index)
        x_rows = x_ref[rows, :]
        queries = (dot_nn(x_rows, w_s[0]) + bq_ref[0]).astype(BF16)
        q_ref[0, rows, :] = queries * jnp.asarray(HEAD**-0.5, BF16) + qaug_ref[rows, :]
        keys = dot_nn(x_rows, w_s[1]).astype(BF16)
        k_ref[0, rows, :] = keys + kaug_ref[rows, :]
        values = (dot_nn(x_rows, w_s[2]) + bv_ref[0]).astype(BF16)
        v_ref[0, rows, :] = values + vaug_ref[...]

    @pl.loop(0, blocks)
    def _(index):
        rows = rows_of(index)
        lanes = lane_index((ROWS, PAD))
        queries = q_ref[0, rows, :]
        attended = jnp.zeros((ROWS, PAD), F32)
        extended = queries
        for head in range(heads):
            masked = jnp.where(head_and_extra(lanes, head, width), queries, 0)
            scores = dot_nt(masked, k_ref[0])
            highest = jnp.max(scores, axis=1, keepdims=True)
            raw = jnp.exp2((scores - highest) * LOG2E).astype(BF16)
            mixed = dot_nn(raw, v_ref[0])
            total = mixed[:, width : width + 1]
            attended = jnp.where(head_only(lanes, head), mixed / total, attended)
            parts = three_parts(-(highest + jnp.log(total)))
            for place, part in enumerate(parts):
                here = lanes == width + DOCS + 3 * head + place
                extended = jnp.where(here, jnp.broadcast_to(part, (ROWS, PAD)), extended)
        q_ref[0, rows, :] = extended
        attended = attended.astype(BF16)
        att_ref[0, rows, :] = attended
        first_ref[rows, :] += dot_nt(attended, w_s[3])


def gelu_parts(values):
    phi = jnp.exp2(values * values * (-0.5 * LOG2E)) * 0.3989422804014327
    total = 0.5 + 0.5 * lax.erf(values * 0.7071067811865476)
    return values * total, total + values * phi


def norm_parts(values):
    average = jnp.mean(values, axis=-1, keepdims=True)
    centred = values - average
    spread = jnp.mean(centred * centred, axis=-1, keepdims=True)
    inverse = lax.rsqrt(spread + EPS)
    return centred * inverse, inverse


def norm_back(grads, gain, unit, inverse):
    scaled = grads * gain
    average = jnp.mean(scaled, axis=-1, keepdims=True)
    along = jnp.mean(scaled * unit, axis=-1, keepdims=True)
    return (scaled - average - unit * along) * inverse


def column_sum(values):
    return jnp.sum(values, axis=0, keepdims=True)


def dense_kernel(
    first_in, wi_ref, wo_ref, bi_ref, vec_ref, cot_ref,
    out_ref, dfirst_ref, dmix_ref, gi_ref, go_ref, dbi_ref, small_ref,
    first_ref, second_ref, normed_s, dsec_s, hidden_s, slope_s, low_s, low_t, back_t, dinner_s,
):
    step = pl.program_id(0)
    count = pl.num_programs(0) // 2
    length, model = first_in.shape
    blocks = length // ROWS
    gain_one, bias_one, b_outer, gain_two, bias_two = (vec_ref[i : i + 1, :] for i in range(5))

    @pl.when(step == 0)
    def _():
        copied = pltpu.sync_copy
        copied(first_in, first_ref)

        @pl.loop(0, blocks)
        def _(index):
            rows = rows_of(index)
            unit, _inverse = norm_parts(first_ref[rows, :])
            normed = unit * gain_one + bias_one
            normed_s[rows, :] = normed
            low_s[rows, :] = normed.astype(BF16)
            low_t[:, rows] = normed.astype(BF16).T
            second_ref[rows, :] = normed + b_outer

    @pl.when(step < count)
    def _():
        @pl.loop(0, blocks)
        def _(index):
            rows = rows_of(index)
            inner = dot_nn(low_s[rows, :], wi_ref[0]) + bi_ref[0]
            value, slope = gelu_parts(inner)
            hidden = value.astype(BF16)
            hidden_s[step, rows, :] = hidden
            slope_s[step, rows, :] = slope.astype(BF16)
            second_ref[rows, :] += dot_nt(hidden, wo_ref[0])

    @pl.when(step == count - 1)
    def _():
        small_ref[...] = jnp.zeros_like(small_ref)

        @pl.loop(0, blocks)
        def _(index):
            rows = rows_of(index)
            unit, inverse = norm_parts(second_ref[rows, :])
            out_ref[rows, :] = (unit * gain_two + bias_two).astype(BF16)
            grads = cot_ref[rows, :].astype(F32)
            d_second = norm_back(grads, gain_two, unit, inverse)
            small_ref[0:1, :] += column_sum(d_second)
            small_ref[1:2, :] += column_sum(grads * unit)
            small_ref[2:3, :] += column_sum(grads)
            dsec_s[rows, :] = d_second
            low = d_second.astype(BF16)
            dmix_ref[rows, :] = low
            back_t[:, rows] = low.T

    @pl.when(step >= count)
    def _():
        place = step - count
        dbi_ref[...] = jnp.zeros_like(dbi_ref)

        @pl.loop(0, blocks)
        def _(index):
            rows = rows_of(index)
            d_hidden = dot_nn(dmix_ref[rows, :], wo_ref[0])
            d_inner = (d_hidden * slope_s[place, rows, :].astype(F32)).astype(BF16)
            dinner_s[rows, :] = d_inner
            dbi_ref[0] += column_sum(d_inner.astype(F32))
            dsec_s[rows, :] += dot_nt(d_inner, wi_ref[0])

        @pl.loop(0, model // ROWS)
        def _(index):
            rows = rows_of(index)
            gi_ref[0, rows, :] = dot_nn(low_t[rows, :], dinner_s[...]).astype(gi_ref.dtype)
            go_ref[0, rows, :] = dot_nn(back_t[rows, :], hidden_s[place]).astype(go_ref.dtype)

    @pl.when(step == 2 * count - 1)
    def _():
        @pl.loop(0, blocks)
        def _(index):
            rows = rows_of(index)
            unit, inverse = norm_parts(first_ref[rows, :])
            grads = dsec_s[rows, :]
            d_first = norm_back(grads, gain_one, unit, inverse)
            small_ref[3:4, :] += column_sum(d_first)
            small_ref[4:5, :] += column_sum(grads * unit)
            small_ref[5:6, :] += column_sum(grads)
            dfirst_ref[rows, :] = d_first
            dmix_ref[rows, :] = d_first.astype(BF16)


def attend_back_kernel(
    x_ref, a_ref, dmix_ref, dfirst_ref, q_ref, k_ref, v_ref, att_ref,
    dtok_ref, ga_ref, dbq_ref, dbv_ref,
    w_s, xt_s, dmixt_s, do_s, kt_s, dq_s, dk_s, dv_s, low_s,
):
    step = pl.program_id(0)
    length, model = x_ref.shape
    width = a_ref.shape[2] // 4
    heads = width // HEAD
    blocks = length // ROWS
    for slot in range(4):
        w_s[slot] = unpack(a_ref.at[0], slot, width)

    @pl.when(step == 0)
    def _():
        dtok_ref[...] = dfirst_ref[...]

        @pl.loop(0, blocks)
        def _(index):
            rows = rows_of(index)
            xt_s[:, rows] = x_ref[rows, :].T
            dmixt_s[:, rows] = dmix_ref[rows, :].T

    dk_s[...] = jnp.zeros_like(dk_s)
    dv_s[...] = jnp.zeros_like(dv_s)
    lanes = lane_index((ROWS, PAD))

    @pl.loop(0, blocks)
    def _(index):
        rows = rows_of(index)
        kt_s[:, rows] = k_ref[0, rows, :].T

    @pl.loop(0, blocks)
    def _(index):
        rows = rows_of(index)
        queries = q_ref[0, rows, :]
        d_att = dot_nn(dmix_ref[rows, :], w_s[3]).astype(BF16)
        product = d_att.astype(F32) * att_ref[0, rows, :].astype(F32)
        extended = d_att
        for head in range(heads):
            centre = jnp.sum(jnp.where(head_only(lanes, head), product, 0.0), axis=1, keepdims=True)
            for place, part in enumerate(three_parts(-centre)):
                here = lanes == width + DOCS + 3 * head + place
                extended = jnp.where(here, jnp.broadcast_to(part, (ROWS, PAD)), extended)
        chances_all = []
        d_scores_all = []
        d_att_all = []
        queries_all = []
        for head in range(heads):
            wide = head_and_extra(lanes, head, width)
            only = head_only(lanes, head)
            chances = jnp.exp2(dot_nt(k_ref[0], jnp.where(wide, queries, 0)) * LOG2E)
            d_chances = dot_nt(v_ref[0], jnp.where(wide, extended, 0))
            d_scores = (chances * d_chances).astype(BF16)
            chances_all.append(chances.astype(BF16))
            d_scores_all.append(d_scores)
            d_att_all.append(jnp.where(only, d_att, 0))
            queries_all.append(jnp.where(only, queries, 0))
            head_rows = slice(head * HEAD, (head + 1) * HEAD)
            dq_s[head_rows, rows] = dot_nn(kt_s[head_rows, :], d_scores)
        dv_s[...] += dot_nn(jnp.concatenate(chances_all, 1), jnp.concatenate(d_att_all, 0))
        dk_s[...] += dot_nn(jnp.concatenate(d_scores_all, 1), jnp.concatenate(queries_all, 0))

    dbq_ref[...] = jnp.zeros_like(dbq_ref)
    dbv_ref[...] = jnp.zeros_like(dbv_ref)

    @pl.loop(0, blocks)
    def _(index):
        rows = rows_of(index)
        d_query = (dq_s[:, rows].T * HEAD**-0.5).astype(BF16)
        d_query = jnp.where(lane_index(d_query.shape) < width, d_query, 0)
        d_key = dk_s[rows, :].astype(BF16)
        d_value = dv_s[rows, :].astype(BF16)
        low_s[0, rows, :] = d_query
        low_s[1, rows, :] = d_key
        low_s[2, rows, :] = d_value
        dbq_ref[0] += column_sum(d_query.astype(F32))
        dbv_ref[0] += column_sum(d_value.astype(F32))
        dtok_ref[rows, :] += (
            dot_nt(d_query, w_s[0]) + dot_nt(d_key, w_s[1]) + dot_nt(d_value, w_s[2])
        )

    @pl.loop(0, model // ROWS)
    def _(index):
        rows = rows_of(index)
        parts = [dot_nn(xt_s[rows, :], low_s[slot])[:, :width] for slot in range(3)]
        parts.append(dot_nn(dmixt_s[rows, :], att_ref[0])[:, :width])
        ga_ref[0, rows, :] = jnp.concatenate(parts, axis=1).astype(ga_ref.dtype)


VMEM_LIMIT = 60 * 1024 * 1024


def resident(shape):
    return pl.BlockSpec(shape, lambda step: (0,) * len(shape))


def stepped(shape):
    return pl.BlockSpec((1,) + shape[1:], lambda step: (step,) + (0,) * (len(shape) - 1))


def spec_list(pairs):
    return [stepped(shape) if moves else resident(shape) for shape, moves in pairs]


def attend_forward(x, a_all, bq, bv, qaug, kaug, vaug, b_mixer):
    length, model = x.shape
    groups = a_all.shape[0]
    block = (groups, length, PAD)
    return pl.pallas_call(
        attend_kernel,
        grid=(groups,),
        out_shape=[jax.ShapeDtypeStruct(block, BF16)] * 4 + [jax.ShapeDtypeStruct(x.shape, F32)],
        in_specs=spec_list(
            [
                (x.shape, 0), (a_all.shape, 1), (bq.shape, 1), (bv.shape, 1),
                (qaug.shape, 0), (kaug.shape, 0), (vaug.shape, 0), (b_mixer.shape, 0),
            ]
        ),
        out_specs=spec_list([(block, 1)] * 4 + [(x.shape, 0)]),
        scratch_shapes=[pltpu.VMEM((4, model, PAD), BF16)],
        compiler_params=pltpu.CompilerParams(vmem_limit_bytes=VMEM_LIMIT),
        name="attend_forward",
    )(x, a_all, bq, bv, qaug, kaug, vaug, b_mixer)


def dense_both(first_sum, wi, wo, bi, vectors, cotangent):
    length, model = first_sum.shape
    groups, _, hidden = wi.shape
    grad = (groups, model, hidden)
    forth = lambda shape: pl.BlockSpec(
        (1,) + shape[1:], lambda step: (lax.rem(step, groups),) + (0,) * (len(shape) - 1)
    )
    late = lambda shape: pl.BlockSpec(
        (1,) + shape[1:], lambda step: (jnp.maximum(step - groups, 0),) + (0,) * (len(shape) - 1)
    )
    return pl.pallas_call(
        dense_kernel,
        grid=(2 * groups,),
        out_shape=[
            jax.ShapeDtypeStruct((length, model), BF16),
            jax.ShapeDtypeStruct((length, model), F32),
            jax.ShapeDtypeStruct((length, model), BF16),
            jax.ShapeDtypeStruct(grad, BF16),
            jax.ShapeDtypeStruct(grad, BF16),
            jax.ShapeDtypeStruct((groups, 1, hidden), F32),
            jax.ShapeDtypeStruct((8, model), F32),
        ],
        in_specs=[
            pl.BlockSpec(memory_space=pl.ANY), forth(wi.shape), forth(wo.shape), forth(bi.shape),
            resident(vectors.shape), resident(cotangent.shape),
        ],
        out_specs=[
            resident((length, model)), resident((length, model)), resident((length, model)),
            late(grad), late(grad), late((groups, 1, hidden)), resident((8, model)),
        ],
        scratch_shapes=[
            pltpu.VMEM((length, model), F32),
            pltpu.VMEM((length, model), F32),
            pltpu.VMEM((length, model), F32),
            pltpu.VMEM((length, model), F32),
            pltpu.VMEM((groups, length, hidden), BF16),
            pltpu.VMEM((groups, length, hidden), BF16),
            pltpu.VMEM((length, model), BF16),
            pltpu.VMEM((model, length), BF16),
            pltpu.VMEM((model, length), BF16),
            pltpu.VMEM((length, hidden), BF16),
        ],
        compiler_params=pltpu.CompilerParams(vmem_limit_bytes=VMEM_LIMIT),
        name="dense_both",
    )(first_sum, wi, wo, bi, vectors, cotangent)


def attend_backward(x, a_all, d_mixed, d_first, q, k, v, attended):
    length, model = x.shape
    groups = a_all.shape[0]
    sums = (groups, 1, PAD)
    return pl.pallas_call(
        attend_back_kernel,
        grid=(groups,),
        out_shape=[
            jax.ShapeDtypeStruct(x.shape, F32),
            jax.ShapeDtypeStruct(a_all.shape, BF16),
            jax.ShapeDtypeStruct(sums, F32),
            jax.ShapeDtypeStruct(sums, F32),
        ],
        in_specs=spec_list(
            [
                (x.shape, 0), (a_all.shape, 1), (d_mixed.shape, 0), (d_first.shape, 0),
                (q.shape, 1), (k.shape, 1), (v.shape, 1), (attended.shape, 1),
            ]
        ),
        out_specs=spec_list([(x.shape, 0), (a_all.shape, 1), (sums, 1), (sums, 1)]),
        scratch_shapes=[
            pltpu.VMEM((4, model, PAD), BF16),
            pltpu.VMEM((model, length), BF16),
            pltpu.VMEM((model, length), BF16),
            pltpu.VMEM((length, PAD), BF16),
            pltpu.VMEM((PAD, length), BF16),
            pltpu.VMEM((PAD, length), F32),
            pltpu.VMEM((length, PAD), F32),
            pltpu.VMEM((length, PAD), F32),
            pltpu.VMEM((3, length, PAD), BF16),
        ],
        compiler_params=pltpu.CompilerParams(vmem_limit_bytes=VMEM_LIMIT),
        name="attend_backward",
    )(x, a_all, d_mixed, d_first, q, k, v, attended)


def augment(labels, width):
    length = labels.shape[0]
    lanes = lax.broadcasted_iota(jnp.int32, (length, PAD), 1)
    in_docs = (lanes >= width) & (lanes < width + DOCS)
    same = (lanes - width) == labels[:, None]
    qaug = jnp.where(in_docs & same, 1.0, 0.0).astype(BF16)
    spare = (lanes >= width + DOCS) & (lanes < width + DOCS + 3 * (width // HEAD))
    kaug = jnp.where(in_docs & ~same, -(2.0**100), jnp.where(spare, 1.0, 0.0)).astype(BF16)
    vaug = jnp.where((lanes[:1] == width) | spare[:1], 1.0, 0.0).astype(BF16)
    return qaug, kaug, vaug


def pad_groups(vector, groups, width):
    parts = vector.reshape(groups, 1, width)
    return jnp.pad(parts, ((0, 0), (0, 0), (0, PAD - width)))


def one_sequence(x, labels, a_all, wi, wo, bq, bv, bi, b_mixer, vectors, cotangent):
    groups = a_all.shape[0]
    width = a_all.shape[2] // 4
    qaug, kaug, vaug = augment(labels, width)
    q, k, v, attended, first_sum = attend_forward(
        x, a_all, pad_groups(bq, groups, width), pad_groups(bv, groups, width),
        qaug, kaug, vaug, b_mixer[None],
    )
    out, d_first, d_mixed, g_inner, g_outer, db_inner, small = dense_both(
        first_sum, wi, wo, bi.reshape(groups, 1, -1), vectors, cotangent
    )
    d_tokens, g_attend, dbq, dbv = attend_backward(
        x, a_all, d_mixed, d_first, q, k, v, attended
    )
    return (
        out, d_tokens, g_attend, g_inner, g_outer,
        dbq[:, 0, :width], dbv[:, 0, :width], db_inner[:, 0], small,
    )


def body(
    tokens, doc_ids, w_query, b_query, w_key, w_value, b_value, w_mixer, b_mixer, gain_one,
    bias_one, w_inner, b_inner, w_outer, b_outer, gain_two, bias_two, cotangent,
):
    groups = lax.axis_size("tensor")
    place = lax.axis_index("tensor")
    width = w_query.shape[1]
    hidden = w_inner.shape[1]
    length = doc_ids.shape[2]
    model = tokens.shape[3]

    def to_sequence(part):
        return lax.all_to_all(part, "tensor", 0, 2, tiled=True).reshape(length, model)

    def from_sequence(whole):
        return lax.all_to_all(whole.reshape(1, 1, length, model), "tensor", 2, 0, tiled=True)

    x = to_sequence(tokens)
    cot = to_sequence(cotangent)
    labels = lax.dynamic_index_in_dim(doc_ids[:, 0], place, 0, keepdims=False)
    shard_a = jnp.concatenate([w_query, w_key, w_value, w_mixer.T], axis=1)

    def gather(shard):
        whole = lax.all_gather(shard, ("tensor", "dp"), axis=0, tiled=True)
        return whole.reshape(groups, model, shard.shape[1])

    a_all = gather(shard_a)
    wi = gather(w_inner)
    wo = gather(w_outer.T)
    biases = lax.all_gather(jnp.concatenate([b_query, b_value, b_inner]), "tensor", axis=0)
    bq = biases[:, :width].reshape(-1)
    bv = biases[:, width : 2 * width].reshape(-1)
    bi = biases[:, 2 * width :].reshape(-1)
    vectors = jnp.stack([gain_one, bias_one, b_outer, gain_two, bias_two] + [b_outer] * 3)
    out, d_tokens, g_attend, g_inner, g_outer, dbq, dbv, dbi, small = one_sequence(
        x, labels, a_all, wi, wo, bq, bv, bi, b_mixer, vectors, cot
    )

    def scatter(grads):
        flat = grads.reshape(-1, grads.shape[2])
        return lax.psum_scatter(flat, ("tensor", "dp"), scatter_dimension=0, tiled=True)

    ga = scatter(g_attend).astype(F32)
    gi = scatter(g_inner).astype(F32)
    go = scatter(g_outer).astype(F32)
    summed = lax.psum(
        jnp.concatenate([dbq.reshape(-1), dbv.reshape(-1), dbi.reshape(-1), small.reshape(-1)]),
        ("dp", "tensor"),
    )
    mine = lambda start, size: lax.dynamic_slice_in_dim(summed, start + place * size, size)
    tail = summed[2 * model + dbi.size :].reshape(8, model)
    return (
        from_sequence(out),
        from_sequence(d_tokens),
        ga[:, :width],
        mine(0, width),
        ga[:, width : 2 * width],
        ga[:, 2 * width : 3 * width],
        mine(model, width),
        ga[:, 3 * width :].T,
        tail[3],
        tail[4],
        tail[5],
        gi,
        mine(2 * model, hidden),
        go.T,
        tail[0],
        tail[1],
        tail[2],
    )


def solution(mesh):
    split = P(None, "dp", "tensor", None)
    both, flipped, part = P("dp", "tensor"), P("tensor", "dp"), P("tensor")
    return jax.shard_map(
        body,
        mesh=mesh,
        in_specs=(
            split, P(None, "dp", None), both, part, both, both, part, flipped, P(), P(), P(),
            both, part, flipped, P(), P(), P(), split,
        ),
        out_specs=(
            split, split, both, part, both, both, part, flipped, P(), P(), P(), both, part,
            flipped, P(), P(), P(),
        ),
        check_vma=False,
    )
```

```python
from functools import partial

import jax
import jax.numpy as jnp
from jax import lax
from jax.experimental import pallas as pl
from jax.experimental.pallas import tpu as pltpu
from jax.sharding import PartitionSpec as P

HEAD = 64
DOCS = 8
PAD = 256
ROWS = 256
LOG2E = 1.4426950408889634
EPS = 1e-12
F32 = jnp.float32
BF16 = jnp.bfloat16


def dot_nn(left, right):
    return lax.dot_general(left, right, (((1,), (0,)), ((), ())), preferred_element_type=F32)


def dot_nt(left, right):
    return lax.dot_general(left, right, (((1,), (1,)), ((), ())), preferred_element_type=F32)


def rows_of(index, size=ROWS):
    return pl.ds(pl.multiple_of(index * size, size), size)


def lane_index(shape):
    return lax.broadcasted_iota(jnp.int32, shape, 1)


def three_parts(values):
    high = values.astype(BF16)
    rest = values - high.astype(F32)
    middle = rest.astype(BF16)
    low = (rest - middle.astype(F32)).astype(BF16)
    return high, middle, low


def head_only(lanes, head):
    return (lanes >= head * HEAD) & (lanes < (head + 1) * HEAD)


def head_and_extra(lanes, head, width):
    extra = width + DOCS + 3 * head
    return (
        head_only(lanes, head)
        | ((lanes >= width) & (lanes < width + DOCS))
        | ((lanes >= extra) & (lanes < extra + 3))
    )


def unpack(block_ref, slot, width):
    part = block_ref[:, slot * width : (slot + 1) * width]
    return jnp.concatenate([part, jnp.zeros((part.shape[0], PAD - width), part.dtype)], axis=1)


def project(x_rows, rows, bq, bv, w_s, qaug_ref, kaug_ref, vaug_ref, q_ref, k_ref, v_ref):
    queries = (dot_nn(x_rows, w_s[0]) + bq).astype(BF16)
    q_ref[0, rows, :] = queries * jnp.asarray(HEAD**-0.5, BF16) + qaug_ref[rows, :]
    keys = dot_nn(x_rows, w_s[1]).astype(BF16)
    k_ref[0, rows, :] = keys + kaug_ref[rows, :]
    values = (dot_nn(x_rows, w_s[2]) + bv).astype(BF16)
    v_ref[0, rows, :] = values + vaug_ref[...]


def attend_rows(rows, width, w_s, q_ref, k_ref, v_ref, att_ref, first_ref):
    lanes = lane_index((ROWS, PAD))
    queries = q_ref[0, rows, :]
    attended = jnp.zeros((ROWS, PAD), F32)
    extended = queries
    for head in range(width // HEAD):
        masked = jnp.where(head_and_extra(lanes, head, width), queries, 0)
        scores = dot_nt(masked, k_ref[0])
        highest = jnp.max(scores, axis=1, keepdims=True)
        raw = jnp.exp2((scores - highest) * LOG2E).astype(BF16)
        mixed = dot_nn(raw, v_ref[0])
        total = mixed[:, width : width + 1]
        attended = jnp.where(head_only(lanes, head), mixed / total, attended)
        for spot, part in enumerate(three_parts(-(highest + jnp.log(total)))):
            here = lanes == width + DOCS + 3 * head + spot
            extended = jnp.where(here, jnp.broadcast_to(part, (ROWS, PAD)), extended)
    q_ref[0, rows, :] = extended
    attended = attended.astype(BF16)
    att_ref[0, rows, :] = attended
    first_ref[rows, :] += dot_nt(attended, w_s[3])


def attend_plain_kernel(
    x_ref, a_ref, bias_ref, qaug_ref, kaug_ref, vaug_ref, bm_ref,
    q_ref, k_ref, v_ref, att_ref, first_ref, w_s,
):
    length, model = x_ref.shape
    width = a_ref.shape[2] // 4
    for slot in range(4):
        w_s[slot] = unpack(a_ref.at[0], slot, width)
    biases = bias_ref[0]

    @pl.when(pl.program_id(0) == 0)
    def _():
        first_ref[...] = x_ref[...].astype(F32) + bm_ref[...]

    @pl.loop(0, length // ROWS)
    def _(index):
        rows = rows_of(index)
        project(
            x_ref[rows, :], rows, biases[:, :PAD], biases[:, PAD : 2 * PAD], w_s, qaug_ref,
            kaug_ref, vaug_ref, q_ref, k_ref, v_ref,
        )

    @pl.loop(0, length // ROWS)
    def _(index):
        attend_rows(rows_of(index), width, w_s, q_ref, k_ref, v_ref, att_ref, first_ref)


MESH = pl.DeviceIdType.MESH


def partner(index, bits, size):
    flipped = index
    for bit in (1, 2, 4):
        if bits & bit and bit < size:
            flipped = flipped + bit - 2 * bit * lax.rem(lax.div(index, bit), 2)
    return flipped


class Wires:
    def __init__(self, send, recv, place, row):
        self.send, self.recv, self.place, self.row = send, recv, place, row

    def to(self, tensor_bits, dp_bits):
        return (partner(self.row, dp_bits, 8), partner(self.place, tensor_bits, 4))

    def copy(self, number, source, target, tensor_bits=0, dp_bits=0):
        return pltpu.make_async_remote_copy(
            src_ref=source,
            dst_ref=target,
            send_sem=self.send.at[number],
            recv_sem=self.recv.at[number],
            device_id=self.to(tensor_bits, dp_bits),
            device_id_type=MESH,
        )


def greet(wires, peers):
    barrier = pltpu.get_barrier_semaphore()
    for tensor_bits, dp_bits in peers:
        pl.semaphore_signal(
            barrier, inc=1, device_id=wires.to(tensor_bits, dp_bits), device_id_type=MESH
        )
    pl.semaphore_wait(barrier, len(peers))


PEERS = ((1, 0), (2, 0), (3, 0), (0, 1), (0, 2), (0, 4), (0, 6))
TOKENS, COTS, BIASES, KIND_A = 0, 3, 6, 9
KIND_I = KIND_A + 17
KIND_O = KIND_I + 17
FORWARD_WIRES = KIND_O + 10


class ShardGather:
    def __init__(self, wires, base, shard, whole):
        self.wires, self.base, self.shard, self.whole = wires, base, shard, whole

    def at(self, slot, dp_bits):
        return self.whole.at[slot, partner(self.wires.row, dp_bits, 8)]

    def cross_x(self):
        return self.wires.copy(self.base, self.shard, self.at(2, 0), 2, 0)

    def along_z(self, slot, step, mine):
        source = self.shard if slot == 0 else self.at(slot, 0)
        number = self.base + 1 + 3 * (slot // 2) + step - 1
        target = self.at(slot, 0) if mine else self.at(slot, 2 * step)
        return self.wires.copy(number, source, target, 0, 2 * step)

    def along_y(self, slot, step, mine):
        source = self.shard if slot == 0 and step == 0 else self.at(slot, 2 * step)
        number = self.base + 7 + 4 * (slot // 2) + step
        target = self.at(slot, 2 * step) if mine else self.at(slot, 2 * step + 1)
        return self.wires.copy(number, source, target, 0, 1)

    def to_core(self, slot, mine):
        number = self.base + 15 + slot // 2
        target = self.whole.at[slot + 1]
        return self.wires.copy(number, self.whole.at[slot], target, 1, 0)

    def start_z(self, slot):
        for step in (1, 2, 3):
            self.along_z(slot, step, True).start()

    def wait_z(self, slot):
        for step in (1, 2, 3):
            self.along_z(slot, step, False).wait_recv()

    def pass_y(self, slot):
        for step in (1, 2, 3):
            self.along_y(slot, step, True).start()

    def wait_y(self, slot):
        for step in range(4):
            self.along_y(slot, step, False).wait_recv()

    def wait_sent(self, x_first=True):
        for slot in (0, 2) if x_first else (0,):
            for step in (1, 2, 3):
                self.along_z(slot, step, True).wait_send()
            for step in range(4):
                self.along_y(slot, step, True).wait_send()
        for slot in (0, 2):
            self.to_core(slot, True).wait_send()


class BlockGather(ShardGather):
    def along_z(self, slot, step, mine):
        target = self.at(0, 0) if mine else self.at(0, 2 * step)
        return self.wires.copy(self.base + step - 1, self.shard, target, 0, 2 * step)

    def along_y(self, slot, step, mine):
        source = self.shard if step == 0 else self.at(0, 2 * step)
        target = self.at(0, 2 * step) if mine else self.at(0, 2 * step + 1)
        return self.wires.copy(self.base + 3 + step, source, target, 0, 1)

    def cross_x(self):
        return self.wires.copy(self.base + 7, self.whole.at[0], self.whole.at[2], 2, 0)

    def to_core(self, slot, mine):
        return self.wires.copy(
            self.base + 8 + slot // 2, self.whole.at[slot], self.whole.at[slot + 1], 1, 0
        )


def attend_kernel(
    tok_ref, cot_ref, sa_ref, si_ref, so_ref, bias_ref, qaug_ref, kaug_ref, vaug_ref, bm_ref,
    q_ref, k_ref, v_ref, att_ref, first_ref, bi_ref, x_out, cot_out, a_out, wi_out, wo_out,
    w_s, x_s, a_s, bias_s, send_sem, recv_sem, here_sem,
):
    step = pl.program_id(0)
    place = lax.axis_index("tensor")
    row = lax.axis_index("dp")
    quarters, part, model = x_s.shape
    length = quarters * part
    width = sa_ref.shape[1] // 4
    blocks = length // ROWS
    share = sa_ref.shape[0]
    wires = Wires(send_sem, recv_sem, place, row)
    attn = ShardGather(wires, KIND_A, sa_ref, a_s)
    inner = ShardGather(wires, KIND_I, si_ref, wi_out)
    outer = BlockGather(wires, KIND_O, so_ref, wo_out)

    def exchange(base, source, target, bits, mine):
        other = partner(place, bits, 4)
        return wires.copy(
            base + bits - 1, source.at[other], target.at[place if mine else other], bits, 0
        )

    def bias_copy(bits, mine):
        return wires.copy(BIASES + bits - 1, bias_ref, bias_s.at[bits], bits, 0)

    local = [
        pltpu.make_async_copy(tok_ref.at[place], x_s.at[place], here_sem.at[0]),
        pltpu.make_async_copy(sa_ref, a_s.at[0, row], here_sem.at[1]),
        pltpu.make_async_copy(si_ref, wi_out.at[0, row], here_sem.at[2]),
        pltpu.make_async_copy(so_ref, wo_out.at[0, row], here_sem.at[3]),
        pltpu.make_async_copy(cot_ref.at[place], cot_out.at[place], here_sem.at[4]),
        pltpu.make_async_copy(bias_ref, bias_s.at[0], here_sem.at[5]),
    ]
    keep_x = pltpu.make_async_copy(x_s, x_out, here_sem.at[6])
    keep_a = pltpu.make_async_copy(a_s, a_out, here_sem.at[7])

    @pl.when(step == 0)
    def _():
        greet(wires, PEERS)
        attn.cross_x().start()
        for bits in (1, 2, 3):
            bias_copy(bits, True).start()
        attn.start_z(0)
        attn.along_y(0, 0, True).start()
        for bits in (2, 3, 1):
            exchange(TOKENS, tok_ref, x_s, bits, True).start()
        for copy in local:
            copy.start()
        for copy in local:
            copy.wait()
        attn.cross_x().wait_recv()
        attn.start_z(2)
        attn.along_y(2, 0, True).start()
        attn.wait_z(0)
        attn.pass_y(0)
        attn.wait_y(0)
        attn.to_core(0, True).start()
        for bits in (1, 2, 3):
            exchange(TOKENS, tok_ref, x_s, bits, False).wait_recv()
            bias_copy(bits, False).wait_recv()
        keep_x.start()

        @pl.loop(0, quarters)
        def _(index):
            rows = rows_of(index, part)
            first_ref[rows, :] = x_s[index].astype(F32) + bm_ref[...]

    @pl.when(step == 1)
    def _():
        attn.to_core(0, False).wait_recv()

    @pl.when(step == 2)
    def _():
        attn.wait_y(2)
        attn.to_core(2, True).start()

    @pl.when(step == 3)
    def _():
        attn.to_core(2, False).wait_recv()
        keep_a.start()

    for dp_row in range(a_s.shape[1]):
        packed = a_s[step, dp_row]
        rest = jnp.zeros((share, PAD - width), packed.dtype)
        for slot in range(4):
            piece = packed[:, slot * width : (slot + 1) * width]
            rows = slice(dp_row * share, (dp_row + 1) * share)
            w_s[slot, rows, :] = jnp.concatenate([piece, rest], axis=1)
    biases = bias_s[step]
    bi_ref[0] = biases[:, 2 * PAD :]

    @pl.loop(0, quarters)
    def _(index):
        rows = rows_of(index, part)
        x_rows = x_s[index]
        project(
            x_rows, rows, biases[:, :PAD], biases[:, PAD : 2 * PAD], w_s, qaug_ref, kaug_ref,
            vaug_ref, q_ref, k_ref, v_ref,
        )

    @pl.loop(0, blocks)
    def _(index):
        attend_rows(rows_of(index), width, w_s, q_ref, k_ref, v_ref, att_ref, first_ref)

        @pl.when((step == 0) & (index == 1))
        def _():
            attn.wait_z(2)
            attn.pass_y(2)
            outer.start_z(0)
            outer.along_y(0, 0, True).start()
            inner.cross_x().start()
            for bits in (2, 3, 1):
                exchange(COTS, cot_ref, cot_out, bits, True).start()

        @pl.when((step == 0) & (index == 3))
        def _():
            inner.cross_x().wait_recv()
            inner.start_z(0)
            inner.along_y(0, 0, True).start()
            inner.start_z(2)
            inner.along_y(2, 0, True).start()

        @pl.when((step == 1) & (index == 2))
        def _():
            outer.wait_z(0)
            outer.pass_y(0)

        @pl.when((step == 2) & (index == 1))
        def _():
            outer.wait_y(0)
            outer.cross_x().start()
            outer.to_core(0, True).start()

        @pl.when((step == 3) & (index == 0))
        def _():
            inner.wait_z(0)
            inner.pass_y(0)

        @pl.when((step == 3) & (index == 2))
        def _():
            inner.wait_z(2)
            inner.pass_y(2)

    @pl.when(step == 3)
    def _():
        inner.wait_y(0)
        inner.to_core(0, True).start()
        inner.wait_y(2)
        inner.to_core(2, True).start()
        outer.cross_x().wait_recv()
        outer.to_core(2, True).start()
        for bits in (1, 2, 3):
            exchange(COTS, cot_ref, cot_out, bits, False).wait_recv()
        for gather in (inner, outer):
            for slot in (0, 2):
                gather.to_core(slot, False).wait_recv()
        for gather in (attn, inner, outer):
            gather.cross_x().wait_send()
            gather.wait_sent(gather is not outer)
        for bits in (1, 2, 3):
            exchange(TOKENS, tok_ref, x_s, bits, True).wait_send()
            exchange(COTS, cot_ref, cot_out, bits, True).wait_send()
            bias_copy(bits, True).wait_send()
        keep_x.wait()
        keep_a.wait()


def gelu_parts(values):
    phi = jnp.exp2(values * values * (-0.5 * LOG2E)) * 0.3989422804014327
    total = 0.5 + 0.5 * lax.erf(values * 0.7071067811865476)
    return values * total, total + values * phi


def norm_parts(values):
    average = jnp.mean(values, axis=-1, keepdims=True)
    centred = values - average
    spread = jnp.mean(centred * centred, axis=-1, keepdims=True)
    inverse = lax.rsqrt(spread + EPS)
    return centred * inverse, inverse


def norm_back(grads, gain, unit, inverse):
    scaled = grads * gain
    average = jnp.mean(scaled, axis=-1, keepdims=True)
    along = jnp.mean(scaled * unit, axis=-1, keepdims=True)
    return (scaled - average - unit * along) * inverse


def column_sum(values):
    return jnp.sum(values, axis=0, keepdims=True)


def dense_kernel(
    first_in, wi_ref, wo_ref, bi_ref, vec_ref, cot_ref,
    out_ref, dfirst_ref, dmix_ref, gi_ref, go_ref, dbi_ref, small_ref,
    first_ref, second_ref, normed_s, dsec_s, hidden_s, slope_s, low_s, low_t, back_t, dinner_s,
):
    step = pl.program_id(0)
    count = pl.num_programs(0) // 2
    length, model = first_in.shape
    blocks = length // ROWS
    gain_one, bias_one, b_outer, gain_two, bias_two = (vec_ref[i : i + 1, :] for i in range(5))

    @pl.when(step == 0)
    def _():
        copied = pltpu.sync_copy
        copied(first_in, first_ref)

        @pl.loop(0, blocks)
        def _(index):
            rows = rows_of(index)
            unit, _inverse = norm_parts(first_ref[rows, :])
            normed = unit * gain_one + bias_one
            normed_s[rows, :] = normed
            low_s[rows, :] = normed.astype(BF16)
            low_t[:, rows] = normed.astype(BF16).T
            second_ref[rows, :] = normed + b_outer

    @pl.when(step < count)
    def _():
        @pl.loop(0, blocks)
        def _(index):
            rows = rows_of(index)
            inner = dot_nn(low_s[rows, :], wi_ref[0]) + bi_ref[0]
            value, slope = gelu_parts(inner)
            hidden = value.astype(BF16)
            hidden_s[step, rows, :] = hidden
            slope_s[step, rows, :] = slope.astype(BF16)
            second_ref[rows, :] += dot_nt(hidden, wo_ref[0])

    @pl.when(step == count - 1)
    def _():
        small_ref[...] = jnp.zeros_like(small_ref)

        @pl.loop(0, blocks)
        def _(index):
            rows = rows_of(index)
            unit, inverse = norm_parts(second_ref[rows, :])
            out_ref[rows, :] = (unit * gain_two + bias_two).astype(BF16)
            grads = cot_ref[rows, :].astype(F32)
            d_second = norm_back(grads, gain_two, unit, inverse)
            small_ref[0:1, :] += column_sum(d_second)
            small_ref[1:2, :] += column_sum(grads * unit)
            small_ref[2:3, :] += column_sum(grads)
            dsec_s[rows, :] = d_second
            low = d_second.astype(BF16)
            dmix_ref[rows, :] = low
            back_t[:, rows] = low.T

    @pl.when(step >= count)
    def _():
        place = step - count
        dbi_ref[...] = jnp.zeros_like(dbi_ref)

        @pl.loop(0, blocks)
        def _(index):
            rows = rows_of(index)
            d_hidden = dot_nn(dmix_ref[rows, :], wo_ref[0])
            d_inner = (d_hidden * slope_s[place, rows, :].astype(F32)).astype(BF16)
            dinner_s[rows, :] = d_inner
            dbi_ref[0] += column_sum(d_inner.astype(F32))
            dsec_s[rows, :] += dot_nt(d_inner, wi_ref[0])

        @pl.loop(0, model // ROWS)
        def _(index):
            rows = rows_of(index)
            gi_ref[0, rows, :] = dot_nn(low_t[rows, :], dinner_s[...]).astype(gi_ref.dtype)
            go_ref[0, rows, :] = dot_nn(back_t[rows, :], hidden_s[place]).astype(go_ref.dtype)

    @pl.when(step == 2 * count - 1)
    def _():
        @pl.loop(0, blocks)
        def _(index):
            rows = rows_of(index)
            unit, inverse = norm_parts(first_ref[rows, :])
            grads = dsec_s[rows, :]
            d_first = norm_back(grads, gain_one, unit, inverse)
            small_ref[3:4, :] += column_sum(d_first)
            small_ref[4:5, :] += column_sum(grads * unit)
            small_ref[5:6, :] += column_sum(grads)
            dfirst_ref[rows, :] = d_first
            dmix_ref[rows, :] = d_first.astype(BF16)


def attend_back_kernel(
    x_ref, a_ref, dmix_ref, dfirst_ref, q_ref, k_ref, v_ref, att_ref,
    dtok_ref, ga_ref, dbq_ref, dbv_ref,
    w_s, xt_s, dmixt_s, do_s, kt_s, dq_s, dk_s, dv_s, low_s,
):
    step = pl.program_id(0)
    length, model = x_ref.shape
    width = a_ref.shape[2] // 4
    heads = width // HEAD
    blocks = length // ROWS
    for slot in range(4):
        w_s[slot] = unpack(a_ref.at[0], slot, width)

    @pl.when(step == 0)
    def _():
        dtok_ref[...] = dfirst_ref[...]

        @pl.loop(0, blocks)
        def _(index):
            rows = rows_of(index)
            xt_s[:, rows] = x_ref[rows, :].T
            dmixt_s[:, rows] = dmix_ref[rows, :].T

    dk_s[...] = jnp.zeros_like(dk_s)
    dv_s[...] = jnp.zeros_like(dv_s)
    lanes = lane_index((ROWS, PAD))

    @pl.loop(0, blocks)
    def _(index):
        rows = rows_of(index)
        kt_s[:, rows] = k_ref[0, rows, :].T

    @pl.loop(0, blocks)
    def _(index):
        rows = rows_of(index)
        queries = q_ref[0, rows, :]
        d_att = dot_nn(dmix_ref[rows, :], w_s[3]).astype(BF16)
        product = d_att.astype(F32) * att_ref[0, rows, :].astype(F32)
        extended = d_att
        for head in range(heads):
            centre = jnp.sum(jnp.where(head_only(lanes, head), product, 0.0), axis=1, keepdims=True)
            for place, part in enumerate(three_parts(-centre)):
                here = lanes == width + DOCS + 3 * head + place
                extended = jnp.where(here, jnp.broadcast_to(part, (ROWS, PAD)), extended)
        chances_all = []
        d_scores_all = []
        d_att_all = []
        queries_all = []
        for head in range(heads):
            wide = head_and_extra(lanes, head, width)
            only = head_only(lanes, head)
            chances = jnp.exp2(dot_nt(k_ref[0], jnp.where(wide, queries, 0)) * LOG2E)
            d_chances = dot_nt(v_ref[0], jnp.where(wide, extended, 0))
            d_scores = (chances * d_chances).astype(BF16)
            chances_all.append(chances.astype(BF16))
            d_scores_all.append(d_scores)
            d_att_all.append(jnp.where(only, d_att, 0))
            queries_all.append(jnp.where(only, queries, 0))
            head_rows = slice(head * HEAD, (head + 1) * HEAD)
            dq_s[head_rows, rows] = dot_nn(kt_s[head_rows, :], d_scores)
        dv_s[...] += dot_nn(jnp.concatenate(chances_all, 1), jnp.concatenate(d_att_all, 0))
        dk_s[...] += dot_nn(jnp.concatenate(d_scores_all, 1), jnp.concatenate(queries_all, 0))

    dbq_ref[...] = jnp.zeros_like(dbq_ref)
    dbv_ref[...] = jnp.zeros_like(dbv_ref)

    @pl.loop(0, blocks)
    def _(index):
        rows = rows_of(index)
        d_query = (dq_s[:, rows].T * HEAD**-0.5).astype(BF16)
        d_query = jnp.where(lane_index(d_query.shape) < width, d_query, 0)
        d_key = dk_s[rows, :].astype(BF16)
        d_value = dv_s[rows, :].astype(BF16)
        low_s[0, rows, :] = d_query
        low_s[1, rows, :] = d_key
        low_s[2, rows, :] = d_value
        dbq_ref[0] += column_sum(d_query.astype(F32))
        dbv_ref[0] += column_sum(d_value.astype(F32))
        dtok_ref[rows, :] += (
            dot_nt(d_query, w_s[0]) + dot_nt(d_key, w_s[1]) + dot_nt(d_value, w_s[2])
        )

    @pl.loop(0, model // ROWS)
    def _(index):
        rows = rows_of(index)
        parts = [dot_nn(xt_s[rows, :], low_s[slot])[:, :width] for slot in range(3)]
        parts.append(dot_nn(dmixt_s[rows, :], att_ref[0])[:, :width])
        ga_ref[0, rows, :] = jnp.concatenate(parts, axis=1).astype(ga_ref.dtype)


VMEM_LIMIT = 60 * 1024 * 1024


def resident(shape):
    return pl.BlockSpec(shape, lambda step: (0,) * len(shape))


def stepped(shape):
    return pl.BlockSpec((1,) + shape[1:], lambda step: (step,) + (0,) * (len(shape) - 1))


def spec_list(pairs):
    return [stepped(shape) if moves else resident(shape) for shape, moves in pairs]


def attend_forward(tokens, cotangent, shard_a, shard_i, shard_o, biases, qaug, kaug, vaug, b_mixer):
    groups, part, model = tokens.shape
    length = groups * part
    share = shard_a.shape[0]
    block = (groups, length, PAD)
    whole = jax.ShapeDtypeStruct((groups, model // share, share, model), BF16)
    hidden = shard_i.shape[1]
    anywhere = pl.BlockSpec(memory_space=pl.ANY)
    return pl.pallas_call(
        attend_kernel,
        grid=(groups,),
        out_shape=[jax.ShapeDtypeStruct(block, BF16)] * 4
        + [
            jax.ShapeDtypeStruct((length, model), F32),
            jax.ShapeDtypeStruct((groups, 1, hidden), F32),
            jax.ShapeDtypeStruct(tokens.shape, BF16),
            jax.ShapeDtypeStruct(tokens.shape, BF16),
            whole,
            whole,
            whole,
        ],
        in_specs=[anywhere] * 5
        + spec_list(
            [
                (biases.shape, 0), (qaug.shape, 0), (kaug.shape, 0), (vaug.shape, 0),
                (b_mixer.shape, 0),
            ]
        ),
        out_specs=spec_list([(block, 1)] * 4 + [((length, model), 0), ((groups, 1, hidden), 1)])
        + [anywhere] * 5,
        scratch_shapes=[
            pltpu.VMEM((4, model, PAD), BF16),
            pltpu.VMEM(tokens.shape, BF16),
            pltpu.VMEM(whole.shape, BF16),
            pltpu.VMEM((groups,) + biases.shape, F32),
            pltpu.SemaphoreType.DMA((FORWARD_WIRES,)),
            pltpu.SemaphoreType.DMA((FORWARD_WIRES,)),
            pltpu.SemaphoreType.DMA((8,)),
        ],
        compiler_params=pltpu.CompilerParams(
            vmem_limit_bytes=VMEM_LIMIT, collective_id=0, has_side_effects=True
        ),
        name="attend_forward",
    )(tokens, cotangent, shard_a, shard_i, shard_o, biases, qaug, kaug, vaug, b_mixer)


def attend_plain(x, a_all, biases, qaug, kaug, vaug, b_mixer):
    length, model = x.shape
    groups = a_all.shape[0]
    block = (groups, length, PAD)
    return pl.pallas_call(
        attend_plain_kernel,
        grid=(groups,),
        out_shape=[jax.ShapeDtypeStruct(block, BF16)] * 4 + [jax.ShapeDtypeStruct(x.shape, F32)],
        in_specs=spec_list(
            [
                (x.shape, 0), (a_all.shape, 1), (biases.shape, 1),
                (qaug.shape, 0), (kaug.shape, 0), (vaug.shape, 0), (b_mixer.shape, 0),
            ]
        ),
        out_specs=spec_list([(block, 1)] * 4 + [(x.shape, 0)]),
        scratch_shapes=[pltpu.VMEM((4, model, PAD), BF16)],
        compiler_params=pltpu.CompilerParams(vmem_limit_bytes=VMEM_LIMIT),
        name="attend_plain",
    )(x, a_all, biases, qaug, kaug, vaug, b_mixer)


def dense_both(first_sum, wi, wo, bi, vectors, cotangent):
    length, model = first_sum.shape
    groups, _, hidden = wi.shape
    grad = (groups, model, hidden)
    forth = lambda shape: pl.BlockSpec(
        (1,) + shape[1:], lambda step: (lax.rem(step, groups),) + (0,) * (len(shape) - 1)
    )
    late = lambda shape: pl.BlockSpec(
        (1,) + shape[1:], lambda step: (jnp.maximum(step - groups, 0),) + (0,) * (len(shape) - 1)
    )
    return pl.pallas_call(
        dense_kernel,
        grid=(2 * groups,),
        out_shape=[
            jax.ShapeDtypeStruct((length, model), BF16),
            jax.ShapeDtypeStruct((length, model), F32),
            jax.ShapeDtypeStruct((length, model), BF16),
            jax.ShapeDtypeStruct(grad, BF16),
            jax.ShapeDtypeStruct(grad, BF16),
            jax.ShapeDtypeStruct((groups, 1, hidden), F32),
            jax.ShapeDtypeStruct((8, model), F32),
        ],
        in_specs=[
            pl.BlockSpec(memory_space=pl.ANY), forth(wi.shape), forth(wo.shape), forth(bi.shape),
            resident(vectors.shape), resident(cotangent.shape),
        ],
        out_specs=[
            resident((length, model)), resident((length, model)), resident((length, model)),
            late(grad), late(grad), late((groups, 1, hidden)), resident((8, model)),
        ],
        scratch_shapes=[
            pltpu.VMEM((length, model), F32),
            pltpu.VMEM((length, model), F32),
            pltpu.VMEM((length, model), F32),
            pltpu.VMEM((length, model), F32),
            pltpu.VMEM((groups, length, hidden), BF16),
            pltpu.VMEM((groups, length, hidden), BF16),
            pltpu.VMEM((length, model), BF16),
            pltpu.VMEM((model, length), BF16),
            pltpu.VMEM((model, length), BF16),
            pltpu.VMEM((length, hidden), BF16),
        ],
        compiler_params=pltpu.CompilerParams(vmem_limit_bytes=VMEM_LIMIT),
        name="dense_both",
    )(first_sum, wi, wo, bi, vectors, cotangent)


def attend_backward(x, a_all, d_mixed, d_first, q, k, v, attended):
    length, model = x.shape
    groups = a_all.shape[0]
    sums = (groups, 1, PAD)
    return pl.pallas_call(
        attend_back_kernel,
        grid=(groups,),
        out_shape=[
            jax.ShapeDtypeStruct(x.shape, F32),
            jax.ShapeDtypeStruct(a_all.shape, BF16),
            jax.ShapeDtypeStruct(sums, F32),
            jax.ShapeDtypeStruct(sums, F32),
        ],
        in_specs=spec_list(
            [
                (x.shape, 0), (a_all.shape, 1), (d_mixed.shape, 0), (d_first.shape, 0),
                (q.shape, 1), (k.shape, 1), (v.shape, 1), (attended.shape, 1),
            ]
        ),
        out_specs=spec_list([(x.shape, 0), (a_all.shape, 1), (sums, 1), (sums, 1)]),
        scratch_shapes=[
            pltpu.VMEM((4, model, PAD), BF16),
            pltpu.VMEM((model, length), BF16),
            pltpu.VMEM((model, length), BF16),
            pltpu.VMEM((length, PAD), BF16),
            pltpu.VMEM((PAD, length), BF16),
            pltpu.VMEM((PAD, length), F32),
            pltpu.VMEM((length, PAD), F32),
            pltpu.VMEM((length, PAD), F32),
            pltpu.VMEM((3, length, PAD), BF16),
        ],
        compiler_params=pltpu.CompilerParams(vmem_limit_bytes=VMEM_LIMIT),
        name="attend_backward",
    )(x, a_all, d_mixed, d_first, q, k, v, attended)


def augment(labels, width):
    length = labels.shape[0]
    lanes = lax.broadcasted_iota(jnp.int32, (length, PAD), 1)
    in_docs = (lanes >= width) & (lanes < width + DOCS)
    same = (lanes - width) == labels[:, None]
    qaug = jnp.where(in_docs & same, 1.0, 0.0).astype(BF16)
    spare = (lanes >= width + DOCS) & (lanes < width + DOCS + 3 * (width // HEAD))
    kaug = jnp.where(in_docs & ~same, -(2.0**100), jnp.where(spare, 1.0, 0.0)).astype(BF16)
    vaug = jnp.where((lanes[:1] == width) | spare[:1], 1.0, 0.0).astype(BF16)
    return qaug, kaug, vaug


def after_attention(first_sum, a_all, wi, wo, bi, vectors, x, cot, saved):
    out, d_first, d_mixed, g_inner, g_outer, db_inner, small = dense_both(
        first_sum, wi, wo, bi, vectors, cot
    )
    d_tokens, g_attend, dbq, dbv = attend_backward(x, a_all, d_mixed, d_first, *saved)
    return out, d_tokens, g_attend, g_inner, g_outer, dbq, dbv, db_inner, small


def body(
    tokens, doc_ids, w_query, b_query, w_key, w_value, b_value, w_mixer, b_mixer, gain_one,
    bias_one, w_inner, b_inner, w_outer, b_outer, gain_two, bias_two, cotangent,
):
    groups = lax.axis_size("tensor")
    rings = lax.axis_size("dp")
    place = lax.axis_index("tensor")
    width = w_query.shape[1]
    hidden = w_inner.shape[1]
    length = doc_ids.shape[2]
    model = tokens.shape[3]
    near = groups == 4 and rings == 8

    labels = lax.dynamic_index_in_dim(doc_ids[:, 0], place, 0, keepdims=False)
    qaug, kaug, vaug = augment(labels, width)
    shard_a = jnp.concatenate([w_query, w_key, w_value, w_mixer.T], axis=1)
    shard_o = w_outer.T
    spare = jnp.zeros((PAD - width,), F32)
    biases = jnp.concatenate([b_query, spare, b_value, spare, b_inner])[None]
    vectors = jnp.stack([gain_one, bias_one, b_outer, gain_two, bias_two] + [b_outer] * 3)
    if near:
        *saved, first_sum, bi, x, cot, a_all, wi, wo = attend_forward(
            tokens[:, 0], cotangent[:, 0], shard_a, w_inner, shard_o, biases, qaug, kaug, vaug,
            b_mixer[None],
        )
        a_all, wi, wo = (part.reshape(groups, model, model) for part in (a_all, wi, wo))
        x, cot = (part.reshape(length, model) for part in (x, cot))
        order = jnp.bitwise_xor(place, jnp.arange(groups))
    else:

        def gather(shard):
            whole = lax.all_gather(shard, ("tensor", "dp"), axis=0, tiled=True)
            return whole.reshape(groups, model, shard.shape[1])

        def to_sequence(part):
            return lax.all_to_all(part, "tensor", 0, 2, tiled=True).reshape(length, model)

        x, cot = to_sequence(tokens), to_sequence(cotangent)
        a_all, wi, wo = gather(shard_a), gather(w_inner), gather(shard_o)
        every = lax.all_gather(biases, "tensor", axis=0)
        *saved, first_sum = attend_plain(x, a_all, every, qaug, kaug, vaug, b_mixer[None])
        bi = every[:, :, 2 * PAD :]
        order = jnp.arange(groups)
    out, d_tokens, *grads = after_attention(
        first_sum, a_all, wi, wo, bi, vectors, x, cot, saved
    )
    g_attend, g_inner, g_outer, dbq, dbv, dbi, small = grads

    def from_sequence(whole):
        return lax.all_to_all(whole.reshape(1, 1, length, model), "tensor", 2, 0, tiled=True)

    def by_place(part):
        return jnp.take(part, order, axis=0) if near else part

    def scatter(part):
        flat = by_place(part).reshape(-1, part.shape[2])
        return lax.psum_scatter(flat, ("tensor", "dp"), scatter_dimension=0, tiled=True)

    ga = scatter(g_attend).astype(F32)
    gi = scatter(g_inner).astype(F32)
    go = scatter(g_outer).astype(F32)
    rows = [by_place(dbq[:, 0, :width]), by_place(dbv[:, 0, :width]), by_place(dbi[:, 0]), small]
    summed = lax.psum(jnp.concatenate([part.reshape(-1) for part in rows]), ("dp", "tensor"))
    mine = lambda start, size: lax.dynamic_slice_in_dim(summed, start + place * size, size)
    tail = summed[2 * model + dbi.size :].reshape(8, model)
    return (
        from_sequence(out),
        from_sequence(d_tokens),
        ga[:, :width],
        mine(0, width),
        ga[:, width : 2 * width],
        ga[:, 2 * width : 3 * width],
        mine(model, width),
        ga[:, 3 * width :].T,
        tail[3],
        tail[4],
        tail[5],
        gi,
        mine(2 * model, hidden),
        go.T,
        tail[0],
        tail[1],
        tail[2],
    )


def solution(mesh):
    split = P(None, "dp", "tensor", None)
    both, flipped, part = P("dp", "tensor"), P("tensor", "dp"), P("tensor")
    return jax.shard_map(
        body,
        mesh=mesh,
        in_specs=(
            split, P(None, "dp", None), both, part, both, both, part, flipped, P(), P(), P(),
            both, part, flipped, P(), P(), P(), split,
        ),
        out_specs=(
            split, split, both, part, both, both, part, flipped, P(), P(), P(), both, part,
            flipped, P(), P(), P(),
        ),
        check_vma=False,
    )
```

```python
from functools import partial

import jax
import jax.numpy as jnp
from jax import lax
from jax.experimental import pallas as pl
from jax.experimental.pallas import tpu as pltpu
from jax.sharding import PartitionSpec as P

HEAD = 64
DOCS = 8
PAD = 256
ROWS = 256
LOG2E = 1.4426950408889634
EPS = 1e-12
F32 = jnp.float32
BF16 = jnp.bfloat16


def dot_nn(left, right):
    return lax.dot_general(left, right, (((1,), (0,)), ((), ())), preferred_element_type=F32)


def dot_nt(left, right):
    return lax.dot_general(left, right, (((1,), (1,)), ((), ())), preferred_element_type=F32)


def rows_of(index, size=ROWS):
    return pl.ds(pl.multiple_of(index * size, size), size)


def lane_index(shape):
    return lax.broadcasted_iota(jnp.int32, shape, 1)


def three_parts(values):
    high = values.astype(BF16)
    rest = values - high.astype(F32)
    middle = rest.astype(BF16)
    low = (rest - middle.astype(F32)).astype(BF16)
    return high, middle, low


def head_only(lanes, head):
    return (lanes >= head * HEAD) & (lanes < (head + 1) * HEAD)


def head_and_extra(lanes, head, width):
    extra = width + DOCS + 3 * head
    return (
        head_only(lanes, head)
        | ((lanes >= width) & (lanes < width + DOCS))
        | ((lanes >= extra) & (lanes < extra + 3))
    )


def unpack(block_ref, slot, width):
    part = block_ref[:, slot * width : (slot + 1) * width]
    return jnp.concatenate([part, jnp.zeros((part.shape[0], PAD - width), part.dtype)], axis=1)


def project(x_rows, rows, bq, bv, w_s, qaug_ref, kaug_ref, vaug_ref, q_ref, k_ref, v_ref):
    queries = (dot_nn(x_rows, w_s[0]) + bq).astype(BF16)
    q_ref[0, rows, :] = queries * jnp.asarray(HEAD**-0.5, BF16) + qaug_ref[rows, :]
    keys = dot_nn(x_rows, w_s[1]).astype(BF16)
    k_ref[0, rows, :] = keys + kaug_ref[rows, :]
    values = (dot_nn(x_rows, w_s[2]) + bv).astype(BF16)
    v_ref[0, rows, :] = values + vaug_ref[...]


def attend_rows(rows, width, w_s, q_ref, k_ref, v_ref, att_ref, first_ref):
    lanes = lane_index((ROWS, PAD))
    queries = q_ref[0, rows, :]
    attended = jnp.zeros((ROWS, PAD), F32)
    extended = queries
    for head in range(width // HEAD):
        masked = jnp.where(head_and_extra(lanes, head, width), queries, 0)
        scores = dot_nt(masked, k_ref[0])
        highest = jnp.max(scores, axis=1, keepdims=True)
        raw = jnp.exp2((scores - highest) * LOG2E).astype(BF16)
        mixed = dot_nn(raw, v_ref[0])
        total = mixed[:, width : width + 1]
        attended = jnp.where(head_only(lanes, head), mixed / total, attended)
        for spot, part in enumerate(three_parts(-(highest + jnp.log(total)))):
            here = lanes == width + DOCS + 3 * head + spot
            extended = jnp.where(here, jnp.broadcast_to(part, (ROWS, PAD)), extended)
    q_ref[0, rows, :] = extended
    attended = attended.astype(BF16)
    att_ref[0, rows, :] = attended
    first_ref[rows, :] += dot_nt(attended, w_s[3])


def attend_plain_kernel(
    x_ref, a_ref, bias_ref, qaug_ref, kaug_ref, vaug_ref, bm_ref,
    q_ref, k_ref, v_ref, att_ref, first_ref, w_s,
):
    length, model = x_ref.shape
    width = a_ref.shape[2] // 4
    for slot in range(4):
        w_s[slot] = unpack(a_ref.at[0], slot, width)
    biases = bias_ref[0]

    @pl.when(pl.program_id(0) == 0)
    def _():
        first_ref[...] = x_ref[...].astype(F32) + bm_ref[...]

    @pl.loop(0, length // ROWS)
    def _(index):
        rows = rows_of(index)
        project(
            x_ref[rows, :], rows, biases[:, :PAD], biases[:, PAD : 2 * PAD], w_s, qaug_ref,
            kaug_ref, vaug_ref, q_ref, k_ref, v_ref,
        )

    @pl.loop(0, length // ROWS)
    def _(index):
        attend_rows(rows_of(index), width, w_s, q_ref, k_ref, v_ref, att_ref, first_ref)


MESH = pl.DeviceIdType.MESH


def partner(index, bits, size):
    flipped = index
    for bit in (1, 2, 4):
        if bits & bit and bit < size:
            flipped = flipped + bit - 2 * bit * lax.rem(lax.div(index, bit), 2)
    return flipped


class Wires:
    def __init__(self, send, recv, place, row):
        self.send, self.recv, self.place, self.row = send, recv, place, row

    def to(self, tensor_bits, dp_bits):
        return (partner(self.row, dp_bits, 8), partner(self.place, tensor_bits, 4))

    def copy(self, number, source, target, tensor_bits=0, dp_bits=0):
        return pltpu.make_async_remote_copy(
            src_ref=source,
            dst_ref=target,
            send_sem=self.send.at[number],
            recv_sem=self.recv.at[number],
            device_id=self.to(tensor_bits, dp_bits),
            device_id_type=MESH,
        )


def greet(wires, peers):
    barrier = pltpu.get_barrier_semaphore()
    for tensor_bits, dp_bits in peers:
        pl.semaphore_signal(
            barrier, inc=1, device_id=wires.to(tensor_bits, dp_bits), device_id_type=MESH
        )
    pl.semaphore_wait(barrier, len(peers))


PEERS = ((1, 0), (2, 0), (3, 0), (0, 1), (0, 2), (0, 4), (0, 6))
TOKENS, COTS, BIASES, KIND_A = 0, 3, 6, 9
KIND_I = KIND_A + 17
KIND_O = KIND_I + 17
FORWARD_WIRES = KIND_O + 10


class ShardGather:
    def __init__(self, wires, base, shard, whole):
        self.wires, self.base, self.shard, self.whole = wires, base, shard, whole

    def at(self, slot, dp_bits):
        return self.whole.at[slot, partner(self.wires.row, dp_bits, 8)]

    def cross_x(self):
        return self.wires.copy(self.base, self.shard, self.at(2, 0), 2, 0)

    def along_z(self, slot, step, mine):
        source = self.shard if slot == 0 else self.at(slot, 0)
        number = self.base + 1 + 3 * (slot // 2) + step - 1
        target = self.at(slot, 0) if mine else self.at(slot, 2 * step)
        return self.wires.copy(number, source, target, 0, 2 * step)

    def along_y(self, slot, step, mine):
        source = self.shard if slot == 0 and step == 0 else self.at(slot, 2 * step)
        number = self.base + 7 + 4 * (slot // 2) + step
        target = self.at(slot, 2 * step) if mine else self.at(slot, 2 * step + 1)
        return self.wires.copy(number, source, target, 0, 1)

    def to_core(self, slot, mine):
        number = self.base + 15 + slot // 2
        target = self.whole.at[slot + 1]
        return self.wires.copy(number, self.whole.at[slot], target, 1, 0)

    def start_z(self, slot):
        for step in (1, 2, 3):
            self.along_z(slot, step, True).start()

    def wait_z(self, slot):
        for step in (1, 2, 3):
            self.along_z(slot, step, False).wait_recv()

    def pass_y(self, slot):
        for step in (1, 2, 3):
            self.along_y(slot, step, True).start()

    def wait_y(self, slot):
        for step in range(4):
            self.along_y(slot, step, False).wait_recv()

    def wait_sent(self, x_first=True):
        for slot in (0, 2) if x_first else (0,):
            for step in (1, 2, 3):
                self.along_z(slot, step, True).wait_send()
            for step in range(4):
                self.along_y(slot, step, True).wait_send()
        for slot in (0, 2):
            self.to_core(slot, True).wait_send()


class BlockGather(ShardGather):
    def along_z(self, slot, step, mine):
        target = self.at(0, 0) if mine else self.at(0, 2 * step)
        return self.wires.copy(self.base + step - 1, self.shard, target, 0, 2 * step)

    def along_y(self, slot, step, mine):
        source = self.shard if step == 0 else self.at(0, 2 * step)
        target = self.at(0, 2 * step) if mine else self.at(0, 2 * step + 1)
        return self.wires.copy(self.base + 3 + step, source, target, 0, 1)

    def cross_x(self):
        return self.wires.copy(self.base + 7, self.whole.at[0], self.whole.at[2], 2, 0)

    def to_core(self, slot, mine):
        return self.wires.copy(
            self.base + 8 + slot // 2, self.whole.at[slot], self.whole.at[slot + 1], 1, 0
        )


def attend_kernel(
    tok_ref, cot_ref, sa_ref, si_ref, so_ref, bias_ref, qaug_ref, kaug_ref, vaug_ref, bm_ref,
    q_ref, k_ref, v_ref, att_ref, first_ref, bi_ref, x_out, cot_out, a_out, wi_out, wo_out,
    w_s, x_s, a_s, bias_s, send_sem, recv_sem, here_sem,
):
    step = pl.program_id(0)
    place = lax.axis_index("tensor")
    row = lax.axis_index("dp")
    quarters, part, model = x_s.shape
    length = quarters * part
    width = sa_ref.shape[1] // 4
    blocks = length // ROWS
    share = sa_ref.shape[0]
    wires = Wires(send_sem, recv_sem, place, row)
    attn = ShardGather(wires, KIND_A, sa_ref, a_s)
    inner = ShardGather(wires, KIND_I, si_ref, wi_out)
    outer = BlockGather(wires, KIND_O, so_ref, wo_out)

    def exchange(base, source, target, bits, mine):
        other = partner(place, bits, 4)
        return wires.copy(
            base + bits - 1, source.at[other], target.at[place if mine else other], bits, 0
        )

    def bias_copy(bits, mine):
        return wires.copy(BIASES + bits - 1, bias_ref, bias_s.at[bits], bits, 0)

    local = [
        pltpu.make_async_copy(tok_ref.at[place], x_s.at[place], here_sem.at[0]),
        pltpu.make_async_copy(sa_ref, a_s.at[0, row], here_sem.at[1]),
        pltpu.make_async_copy(si_ref, wi_out.at[0, row], here_sem.at[2]),
        pltpu.make_async_copy(so_ref, wo_out.at[0, row], here_sem.at[3]),
        pltpu.make_async_copy(cot_ref.at[place], cot_out.at[place], here_sem.at[4]),
        pltpu.make_async_copy(bias_ref, bias_s.at[0], here_sem.at[5]),
    ]
    keep_x = pltpu.make_async_copy(x_s, x_out, here_sem.at[6])
    keep_a = pltpu.make_async_copy(a_s, a_out, here_sem.at[7])

    @pl.when(step == 0)
    def _():
        greet(wires, PEERS)
        attn.cross_x().start()
        for bits in (1, 2, 3):
            bias_copy(bits, True).start()
        attn.start_z(0)
        attn.along_y(0, 0, True).start()
        for bits in (2, 3, 1):
            exchange(TOKENS, tok_ref, x_s, bits, True).start()
        for copy in local:
            copy.start()
        for copy in local:
            copy.wait()
        attn.cross_x().wait_recv()
        attn.start_z(2)
        attn.along_y(2, 0, True).start()
        attn.wait_z(0)
        attn.pass_y(0)
        attn.wait_y(0)
        attn.to_core(0, True).start()
        for bits in (1, 2, 3):
            exchange(TOKENS, tok_ref, x_s, bits, False).wait_recv()
            bias_copy(bits, False).wait_recv()
        keep_x.start()

        @pl.loop(0, quarters)
        def _(index):
            rows = rows_of(index, part)
            first_ref[rows, :] = x_s[index].astype(F32) + bm_ref[...]

    @pl.when(step == 1)
    def _():
        attn.to_core(0, False).wait_recv()

    @pl.when(step == 2)
    def _():
        attn.wait_y(2)
        attn.to_core(2, True).start()

    @pl.when(step == 3)
    def _():
        attn.to_core(2, False).wait_recv()
        keep_a.start()

    for dp_row in range(a_s.shape[1]):
        packed = a_s[step, dp_row]
        rest = jnp.zeros((share, PAD - width), packed.dtype)
        for slot in range(4):
            piece = packed[:, slot * width : (slot + 1) * width]
            rows = slice(dp_row * share, (dp_row + 1) * share)
            w_s[slot, rows, :] = jnp.concatenate([piece, rest], axis=1)
    biases = bias_s[step]
    bi_ref[0] = biases[:, 2 * PAD :]

    @pl.loop(0, quarters)
    def _(index):
        rows = rows_of(index, part)
        x_rows = x_s[index]
        project(
            x_rows, rows, biases[:, :PAD], biases[:, PAD : 2 * PAD], w_s, qaug_ref, kaug_ref,
            vaug_ref, q_ref, k_ref, v_ref,
        )

    @pl.loop(0, blocks)
    def _(index):
        attend_rows(rows_of(index), width, w_s, q_ref, k_ref, v_ref, att_ref, first_ref)

        @pl.when((step == 0) & (index == 1))
        def _():
            attn.wait_z(2)
            attn.pass_y(2)
            outer.start_z(0)
            outer.along_y(0, 0, True).start()
            inner.cross_x().start()
            for bits in (2, 3, 1):
                exchange(COTS, cot_ref, cot_out, bits, True).start()

        @pl.when((step == 0) & (index == 3))
        def _():
            inner.cross_x().wait_recv()
            inner.start_z(0)
            inner.along_y(0, 0, True).start()
            inner.start_z(2)
            inner.along_y(2, 0, True).start()

        @pl.when((step == 1) & (index == 2))
        def _():
            outer.wait_z(0)
            outer.pass_y(0)

        @pl.when((step == 2) & (index == 1))
        def _():
            outer.wait_y(0)
            outer.cross_x().start()
            outer.to_core(0, True).start()

        @pl.when((step == 3) & (index == 0))
        def _():
            inner.wait_z(0)
            inner.pass_y(0)

        @pl.when((step == 3) & (index == 2))
        def _():
            inner.wait_z(2)
            inner.pass_y(2)

    @pl.when(step == 3)
    def _():
        inner.wait_y(0)
        inner.to_core(0, True).start()
        inner.wait_y(2)
        inner.to_core(2, True).start()
        outer.cross_x().wait_recv()
        outer.to_core(2, True).start()
        for bits in (1, 2, 3):
            exchange(COTS, cot_ref, cot_out, bits, False).wait_recv()
        for gather in (inner, outer):
            for slot in (0, 2):
                gather.to_core(slot, False).wait_recv()
        for gather in (attn, inner, outer):
            gather.cross_x().wait_send()
            gather.wait_sent(gather is not outer)
        for bits in (1, 2, 3):
            exchange(TOKENS, tok_ref, x_s, bits, True).wait_send()
            exchange(COTS, cot_ref, cot_out, bits, True).wait_send()
            bias_copy(bits, True).wait_send()
        keep_x.wait()
        keep_a.wait()


def gelu_parts(values):
    phi = jnp.exp2(values * values * (-0.5 * LOG2E)) * 0.3989422804014327
    total = 0.5 + 0.5 * lax.erf(values * 0.7071067811865476)
    return values * total, total + values * phi


def norm_parts(values):
    average = jnp.mean(values, axis=-1, keepdims=True)
    centred = values - average
    spread = jnp.mean(centred * centred, axis=-1, keepdims=True)
    inverse = lax.rsqrt(spread + EPS)
    return centred * inverse, inverse


def norm_back(grads, gain, unit, inverse):
    scaled = grads * gain
    average = jnp.mean(scaled, axis=-1, keepdims=True)
    along = jnp.mean(scaled * unit, axis=-1, keepdims=True)
    return (scaled - average - unit * along) * inverse


def column_sum(values):
    return jnp.sum(values, axis=0, keepdims=True)


def dense_kernel(
    first_in, wi_ref, wo_ref, bi_ref, vec_ref, cot_ref,
    out_ref, dfirst_ref, dmix_ref, gi_ref, go_ref, dbi_ref, small_ref,
    first_ref, second_ref, normed_s, dsec_s, hidden_s, slope_s, low_s, low_t, back_t, dinner_s,
):
    step = pl.program_id(0)
    count = pl.num_programs(0) // 2
    length, model = first_in.shape
    blocks = length // ROWS
    gain_one, bias_one, b_outer, gain_two, bias_two = (vec_ref[i : i + 1, :] for i in range(5))

    @pl.when(step == 0)
    def _():
        copied = pltpu.sync_copy
        copied(first_in, first_ref)

        @pl.loop(0, blocks)
        def _(index):
            rows = rows_of(index)
            unit, _inverse = norm_parts(first_ref[rows, :])
            normed = unit * gain_one + bias_one
            normed_s[rows, :] = normed
            low_s[rows, :] = normed.astype(BF16)
            low_t[:, rows] = normed.astype(BF16).T
            second_ref[rows, :] = normed + b_outer

    @pl.when(step < count)
    def _():
        @pl.loop(0, blocks)
        def _(index):
            rows = rows_of(index)
            inner = dot_nn(low_s[rows, :], wi_ref[0]) + bi_ref[0]
            value, slope = gelu_parts(inner)
            hidden = value.astype(BF16)
            hidden_s[step, rows, :] = hidden
            slope_s[step, rows, :] = slope.astype(BF16)
            second_ref[rows, :] += dot_nt(hidden, wo_ref[0])

    @pl.when(step == count - 1)
    def _():
        small_ref[...] = jnp.zeros_like(small_ref)

        @pl.loop(0, blocks)
        def _(index):
            rows = rows_of(index)
            unit, inverse = norm_parts(second_ref[rows, :])
            out_ref[rows, :] = (unit * gain_two + bias_two).astype(BF16)
            grads = cot_ref[rows, :].astype(F32)
            d_second = norm_back(grads, gain_two, unit, inverse)
            small_ref[0:1, :] += column_sum(d_second)
            small_ref[1:2, :] += column_sum(grads * unit)
            small_ref[2:3, :] += column_sum(grads)
            dsec_s[rows, :] = d_second
            low = d_second.astype(BF16)
            dmix_ref[rows, :] = low
            back_t[:, rows] = low.T

    @pl.when(step >= count)
    def _():
        place = step - count
        dbi_ref[...] = jnp.zeros_like(dbi_ref)

        @pl.loop(0, blocks)
        def _(index):
            rows = rows_of(index)
            d_hidden = dot_nn(dmix_ref[rows, :], wo_ref[0])
            d_inner = (d_hidden * slope_s[place, rows, :].astype(F32)).astype(BF16)
            dinner_s[rows, :] = d_inner
            dbi_ref[0] += column_sum(d_inner.astype(F32))
            dsec_s[rows, :] += dot_nt(d_inner, wi_ref[0])

        @pl.loop(0, model // ROWS)
        def _(index):
            rows = rows_of(index)
            gi_ref[0, rows, :] = dot_nn(low_t[rows, :], dinner_s[...]).astype(gi_ref.dtype)
            go_ref[0, rows, :] = dot_nn(back_t[rows, :], hidden_s[place]).astype(go_ref.dtype)

    @pl.when(step == 2 * count - 1)
    def _():
        @pl.loop(0, blocks)
        def _(index):
            rows = rows_of(index)
            unit, inverse = norm_parts(first_ref[rows, :])
            grads = dsec_s[rows, :]
            d_first = norm_back(grads, gain_one, unit, inverse)
            small_ref[3:4, :] += column_sum(d_first)
            small_ref[4:5, :] += column_sum(grads * unit)
            small_ref[5:6, :] += column_sum(grads)
            dfirst_ref[rows, :] = d_first
            dmix_ref[rows, :] = d_first.astype(BF16)


def back_rows(rows, width, w_s, dmix_rows, q_ref, k_ref, v_ref, att_ref, kt_s, dq_s, dk_s, dv_s):
    lanes = lane_index((ROWS, PAD))
    queries = q_ref[0, rows, :]
    d_att = dot_nn(dmix_rows, w_s[3]).astype(BF16)
    product = d_att.astype(F32) * att_ref[0, rows, :].astype(F32)
    heads = range(width // HEAD)
    extended = d_att
    for head in heads:
        centre = jnp.sum(jnp.where(head_only(lanes, head), product, 0.0), axis=1, keepdims=True)
        for spot, part in enumerate(three_parts(-centre)):
            here = lanes == width + DOCS + 3 * head + spot
            extended = jnp.where(here, jnp.broadcast_to(part, (ROWS, PAD)), extended)
    chances_all = []
    d_scores_all = []
    d_att_all = []
    queries_all = []
    for head in heads:
        wide = head_and_extra(lanes, head, width)
        only = head_only(lanes, head)
        chances = jnp.exp2(dot_nt(k_ref[0], jnp.where(wide, queries, 0)) * LOG2E)
        d_chances = dot_nt(v_ref[0], jnp.where(wide, extended, 0))
        d_scores = (chances * d_chances).astype(BF16)
        chances_all.append(chances.astype(BF16))
        d_scores_all.append(d_scores)
        d_att_all.append(jnp.where(only, d_att, 0))
        queries_all.append(jnp.where(only, queries, 0))
        head_rows = slice(head * HEAD, (head + 1) * HEAD)
        dq_s[head_rows, rows] = dot_nn(kt_s[head_rows, :], d_scores)
    dv_s[...] += dot_nn(jnp.concatenate(chances_all, 1), jnp.concatenate(d_att_all, 0))
    dk_s[...] += dot_nn(jnp.concatenate(d_scores_all, 1), jnp.concatenate(queries_all, 0))


def back_low(rows, width, dq_s, dk_s, dv_s, low_s):
    d_query = (dq_s[:, rows].T * HEAD**-0.5).astype(BF16)
    d_query = jnp.where(lane_index(d_query.shape) < width, d_query, 0)
    d_value = dv_s[rows, :].astype(BF16)
    low_s[0, rows, :] = d_query
    low_s[1, rows, :] = dk_s[rows, :].astype(BF16)
    low_s[2, rows, :] = d_value
    return column_sum(d_query.astype(F32)), column_sum(d_value.astype(F32))


def back_tokens(rows, w_s, low_s):
    return sum(dot_nt(low_s[slot, rows, :], w_s[slot]) for slot in range(3))


def back_weights(rows, width, slots, xt_s, dmixt_s, low_s, att_ref):
    parts = []
    for slot in slots:
        if slot < 3:
            part = dot_nn(xt_s[rows, :], low_s[slot])
        else:
            part = dot_nn(dmixt_s[rows, :], att_ref[0])
        parts.append(part[:, :width])
    return jnp.concatenate(parts, axis=1).astype(BF16)


def attend_back_kernel(
    x_ref, a_ref, dmix_ref, dfirst_ref, q_ref, k_ref, v_ref, att_ref,
    dtok_ref, ga_ref, dbq_ref, dbv_ref,
    w_s, xt_s, dmixt_s, kt_s, dq_s, dk_s, dv_s, low_s,
):
    length, model = x_ref.shape
    width = a_ref.shape[2] // 4
    blocks = length // ROWS
    for slot in range(4):
        w_s[slot] = unpack(a_ref.at[0], slot, width)

    @pl.when(pl.program_id(0) == 0)
    def _():
        dtok_ref[...] = dfirst_ref[...]

        @pl.loop(0, blocks)
        def _(index):
            rows = rows_of(index)
            xt_s[:, rows] = x_ref[rows, :].T
            dmixt_s[:, rows] = dmix_ref[rows, :].T

    for sums in (dk_s, dv_s, dbq_ref, dbv_ref):
        sums[...] = jnp.zeros_like(sums)

    @pl.loop(0, blocks)
    def _(index):
        rows = rows_of(index)
        kt_s[:, rows] = k_ref[0, rows, :].T

    @pl.loop(0, blocks)
    def _(index):
        rows = rows_of(index)
        dmix_rows = dmix_ref[rows, :]
        back_rows(
            rows, width, w_s, dmix_rows, q_ref, k_ref, v_ref, att_ref, kt_s, dq_s, dk_s, dv_s
        )

    @pl.loop(0, blocks)
    def _(index):
        rows = rows_of(index)
        for_query, for_value = back_low(rows, width, dq_s, dk_s, dv_s, low_s)
        dbq_ref[0] += for_query
        dbv_ref[0] += for_value
        dtok_ref[rows, :] += back_tokens(rows, w_s, low_s)

    @pl.loop(0, model // ROWS)
    def _(index):
        rows = rows_of(index)
        ga_ref[0, rows, :] = back_weights(rows, width, range(4), xt_s, dmixt_s, low_s, att_ref)


def add_into(target, source):
    target[...] = (target[...].astype(F32) + source[...].astype(F32)).astype(target.dtype)


class Reduce:
    COUNT = 11

    def __init__(self, wires, base, held, core, by_y, by_z, by_x):
        self.wires, self.base, self.held, self.core = wires, base, held, core
        self.by_y, self.by_z, self.by_x = by_y, by_z, by_x
        self.z, self.y = lax.div(wires.row, 2), lax.rem(wires.row, 2)

    def core_copy(self, j, source):
        return self.wires.copy(self.base + j, source, self.core.at[j], 1, 0)

    def add_core(self, j):
        self.core_copy(j, self.held.at[j]).wait_recv()
        for z in range(4):
            for y in range(2):
                add_into(self.held.at[j, z, y], self.core.at[j, z, y])

    def y_copy(self, j):
        source = self.held.at[j, :, 1 - self.y]
        return self.wires.copy(self.base + 2 + j, source, self.by_y.at[j], 0, 1)

    def add_y(self, j):
        self.y_copy(j).wait_recv()
        for z in range(4):
            add_into(self.held.at[j, z, self.y], self.by_y.at[j, z])

    def z_copy(self, j, step):
        source = self.held.at[j, lax.div(partner(self.wires.row, 2 * step, 8), 2), self.y]
        number = self.base + 4 + 3 * j + step - 1
        return self.wires.copy(number, source, self.by_z.at[j, step - 1], 0, 2 * step)

    def start_z(self, j):
        for step in (1, 2, 3):
            self.z_copy(j, step).start()

    def total_z(self, j):
        total = self.held[j, self.z, self.y].astype(F32)
        for step in (1, 2, 3):
            self.z_copy(j, step).wait_recv()
            total = total + self.by_z[j, step - 1].astype(F32)
        return total

    def x_copy(self):
        source = self.held.at[1, self.z, self.y]
        return self.wires.copy(self.base + 10, source, self.by_x, 2, 0)

    def send_x(self):
        self.held[1, self.z, self.y] = self.total_z(1).astype(BF16)
        self.x_copy().start()

    def whole_x_copy(self):
        return self.wires.copy(self.base + 10, self.held.at[1], self.by_x, 2, 0)

    def add_whole_x(self):
        self.whole_x_copy().wait_recv()
        for z in range(4):
            for y in range(2):
                add_into(self.held.at[0, z, y], self.by_x.at[z, y])

    def wait_sent(self, j_all):
        for j in j_all:
            self.y_copy(j).wait_send()
            for step in (1, 2, 3):
                self.z_copy(j, step).wait_send()


OUTPUTS, TOKEN_GRADS, SUMS, LATE_SUMS = 0, 3, 6, 11
RED_I = 16
RED_O = RED_I + Reduce.COUNT
RED_A = RED_O + Reduce.COUNT
BACKWARD_WIRES = RED_A + 2 * Reduce.COUNT
HOPS = ((1, 0), (2, 0), (0, 1), (0, 2), (0, 4))


def slot_at(step):
    return jnp.where(step < 2, 3 - 2 * step, 6 - 2 * step)


def attend_reduce_kernel(
    x_ref, a_ref, dmix_ref, dfirst_ref, q_ref, k_ref, v_ref, att_ref, gi_ref, go_ref, out_ref,
    dbi_ref, small_ref,
    out_res, dtok_res, ga_one, ga_two, gi_res, go_res, sum_res, late_res,
    w_s, xt_s, dmixt_s, kt_s, dq_s, dk_s, dv_s, low_s, dmix_s, dtok_s, dlow_s, sums_s, late_s,
    sums_r, late_r,
    held_i, core_i, y_i, z_i, x_i, held_o, core_o, y_o, z_o, x_o,
    send_a, held_a, core_a, y_a, z_a, x_a,
    send_sem, recv_sem, here_sem,
):
    step = pl.program_id(0)
    place = lax.axis_index("tensor")
    row = lax.axis_index("dp")
    length, model = dmix_s.shape
    quarters, part, _ = dlow_s.shape
    width = a_ref.shape[2] // 4
    blocks = length // ROWS
    wires = Wires(send_sem, recv_sem, place, row)
    inner = Reduce(wires, RED_I, held_i, core_i, y_i, z_i, x_i)
    outer = Reduce(wires, RED_O, held_o, core_o, y_o, z_o, x_o)
    attn = [
        Reduce(
            wires, RED_A + half * Reduce.COUNT, held_a.at[half], core_a.at[half], y_a.at[half],
            z_a.at[half], x_a.at[half],
        )
        for half in range(2)
    ]

    def exchange(base, source, target, bits, mine):
        other = partner(place, bits, 4)
        return wires.copy(
            base + bits - 1, source.at[other], target.at[place if mine else other], bits, 0
        )

    def hop(base, kept, got, number):
        bits = HOPS[number]
        return wires.copy(base + number, kept.at[number], got.at[number], *bits)

    def add_hop(base, kept, got, number):
        hop(base, kept, got, number).wait_recv()
        kept[number + 1] = kept[number] + got[number]

    def next_hop(base, kept, got, number):
        add_hop(base, kept, got, number)
        if number + 1 < len(HOPS):
            hop(base, kept, got, number + 1).start()

    loads = [
        pltpu.make_async_copy(gi_ref.at[0], held_i.at[0], here_sem.at[0]),
        pltpu.make_async_copy(gi_ref.at[2], held_i.at[1], here_sem.at[1]),
        pltpu.make_async_copy(go_ref.at[0], held_o.at[0], here_sem.at[2]),
        pltpu.make_async_copy(go_ref.at[2], held_o.at[1], here_sem.at[3]),
        pltpu.make_async_copy(dmix_ref, dmix_s, here_sem.at[4]),
        pltpu.make_async_copy(dfirst_ref, dtok_s, here_sem.at[5]),
    ]
    keep_out = pltpu.make_async_copy(out_ref.at[place], out_res.at[place], here_sem.at[6])
    keep_dtok = pltpu.make_async_copy(dlow_s.at[place], dtok_res.at[place], here_sem.at[7])
    load_x = pltpu.make_async_copy(x_ref, dlow_s, here_sem.at[8])

    def core_sends(kind, source):
        return [kind.core_copy(0, source.at[1]), kind.core_copy(1, source.at[3])]

    @pl.when(step == 0)
    def _():
        for copy in loads:
            copy.start()
        load_x.start()
        sums_s[0] = jnp.zeros_like(sums_s[0])
        late_s[0] = jnp.zeros_like(late_s[0])
        for bits in range(4):
            sums_s[0, pl.ds(partner(place, bits, 4), 1), :] = dbi_ref[bits]
        sums_s[0, 8:16, :] = small_ref[...]
        greet(wires, PEERS)
        for copy in core_sends(inner, gi_ref) + core_sends(outer, go_ref):
            copy.start()
        hop(SUMS, sums_s, sums_r, 0).start()
        for copy in loads:
            copy.wait()
        load_x.wait()

        @pl.loop(0, quarters)
        def _(index):
            rows = rows_of(index, part)
            xt_s[:, rows] = dlow_s[index].T
            dmixt_s[:, rows] = dmix_s[rows, :].T

        for j in (1, 0):
            inner.add_core(j)
            inner.y_copy(j).start()
        outer.add_core(1)
        outer.whole_x_copy().start()
        outer.add_core(0)
        next_hop(SUMS, sums_s, sums_r, 0)

    @pl.when(step == 3)
    def _():
        for reduce in attn:
            reduce.add_core(1)
            reduce.y_copy(1).start()

    for slot in range(4):
        w_s[slot] = unpack(a_ref.at[0], slot, width)
    for sums in (dk_s, dv_s):
        sums[...] = jnp.zeros_like(sums)

    @pl.loop(0, blocks)
    def _(index):
        rows = rows_of(index)
        kt_s[:, rows] = k_ref[0, rows, :].T

    @pl.loop(0, blocks)
    def _(index):
        rows = rows_of(index)
        dmix_rows = dmix_s[rows, :]
        back_rows(
            rows, width, w_s, dmix_rows, q_ref, k_ref, v_ref, att_ref, kt_s, dq_s, dk_s, dv_s
        )

        for number in range(1, 4):

            @pl.when((step == 0) & (index == number))
            def _(number=number):
                next_hop(SUMS, sums_s, sums_r, number)

        @pl.when((step == 1) & (index == 0))
        def _():
            add_hop(SUMS, sums_s, sums_r, 4)

        @pl.when((step == 1) & (index == 2))
        def _():
            for j in (1, 0):
                inner.add_y(j)
                inner.start_z(j)

        @pl.when((step == 1) & (index == 3))
        def _():
            outer.add_whole_x()
            outer.y_copy(0).start()
            for bits in (2, 3, 1):
                exchange(OUTPUTS, out_ref, out_res, bits, True).start()
            keep_out.start()

        @pl.when((step == 2) & (index == 2))
        def _():
            outer.add_y(0)
            outer.start_z(0)

        @pl.when((step == 3) & (index == 1))
        def _():
            inner.send_x()

        @pl.when((step == 3) & (index == 3))
        def _():
            for reduce in attn:
                reduce.add_y(1)
                reduce.start_z(1)

    @pl.loop(0, blocks)
    def _(index):
        rows = rows_of(index)
        for_query, for_value = back_low(rows, width, dq_s, dk_s, dv_s, low_s)
        for number, bits in enumerate((3, 1, 2, 0)):

            @pl.when(step == number)
            def _(bits=bits):
                late_s[0, pl.ds(partner(place, bits, 4), 1), :] += for_query
                late_s[0, pl.ds(4 + partner(place, bits, 4), 1), :] += for_value

    share = held_i.shape[3]
    for half in range(2):

        @pl.loop(0, model // (2 * share))
        def _(z):
            rows = pl.ds(pl.multiple_of(z * 2 * share, 2 * share), 2 * share)
            slots = (0, 1) if half == 0 else (2, 3)
            grads = back_weights(rows, width, slots, xt_s, dmixt_s, low_s, att_ref)
            for y in range(2):
                piece = grads[y * share : (y + 1) * share]

                @pl.when(step < 2)
                def _(y=y, piece=piece):
                    send_a[half, step, z, y] = piece

                @pl.when(step >= 2)
                def _(y=y, piece=piece):
                    held_a[half, 3 - step, z, y] = piece

        for number, j in ((0, 1), (1, 0)):

            @pl.when(step == number)
            def _(number=number, j=j):
                attn[half].core_copy(j, send_a.at[half, number]).start()

        @pl.when(step == 3)
        def _():
            attn[half].add_core(0)
            attn[half].y_copy(0).start()

    @pl.when(step == 3)
    def _():
        hop(LATE_SUMS, late_s, late_r, 0).start()

    @pl.loop(0, quarters)
    def _(index):
        rows = rows_of(index, part)
        dtok_s[rows, :] += back_tokens(rows, w_s, low_s)

        @pl.when(step == 3)
        def _():
            dlow_s[index] = dtok_s[rows, :].astype(BF16)

    @pl.when(step == 3)
    def _():
        for bits in (2, 3, 1):
            exchange(TOKEN_GRADS, dlow_s, dtok_res, bits, True).start()
        keep_dtok.start()
        next_hop(LATE_SUMS, late_s, late_r, 0)
        go_res[...] = outer.total_z(0)
        inner.x_copy().wait_recv()
        gi_res[...] = inner.total_z(0) + x_i[...].astype(F32)
        next_hop(LATE_SUMS, late_s, late_r, 1)
        for reduce in attn:
            reduce.send_x()
        next_hop(LATE_SUMS, late_s, late_r, 2)
        for reduce in attn:
            reduce.add_y(0)
            reduce.start_z(0)
        next_hop(LATE_SUMS, late_s, late_r, 3)
        add_hop(LATE_SUMS, late_s, late_r, 4)
        sum_res[...] = sums_s[5]
        late_res[...] = late_s[5]
        for half, result in enumerate((ga_one, ga_two)):
            attn[half].x_copy().wait_recv()
            result[...] = attn[half].total_z(0) + x_a[half].astype(F32)
        for bits in (1, 2, 3):
            for base, source, target in (
                (OUTPUTS, out_ref, out_res), (TOKEN_GRADS, dlow_s, dtok_res),
            ):
                exchange(base, source, target, bits, False).wait_recv()
                exchange(base, source, target, bits, True).wait_send()
        keep_out.wait()
        keep_dtok.wait()
        for number in range(len(HOPS)):
            hop(SUMS, sums_s, sums_r, number).wait_send()
            hop(LATE_SUMS, late_s, late_r, number).wait_send()
        for copy in core_sends(inner, gi_ref) + core_sends(outer, go_ref):
            copy.wait_send()
        inner.wait_sent((0, 1))
        inner.x_copy().wait_send()
        outer.wait_sent((0,))
        outer.whole_x_copy().wait_send()
        for half, reduce in enumerate(attn):
            for number, j in ((0, 1), (1, 0)):
                reduce.core_copy(j, send_a.at[half, number]).wait_send()
            reduce.wait_sent((0, 1))
            reduce.x_copy().wait_send()


VMEM_LIMIT = 60 * 1024 * 1024


def resident(shape):
    return pl.BlockSpec(shape, lambda step: (0,) * len(shape))


def stepped(shape):
    return pl.BlockSpec((1,) + shape[1:], lambda step: (step,) + (0,) * (len(shape) - 1))


def spec_list(pairs):
    return [stepped(shape) if moves else resident(shape) for shape, moves in pairs]


def attend_forward(tokens, cotangent, shard_a, shard_i, shard_o, biases, qaug, kaug, vaug, b_mixer):
    groups, part, model = tokens.shape
    length = groups * part
    share = shard_a.shape[0]
    block = (groups, length, PAD)
    whole = jax.ShapeDtypeStruct((groups, model // share, share, model), BF16)
    hidden = shard_i.shape[1]
    anywhere = pl.BlockSpec(memory_space=pl.ANY)
    return pl.pallas_call(
        attend_kernel,
        grid=(groups,),
        out_shape=[jax.ShapeDtypeStruct(block, BF16)] * 4
        + [
            jax.ShapeDtypeStruct((length, model), F32),
            jax.ShapeDtypeStruct((groups, 1, hidden), F32),
            jax.ShapeDtypeStruct(tokens.shape, BF16),
            jax.ShapeDtypeStruct(tokens.shape, BF16),
            whole,
            whole,
            whole,
        ],
        in_specs=[anywhere] * 5
        + spec_list(
            [
                (biases.shape, 0), (qaug.shape, 0), (kaug.shape, 0), (vaug.shape, 0),
                (b_mixer.shape, 0),
            ]
        ),
        out_specs=spec_list([(block, 1)] * 4 + [((length, model), 0), ((groups, 1, hidden), 1)])
        + [anywhere] * 5,
        scratch_shapes=[
            pltpu.VMEM((4, model, PAD), BF16),
            pltpu.VMEM(tokens.shape, BF16),
            pltpu.VMEM(whole.shape, BF16),
            pltpu.VMEM((groups,) + biases.shape, F32),
            pltpu.SemaphoreType.DMA((FORWARD_WIRES,)),
            pltpu.SemaphoreType.DMA((FORWARD_WIRES,)),
            pltpu.SemaphoreType.DMA((8,)),
        ],
        compiler_params=pltpu.CompilerParams(
            vmem_limit_bytes=VMEM_LIMIT, collective_id=0, has_side_effects=True
        ),
        name="attend_forward",
    )(tokens, cotangent, shard_a, shard_i, shard_o, biases, qaug, kaug, vaug, b_mixer)


def attend_plain(x, a_all, biases, qaug, kaug, vaug, b_mixer):
    length, model = x.shape
    groups = a_all.shape[0]
    block = (groups, length, PAD)
    return pl.pallas_call(
        attend_plain_kernel,
        grid=(groups,),
        out_shape=[jax.ShapeDtypeStruct(block, BF16)] * 4 + [jax.ShapeDtypeStruct(x.shape, F32)],
        in_specs=spec_list(
            [
                (x.shape, 0), (a_all.shape, 1), (biases.shape, 1),
                (qaug.shape, 0), (kaug.shape, 0), (vaug.shape, 0), (b_mixer.shape, 0),
            ]
        ),
        out_specs=spec_list([(block, 1)] * 4 + [(x.shape, 0)]),
        scratch_shapes=[pltpu.VMEM((4, model, PAD), BF16)],
        compiler_params=pltpu.CompilerParams(vmem_limit_bytes=VMEM_LIMIT),
        name="attend_plain",
    )(x, a_all, biases, qaug, kaug, vaug, b_mixer)


def dense_both(first_sum, wi, wo, bi, vectors, cotangent):
    length, model = first_sum.shape
    groups, _, hidden = wi.shape
    grad = (groups, model, hidden)
    forth = lambda shape: pl.BlockSpec(
        (1,) + shape[1:], lambda step: (lax.rem(step, groups),) + (0,) * (len(shape) - 1)
    )
    late = lambda shape: pl.BlockSpec(
        (1,) + shape[1:], lambda step: (jnp.maximum(step - groups, 0),) + (0,) * (len(shape) - 1)
    )
    return pl.pallas_call(
        dense_kernel,
        grid=(2 * groups,),
        out_shape=[
            jax.ShapeDtypeStruct((length, model), BF16),
            jax.ShapeDtypeStruct((length, model), F32),
            jax.ShapeDtypeStruct((length, model), BF16),
            jax.ShapeDtypeStruct(grad, BF16),
            jax.ShapeDtypeStruct(grad, BF16),
            jax.ShapeDtypeStruct((groups, 1, hidden), F32),
            jax.ShapeDtypeStruct((8, model), F32),
        ],
        in_specs=[
            pl.BlockSpec(memory_space=pl.ANY), forth(wi.shape), forth(wo.shape), forth(bi.shape),
            resident(vectors.shape), resident(cotangent.shape),
        ],
        out_specs=[
            resident((length, model)), resident((length, model)), resident((length, model)),
            late(grad), late(grad), late((groups, 1, hidden)), resident((8, model)),
        ],
        scratch_shapes=[
            pltpu.VMEM((length, model), F32),
            pltpu.VMEM((length, model), F32),
            pltpu.VMEM((length, model), F32),
            pltpu.VMEM((length, model), F32),
            pltpu.VMEM((groups, length, hidden), BF16),
            pltpu.VMEM((groups, length, hidden), BF16),
            pltpu.VMEM((length, model), BF16),
            pltpu.VMEM((model, length), BF16),
            pltpu.VMEM((model, length), BF16),
            pltpu.VMEM((length, hidden), BF16),
        ],
        compiler_params=pltpu.CompilerParams(vmem_limit_bytes=VMEM_LIMIT),
        name="dense_both",
    )(first_sum, wi, wo, bi, vectors, cotangent)


def attend_backward(x, a_all, d_mixed, d_first, q, k, v, attended):
    length, model = x.shape
    groups = a_all.shape[0]
    sums = (groups, 1, PAD)
    return pl.pallas_call(
        attend_back_kernel,
        grid=(groups,),
        out_shape=[
            jax.ShapeDtypeStruct(x.shape, F32),
            jax.ShapeDtypeStruct(a_all.shape, BF16),
            jax.ShapeDtypeStruct(sums, F32),
            jax.ShapeDtypeStruct(sums, F32),
        ],
        in_specs=spec_list(
            [
                (x.shape, 0), (a_all.shape, 1), (d_mixed.shape, 0), (d_first.shape, 0),
                (q.shape, 1), (k.shape, 1), (v.shape, 1), (attended.shape, 1),
            ]
        ),
        out_specs=spec_list([(x.shape, 0), (a_all.shape, 1), (sums, 1), (sums, 1)]),
        scratch_shapes=[
            pltpu.VMEM((4, model, PAD), BF16),
            pltpu.VMEM((model, length), BF16),
            pltpu.VMEM((model, length), BF16),
            pltpu.VMEM((PAD, length), BF16),
            pltpu.VMEM((PAD, length), F32),
            pltpu.VMEM((length, PAD), F32),
            pltpu.VMEM((length, PAD), F32),
            pltpu.VMEM((3, length, PAD), BF16),
        ],
        compiler_params=pltpu.CompilerParams(vmem_limit_bytes=VMEM_LIMIT),
        name="attend_backward",
    )(x, a_all, d_mixed, d_first, q, k, v, attended)


def attend_reduce(x, a_all, d_mixed, d_first, q, k, v, attended, g_inner, g_outer, out, dbi, small):
    quarters, part, model = x.shape
    length = quarters * part
    share = model // 8
    half = model // 2
    block = (4, 2, share, model)
    anywhere = pl.BlockSpec(memory_space=pl.ANY)

    def ordered(shape):
        return pl.BlockSpec(
            (1,) + shape[1:], lambda step: (slot_at(step),) + (0,) * (len(shape) - 1)
        )

    def vmem(*shape, kind=BF16):
        return pltpu.VMEM(shape, kind)

    final = [
        ((share, half), F32), ((share, half), F32), ((share, model), F32), ((share, model), F32),
        ((16, model), F32), ((8, PAD), F32),
    ]
    return pl.pallas_call(
        attend_reduce_kernel,
        grid=(4,),
        out_shape=[jax.ShapeDtypeStruct(x.shape, BF16)] * 2
        + [jax.ShapeDtypeStruct(*each) for each in final],
        in_specs=[anywhere, ordered(a_all.shape), anywhere, anywhere]
        + [ordered(q.shape)] * 4
        + [anywhere] * 3
        + [resident(dbi.shape), resident(small.shape)],
        out_specs=[anywhere] * 2 + [resident(each[0]) for each in final],
        scratch_shapes=[
            vmem(4, model, PAD), vmem(model, length), vmem(model, length), vmem(PAD, length),
            vmem(PAD, length, kind=F32), vmem(length, PAD, kind=F32),
            vmem(length, PAD, kind=F32), vmem(3, length, PAD), vmem(length, model),
            vmem(length, model, kind=F32), vmem(quarters, part, model),
            vmem(6, 16, model, kind=F32), vmem(6, 8, PAD, kind=F32),
            vmem(5, 16, model, kind=F32), vmem(5, 8, PAD, kind=F32),
            vmem(2, *block), vmem(2, *block), vmem(2, 4, share, model),
            vmem(2, 3, share, model), vmem(share, model),
            vmem(2, *block), vmem(2, *block), vmem(1, 4, share, model),
            vmem(1, 3, share, model), vmem(*block),
            vmem(2, 2, 4, 2, share, half), vmem(2, 2, 4, 2, share, half),
            vmem(2, 2, 4, 2, share, half), vmem(2, 2, 4, share, half),
            vmem(2, 2, 3, share, half), vmem(2, share, half),
            pltpu.SemaphoreType.DMA((BACKWARD_WIRES,)),
            pltpu.SemaphoreType.DMA((BACKWARD_WIRES,)),
            pltpu.SemaphoreType.DMA((9,)),
        ],
        compiler_params=pltpu.CompilerParams(
            vmem_limit_bytes=VMEM_LIMIT, collective_id=1, has_side_effects=True
        ),
        name="attend_reduce",
    )(x, a_all, d_mixed, d_first, q, k, v, attended, g_inner, g_outer, out, dbi, small)


def augment(labels, width):
    length = labels.shape[0]
    lanes = lax.broadcasted_iota(jnp.int32, (length, PAD), 1)
    in_docs = (lanes >= width) & (lanes < width + DOCS)
    same = (lanes - width) == labels[:, None]
    qaug = jnp.where(in_docs & same, 1.0, 0.0).astype(BF16)
    spare = (lanes >= width + DOCS) & (lanes < width + DOCS + 3 * (width // HEAD))
    kaug = jnp.where(in_docs & ~same, -(2.0**100), jnp.where(spare, 1.0, 0.0)).astype(BF16)
    vaug = jnp.where((lanes[:1] == width) | spare[:1], 1.0, 0.0).astype(BF16)
    return qaug, kaug, vaug


def body(
    tokens, doc_ids, w_query, b_query, w_key, w_value, b_value, w_mixer, b_mixer, gain_one,
    bias_one, w_inner, b_inner, w_outer, b_outer, gain_two, bias_two, cotangent,
):
    groups = lax.axis_size("tensor")
    rings = lax.axis_size("dp")
    place = lax.axis_index("tensor")
    width = w_query.shape[1]
    hidden = w_inner.shape[1]
    length = doc_ids.shape[2]
    model = tokens.shape[3]
    near = groups == 4 and rings == 8

    labels = lax.dynamic_index_in_dim(doc_ids[:, 0], place, 0, keepdims=False)
    qaug, kaug, vaug = augment(labels, width)
    shard_a = jnp.concatenate([w_query, w_key, w_value, w_mixer.T], axis=1)
    shard_o = w_outer.T
    spare = jnp.zeros((PAD - width,), F32)
    biases = jnp.concatenate([b_query, spare, b_value, spare, b_inner])[None]
    vectors = jnp.stack([gain_one, bias_one, b_outer, gain_two, bias_two] + [b_outer] * 3)
    if near:
        *saved, first_sum, bi, x, cot, a_all, wi, wo = attend_forward(
            tokens[:, 0], cotangent[:, 0], shard_a, w_inner, shard_o, biases, qaug, kaug, vaug,
            b_mixer[None],
        )
        a_all, wi, wo = (part.reshape(groups, model, model) for part in (a_all, wi, wo))
        out, d_first, d_mixed, g_inner, g_outer, dbi, small = dense_both(
            first_sum, wi, wo, bi, vectors, cot.reshape(length, model)
        )
        pieces = (groups, 4, 2, model // rings, model)
        out, d_tokens, ga_one, ga_two, gi, go, tail, late = attend_reduce(
            x, a_all, d_mixed, d_first, *saved, g_inner.reshape(pieces), g_outer.reshape(pieces),
            out.reshape(x.shape), dbi, small,
        )
        ga = jnp.concatenate([ga_one, ga_two], axis=1)
        own = lambda whole, start: lax.dynamic_index_in_dim(whole, start + place, 0, False)
        dbq, dbv = own(late, 0)[:width], own(late, groups)[:width]
        dbi = own(tail, 0)
        tail = tail[2 * groups :]
        out, d_tokens = out[:, None], d_tokens[:, None].astype(F32)
    else:

        def gather(shard):
            whole = lax.all_gather(shard, ("tensor", "dp"), axis=0, tiled=True)
            return whole.reshape(groups, model, shard.shape[1])

        def to_sequence(part):
            return lax.all_to_all(part, "tensor", 0, 2, tiled=True).reshape(length, model)

        def from_sequence(whole):
            return lax.all_to_all(whole.reshape(1, 1, length, model), "tensor", 2, 0, tiled=True)

        def scatter(part):
            flat = part.reshape(-1, part.shape[2])
            total = lax.psum_scatter(flat, ("tensor", "dp"), scatter_dimension=0, tiled=True)
            return total.astype(F32)

        x, cot = to_sequence(tokens), to_sequence(cotangent)
        a_all, wi, wo = gather(shard_a), gather(w_inner), gather(shard_o)
        every = lax.all_gather(biases, "tensor", axis=0)
        *saved, first_sum = attend_plain(x, a_all, every, qaug, kaug, vaug, b_mixer[None])
        out, d_first, d_mixed, g_inner, g_outer, dbi, small = dense_both(
            first_sum, wi, wo, every[:, :, 2 * PAD :], vectors, cot
        )
        d_tokens, g_attend, dbq, dbv = attend_backward(x, a_all, d_mixed, d_first, *saved)
        ga, gi, go = scatter(g_attend), scatter(g_inner), scatter(g_outer)
        rows = [dbq[:, 0, :width], dbv[:, 0, :width], dbi[:, 0], small]
        summed = lax.psum(jnp.concatenate([part.reshape(-1) for part in rows]), ("dp", "tensor"))
        own = lambda start, size: lax.dynamic_slice_in_dim(summed, start + place * size, size)
        dbq, dbv, dbi = own(0, width), own(model, width), own(2 * model, hidden)
        tail = summed[-small.size :].reshape(small.shape)
        out, d_tokens = from_sequence(out), from_sequence(d_tokens)
    return (
        out,
        d_tokens,
        ga[:, :width],
        dbq,
        ga[:, width : 2 * width],
        ga[:, 2 * width : 3 * width],
        dbv,
        ga[:, 3 * width :].T,
        tail[3],
        tail[4],
        tail[5],
        gi,
        dbi,
        go.T,
        tail[0],
        tail[1],
        tail[2],
    )


def solution(mesh):
    split = P(None, "dp", "tensor", None)
    both, flipped, part = P("dp", "tensor"), P("tensor", "dp"), P("tensor")
    return jax.shard_map(
        body,
        mesh=mesh,
        in_specs=(
            split, P(None, "dp", None), both, part, both, both, part, flipped, P(), P(), P(),
            both, part, flipped, P(), P(), P(), split,
        ),
        out_specs=(
            split, split, both, part, both, both, part, flipped, P(), P(), P(), both, part,
            flipped, P(), P(), P(),
        ),
        check_vma=False,
    )
```

```python
from functools import partial

import jax
import jax.numpy as jnp
from jax import lax
from jax.experimental import pallas as pl
from jax.experimental.pallas import tpu as pltpu
from jax.sharding import PartitionSpec as P

HEAD = 64
DOCS = 8
PAD = 256
ROWS = 256
LOG2E = 1.4426950408889634
EPS = 1e-12
F32 = jnp.float32
BF16 = jnp.bfloat16


def dot_nn(left, right):
    return lax.dot_general(left, right, (((1,), (0,)), ((), ())), preferred_element_type=F32)


def dot_nt(left, right):
    return lax.dot_general(left, right, (((1,), (1,)), ((), ())), preferred_element_type=F32)


def rows_of(index, size=ROWS):
    return pl.ds(pl.multiple_of(index * size, size), size)


def lane_index(shape):
    return lax.broadcasted_iota(jnp.int32, shape, 1)


def three_parts(values):
    high = values.astype(BF16)
    rest = values - high.astype(F32)
    middle = rest.astype(BF16)
    low = (rest - middle.astype(F32)).astype(BF16)
    return high, middle, low


def head_only(lanes, head):
    return (lanes >= head * HEAD) & (lanes < (head + 1) * HEAD)


def head_and_extra(lanes, head, width):
    extra = width + DOCS + 3 * head
    return (
        head_only(lanes, head)
        | ((lanes >= width) & (lanes < width + DOCS))
        | ((lanes >= extra) & (lanes < extra + 3))
    )


def unpack(block_ref, slot, width):
    part = block_ref[:, slot * width : (slot + 1) * width]
    return jnp.concatenate([part, jnp.zeros((part.shape[0], PAD - width), part.dtype)], axis=1)


def project(x_rows, rows, bq, bv, w_s, qaug_ref, kaug_ref, vaug_ref, q_ref, k_ref, v_ref):
    queries = (dot_nn(x_rows, w_s[0]) + bq).astype(BF16)
    q_ref[rows, :] = queries * jnp.asarray(HEAD**-0.5, BF16) + qaug_ref[rows, :]
    keys = dot_nn(x_rows, w_s[1]).astype(BF16)
    k_ref[rows, :] = keys + kaug_ref[rows, :]
    values = (dot_nn(x_rows, w_s[2]) + bv).astype(BF16)
    v_ref[rows, :] = values + vaug_ref[...]


def attend_rows(rows, width, w_s, q_ref, k_ref, v_ref, att_ref, first_ref):
    lanes = lane_index((ROWS, PAD))
    queries = q_ref[rows, :]
    attended = jnp.zeros((ROWS, PAD), F32)
    extended = queries
    for head in range(width // HEAD):
        masked = jnp.where(head_and_extra(lanes, head, width), queries, 0)
        scores = dot_nt(masked, k_ref[...])
        highest = jnp.max(scores, axis=1, keepdims=True)
        raw = jnp.exp2((scores - highest) * LOG2E).astype(BF16)
        mixed = dot_nn(raw, v_ref[...])
        total = mixed[:, width : width + 1]
        attended = jnp.where(head_only(lanes, head), mixed / total, attended)
        for spot, part in enumerate(three_parts(-(highest + jnp.log(total)))):
            here = lanes == width + DOCS + 3 * head + spot
            extended = jnp.where(here, jnp.broadcast_to(part, (ROWS, PAD)), extended)
    q_ref[rows, :] = extended
    attended = attended.astype(BF16)
    att_ref[rows, :] = attended
    first_ref[rows, :] += dot_nt(attended, w_s[3])


def attend_plain_kernel(
    x_ref, a_ref, bias_ref, qaug_ref, kaug_ref, vaug_ref, bm_ref,
    q_ref, k_ref, v_ref, att_ref, first_ref, w_s,
):
    length, model = x_ref.shape
    width = a_ref.shape[2] // 4
    for slot in range(4):
        w_s[slot] = unpack(a_ref.at[0], slot, width)
    biases = bias_ref[0]

    @pl.when(pl.program_id(0) == 0)
    def _():
        first_ref[...] = x_ref[...].astype(F32) + bm_ref[...]

    @pl.loop(0, length // ROWS)
    def _(index):
        rows = rows_of(index)
        project(
            x_ref[rows, :], rows, biases[:, :PAD], biases[:, PAD : 2 * PAD], w_s, qaug_ref,
            kaug_ref, vaug_ref, q_ref.at[0], k_ref.at[0], v_ref.at[0],
        )

    @pl.loop(0, length // ROWS)
    def _(index):
        refs = (ref.at[0] for ref in (q_ref, k_ref, v_ref, att_ref))
        attend_rows(rows_of(index), width, w_s, *refs, first_ref)


MESH = pl.DeviceIdType.MESH


def partner(index, bits, size):
    flipped = index
    for bit in (1, 2, 4):
        if bits & bit and bit < size:
            flipped = flipped + bit - 2 * bit * lax.rem(lax.div(index, bit), 2)
    return flipped


class Wires:
    def __init__(self, send, recv, place, row):
        self.send, self.recv, self.place, self.row = send, recv, place, row

    def to(self, tensor_bits, dp_bits):
        return (partner(self.row, dp_bits, 8), partner(self.place, tensor_bits, 4))

    def copy(self, number, source, target, tensor_bits=0, dp_bits=0):
        return pltpu.make_async_remote_copy(
            src_ref=source,
            dst_ref=target,
            send_sem=self.send.at[number],
            recv_sem=self.recv.at[number],
            device_id=self.to(tensor_bits, dp_bits),
            device_id_type=MESH,
        )


def greet(wires, peers):
    barrier = pltpu.get_barrier_semaphore()
    for tensor_bits, dp_bits in peers:
        pl.semaphore_signal(
            barrier, inc=1, device_id=wires.to(tensor_bits, dp_bits), device_id_type=MESH
        )
    pl.semaphore_wait(barrier, len(peers))


PEERS = ((1, 0), (2, 0), (3, 0), (0, 1), (0, 2), (0, 4), (0, 6))
TOKENS, COTS, BIASES, KIND_A = 0, 3, 6, 9
KIND_I = KIND_A + 17
KIND_O = KIND_I + 17
FORWARD_WIRES = KIND_O + 10


class ShardGather:
    def __init__(self, wires, base, shard, whole):
        self.wires, self.base, self.shard, self.whole = wires, base, shard, whole

    def at(self, slot, dp_bits):
        return self.whole.at[slot, partner(self.wires.row, dp_bits, 8)]

    def cross_x(self):
        return self.wires.copy(self.base, self.shard, self.at(2, 0), 2, 0)

    def along_z(self, slot, step, mine):
        source = self.shard if slot == 0 else self.at(slot, 0)
        number = self.base + 1 + 3 * (slot // 2) + step - 1
        target = self.at(slot, 0) if mine else self.at(slot, 2 * step)
        return self.wires.copy(number, source, target, 0, 2 * step)

    def along_y(self, slot, step, mine):
        source = self.shard if slot == 0 and step == 0 else self.at(slot, 2 * step)
        number = self.base + 7 + 4 * (slot // 2) + step
        target = self.at(slot, 2 * step) if mine else self.at(slot, 2 * step + 1)
        return self.wires.copy(number, source, target, 0, 1)

    def to_core(self, slot, mine):
        number = self.base + 15 + slot // 2
        target = self.whole.at[slot + 1]
        return self.wires.copy(number, self.whole.at[slot], target, 1, 0)

    def start_z(self, slot):
        for step in (1, 2, 3):
            self.along_z(slot, step, True).start()

    def wait_z(self, slot):
        for step in (1, 2, 3):
            self.along_z(slot, step, False).wait_recv()

    def pass_y(self, slot):
        for step in (1, 2, 3):
            self.along_y(slot, step, True).start()

    def wait_y(self, slot):
        for step in range(4):
            self.along_y(slot, step, False).wait_recv()

    def wait_sent(self, x_first=True):
        for slot in (0, 2) if x_first else (0,):
            for step in (1, 2, 3):
                self.along_z(slot, step, True).wait_send()
            for step in range(4):
                self.along_y(slot, step, True).wait_send()
        for slot in (0, 2):
            self.to_core(slot, True).wait_send()


class BlockGather(ShardGather):
    def along_z(self, slot, step, mine):
        target = self.at(0, 0) if mine else self.at(0, 2 * step)
        return self.wires.copy(self.base + step - 1, self.shard, target, 0, 2 * step)

    def along_y(self, slot, step, mine):
        source = self.shard if step == 0 else self.at(0, 2 * step)
        target = self.at(0, 2 * step) if mine else self.at(0, 2 * step + 1)
        return self.wires.copy(self.base + 3 + step, source, target, 0, 1)

    def cross_x(self):
        return self.wires.copy(self.base + 7, self.whole.at[0], self.whole.at[2], 2, 0)

    def to_core(self, slot, mine):
        return self.wires.copy(
            self.base + 8 + slot // 2, self.whole.at[slot], self.whole.at[slot + 1], 1, 0
        )


def gelu_parts(values):
    phi = jnp.exp2(values * values * (-0.5 * LOG2E)) * 0.3989422804014327
    total = 0.5 + 0.5 * lax.erf(values * 0.7071067811865476)
    return values * total, total + values * phi


def norm_parts(values):
    average = jnp.mean(values, axis=-1, keepdims=True)
    centred = values - average
    spread = jnp.mean(centred * centred, axis=-1, keepdims=True)
    inverse = lax.rsqrt(spread + EPS)
    return centred * inverse, inverse


def norm_back(grads, gain, unit, inverse):
    scaled = grads * gain
    average = jnp.mean(scaled, axis=-1, keepdims=True)
    along = jnp.mean(scaled * unit, axis=-1, keepdims=True)
    return (scaled - average - unit * along) * inverse


def column_sum(values):
    return jnp.sum(values, axis=0, keepdims=True)


def forward_kernel(
    tok_ref, cot_ref, sa_ref, si_ref, so_ref, bias_ref, qaug_ref, kaug_ref, vaug_ref, bm_ref,
    vec_ref,
    acts_ref, att_ref, slope_ref, first_out, second_out, low_out, x_out, cot_out, wia_out, wo_out,
    w_s, x_s, a_s, i_s, o_s, bias_s, first_s, second_s, low_s, send_sem, recv_sem, here_sem,
):
    step = pl.program_id(0)
    place = lax.axis_index("tensor")
    row = lax.axis_index("dp")
    quarters, part, model = x_s.shape
    length = quarters * part
    width = sa_ref.shape[1] // 4
    blocks = length // ROWS
    share = sa_ref.shape[0]
    wires = Wires(send_sem, recv_sem, place, row)
    attn = ShardGather(wires, KIND_A, sa_ref, a_s)
    inner = ShardGather(wires, KIND_I, si_ref, i_s)
    outer = BlockGather(wires, KIND_O, so_ref, o_s)
    gain_one, bias_one, b_outer = (vec_ref[i : i + 1, :] for i in range(3))
    q_ref, k_ref, v_ref = (acts_ref.at[0, :, i * PAD : (i + 1) * PAD] for i in range(3))

    def exchange(base, source, target, bits, mine):
        other = partner(place, bits, 4)
        return wires.copy(
            base + bits - 1, source.at[other], target.at[place if mine else other], bits, 0
        )

    def bias_copy(bits, mine):
        return wires.copy(BIASES + bits - 1, bias_ref, bias_s.at[bits], bits, 0)

    local = [
        pltpu.make_async_copy(tok_ref.at[place], x_s.at[place], here_sem.at[0]),
        pltpu.make_async_copy(sa_ref, a_s.at[0, row], here_sem.at[1]),
        pltpu.make_async_copy(si_ref, i_s.at[0, row], here_sem.at[2]),
        pltpu.make_async_copy(so_ref, o_s.at[0, row], here_sem.at[3]),
        pltpu.make_async_copy(bias_ref, bias_s.at[0], here_sem.at[4]),
    ]
    own_cot = pltpu.make_async_copy(cot_ref.at[place], cot_out.at[place], here_sem.at[5])
    keep_x = pltpu.make_async_copy(x_s, x_out, here_sem.at[6])
    keep_a = pltpu.make_async_copy(a_s, wia_out.at[1], here_sem.at[7])
    keep_i = pltpu.make_async_copy(i_s, wia_out.at[0], here_sem.at[8])
    keep_o = pltpu.make_async_copy(o_s, wo_out, here_sem.at[9])
    keep_first = pltpu.make_async_copy(first_s, first_out, here_sem.at[10])
    keep_low = pltpu.make_async_copy(low_s, low_out, here_sem.at[11])
    keep_second = pltpu.make_async_copy(second_s, second_out, here_sem.at[12])

    @pl.when(step == 0)
    def _():
        greet(wires, PEERS)
        attn.cross_x().start()
        for bits in (1, 2, 3):
            bias_copy(bits, True).start()
        attn.start_z(0)
        attn.along_y(0, 0, True).start()
        for bits in (2, 3, 1):
            exchange(TOKENS, tok_ref, x_s, bits, True).start()
        for copy in local:
            copy.start()
        own_cot.start()
        for copy in local:
            copy.wait()
        attn.cross_x().wait_recv()
        attn.start_z(2)
        attn.along_y(2, 0, True).start()
        attn.wait_z(0)
        attn.pass_y(0)
        attn.wait_y(0)
        attn.to_core(0, True).start()
        inner.cross_x().start()
        for bits in (1, 2, 3):
            exchange(TOKENS, tok_ref, x_s, bits, False).wait_recv()
            bias_copy(bits, False).wait_recv()
        keep_x.start()

        @pl.loop(0, quarters)
        def _(index):
            rows = rows_of(index, part)
            first_s[rows, :] = x_s[index].astype(F32) + bm_ref[...]

    @pl.when(step == 1)
    def _():
        attn.to_core(0, False).wait_recv()

    @pl.when(step == 2)
    def _():
        attn.wait_y(2)
        attn.to_core(2, True).start()

    @pl.when(step == 3)
    def _():
        attn.to_core(2, False).wait_recv()
        keep_a.start()

    @pl.when(step < 4)
    def _():
        for dp_row in range(a_s.shape[1]):
            packed = a_s[step, dp_row]
            rest = jnp.zeros((share, PAD - width), packed.dtype)
            for slot in range(4):
                piece = packed[:, slot * width : (slot + 1) * width]
                rows = slice(dp_row * share, (dp_row + 1) * share)
                w_s[slot, rows, :] = jnp.concatenate([piece, rest], axis=1)
        biases = bias_s[step]

        @pl.loop(0, quarters)
        def _(index):
            rows = rows_of(index, part)
            x_rows = x_s[index]
            project(
                x_rows, rows, biases[:, :PAD], biases[:, PAD : 2 * PAD], w_s, qaug_ref, kaug_ref,
                vaug_ref, q_ref, k_ref, v_ref,
            )

        @pl.loop(0, blocks)
        def _(index):
            attend_rows(
                rows_of(index), width, w_s, q_ref, k_ref, v_ref, att_ref.at[0], first_s
            )

            @pl.when((step == 0) & (index == 0))
            def _():
                outer.start_z(0)
                outer.along_y(0, 0, True).start()
                for bits in (2, 3, 1):
                    exchange(COTS, cot_ref, cot_out, bits, True).start()

            @pl.when((step == 0) & (index == 1))
            def _():
                attn.wait_z(2)
                attn.pass_y(2)

            @pl.when((step == 0) & (index == 3))
            def _():
                inner.start_z(0)
                inner.along_y(0, 0, True).start()

            @pl.when((step == 1) & (index == 1))
            def _():
                outer.wait_z(0)
                outer.pass_y(0)

            @pl.when((step == 1) & (index == 2))
            def _():
                inner.cross_x().wait_recv()
                inner.start_z(2)
                inner.along_y(2, 0, True).start()

            @pl.when((step == 2) & (index == 2))
            def _():
                inner.wait_z(0)
                inner.pass_y(0)

            @pl.when((step == 2) & (index == 3))
            def _():
                outer.wait_y(0)
                outer.cross_x().start()
                outer.to_core(0, True).start()

            @pl.when((step == 3) & (index == 1))
            def _():
                inner.wait_y(0)
                inner.to_core(0, True).start()

            @pl.when((step == 3) & (index == 3))
            def _():
                inner.wait_z(2)
                inner.pass_y(2)

    @pl.when(step == 4)
    def _():
        keep_first.start()

        @pl.loop(0, blocks)
        def _(index):
            rows = rows_of(index)
            unit, _inverse = norm_parts(first_s[rows, :])
            normed = unit * gain_one + bias_one
            low_s[rows, :] = normed.astype(BF16)
            second_s[rows, :] = normed + b_outer

        keep_low.start()

    @pl.when(step == 5)
    def _():
        inner.to_core(0, False).wait_recv()
        outer.to_core(0, False).wait_recv()

    @pl.when(step == 6)
    def _():
        inner.wait_y(2)
        inner.to_core(2, True).start()
        outer.cross_x().wait_recv()
        outer.to_core(2, True).start()

    @pl.when(step == 7)
    def _():
        inner.to_core(2, False).wait_recv()
        outer.to_core(2, False).wait_recv()
        keep_i.start()
        keep_o.start()

    @pl.when(step >= 4)
    def _():
        slot = step - 4
        w_inner = i_s[slot].reshape(model, model)
        w_outer = o_s[slot].reshape(model, model)
        b_inner = bias_s[slot][:, 2 * PAD :]

        @pl.loop(0, blocks)
        def _(index):
            rows = rows_of(index)
            value, slope = gelu_parts(dot_nn(low_s[rows, :], w_inner) + b_inner)
            hidden = value.astype(BF16)
            acts_ref[0, rows, :] = hidden
            slope_ref[0, rows, :] = slope.astype(BF16)
            second_s[rows, :] += dot_nt(hidden, w_outer)

    @pl.when(step == 7)
    def _():
        keep_second.start()
        for bits in (1, 2, 3):
            exchange(COTS, cot_ref, cot_out, bits, False).wait_recv()
        for gather in (attn, inner, outer):
            gather.cross_x().wait_send()
            gather.wait_sent(gather is not outer)
        for bits in (1, 2, 3):
            exchange(TOKENS, tok_ref, x_s, bits, True).wait_send()
            exchange(COTS, cot_ref, cot_out, bits, True).wait_send()
            bias_copy(bits, True).wait_send()
        for copy in (
            own_cot, keep_x, keep_a, keep_i, keep_o, keep_first, keep_low, keep_second,
        ):
            copy.wait()


def dense_kernel(
    first_in, wi_ref, wo_ref, bi_ref, vec_ref, cot_ref,
    out_ref, dfirst_ref, dmix_ref, gi_ref, go_ref, dbi_ref, small_ref,
    first_ref, second_ref, normed_s, dsec_s, hidden_s, slope_s, low_s, low_t, back_t, dinner_s,
):
    step = pl.program_id(0)
    count = pl.num_programs(0) // 2
    length, model = first_in.shape
    blocks = length // ROWS
    gain_one, bias_one, b_outer, gain_two, bias_two = (vec_ref[i : i + 1, :] for i in range(5))

    @pl.when(step == 0)
    def _():
        copied = pltpu.sync_copy
        copied(first_in, first_ref)

        @pl.loop(0, blocks)
        def _(index):
            rows = rows_of(index)
            unit, _inverse = norm_parts(first_ref[rows, :])
            normed = unit * gain_one + bias_one
            normed_s[rows, :] = normed
            low_s[rows, :] = normed.astype(BF16)
            low_t[:, rows] = normed.astype(BF16).T
            second_ref[rows, :] = normed + b_outer

    @pl.when(step < count)
    def _():
        @pl.loop(0, blocks)
        def _(index):
            rows = rows_of(index)
            inner = dot_nn(low_s[rows, :], wi_ref[0]) + bi_ref[0]
            value, slope = gelu_parts(inner)
            hidden = value.astype(BF16)
            hidden_s[step, rows, :] = hidden
            slope_s[step, rows, :] = slope.astype(BF16)
            second_ref[rows, :] += dot_nt(hidden, wo_ref[0])

    @pl.when(step == count - 1)
    def _():
        small_ref[...] = jnp.zeros_like(small_ref)

        @pl.loop(0, blocks)
        def _(index):
            rows = rows_of(index)
            unit, inverse = norm_parts(second_ref[rows, :])
            out_ref[rows, :] = (unit * gain_two + bias_two).astype(BF16)
            grads = cot_ref[rows, :].astype(F32)
            d_second = norm_back(grads, gain_two, unit, inverse)
            small_ref[0:1, :] += column_sum(d_second)
            small_ref[1:2, :] += column_sum(grads * unit)
            small_ref[2:3, :] += column_sum(grads)
            dsec_s[rows, :] = d_second
            low = d_second.astype(BF16)
            dmix_ref[rows, :] = low
            back_t[:, rows] = low.T

    @pl.when(step >= count)
    def _():
        place = step - count
        dbi_ref[...] = jnp.zeros_like(dbi_ref)

        @pl.loop(0, blocks)
        def _(index):
            rows = rows_of(index)
            d_hidden = dot_nn(dmix_ref[rows, :], wo_ref[0])
            d_inner = (d_hidden * slope_s[place, rows, :].astype(F32)).astype(BF16)
            dinner_s[rows, :] = d_inner
            dbi_ref[0] += column_sum(d_inner.astype(F32))
            dsec_s[rows, :] += dot_nt(d_inner, wi_ref[0])

        @pl.loop(0, model // ROWS)
        def _(index):
            rows = rows_of(index)
            gi_ref[0, rows, :] = dot_nn(low_t[rows, :], dinner_s[...]).astype(gi_ref.dtype)
            go_ref[0, rows, :] = dot_nn(back_t[rows, :], hidden_s[place]).astype(go_ref.dtype)

    @pl.when(step == 2 * count - 1)
    def _():
        @pl.loop(0, blocks)
        def _(index):
            rows = rows_of(index)
            unit, inverse = norm_parts(first_ref[rows, :])
            grads = dsec_s[rows, :]
            d_first = norm_back(grads, gain_one, unit, inverse)
            small_ref[3:4, :] += column_sum(d_first)
            small_ref[4:5, :] += column_sum(grads * unit)
            small_ref[5:6, :] += column_sum(grads)
            dfirst_ref[rows, :] = d_first
            dmix_ref[rows, :] = d_first.astype(BF16)


def back_rows(rows, width, w_s, dmix_rows, q_ref, k_ref, v_ref, att_ref, kt_s, dq_s, dk_s, dv_s):
    lanes = lane_index((ROWS, PAD))
    queries = q_ref[rows, :]
    d_att = dot_nn(dmix_rows, w_s[3]).astype(BF16)
    product = d_att.astype(F32) * att_ref[rows, :].astype(F32)
    heads = range(width // HEAD)
    extended = d_att
    for head in heads:
        centre = jnp.sum(jnp.where(head_only(lanes, head), product, 0.0), axis=1, keepdims=True)
        for spot, part in enumerate(three_parts(-centre)):
            here = lanes == width + DOCS + 3 * head + spot
            extended = jnp.where(here, jnp.broadcast_to(part, (ROWS, PAD)), extended)
    chances_all = []
    d_scores_all = []
    d_att_all = []
    queries_all = []
    for head in heads:
        wide = head_and_extra(lanes, head, width)
        only = head_only(lanes, head)
        chances = jnp.exp2(dot_nt(k_ref[...], jnp.where(wide, queries, 0)) * LOG2E)
        d_chances = dot_nt(v_ref[...], jnp.where(wide, extended, 0))
        d_scores = (chances * d_chances).astype(BF16)
        chances_all.append(chances.astype(BF16))
        d_scores_all.append(d_scores)
        d_att_all.append(jnp.where(only, d_att, 0))
        queries_all.append(jnp.where(only, queries, 0))
        head_rows = slice(head * HEAD, (head + 1) * HEAD)
        dq_s[head_rows, rows] = dot_nn(kt_s[head_rows, :], d_scores)
    dv_s[...] += dot_nn(jnp.concatenate(chances_all, 1), jnp.concatenate(d_att_all, 0))
    dk_s[...] += dot_nn(jnp.concatenate(d_scores_all, 1), jnp.concatenate(queries_all, 0))


def back_low(rows, width, dq_s, dk_s, dv_s, low_s):
    d_query = (dq_s[:, rows].T * HEAD**-0.5).astype(BF16)
    d_query = jnp.where(lane_index(d_query.shape) < width, d_query, 0)
    d_value = dv_s[rows, :].astype(BF16)
    low_s[rows, :PAD] = d_query
    low_s[rows, PAD : 2 * PAD] = dk_s[rows, :].astype(BF16)
    low_s[rows, 2 * PAD :] = d_value
    return column_sum(d_query.astype(F32)), column_sum(d_value.astype(F32))


def back_tokens(rows, w_s, low_s):
    return sum(dot_nt(low_s[rows, slot * PAD : (slot + 1) * PAD], w_s[slot]) for slot in range(3))


def back_weights(rows, width, slots, xt_s, dmixt_s, low_s, att_ref):
    parts = []
    for slot in slots:
        if slot < 3:
            part = dot_nn(xt_s[rows, :], low_s[:, slot * PAD : (slot + 1) * PAD])
        else:
            part = dot_nn(dmixt_s[rows, :], att_ref[...])
        parts.append(part[:, :width])
    return jnp.concatenate(parts, axis=1).astype(BF16)


def attend_back_kernel(
    x_ref, a_ref, dmix_ref, dfirst_ref, q_ref, k_ref, v_ref, att_ref,
    dtok_ref, ga_ref, dbq_ref, dbv_ref,
    w_s, xt_s, dmixt_s, kt_s, dq_s, dk_s, dv_s, low_s,
):
    length, model = x_ref.shape
    width = a_ref.shape[2] // 4
    blocks = length // ROWS
    for slot in range(4):
        w_s[slot] = unpack(a_ref.at[0], slot, width)

    @pl.when(pl.program_id(0) == 0)
    def _():
        dtok_ref[...] = dfirst_ref[...]

        @pl.loop(0, blocks)
        def _(index):
            rows = rows_of(index)
            xt_s[:, rows] = x_ref[rows, :].T
            dmixt_s[:, rows] = dmix_ref[rows, :].T

    for sums in (dk_s, dv_s, dbq_ref, dbv_ref):
        sums[...] = jnp.zeros_like(sums)

    @pl.loop(0, blocks)
    def _(index):
        rows = rows_of(index)
        kt_s[:, rows] = k_ref[0, rows, :].T

    @pl.loop(0, blocks)
    def _(index):
        rows = rows_of(index)
        dmix_rows = dmix_ref[rows, :]
        refs = (ref.at[0] for ref in (q_ref, k_ref, v_ref, att_ref))
        back_rows(rows, width, w_s, dmix_rows, *refs, kt_s, dq_s, dk_s, dv_s)

    @pl.loop(0, blocks)
    def _(index):
        rows = rows_of(index)
        for_query, for_value = back_low(rows, width, dq_s, dk_s, dv_s, low_s)
        dbq_ref[0] += for_query
        dbv_ref[0] += for_value
        dtok_ref[rows, :] += back_tokens(rows, w_s, low_s)

    @pl.loop(0, model // ROWS)
    def _(index):
        rows = rows_of(index)
        ga_ref[0, rows, :] = back_weights(
            rows, width, range(4), xt_s, dmixt_s, low_s, att_ref.at[0]
        )


def add_into(target, source):
    target[...] = (target[...].astype(F32) + source[...].astype(F32)).astype(target.dtype)


class Reduce:
    COUNT = 11

    def __init__(self, wires, base, held, core, by_y, by_z, by_x, cols=slice(None)):
        self.wires, self.base, self.held, self.core = wires, base, held, core
        self.by_y, self.by_z, self.by_x = by_y, by_z, by_x
        self.cols = cols
        self.z, self.y = lax.div(wires.row, 2), lax.rem(wires.row, 2)

    def part(self, ref, *index):
        return ref.at[index + (slice(None), self.cols)]

    def core_copy(self, j, source):
        everything = (slice(None), slice(None))
        return self.wires.copy(
            self.base + j, self.part(source, *everything), self.part(self.core, j, *everything), 1, 0
        )

    def add_core(self, j):
        self.core_copy(j, self.held.at[j]).wait_recv()
        for z in range(4):
            for y in range(2):
                add_into(self.part(self.held, j, z, y), self.part(self.core, j, z, y))

    def y_copy(self, j):
        source = self.part(self.held, j, slice(None), 1 - self.y)
        return self.wires.copy(
            self.base + 2 + j, source, self.part(self.by_y, j, slice(None)), 0, 1
        )

    def add_y(self, j):
        self.y_copy(j).wait_recv()
        for z in range(4):
            add_into(self.part(self.held, j, z, self.y), self.part(self.by_y, j, z))

    def z_copy(self, j, step):
        other = lax.div(partner(self.wires.row, 2 * step, 8), 2)
        number = self.base + 4 + 3 * j + step - 1
        return self.wires.copy(
            number, self.part(self.held, j, other, self.y), self.part(self.by_z, j, step - 1),
            0, 2 * step,
        )

    def start_z(self, j):
        for step in (1, 2, 3):
            self.z_copy(j, step).start()

    def total_z(self, j):
        total = self.part(self.held, j, self.z, self.y)[...].astype(F32)
        for step in (1, 2, 3):
            self.z_copy(j, step).wait_recv()
            total = total + self.part(self.by_z, j, step - 1)[...].astype(F32)
        return total

    def x_copy(self):
        source = self.part(self.held, 1, self.z, self.y)
        return self.wires.copy(self.base + 10, source, self.part(self.by_x), 2, 0)

    def send_x(self):
        self.part(self.held, 1, self.z, self.y)[...] = self.total_z(1).astype(BF16)
        self.x_copy().start()

    def total(self):
        self.x_copy().wait_recv()
        return self.total_z(0) + self.part(self.by_x)[...].astype(F32)

    def whole_x_copy(self):
        return self.wires.copy(self.base + 10, self.held.at[1], self.by_x, 2, 0)

    def add_whole_x(self):
        self.whole_x_copy().wait_recv()
        for z in range(4):
            for y in range(2):
                add_into(self.held.at[0, z, y], self.by_x.at[z, y])

    def wait_sent(self, j_all):
        for j in j_all:
            self.y_copy(j).wait_send()
            for step in (1, 2, 3):
                self.z_copy(j, step).wait_send()


OUTPUTS, TOKEN_GRADS, SUMS, LATE_SUMS = 0, 3, 6, 11
RED_I = 16
RED_O = RED_I + Reduce.COUNT
RED_A = RED_O + Reduce.COUNT
BACKWARD_WIRES = RED_A + 2 * Reduce.COUNT
HOPS = ((1, 0), (2, 0), (0, 1), (0, 2), (0, 4))


def slot_at(step):
    return jnp.where(step < 2, 3 - 2 * step, 6 - 2 * step)


def backward_kernel(
    acts_ref, att_ref, slope_ref, wia_ref, wo_ref, vec_ref, second_ref, first_ref, low_ref, x_ref,
    cot_ref,
    out_res, dtok_res, ga_res, gi_res, go_res, sum_res, late_res,
    low_t, back_t, dmix_s, low_s, flow_s, out_s, grad_s, first_s, w_s, kt_s, dq_s, dk_s, dv_s,
    sums_s, late_s, sums_r, late_r,
    send_i, held_i, core_i, y_i, z_i, x_i, send_o, held_o, core_o, y_o, z_o, x_o,
    held_a, core_a, y_a, z_a, x_a,
    send_sem, recv_sem, here_sem,
):
    step = pl.program_id(0)
    place = lax.axis_index("tensor")
    row = lax.axis_index("dp")
    length, model = dmix_s.shape
    quarters, part, _ = flow_s.shape
    width = wia_ref.shape[2] // 4
    blocks = length // ROWS
    share = held_i.shape[3]
    wires = Wires(send_sem, recv_sem, place, row)
    inner = Reduce(wires, RED_I, held_i, core_i, y_i, z_i, x_i)
    outer = Reduce(wires, RED_O, held_o, core_o, y_o, z_o, x_o)
    halves = (slice(0, model // 2), slice(model // 2, model))
    send_a = send_i
    attn = [
        Reduce(wires, RED_A + half * Reduce.COUNT, held_a, core_a, y_a, z_a, x_a, cols)
        for half, cols in enumerate(halves)
    ]
    gain_one, gain_two, bias_two = (vec_ref[i : i + 1, :] for i in (0, 3, 4))
    q_ref, k_ref, v_ref = (acts_ref.at[0, :, i * PAD : (i + 1) * PAD] for i in range(3))

    def exchange(base, source, target, bits, mine):
        other = partner(place, bits, 4)
        return wires.copy(
            base + bits - 1, source.at[other], target.at[place if mine else other], bits, 0
        )

    def hop(base, kept, got, number):
        bits = HOPS[number]
        return wires.copy(base + number, kept.at[number], got.at[number], *bits)

    def next_hop(base, kept, got, number):
        hop(base, kept, got, number).wait_recv()
        kept[number + 1] = kept[number] + got[number]
        if number + 1 < len(HOPS):
            hop(base, kept, got, number + 1).start()

    load_second = pltpu.make_async_copy(second_ref, grad_s, here_sem.at[0])
    load_cot = pltpu.make_async_copy(cot_ref, flow_s, here_sem.at[1])
    load_low = pltpu.make_async_copy(low_ref, low_s, here_sem.at[2])
    load_x = pltpu.make_async_copy(x_ref, flow_s, here_sem.at[3])
    keep_out = pltpu.make_async_copy(out_s.at[place], out_res.at[place], here_sem.at[4])
    keep_dtok = pltpu.make_async_copy(flow_s.at[place], dtok_res.at[place], here_sem.at[5])

    def load_first(index):
        return pltpu.make_async_copy(
            first_ref.at[rows_of(index)], first_s.at[index % 2], here_sem.at[6 + index % 2]
        )

    order = (3, 1, 2, 0)

    @pl.when(step == 0)
    def _():
        load_second.start()
        load_cot.start()
        load_low.start()
        sums_s[0] = jnp.zeros_like(sums_s[0])
        late_s[0] = jnp.zeros_like(late_s[0])
        greet(wires, PEERS)
        load_second.wait()
        load_cot.wait()
        load_low.wait()

        @pl.loop(0, quarters)
        def _(index):
            rows = rows_of(index, part)
            low_t[:, rows] = low_s[rows, :].T
            unit, inverse = norm_parts(grad_s[rows, :])
            out_s[index] = (unit * gain_two + bias_two).astype(BF16)
            grads = flow_s[index].astype(F32)
            d_second = norm_back(grads, gain_two, unit, inverse)
            sums_s[0, 8:9, :] += column_sum(d_second)
            sums_s[0, 9:10, :] += column_sum(grads * unit)
            sums_s[0, 10:11, :] += column_sum(grads)
            grad_s[rows, :] = d_second
            lower = d_second.astype(BF16)
            dmix_s[rows, :] = lower
            back_t[:, rows] = lower.T

        for bits in (2, 3, 1):
            exchange(OUTPUTS, out_s, out_res, bits, True).start()
        keep_out.start()
        load_x.start()

    @pl.when(step < 4)
    def _():
        @pl.loop(0, blocks)
        def _(index):
            rows = rows_of(index)
            d_hidden = dot_nn(dmix_s[rows, :], wo_ref[0])
            d_inner = (d_hidden * slope_ref[0, rows, :].astype(F32)).astype(BF16)
            low_s[rows, :] = d_inner
            for_inner = column_sum(d_inner.astype(F32))
            for number, bits in enumerate(order):

                @pl.when(step == number)
                def _(bits=bits):
                    sums_s[0, pl.ds(partner(place, bits, 4), 1), :] += for_inner

            grad_s[rows, :] += dot_nt(d_inner, wia_ref[0])

        @pl.loop(0, model // (2 * share))
        def _(z):
            rows = pl.ds(pl.multiple_of(z * 2 * share, 2 * share), 2 * share)
            for transposed, right, sent, held in (
                (back_t, acts_ref.at[0], send_o, held_o), (low_t, low_s, send_i, held_i),
            ):
                grads = dot_nn(transposed[rows, :], right[...]).astype(BF16)
                for y in range(2):
                    piece = grads[y * share : (y + 1) * share]

                    @pl.when(step < 2)
                    def _(y=y, piece=piece, sent=sent):
                        sent[step, z, y] = piece

                    @pl.when(step >= 2)
                    def _(y=y, piece=piece, held=held):
                        held[3 - step, z, y] = piece

    for number, j in ((0, 1), (1, 0)):

        @pl.when(step == number)
        def _(number=number, j=j):
            outer.core_copy(j, send_o.at[number]).start()
            inner.core_copy(j, send_i.at[number]).start()

    @pl.when(step == 2)
    def _():
        load_first(0).start()
        load_first(1).start()
        outer.add_core(1)
        outer.whole_x_copy().start()
        inner.add_core(1)
        inner.y_copy(1).start()

    @pl.when(step == 3)
    def _():
        inner.add_core(0)
        inner.y_copy(0).start()
        outer.add_core(0)
        load_x.wait()
        for index in range(blocks):
            rows = slice(index * ROWS, (index + 1) * ROWS)
            load_first(index).wait()
            unit, inverse = norm_parts(first_s[index % 2])
            if index + 2 < blocks:
                load_first(index + 2).start()
            grads = grad_s[rows, :]
            d_first = norm_back(grads, gain_one, unit, inverse)
            sums_s[0, 11:12, :] += column_sum(d_first)
            sums_s[0, 12:13, :] += column_sum(grads * unit)
            sums_s[0, 13:14, :] += column_sum(grads)
            grad_s[rows, :] = d_first
            lower = d_first.astype(BF16)
            dmix_s[rows, :] = lower
            back_t[:, rows] = lower.T
            low_t[:, rows] = flow_s[index].T
        hop(SUMS, sums_s, sums_r, 0).start()

    @pl.when(step == 4)
    def _():
        for number, j in ((0, 1), (1, 0)):
            inner.core_copy(j, send_i.at[number]).wait_send()

    @pl.when(step == 7)
    def _():
        for reduce in attn:
            reduce.add_core(1)
            reduce.y_copy(1).start()

    @pl.when(step >= 4)
    def _():
        for slot in range(4):
            w_s[slot] = unpack(wia_ref.at[0], slot, width)
        for sums in (dk_s, dv_s):
            sums[...] = jnp.zeros_like(sums)

        @pl.loop(0, blocks)
        def _(index):
            rows = rows_of(index)
            kt_s[:, rows] = k_ref[rows, :].T

        @pl.loop(0, blocks)
        def _(index):
            rows = rows_of(index)
            back_rows(
                rows, width, w_s, dmix_s[rows, :], q_ref, k_ref, v_ref, att_ref.at[0], kt_s,
                dq_s, dk_s, dv_s,
            )

            @pl.when((step == 4) & (index == 0))
            def _():
                next_hop(SUMS, sums_s, sums_r, 0)
                inner.add_y(1)
                inner.start_z(1)

            @pl.when((step == 4) & (index == 1))
            def _():
                next_hop(SUMS, sums_s, sums_r, 1)

            @pl.when((step == 4) & (index == 3))
            def _():
                next_hop(SUMS, sums_s, sums_r, 2)
                inner.add_y(0)
                inner.start_z(0)
                outer.add_whole_x()
                outer.y_copy(0).start()

            @pl.when((step == 5) & (index == 0))
            def _():
                next_hop(SUMS, sums_s, sums_r, 3)

            @pl.when((step == 5) & (index == 1))
            def _():
                next_hop(SUMS, sums_s, sums_r, 4)
                inner.send_x()

            @pl.when((step == 5) & (index == 3))
            def _():
                outer.add_y(0)
                outer.start_z(0)

            @pl.when((step == 6) & (index == 1))
            def _():
                gi_res[...] = inner.total()

            @pl.when((step == 6) & (index == 3))
            def _():
                go_res[...] = outer.total_z(0)

            @pl.when((step == 7) & (index == 3))
            def _():
                for reduce in attn:
                    reduce.add_y(1)
                    reduce.start_z(1)

        @pl.loop(0, blocks)
        def _(index):
            rows = rows_of(index)
            for_query, for_value = back_low(rows, width, dq_s, dk_s, dv_s, low_s)
            for number, bits in enumerate(order):

                @pl.when(step == 4 + number)
                def _(bits=bits):
                    late_s[0, pl.ds(partner(place, bits, 4), 1), :] += for_query
                    late_s[0, pl.ds(4 + partner(place, bits, 4), 1), :] += for_value

        for half, cols in enumerate(halves):

            @pl.loop(0, model // (2 * share))
            def _(z):
                rows = pl.ds(pl.multiple_of(z * 2 * share, 2 * share), 2 * share)
                slots = (0, 1) if half == 0 else (2, 3)
                grads = back_weights(rows, width, slots, low_t, back_t, low_s, att_ref.at[0])
                for y in range(2):
                    piece = grads[y * share : (y + 1) * share]

                    @pl.when(step < 6)
                    def _(y=y, piece=piece):
                        send_a[step - 4, z, y, :, cols] = piece

                    @pl.when(step >= 6)
                    def _(y=y, piece=piece):
                        held_a[7 - step, z, y, :, cols] = piece

            for number, j in ((0, 1), (1, 0)):

                @pl.when(step == 4 + number)
                def _(number=number, j=j):
                    attn[half].core_copy(j, send_a.at[number]).start()

            @pl.when(step == 7)
            def _():
                attn[half].add_core(0)
                attn[half].y_copy(0).start()

        @pl.when(step == 7)
        def _():
            hop(LATE_SUMS, late_s, late_r, 0).start()

        @pl.loop(0, quarters)
        def _(index):
            rows = rows_of(index, part)
            grad_s[rows, :] += back_tokens(rows, w_s, low_s)

            @pl.when(step == 7)
            def _():
                flow_s[index] = grad_s[rows, :].astype(BF16)

    @pl.when(step == 7)
    def _():
        for bits in (2, 3, 1):
            exchange(TOKEN_GRADS, flow_s, dtok_res, bits, True).start()
        keep_dtok.start()
        next_hop(LATE_SUMS, late_s, late_r, 0)
        for reduce in attn:
            reduce.send_x()
            reduce.add_y(0)
            reduce.start_z(0)
        for number in range(1, len(HOPS)):
            next_hop(LATE_SUMS, late_s, late_r, number)
        sum_res[...] = sums_s[5]
        late_res[...] = late_s[5]
        for reduce, cols in zip(attn, halves):
            ga_res[:, cols] = reduce.total()
        for bits in (1, 2, 3):
            for base, source, target in (
                (OUTPUTS, out_s, out_res), (TOKEN_GRADS, flow_s, dtok_res),
            ):
                exchange(base, source, target, bits, False).wait_recv()
                exchange(base, source, target, bits, True).wait_send()
        keep_out.wait()
        keep_dtok.wait()
        for number in range(len(HOPS)):
            hop(SUMS, sums_s, sums_r, number).wait_send()
            hop(LATE_SUMS, late_s, late_r, number).wait_send()
        for number, j in ((0, 1), (1, 0)):
            outer.core_copy(j, send_o.at[number]).wait_send()
            for reduce in attn:
                reduce.core_copy(j, send_a.at[number]).wait_send()
        inner.wait_sent((0, 1))
        inner.x_copy().wait_send()
        outer.wait_sent((0,))
        outer.whole_x_copy().wait_send()
        for reduce in attn:
            reduce.wait_sent((0, 1))
            reduce.x_copy().wait_send()


VMEM_LIMIT = 62 * 1024 * 1024


def resident(shape):
    return pl.BlockSpec(shape, lambda step: (0,) * len(shape))


def stepped(shape):
    return pl.BlockSpec((1,) + shape[1:], lambda step: (step,) + (0,) * (len(shape) - 1))


def spec_list(pairs):
    return [stepped(shape) if moves else resident(shape) for shape, moves in pairs]


def near_forward(tokens, cotangent, shard_a, shard_i, shard_o, biases, augs, b_mixer, vectors):
    groups, part, model = tokens.shape
    length = groups * part
    share = shard_a.shape[0]
    whole = (groups, model // share, share, model)
    attended = (groups, length, PAD)
    slopes = (groups, length, model)
    flat = (length, model)
    anywhere = pl.BlockSpec(memory_space=pl.ANY)

    def early(shape):
        return pl.BlockSpec(
            (1,) + shape[1:], lambda step: (jnp.minimum(step, 3),) + (0,) * (len(shape) - 1)
        )

    def late(shape):
        return pl.BlockSpec(
            (1,) + shape[1:], lambda step: (jnp.maximum(step - 4, 0),) + (0,) * (len(shape) - 1)
        )

    kept = [biases, *augs, b_mixer, vectors]
    return pl.pallas_call(
        forward_kernel,
        grid=(2 * groups,),
        out_shape=[
            jax.ShapeDtypeStruct((2 * groups, length, model), BF16),
            jax.ShapeDtypeStruct(attended, BF16),
            jax.ShapeDtypeStruct(slopes, BF16),
            jax.ShapeDtypeStruct(flat, F32),
            jax.ShapeDtypeStruct(flat, F32),
            jax.ShapeDtypeStruct(flat, BF16),
            jax.ShapeDtypeStruct(tokens.shape, BF16),
            jax.ShapeDtypeStruct(tokens.shape, BF16),
            jax.ShapeDtypeStruct((2,) + whole, BF16),
            jax.ShapeDtypeStruct(whole, BF16),
        ],
        in_specs=[anywhere] * 5 + [resident(each.shape) for each in kept],
        out_specs=[stepped((2 * groups, length, model)), early(attended), late(slopes)]
        + [anywhere] * 7,
        scratch_shapes=[
            pltpu.VMEM((4, model, PAD), BF16),
            pltpu.VMEM(tokens.shape, BF16),
            pltpu.VMEM(whole, BF16),
            pltpu.VMEM(whole, BF16),
            pltpu.VMEM(whole, BF16),
            pltpu.VMEM((groups,) + biases.shape, F32),
            pltpu.VMEM(flat, F32),
            pltpu.VMEM(flat, F32),
            pltpu.VMEM(flat, BF16),
            pltpu.SemaphoreType.DMA((FORWARD_WIRES,)),
            pltpu.SemaphoreType.DMA((FORWARD_WIRES,)),
            pltpu.SemaphoreType.DMA((13,)),
        ],
        compiler_params=pltpu.CompilerParams(
            vmem_limit_bytes=VMEM_LIMIT, collective_id=0, has_side_effects=True
        ),
        name="near_forward",
    )(tokens, cotangent, shard_a, shard_i, shard_o, *kept)


def attend_plain(x, a_all, biases, qaug, kaug, vaug, b_mixer):
    length, model = x.shape
    groups = a_all.shape[0]
    block = (groups, length, PAD)
    return pl.pallas_call(
        attend_plain_kernel,
        grid=(groups,),
        out_shape=[jax.ShapeDtypeStruct(block, BF16)] * 4 + [jax.ShapeDtypeStruct(x.shape, F32)],
        in_specs=spec_list(
            [
                (x.shape, 0), (a_all.shape, 1), (biases.shape, 1),
                (qaug.shape, 0), (kaug.shape, 0), (vaug.shape, 0), (b_mixer.shape, 0),
            ]
        ),
        out_specs=spec_list([(block, 1)] * 4 + [(x.shape, 0)]),
        scratch_shapes=[pltpu.VMEM((4, model, PAD), BF16)],
        compiler_params=pltpu.CompilerParams(vmem_limit_bytes=VMEM_LIMIT),
        name="attend_plain",
    )(x, a_all, biases, qaug, kaug, vaug, b_mixer)


def dense_both(first_sum, wi, wo, bi, vectors, cotangent):
    length, model = first_sum.shape
    groups, _, hidden = wi.shape
    grad = (groups, model, hidden)
    forth = lambda shape: pl.BlockSpec(
        (1,) + shape[1:], lambda step: (lax.rem(step, groups),) + (0,) * (len(shape) - 1)
    )
    late = lambda shape: pl.BlockSpec(
        (1,) + shape[1:], lambda step: (jnp.maximum(step - groups, 0),) + (0,) * (len(shape) - 1)
    )
    return pl.pallas_call(
        dense_kernel,
        grid=(2 * groups,),
        out_shape=[
            jax.ShapeDtypeStruct((length, model), BF16),
            jax.ShapeDtypeStruct((length, model), F32),
            jax.ShapeDtypeStruct((length, model), BF16),
            jax.ShapeDtypeStruct(grad, BF16),
            jax.ShapeDtypeStruct(grad, BF16),
            jax.ShapeDtypeStruct((groups, 1, hidden), F32),
            jax.ShapeDtypeStruct((8, model), F32),
        ],
        in_specs=[
            pl.BlockSpec(memory_space=pl.ANY), forth(wi.shape), forth(wo.shape), forth(bi.shape),
            resident(vectors.shape), resident(cotangent.shape),
        ],
        out_specs=[
            resident((length, model)), resident((length, model)), resident((length, model)),
            late(grad), late(grad), late((groups, 1, hidden)), resident((8, model)),
        ],
        scratch_shapes=[
            pltpu.VMEM((length, model), F32),
            pltpu.VMEM((length, model), F32),
            pltpu.VMEM((length, model), F32),
            pltpu.VMEM((length, model), F32),
            pltpu.VMEM((groups, length, hidden), BF16),
            pltpu.VMEM((groups, length, hidden), BF16),
            pltpu.VMEM((length, model), BF16),
            pltpu.VMEM((model, length), BF16),
            pltpu.VMEM((model, length), BF16),
            pltpu.VMEM((length, hidden), BF16),
        ],
        compiler_params=pltpu.CompilerParams(vmem_limit_bytes=VMEM_LIMIT),
        name="dense_both",
    )(first_sum, wi, wo, bi, vectors, cotangent)


def attend_backward(x, a_all, d_mixed, d_first, q, k, v, attended):
    length, model = x.shape
    groups = a_all.shape[0]
    sums = (groups, 1, PAD)
    return pl.pallas_call(
        attend_back_kernel,
        grid=(groups,),
        out_shape=[
            jax.ShapeDtypeStruct(x.shape, F32),
            jax.ShapeDtypeStruct(a_all.shape, BF16),
            jax.ShapeDtypeStruct(sums, F32),
            jax.ShapeDtypeStruct(sums, F32),
        ],
        in_specs=spec_list(
            [
                (x.shape, 0), (a_all.shape, 1), (d_mixed.shape, 0), (d_first.shape, 0),
                (q.shape, 1), (k.shape, 1), (v.shape, 1), (attended.shape, 1),
            ]
        ),
        out_specs=spec_list([(x.shape, 0), (a_all.shape, 1), (sums, 1), (sums, 1)]),
        scratch_shapes=[
            pltpu.VMEM((4, model, PAD), BF16),
            pltpu.VMEM((model, length), BF16),
            pltpu.VMEM((model, length), BF16),
            pltpu.VMEM((PAD, length), BF16),
            pltpu.VMEM((PAD, length), F32),
            pltpu.VMEM((length, PAD), F32),
            pltpu.VMEM((length, PAD), F32),
            pltpu.VMEM((length, 3 * PAD), BF16),
        ],
        compiler_params=pltpu.CompilerParams(vmem_limit_bytes=VMEM_LIMIT),
        name="attend_backward",
    )(x, a_all, d_mixed, d_first, q, k, v, attended)


def near_backward(acts, attended, slopes, w_ia, w_o, vectors, second, first, low, x, cotangent):
    quarters, part, model = x.shape
    length = quarters * part
    share = model // 8
    block = (4, 2, share, model)
    anywhere = pl.BlockSpec(memory_space=pl.ANY)

    def ordered(shape, place):
        return pl.BlockSpec(
            (1,) + shape[1:], lambda step: (place(step),) + (0,) * (len(shape) - 1)
        )

    def acts_at(step):
        return jnp.where(step < 4, 4 + slot_at(step), slot_at(step - 4))

    def weights_at(step):
        return jnp.where(step < 4, slot_at(step), 4 + slot_at(step - 4))

    def first_half(step):
        return slot_at(jnp.minimum(step, 3))

    def last_half(step):
        return slot_at(jnp.maximum(step - 4, 0))

    def vmem(*shape, kind=BF16):
        return pltpu.VMEM(shape, kind)

    final = [
        ((share, model), F32), ((share, model), F32), ((share, model), F32), ((16, model), F32),
        ((8, PAD), F32),
    ]
    return pl.pallas_call(
        backward_kernel,
        grid=(8,),
        out_shape=[jax.ShapeDtypeStruct(x.shape, BF16)] * 2
        + [jax.ShapeDtypeStruct(*each) for each in final],
        in_specs=[
            ordered(acts.shape, acts_at), ordered(attended.shape, last_half),
            ordered(slopes.shape, first_half), ordered(w_ia.shape, weights_at),
            ordered(w_o.shape, first_half), resident(vectors.shape),
        ]
        + [anywhere] * 5,
        out_specs=[anywhere] * 2 + [resident(each[0]) for each in final],
        scratch_shapes=[
            vmem(model, length), vmem(model, length), vmem(length, model), vmem(length, 3 * PAD),
            vmem(*x.shape), vmem(*x.shape), vmem(length, model, kind=F32),
            vmem(2, ROWS, model, kind=F32),
            vmem(4, model, PAD), vmem(PAD, length), vmem(PAD, length, kind=F32),
            vmem(length, PAD, kind=F32), vmem(length, PAD, kind=F32),
            vmem(6, 16, model, kind=F32), vmem(6, 8, PAD, kind=F32),
            vmem(5, 16, model, kind=F32), vmem(5, 8, PAD, kind=F32),
            vmem(2, *block), vmem(2, *block), vmem(2, *block), vmem(2, 4, share, model),
            vmem(2, 3, share, model), vmem(share, model),
            vmem(2, *block), vmem(2, *block), vmem(2, *block), vmem(1, 4, share, model),
            vmem(1, 3, share, model), vmem(*block),
            vmem(2, *block), vmem(2, *block), vmem(2, 4, share, model),
            vmem(2, 3, share, model), vmem(share, model),
            pltpu.SemaphoreType.DMA((BACKWARD_WIRES,)),
            pltpu.SemaphoreType.DMA((BACKWARD_WIRES,)),
            pltpu.SemaphoreType.DMA((8,)),
        ],
        compiler_params=pltpu.CompilerParams(
            vmem_limit_bytes=VMEM_LIMIT, collective_id=1, has_side_effects=True
        ),
        name="near_backward",
    )(acts, attended, slopes, w_ia, w_o, vectors, second, first, low, x, cotangent)


def augment(labels, width):
    length = labels.shape[0]
    lanes = lax.broadcasted_iota(jnp.int32, (length, PAD), 1)
    in_docs = (lanes >= width) & (lanes < width + DOCS)
    same = (lanes - width) == labels[:, None]
    qaug = jnp.where(in_docs & same, 1.0, 0.0).astype(BF16)
    spare = (lanes >= width + DOCS) & (lanes < width + DOCS + 3 * (width // HEAD))
    kaug = jnp.where(in_docs & ~same, -(2.0**100), jnp.where(spare, 1.0, 0.0)).astype(BF16)
    vaug = jnp.where((lanes[:1] == width) | spare[:1], 1.0, 0.0).astype(BF16)
    return qaug, kaug, vaug


def body(
    tokens, doc_ids, w_query, b_query, w_key, w_value, b_value, w_mixer, b_mixer, gain_one,
    bias_one, w_inner, b_inner, w_outer, b_outer, gain_two, bias_two, cotangent,
):
    groups = lax.axis_size("tensor")
    rings = lax.axis_size("dp")
    place = lax.axis_index("tensor")
    width = w_query.shape[1]
    hidden = w_inner.shape[1]
    length = doc_ids.shape[2]
    model = tokens.shape[3]
    near = groups == 4 and rings == 8

    labels = lax.dynamic_index_in_dim(doc_ids[:, 0], place, 0, keepdims=False)
    qaug, kaug, vaug = augment(labels, width)
    shard_a = jnp.concatenate([w_query, w_key, w_value, w_mixer.T], axis=1)
    shard_o = w_outer.T
    spare = jnp.zeros((PAD - width,), F32)
    biases = jnp.concatenate([b_query, spare, b_value, spare, b_inner])[None]
    vectors = jnp.stack([gain_one, bias_one, b_outer, gain_two, bias_two] + [b_outer] * 3)
    if near:
        acts, attended, slopes, first, second, low, x, cot, w_ia, w_o = near_forward(
            tokens[:, 0], cotangent[:, 0], shard_a, w_inner, shard_o, biases, (qaug, kaug, vaug),
            b_mixer[None], vectors,
        )
        out, d_tokens, ga, gi, go, tail, late = near_backward(
            acts, attended, slopes, w_ia.reshape(2 * groups, model, model),
            w_o.reshape(groups, model, model), vectors, second, first, low, x, cot,
        )
        own = lambda whole, start: lax.dynamic_index_in_dim(whole, start + place, 0, False)
        dbq, dbv = own(late, 0)[:width], own(late, groups)[:width]
        dbi = own(tail, 0)
        tail = tail[2 * groups :]
        out, d_tokens = out[:, None], d_tokens[:, None].astype(F32)
    else:

        def gather(shard):
            whole = lax.all_gather(shard, ("tensor", "dp"), axis=0, tiled=True)
            return whole.reshape(groups, model, shard.shape[1])

        def to_sequence(part):
            return lax.all_to_all(part, "tensor", 0, 2, tiled=True).reshape(length, model)

        def from_sequence(whole):
            return lax.all_to_all(whole.reshape(1, 1, length, model), "tensor", 2, 0, tiled=True)

        def scatter(part):
            flat = part.reshape(-1, part.shape[2])
            total = lax.psum_scatter(flat, ("tensor", "dp"), scatter_dimension=0, tiled=True)
            return total.astype(F32)

        x, cot = to_sequence(tokens), to_sequence(cotangent)
        a_all, wi, wo = gather(shard_a), gather(w_inner), gather(shard_o)
        every = lax.all_gather(biases, "tensor", axis=0)
        *saved, first_sum = attend_plain(x, a_all, every, qaug, kaug, vaug, b_mixer[None])
        out, d_first, d_mixed, g_inner, g_outer, dbi, small = dense_both(
            first_sum, wi, wo, every[:, :, 2 * PAD :], vectors, cot
        )
        d_tokens, g_attend, dbq, dbv = attend_backward(x, a_all, d_mixed, d_first, *saved)
        ga, gi, go = scatter(g_attend), scatter(g_inner), scatter(g_outer)
        rows = [dbq[:, 0, :width], dbv[:, 0, :width], dbi[:, 0], small]
        summed = lax.psum(jnp.concatenate([part.reshape(-1) for part in rows]), ("dp", "tensor"))
        own = lambda start, size: lax.dynamic_slice_in_dim(summed, start + place * size, size)
        dbq, dbv, dbi = own(0, width), own(model, width), own(2 * model, hidden)
        tail = summed[-small.size :].reshape(small.shape)
        out, d_tokens = from_sequence(out), from_sequence(d_tokens)
    return (
        out,
        d_tokens,
        ga[:, :width],
        dbq,
        ga[:, width : 2 * width],
        ga[:, 2 * width : 3 * width],
        dbv,
        ga[:, 3 * width :].T,
        tail[3],
        tail[4],
        tail[5],
        gi,
        dbi,
        go.T,
        tail[0],
        tail[1],
        tail[2],
    )


def solution(mesh):
    split = P(None, "dp", "tensor", None)
    both, flipped, part = P("dp", "tensor"), P("tensor", "dp"), P("tensor")
    return jax.shard_map(
        body,
        mesh=mesh,
        in_specs=(
            split, P(None, "dp", None), both, part, both, both, part, flipped, P(), P(), P(),
            both, part, flipped, P(), P(), P(), split,
        ),
        out_specs=(
            split, split, both, part, both, both, part, flipped, P(), P(), P(), both, part,
            flipped, P(), P(), P(),
        ),
        check_vma=False,
    )
```

```python
from functools import partial

import jax
import jax.numpy as jnp
from jax import lax
from jax.experimental import pallas as pl
from jax.experimental.pallas import tpu as pltpu
from jax.sharding import PartitionSpec as P

HEAD = 64
DOCS = 8
PAD = 256
ROWS = 256
LOG2E = 1.4426950408889634
EPS = 1e-12
F32 = jnp.float32
BF16 = jnp.bfloat16


def dot_nn(left, right):
    return lax.dot_general(left, right, (((1,), (0,)), ((), ())), preferred_element_type=F32)


def dot_nt(left, right):
    return lax.dot_general(left, right, (((1,), (1,)), ((), ())), preferred_element_type=F32)


def rows_of(index, size=ROWS):
    return pl.ds(pl.multiple_of(index * size, size), size)


def lane_index(shape):
    return lax.broadcasted_iota(jnp.int32, shape, 1)


def three_parts(values):
    high = values.astype(BF16)
    rest = values - high.astype(F32)
    middle = rest.astype(BF16)
    low = (rest - middle.astype(F32)).astype(BF16)
    return high, middle, low


def head_only(lanes, head):
    return (lanes >= head * HEAD) & (lanes < (head + 1) * HEAD)


def head_and_extra(lanes, head, width):
    extra = width + DOCS + 3 * head
    return (
        head_only(lanes, head)
        | ((lanes >= width) & (lanes < width + DOCS))
        | ((lanes >= extra) & (lanes < extra + 3))
    )


def unpack(block_ref, slot, width):
    part = block_ref[:, slot * width : (slot + 1) * width]
    return jnp.concatenate([part, jnp.zeros((part.shape[0], PAD - width), part.dtype)], axis=1)


def project(x_rows, rows, bq, bv, w_s, qaug_ref, kaug_ref, vaug_ref, q_ref, k_ref, v_ref):
    queries = (dot_nn(x_rows, w_s[0]) + bq).astype(BF16)
    q_ref[rows, :] = queries * jnp.asarray(HEAD**-0.5, BF16) + qaug_ref[rows, :]
    keys = dot_nn(x_rows, w_s[1]).astype(BF16)
    k_ref[rows, :] = keys + kaug_ref[rows, :]
    values = (dot_nn(x_rows, w_s[2]) + bv).astype(BF16)
    v_ref[rows, :] = values + vaug_ref[...]


def attend_rows(rows, width, w_s, q_ref, k_ref, v_ref, att_ref, first_ref):
    lanes = lane_index((ROWS, PAD))
    queries = q_ref[rows, :]
    attended = jnp.zeros((ROWS, PAD), F32)
    extended = queries
    for head in range(width // HEAD):
        masked = jnp.where(head_and_extra(lanes, head, width), queries, 0)
        scores = dot_nt(masked, k_ref[...])
        highest = jnp.max(scores, axis=1, keepdims=True)
        raw = jnp.exp2((scores - highest) * LOG2E).astype(BF16)
        mixed = dot_nn(raw, v_ref[...])
        total = mixed[:, width : width + 1]
        attended = jnp.where(head_only(lanes, head), mixed / total, attended)
        for spot, part in enumerate(three_parts(-(highest + jnp.log(total)))):
            here = lanes == width + DOCS + 3 * head + spot
            extended = jnp.where(here, jnp.broadcast_to(part, (ROWS, PAD)), extended)
    q_ref[rows, :] = extended
    attended = attended.astype(BF16)
    att_ref[rows, :] = attended
    first_ref[rows, :] += dot_nt(attended, w_s[3])


def attend_plain_kernel(
    x_ref, a_ref, bias_ref, qaug_ref, kaug_ref, vaug_ref, bm_ref,
    q_ref, k_ref, v_ref, att_ref, first_ref, w_s,
):
    length, model = x_ref.shape
    width = a_ref.shape[2] // 4
    for slot in range(4):
        w_s[slot] = unpack(a_ref.at[0], slot, width)
    biases = bias_ref[0]

    @pl.when(pl.program_id(0) == 0)
    def _():
        first_ref[...] = x_ref[...].astype(F32) + bm_ref[...]

    @pl.loop(0, length // ROWS)
    def _(index):
        rows = rows_of(index)
        project(
            x_ref[rows, :], rows, biases[:, :PAD], biases[:, PAD : 2 * PAD], w_s, qaug_ref,
            kaug_ref, vaug_ref, q_ref.at[0], k_ref.at[0], v_ref.at[0],
        )

    @pl.loop(0, length // ROWS)
    def _(index):
        refs = (ref.at[0] for ref in (q_ref, k_ref, v_ref, att_ref))
        attend_rows(rows_of(index), width, w_s, *refs, first_ref)


MESH = pl.DeviceIdType.MESH


def partner(index, bits, size):
    flipped = index
    for bit in (1, 2, 4):
        if bits & bit and bit < size:
            flipped = flipped + bit - 2 * bit * lax.rem(lax.div(index, bit), 2)
    return flipped


class Wires:
    def __init__(self, send, recv, place, row):
        self.send, self.recv, self.place, self.row = send, recv, place, row

    def to(self, tensor_bits, dp_bits):
        return (partner(self.row, dp_bits, 8), partner(self.place, tensor_bits, 4))

    def copy(self, number, source, target, tensor_bits=0, dp_bits=0):
        return pltpu.make_async_remote_copy(
            src_ref=source,
            dst_ref=target,
            send_sem=self.send.at[number],
            recv_sem=self.recv.at[number],
            device_id=self.to(tensor_bits, dp_bits),
            device_id_type=MESH,
        )


def greet(wires, peers):
    barrier = pltpu.get_barrier_semaphore()
    for tensor_bits, dp_bits in peers:
        pl.semaphore_signal(
            barrier, inc=1, device_id=wires.to(tensor_bits, dp_bits), device_id_type=MESH
        )
    pl.semaphore_wait(barrier, len(peers))


PEERS = ((1, 0), (2, 0), (3, 0), (0, 1), (0, 2), (0, 4), (0, 6))
TOKENS, COTS, BIASES, KIND_A = 0, 3, 6, 9
KIND_I = KIND_A + 17
KIND_O = KIND_I + 17
FORWARD_WIRES = KIND_O + 10


class ShardGather:
    def __init__(self, wires, base, shard, whole):
        self.wires, self.base, self.shard, self.whole = wires, base, shard, whole

    def at(self, slot, dp_bits):
        return self.whole.at[slot, partner(self.wires.row, dp_bits, 8)]

    def cross_x(self):
        return self.wires.copy(self.base, self.shard, self.at(2, 0), 2, 0)

    def along_z(self, slot, step, mine):
        source = self.shard if slot == 0 else self.at(slot, 0)
        number = self.base + 1 + 3 * (slot // 2) + step - 1
        target = self.at(slot, 0) if mine else self.at(slot, 2 * step)
        return self.wires.copy(number, source, target, 0, 2 * step)

    def along_y(self, slot, step, mine):
        source = self.shard if slot == 0 and step == 0 else self.at(slot, 2 * step)
        number = self.base + 7 + 4 * (slot // 2) + step
        target = self.at(slot, 2 * step) if mine else self.at(slot, 2 * step + 1)
        return self.wires.copy(number, source, target, 0, 1)

    def to_core(self, slot, mine):
        number = self.base + 15 + slot // 2
        target = self.whole.at[slot + 1]
        return self.wires.copy(number, self.whole.at[slot], target, 1, 0)

    def start_z(self, slot):
        for step in (1, 2, 3):
            self.along_z(slot, step, True).start()

    def wait_z(self, slot):
        for step in (1, 2, 3):
            self.along_z(slot, step, False).wait_recv()

    def pass_y(self, slot):
        for step in (1, 2, 3):
            self.along_y(slot, step, True).start()

    def wait_y(self, slot):
        for step in range(4):
            self.along_y(slot, step, False).wait_recv()

    def wait_sent(self, x_first=True):
        for slot in (0, 2) if x_first else (0,):
            for step in (1, 2, 3):
                self.along_z(slot, step, True).wait_send()
            for step in range(4):
                self.along_y(slot, step, True).wait_send()
        for slot in (0, 2):
            self.to_core(slot, True).wait_send()


class BlockGather(ShardGather):
    def along_z(self, slot, step, mine):
        target = self.at(0, 0) if mine else self.at(0, 2 * step)
        return self.wires.copy(self.base + step - 1, self.shard, target, 0, 2 * step)

    def along_y(self, slot, step, mine):
        source = self.shard if step == 0 else self.at(0, 2 * step)
        target = self.at(0, 2 * step) if mine else self.at(0, 2 * step + 1)
        return self.wires.copy(self.base + 3 + step, source, target, 0, 1)

    def cross_x(self):
        return self.wires.copy(self.base + 7, self.whole.at[0], self.whole.at[2], 2, 0)

    def to_core(self, slot, mine):
        return self.wires.copy(
            self.base + 8 + slot // 2, self.whole.at[slot], self.whole.at[slot + 1], 1, 0
        )


def gelu_parts(values):
    phi = jnp.exp2(values * values * (-0.5 * LOG2E)) * 0.3989422804014327
    total = 0.5 + 0.5 * lax.erf(values * 0.7071067811865476)
    return values * total, total + values * phi


def norm_parts(values):
    average = jnp.mean(values, axis=-1, keepdims=True)
    centred = values - average
    spread = jnp.mean(centred * centred, axis=-1, keepdims=True)
    inverse = lax.rsqrt(spread + EPS)
    return centred * inverse, inverse


def norm_back(grads, gain, unit, inverse):
    scaled = grads * gain
    average = jnp.mean(scaled, axis=-1, keepdims=True)
    along = jnp.mean(scaled * unit, axis=-1, keepdims=True)
    return (scaled - average - unit * along) * inverse


def column_sum(values):
    return jnp.sum(values, axis=0, keepdims=True)


WIDE = 512
SEG = 16


def head_rows(head):
    return slice(head * HEAD, (head + 1) * HEAD)


def extra_rows(head, width):
    return slice(width + head * SEG, width + (head + 1) * SEG)


def place_head(part, extra, head, width):
    count = part.shape[1]
    zeros = lambda rows: [jnp.zeros((rows, count), part.dtype)] if rows else []
    pieces = zeros(head * HEAD) + [part] + zeros(width - (head + 1) * HEAD)
    pieces += zeros(head * SEG) + [extra] + zeros(PAD - width - (head + 1) * SEG)
    return jnp.concatenate(pieces, axis=0)


def parts_rows(values, before):
    parts = [part for part in three_parts(values)]
    rest = jnp.zeros((SEG - DOCS - 3, values.shape[1]), BF16)
    return jnp.concatenate([before] + parts + [rest], axis=0)


def attend_block(cols, width, key_ref, vt_s, side_ref):
    outs = []
    for head in range(width // HEAD):
        docs = side_ref[extra_rows(head, width), cols]
        queries = place_head(side_ref[head_rows(head), cols], docs, head, width)
        scores = dot_nn(key_ref[...], queries)
        highest = jnp.max(scores, axis=0, keepdims=True)
        raw = jnp.exp2((scores - highest) * LOG2E).astype(BF16)
        mixed = dot_nn(vt_s[head], raw)
        total = mixed[HEAD : HEAD + 1]
        outs.append((mixed[:HEAD] / total).astype(BF16))
        logs = -(highest + jnp.log(total))
        side_ref[extra_rows(head, width), cols] = parts_rows(logs, docs[:DOCS])
    return jnp.concatenate(outs, axis=0)


def attend_block_back(cols, width, key_ref, value_ref, side_ref, do_s, kt_s, all_t, dk_t, dv_t):
    for head in range(width // HEAD):
        queries = side_ref[head_rows(head), cols]
        d_att = do_s[head_rows(head), cols]
        extra = extra_rows(head, width)
        chances = jnp.exp2(
            dot_nn(key_ref[...], place_head(queries, side_ref[extra, cols], head, width)) * LOG2E
        )
        d_chances = dot_nn(value_ref[...], place_head(d_att, do_s[extra, cols], head, width))
        d_scores = (chances * d_chances).astype(BF16)
        d_query = dot_nn(kt_s[head_rows(head), :], d_scores) * HEAD**-0.5
        all_t[head_rows(head), cols] = d_query.astype(BF16)
        dk_t[head_rows(head), :] += dot_nt(queries, d_scores)
        dv_t[head_rows(head), :] += dot_nt(d_att, chances.astype(BF16))


def forward_kernel(
    tok_ref, cot_ref, si_ref, wq_ref, wk_ref, wv_ref, wm_ref, wo_ref, doc_ref, vec_ref,
    acts_ref, side_ref, slope_ref, first_out, second_out, low_out, xt_out, cot_out, wia_out,
    wo_out,
    sa_s, so_s, w_s, wm_s, x_s, xt_s, a_s, i_s, o_s, bias_s, kaug_s, qdoc_s, vt_s, mix_s,
    first_s, second_s, low_s, send_sem, recv_sem, here_sem,
):
    step = pl.program_id(0)
    place = lax.axis_index("tensor")
    row = lax.axis_index("dp")
    quarters, part, model = x_s.shape
    length = quarters * part
    share, width = wq_ref.shape
    heads = width // HEAD
    blocks = length // ROWS
    wides = length // WIDE
    wires = Wires(send_sem, recv_sem, place, row)
    attn = ShardGather(wires, KIND_A, sa_s, a_s)
    inner = ShardGather(wires, KIND_I, si_ref, i_s)
    outer = BlockGather(wires, KIND_O, so_s, o_s)
    b_mixer, gain_one, bias_one, b_outer = (vec_ref[i : i + 1, :] for i in range(4))
    key_ref, value_ref = (acts_ref.at[0, :, i * PAD : (i + 1) * PAD] for i in range(2))

    def exchange(base, source, target, bits, mine):
        other = partner(place, bits, 4)
        return wires.copy(
            base + bits - 1, source.at[other], target.at[place if mine else other], bits, 0
        )

    def bias_copy(bits, mine):
        return wires.copy(BIASES + bits - 1, vec_ref, bias_s.at[bits], bits, 0)

    local = [
        pltpu.make_async_copy(tok_ref.at[place], x_s.at[place], here_sem.at[0]),
        pltpu.make_async_copy(sa_s, a_s.at[0, row], here_sem.at[1]),
        pltpu.make_async_copy(si_ref, i_s.at[0, row], here_sem.at[2]),
        pltpu.make_async_copy(so_s, o_s.at[0, row], here_sem.at[3]),
        pltpu.make_async_copy(vec_ref, bias_s.at[0], here_sem.at[4]),
    ]
    own_cot = pltpu.make_async_copy(cot_ref.at[place], cot_out.at[place], here_sem.at[5])
    keep_x = pltpu.make_async_copy(xt_s, xt_out, here_sem.at[6])
    keep_a = pltpu.make_async_copy(a_s, wia_out.at[1], here_sem.at[7])
    keep_i = pltpu.make_async_copy(i_s, wia_out.at[0], here_sem.at[8])
    keep_o = pltpu.make_async_copy(o_s, wo_out, here_sem.at[9])
    keep_first = pltpu.make_async_copy(first_s, first_out, here_sem.at[10])
    keep_low = pltpu.make_async_copy(low_s, low_out, here_sem.at[11])
    keep_second = pltpu.make_async_copy(second_s, second_out, here_sem.at[12])

    @pl.when(step == 0)
    def _():
        sa_s[...] = jnp.concatenate(
            [wq_ref[...], wk_ref[...], wv_ref[...], wm_ref[...].T], axis=1
        )
        greet(wires, PEERS)
        attn.cross_x().start()
        for bits in (1, 2, 3):
            bias_copy(bits, True).start()
        attn.start_z(0)
        attn.along_y(0, 0, True).start()
        for bits in (2, 3, 1):
            exchange(TOKENS, tok_ref, x_s, bits, True).start()
        so_s[...] = wo_ref[...].T
        for copy in local:
            copy.start()
        own_cot.start()
        labels = doc_ref[place]
        docs = lax.broadcasted_iota(jnp.int32, (DOCS, length), 0)
        same = docs == labels
        ones = jnp.ones((3, length), F32)
        rest = jnp.zeros((SEG - DOCS - 3, length), F32)
        qdoc_s[...] = jnp.concatenate(
            [jnp.where(same, 1.0, 0.0), jnp.zeros((SEG - DOCS, length), F32)], axis=0
        ).astype(BF16)
        one_head = jnp.concatenate([jnp.where(same, 0.0, -(2.0**100)), ones, rest], axis=0)
        tall = jnp.zeros((width - PAD // 2, length), F32)
        last = jnp.zeros((PAD - width - heads * SEG, length), F32)
        kaug_s[...] = jnp.concatenate([tall] + [one_head] * heads + [last], axis=0).astype(BF16).T
        for head in range(heads):
            vt_s[head, HEAD:, :] = jnp.ones((SEG, length), BF16)
        for copy in local:
            copy.wait()
        attn.cross_x().wait_recv()
        attn.start_z(2)
        attn.along_y(2, 0, True).start()
        attn.wait_z(0)
        attn.pass_y(0)
        attn.wait_y(0)
        attn.to_core(0, True).start()
        inner.cross_x().start()
        for bits in (1, 2, 3):
            exchange(TOKENS, tok_ref, x_s, bits, False).wait_recv()
            bias_copy(bits, False).wait_recv()

        @pl.loop(0, quarters)
        def _(index):
            rows = rows_of(index, part)
            first_s[rows, :] = x_s[index].astype(F32) + b_mixer

    @pl.when(step == 1)
    def _():
        @pl.loop(0, quarters)
        def _(index):
            xt_s[:, rows_of(index, part)] = x_s[index].T

        keep_x.start()

    @pl.when(step == 1)
    def _():
        attn.to_core(0, False).wait_recv()

    @pl.when(step == 2)
    def _():
        attn.wait_y(2)
        attn.to_core(2, True).start()

    @pl.when(step == 3)
    def _():
        attn.to_core(2, False).wait_recv()
        keep_a.start()

    @pl.when(step < 4)
    def _():
        for dp_row in range(a_s.shape[1]):
            packed = a_s[step, dp_row]
            rest = jnp.zeros((share, PAD - width), packed.dtype)
            rows = slice(dp_row * share, (dp_row + 1) * share)
            for slot in range(4):
                piece = packed[:, slot * width : (slot + 1) * width]
                piece = jnp.concatenate([piece, rest], axis=1)
                if slot < 3:
                    w_s[rows, slot * PAD : (slot + 1) * PAD] = piece
                else:
                    wm_s[rows, :] = piece
        bias = bias_s[step][7:8]
        lanes = lax.broadcasted_iota(jnp.int32, (1, PAD), 1) - width
        spare = (lanes >= 0) & (lanes < heads * SEG) & (lax.rem(lanes + SEG, SEG) >= DOCS)
        vaug = jnp.where(spare & (lax.rem(lanes + SEG, SEG) < DOCS + 3), 1.0, 0.0).astype(BF16)

        @pl.loop(0, wides)
        def _(index):
            rows = rows_of(index, WIDE)
            x_rows = x_s[pl.ds(index * (WIDE // part), WIDE // part)].reshape(WIDE, model)
            result = dot_nn(x_rows, w_s[...])
            queries = (result[:, :PAD] + bias[:, :PAD]).astype(BF16)
            queries = (queries * jnp.asarray(HEAD**-0.5, BF16)).T
            side_ref[0, :width, rows] = queries[:width]
            side_ref[0, PAD + width :, rows] = jnp.zeros((PAD - width, WIDE), BF16)
            keys = result[:, PAD : 2 * PAD].astype(BF16)
            key_ref[rows, : PAD // 2] = keys[:, : PAD // 2]
            key_ref[rows, PAD // 2 :] = keys[:, PAD // 2 :] + kaug_s[rows, :]
            values = (result[:, 2 * PAD :] + bias[:, PAD : 2 * PAD]).astype(BF16)
            value_ref[rows, :] = values + vaug
            values_t = values.T
            for head in range(heads):
                vt_s[head, :HEAD, rows] = values_t[head_rows(head)]

        for head in range(heads):
            side_ref[0, extra_rows(head, width), :] = qdoc_s[...]
        side_ref[0, width + heads * SEG : PAD, :] = jnp.zeros(
            (PAD - width - heads * SEG, length), BF16
        )

        @pl.loop(0, blocks)
        def _(index):
            cols = rows_of(index)
            attended = attend_block(cols, width, key_ref, vt_s, side_ref.at[0])
            side_ref[0, PAD : PAD + width, cols] = attended
            rest = jnp.zeros((PAD - width, ROWS), BF16)
            mix_s[cols, :] = jnp.concatenate([attended, rest], axis=0).T

            @pl.when((step == 0) & (index == 0))
            def _():
                outer.start_z(0)
                outer.along_y(0, 0, True).start()
                for bits in (2, 3, 1):
                    exchange(COTS, cot_ref, cot_out, bits, True).start()

            @pl.when((step == 0) & (index == 1))
            def _():
                attn.wait_z(2)
                attn.pass_y(2)

            @pl.when((step == 0) & (index == 3))
            def _():
                inner.start_z(0)
                inner.along_y(0, 0, True).start()

            @pl.when((step == 1) & (index == 1))
            def _():
                outer.wait_z(0)
                outer.pass_y(0)

            @pl.when((step == 1) & (index == 2))
            def _():
                inner.cross_x().wait_recv()
                inner.start_z(2)
                inner.along_y(2, 0, True).start()

            @pl.when((step == 2) & (index == 2))
            def _():
                inner.wait_z(0)
                inner.pass_y(0)

            @pl.when((step == 2) & (index == 3))
            def _():
                outer.wait_y(0)
                outer.cross_x().start()
                outer.to_core(0, True).start()

            @pl.when((step == 3) & (index == 1))
            def _():
                inner.wait_y(0)
                inner.to_core(0, True).start()

            @pl.when((step == 3) & (index == 3))
            def _():
                inner.wait_z(2)
                inner.pass_y(2)

        @pl.loop(0, wides)
        def _(index):
            rows = rows_of(index, WIDE)
            first_s[rows, :] += dot_nt(mix_s[rows, :], wm_s[...])

    @pl.when(step == 4)
    def _():
        keep_first.start()

        @pl.loop(0, blocks)
        def _(index):
            rows = rows_of(index)
            unit, _inverse = norm_parts(first_s[rows, :])
            normed = unit * gain_one + bias_one
            low_s[rows, :] = normed.astype(BF16)
            second_s[rows, :] = normed + b_outer

        keep_low.start()

    @pl.when(step == 5)
    def _():
        inner.to_core(0, False).wait_recv()
        outer.to_core(0, False).wait_recv()

    @pl.when(step == 6)
    def _():
        inner.wait_y(2)
        inner.to_core(2, True).start()
        outer.cross_x().wait_recv()
        outer.to_core(2, True).start()

    @pl.when(step == 7)
    def _():
        inner.to_core(2, False).wait_recv()
        outer.to_core(2, False).wait_recv()
        keep_i.start()
        keep_o.start()

    @pl.when(step >= 4)
    def _():
        slot = step - 4
        w_inner = i_s[slot].reshape(model, model)
        w_outer = o_s[slot].reshape(model, model)
        b_inner = bias_s[slot][6:7]

        @pl.loop(0, wides)
        def _(index):
            rows = rows_of(index, WIDE)
            value, slope = gelu_parts(dot_nn(low_s[rows, :], w_inner) + b_inner)
            hidden = value.astype(BF16)
            acts_ref[0, rows, :] = hidden
            slope_ref[0, rows, :] = slope.astype(BF16)
            second_s[rows, :] += dot_nt(hidden, w_outer)

    @pl.when(step == 7)
    def _():
        keep_second.start()
        for bits in (1, 2, 3):
            exchange(COTS, cot_ref, cot_out, bits, False).wait_recv()
        for gather in (attn, inner, outer):
            gather.cross_x().wait_send()
            gather.wait_sent(gather is not outer)
        for bits in (1, 2, 3):
            exchange(TOKENS, tok_ref, x_s, bits, True).wait_send()
            exchange(COTS, cot_ref, cot_out, bits, True).wait_send()
            bias_copy(bits, True).wait_send()
        for copy in (
            own_cot, keep_x, keep_a, keep_i, keep_o, keep_first, keep_low, keep_second,
        ):
            copy.wait()


def dense_kernel(
    first_in, wi_ref, wo_ref, bi_ref, vec_ref, cot_ref,
    out_ref, dfirst_ref, dmix_ref, gi_ref, go_ref, dbi_ref, small_ref,
    first_ref, second_ref, normed_s, dsec_s, hidden_s, slope_s, low_s, low_t, back_t, dinner_s,
):
    step = pl.program_id(0)
    count = pl.num_programs(0) // 2
    length, model = first_in.shape
    blocks = length // ROWS
    gain_one, bias_one, b_outer, gain_two, bias_two = (vec_ref[i : i + 1, :] for i in range(5))

    @pl.when(step == 0)
    def _():
        copied = pltpu.sync_copy
        copied(first_in, first_ref)

        @pl.loop(0, blocks)
        def _(index):
            rows = rows_of(index)
            unit, _inverse = norm_parts(first_ref[rows, :])
            normed = unit * gain_one + bias_one
            normed_s[rows, :] = normed
            low_s[rows, :] = normed.astype(BF16)
            low_t[:, rows] = normed.astype(BF16).T
            second_ref[rows, :] = normed + b_outer

    @pl.when(step < count)
    def _():
        @pl.loop(0, blocks)
        def _(index):
            rows = rows_of(index)
            inner = dot_nn(low_s[rows, :], wi_ref[0]) + bi_ref[0]
            value, slope = gelu_parts(inner)
            hidden = value.astype(BF16)
            hidden_s[step, rows, :] = hidden
            slope_s[step, rows, :] = slope.astype(BF16)
            second_ref[rows, :] += dot_nt(hidden, wo_ref[0])

    @pl.when(step == count - 1)
    def _():
        small_ref[...] = jnp.zeros_like(small_ref)

        @pl.loop(0, blocks)
        def _(index):
            rows = rows_of(index)
            unit, inverse = norm_parts(second_ref[rows, :])
            out_ref[rows, :] = (unit * gain_two + bias_two).astype(BF16)
            grads = cot_ref[rows, :].astype(F32)
            d_second = norm_back(grads, gain_two, unit, inverse)
            small_ref[0:1, :] += column_sum(d_second)
            small_ref[1:2, :] += column_sum(grads * unit)
            small_ref[2:3, :] += column_sum(grads)
            dsec_s[rows, :] = d_second
            low = d_second.astype(BF16)
            dmix_ref[rows, :] = low
            back_t[:, rows] = low.T

    @pl.when(step >= count)
    def _():
        place = step - count
        dbi_ref[...] = jnp.zeros_like(dbi_ref)

        @pl.loop(0, blocks)
        def _(index):
            rows = rows_of(index)
            d_hidden = dot_nn(dmix_ref[rows, :], wo_ref[0])
            d_inner = (d_hidden * slope_s[place, rows, :].astype(F32)).astype(BF16)
            dinner_s[rows, :] = d_inner
            dbi_ref[0] += column_sum(d_inner.astype(F32))
            dsec_s[rows, :] += dot_nt(d_inner, wi_ref[0])

        @pl.loop(0, model // ROWS)
        def _(index):
            rows = rows_of(index)
            gi_ref[0, rows, :] = dot_nn(low_t[rows, :], dinner_s[...]).astype(gi_ref.dtype)
            go_ref[0, rows, :] = dot_nn(back_t[rows, :], hidden_s[place]).astype(go_ref.dtype)

    @pl.when(step == 2 * count - 1)
    def _():
        @pl.loop(0, blocks)
        def _(index):
            rows = rows_of(index)
            unit, inverse = norm_parts(first_ref[rows, :])
            grads = dsec_s[rows, :]
            d_first = norm_back(grads, gain_one, unit, inverse)
            small_ref[3:4, :] += column_sum(d_first)
            small_ref[4:5, :] += column_sum(grads * unit)
            small_ref[5:6, :] += column_sum(grads)
            dfirst_ref[rows, :] = d_first
            dmix_ref[rows, :] = d_first.astype(BF16)


def back_rows(rows, width, w_s, dmix_rows, q_ref, k_ref, v_ref, att_ref, kt_s, dq_s, dk_s, dv_s):
    lanes = lane_index((ROWS, PAD))
    queries = q_ref[rows, :]
    d_att = dot_nn(dmix_rows, w_s[3]).astype(BF16)
    product = d_att.astype(F32) * att_ref[rows, :].astype(F32)
    heads = range(width // HEAD)
    extended = d_att
    for head in heads:
        centre = jnp.sum(jnp.where(head_only(lanes, head), product, 0.0), axis=1, keepdims=True)
        for spot, part in enumerate(three_parts(-centre)):
            here = lanes == width + DOCS + 3 * head + spot
            extended = jnp.where(here, jnp.broadcast_to(part, (ROWS, PAD)), extended)
    chances_all = []
    d_scores_all = []
    d_att_all = []
    queries_all = []
    for head in heads:
        wide = head_and_extra(lanes, head, width)
        only = head_only(lanes, head)
        chances = jnp.exp2(dot_nt(k_ref[...], jnp.where(wide, queries, 0)) * LOG2E)
        d_chances = dot_nt(v_ref[...], jnp.where(wide, extended, 0))
        d_scores = (chances * d_chances).astype(BF16)
        chances_all.append(chances.astype(BF16))
        d_scores_all.append(d_scores)
        d_att_all.append(jnp.where(only, d_att, 0))
        queries_all.append(jnp.where(only, queries, 0))
        head_rows = slice(head * HEAD, (head + 1) * HEAD)
        dq_s[head_rows, rows] = dot_nn(kt_s[head_rows, :], d_scores)
    dv_s[...] += dot_nn(jnp.concatenate(chances_all, 1), jnp.concatenate(d_att_all, 0))
    dk_s[...] += dot_nn(jnp.concatenate(d_scores_all, 1), jnp.concatenate(queries_all, 0))


def back_low(rows, width, dq_s, dk_s, dv_s, low_s):
    d_query = (dq_s[:, rows].T * HEAD**-0.5).astype(BF16)
    d_query = jnp.where(lane_index(d_query.shape) < width, d_query, 0)
    d_value = dv_s[rows, :].astype(BF16)
    low_s[rows, :PAD] = d_query
    low_s[rows, PAD : 2 * PAD] = dk_s[rows, :].astype(BF16)
    low_s[rows, 2 * PAD :] = d_value
    return column_sum(d_query.astype(F32)), column_sum(d_value.astype(F32))


def back_tokens(rows, w_s, low_s):
    return sum(dot_nt(low_s[rows, slot * PAD : (slot + 1) * PAD], w_s[slot]) for slot in range(3))


def back_weights(rows, width, slots, xt_s, dmixt_s, low_s, att_ref):
    parts = []
    for slot in slots:
        if slot < 3:
            part = dot_nn(xt_s[rows, :], low_s[:, slot * PAD : (slot + 1) * PAD])
        else:
            part = dot_nn(dmixt_s[rows, :], att_ref[...])
        parts.append(part[:, :width])
    return jnp.concatenate(parts, axis=1).astype(BF16)


def attend_back_kernel(
    x_ref, a_ref, dmix_ref, dfirst_ref, q_ref, k_ref, v_ref, att_ref,
    dtok_ref, ga_ref, dbq_ref, dbv_ref,
    w_s, xt_s, dmixt_s, kt_s, dq_s, dk_s, dv_s, low_s,
):
    length, model = x_ref.shape
    width = a_ref.shape[2] // 4
    blocks = length // ROWS
    for slot in range(4):
        w_s[slot] = unpack(a_ref.at[0], slot, width)

    @pl.when(pl.program_id(0) == 0)
    def _():
        dtok_ref[...] = dfirst_ref[...]

        @pl.loop(0, blocks)
        def _(index):
            rows = rows_of(index)
            xt_s[:, rows] = x_ref[rows, :].T
            dmixt_s[:, rows] = dmix_ref[rows, :].T

    for sums in (dk_s, dv_s, dbq_ref, dbv_ref):
        sums[...] = jnp.zeros_like(sums)

    @pl.loop(0, blocks)
    def _(index):
        rows = rows_of(index)
        kt_s[:, rows] = k_ref[0, rows, :].T

    @pl.loop(0, blocks)
    def _(index):
        rows = rows_of(index)
        dmix_rows = dmix_ref[rows, :]
        refs = (ref.at[0] for ref in (q_ref, k_ref, v_ref, att_ref))
        back_rows(rows, width, w_s, dmix_rows, *refs, kt_s, dq_s, dk_s, dv_s)

    @pl.loop(0, blocks)
    def _(index):
        rows = rows_of(index)
        for_query, for_value = back_low(rows, width, dq_s, dk_s, dv_s, low_s)
        dbq_ref[0] += for_query
        dbv_ref[0] += for_value
        dtok_ref[rows, :] += back_tokens(rows, w_s, low_s)

    @pl.loop(0, model // ROWS)
    def _(index):
        rows = rows_of(index)
        ga_ref[0, rows, :] = back_weights(
            rows, width, range(4), xt_s, dmixt_s, low_s, att_ref.at[0]
        )


def add_into(target, source):
    target[...] = (target[...].astype(F32) + source[...].astype(F32)).astype(target.dtype)


class Reduce:
    COUNT = 11

    def __init__(self, wires, base, held, core, by_y, by_z, by_x, cols=slice(None)):
        self.wires, self.base, self.held, self.core = wires, base, held, core
        self.by_y, self.by_z, self.by_x = by_y, by_z, by_x
        self.cols = cols
        self.z, self.y = lax.div(wires.row, 2), lax.rem(wires.row, 2)

    def part(self, ref, *index):
        return ref.at[index + (slice(None), self.cols)]

    def core_copy(self, j, source):
        everything = (slice(None), slice(None))
        return self.wires.copy(
            self.base + j, self.part(source, *everything), self.part(self.core, j, *everything), 1, 0
        )

    def add_core(self, j):
        self.core_copy(j, self.held.at[j]).wait_recv()
        for z in range(4):
            for y in range(2):
                add_into(self.part(self.held, j, z, y), self.part(self.core, j, z, y))

    def y_copy(self, j):
        source = self.part(self.held, j, slice(None), 1 - self.y)
        return self.wires.copy(
            self.base + 2 + j, source, self.part(self.by_y, j, slice(None)), 0, 1
        )

    def add_y(self, j):
        self.y_copy(j).wait_recv()
        for z in range(4):
            add_into(self.part(self.held, j, z, self.y), self.part(self.by_y, j, z))

    def z_copy(self, j, step):
        other = lax.div(partner(self.wires.row, 2 * step, 8), 2)
        number = self.base + 4 + 3 * j + step - 1
        return self.wires.copy(
            number, self.part(self.held, j, other, self.y), self.part(self.by_z, j, step - 1),
            0, 2 * step,
        )

    def start_z(self, j):
        for step in (1, 2, 3):
            self.z_copy(j, step).start()

    def total_z(self, j):
        total = self.part(self.held, j, self.z, self.y)[...].astype(F32)
        for step in (1, 2, 3):
            self.z_copy(j, step).wait_recv()
            total = total + self.part(self.by_z, j, step - 1)[...].astype(F32)
        return total

    def x_copy(self):
        source = self.part(self.held, 1, self.z, self.y)
        return self.wires.copy(self.base + 10, source, self.part(self.by_x), 2, 0)

    def send_x(self):
        self.part(self.held, 1, self.z, self.y)[...] = self.total_z(1).astype(BF16)
        self.x_copy().start()

    def total(self):
        self.x_copy().wait_recv()
        return self.total_z(0) + self.part(self.by_x)[...].astype(F32)

    def whole_x_copy(self):
        return self.wires.copy(self.base + 10, self.held.at[1], self.by_x, 2, 0)

    def add_whole_x(self):
        self.whole_x_copy().wait_recv()
        for z in range(4):
            for y in range(2):
                add_into(self.held.at[0, z, y], self.by_x.at[z, y])

    def wait_sent(self, j_all):
        for j in j_all:
            self.y_copy(j).wait_send()
            for step in (1, 2, 3):
                self.z_copy(j, step).wait_send()


OUTPUTS, TOKEN_GRADS, SUMS, LATE_SUMS = 0, 3, 6, 11
RED_I = 16
RED_O = RED_I + Reduce.COUNT
RED_A = RED_O + Reduce.COUNT
BACKWARD_WIRES = RED_A + 2 * Reduce.COUNT
HOPS = ((1, 0), (2, 0), (0, 1), (0, 2), (0, 4))


def slot_at(step):
    return jnp.where(step < 2, 3 - 2 * step, 6 - 2 * step)


def backward_kernel(
    acts_ref, side_ref, slope_ref, wia_ref, wo_ref, vec_ref, second_ref, first_ref, low_ref, xt_ref,
    cot_ref,
    out_res, dtok_res, ga_res, gi_res, go_res, sum_res, late_res,
    low_t, back_t, dmix_s, low_s, flow_s, out_s, grad_s, first_s, wmt_s, do_s, kt_s, all_t, dk_t,
    dv_t, sums_s, late_s, sums_r, late_r,
    send_i, held_i, core_i, y_i, z_i, x_i, send_o, held_o, core_o, y_o, z_o, x_o,
    held_a, core_a, y_a, z_a, x_a,
    send_sem, recv_sem, here_sem,
):
    step = pl.program_id(0)
    place = lax.axis_index("tensor")
    row = lax.axis_index("dp")
    length, model = dmix_s.shape
    quarters, part, _ = flow_s.shape
    width = wia_ref.shape[2] // 4
    heads = width // HEAD
    blocks = length // ROWS
    wides = length // WIDE
    share = held_i.shape[3]
    wires = Wires(send_sem, recv_sem, place, row)
    inner = Reduce(wires, RED_I, held_i, core_i, y_i, z_i, x_i)
    outer = Reduce(wires, RED_O, held_o, core_o, y_o, z_o, x_o)
    halves = (slice(0, model // 2), slice(model // 2, model))
    send_a = send_i
    attn = [
        Reduce(wires, RED_A + half * Reduce.COUNT, held_a, core_a, y_a, z_a, x_a, cols)
        for half, cols in enumerate(halves)
    ]
    gain_one, gain_two, bias_two = (vec_ref[i : i + 1, :] for i in (1, 4, 5))
    key_ref, value_ref = (acts_ref.at[0, :, i * PAD : (i + 1) * PAD] for i in range(2))
    att_ref = side_ref.at[0, PAD : PAD + width]

    def exchange(base, source, target, bits, mine):
        other = partner(place, bits, 4)
        return wires.copy(
            base + bits - 1, source.at[other], target.at[place if mine else other], bits, 0
        )

    def hop(base, kept, got, number):
        bits = HOPS[number]
        return wires.copy(base + number, kept.at[number], got.at[number], *bits)

    def next_hop(base, kept, got, number):
        hop(base, kept, got, number).wait_recv()
        kept[number + 1] = kept[number] + got[number]
        if number + 1 < len(HOPS):
            hop(base, kept, got, number + 1).start()

    load_second = pltpu.make_async_copy(second_ref, grad_s, here_sem.at[0])
    load_cot = pltpu.make_async_copy(cot_ref, flow_s, here_sem.at[1])
    load_low = pltpu.make_async_copy(low_ref, low_s, here_sem.at[2])
    load_x = pltpu.make_async_copy(xt_ref, low_t, here_sem.at[3])
    keep_out = pltpu.make_async_copy(out_s.at[place], out_res.at[place], here_sem.at[4])
    keep_dtok = pltpu.make_async_copy(flow_s.at[place], dtok_res.at[place], here_sem.at[5])

    def load_first(index):
        return pltpu.make_async_copy(
            first_ref.at[rows_of(index)], first_s.at[index % 2], here_sem.at[6 + index % 2]
        )

    order = (3, 1, 2, 0)

    @pl.when(step == 0)
    def _():
        load_second.start()
        load_cot.start()
        load_low.start()
        sums_s[0] = jnp.zeros_like(sums_s[0])
        late_s[0] = jnp.zeros_like(late_s[0])
        greet(wires, PEERS)
        load_second.wait()
        load_cot.wait()
        load_low.wait()

        @pl.loop(0, quarters)
        def _(index):
            rows = rows_of(index, part)
            low_t[:, rows] = low_s[rows, :].T
            unit, inverse = norm_parts(grad_s[rows, :])
            out_s[index] = (unit * gain_two + bias_two).astype(BF16)
            grads = flow_s[index].astype(F32)
            d_second = norm_back(grads, gain_two, unit, inverse)
            sums_s[0, 8:9, :] += column_sum(d_second)
            sums_s[0, 9:10, :] += column_sum(grads * unit)
            sums_s[0, 10:11, :] += column_sum(grads)
            grad_s[rows, :] = d_second
            lower = d_second.astype(BF16)
            dmix_s[rows, :] = lower
            back_t[:, rows] = lower.T

        for bits in (2, 3, 1):
            exchange(OUTPUTS, out_s, out_res, bits, True).start()
        keep_out.start()

    @pl.when(step < 4)
    def _():
        @pl.loop(0, wides)
        def _(index):
            rows = rows_of(index, WIDE)
            d_hidden = dot_nn(dmix_s[rows, :], wo_ref[0])
            d_inner = (d_hidden * slope_ref[0, rows, :].astype(F32)).astype(BF16)
            low_s[rows, :] = d_inner
            for_inner = column_sum(d_inner.astype(F32))
            for number, bits in enumerate(order):

                @pl.when(step == number)
                def _(bits=bits):
                    sums_s[0, pl.ds(partner(place, bits, 4), 1), :] += for_inner

            grad_s[rows, :] += dot_nt(d_inner, wia_ref[0])

        @pl.loop(0, model // (4 * share))
        def _(pair):
            rows = rows_of(pair, 4 * share)
            for transposed, right, sent, held in (
                (back_t, acts_ref.at[0], send_o, held_o), (low_t, low_s, send_i, held_i),
            ):
                grads = dot_nn(transposed[rows, :], right[...]).astype(BF16)
                pieces = grads.reshape(2, 2, share, model)

                @pl.when(step < 2)
                def _(pieces=pieces, sent=sent):
                    sent[step, pl.ds(2 * pair, 2)] = pieces

                @pl.when(step >= 2)
                def _(pieces=pieces, held=held):
                    held[3 - step, pl.ds(2 * pair, 2)] = pieces

    for number, j in ((0, 1), (1, 0)):

        @pl.when(step == number)
        def _(number=number, j=j):
            outer.core_copy(j, send_o.at[number]).start()
            inner.core_copy(j, send_i.at[number]).start()

    @pl.when(step == 2)
    def _():
        load_first(0).start()
        load_first(1).start()
        outer.add_core(1)
        outer.whole_x_copy().start()
        inner.add_core(1)
        inner.y_copy(1).start()

    @pl.when(step == 3)
    def _():
        inner.add_core(0)
        inner.y_copy(0).start()
        outer.add_core(0)
        load_x.start()
        for index in range(blocks):
            rows = slice(index * ROWS, (index + 1) * ROWS)
            load_first(index).wait()
            unit, inverse = norm_parts(first_s[index % 2])
            if index + 2 < blocks:
                load_first(index + 2).start()
            grads = grad_s[rows, :]
            d_first = norm_back(grads, gain_one, unit, inverse)
            sums_s[0, 11:12, :] += column_sum(d_first)
            sums_s[0, 12:13, :] += column_sum(grads * unit)
            sums_s[0, 13:14, :] += column_sum(grads)
            grad_s[rows, :] = d_first
            lower = d_first.astype(BF16)
            dmix_s[rows, :] = lower
            back_t[:, rows] = lower.T
        load_x.wait()
        hop(SUMS, sums_s, sums_r, 0).start()

    @pl.when(step == 4)
    def _():
        for number, j in ((0, 1), (1, 0)):
            inner.core_copy(j, send_i.at[number]).wait_send()

    @pl.when(step == 7)
    def _():
        for reduce in attn:
            reduce.add_core(1)
            reduce.y_copy(1).start()

    @pl.when(step >= 4)
    def _():
        wmt_s[...] = wia_ref[0, :, 3 * width :].T
        for sums in (dk_t, dv_t):
            sums[...] = jnp.zeros_like(sums)

        @pl.loop(0, wides)
        def _(index):
            cols = rows_of(index, WIDE)
            kt_s[:, cols] = key_ref[cols, :].T[:width]
            d_att = dot_nn(wmt_s[...], back_t[:, cols]).astype(BF16)
            do_s[:width, cols] = d_att
            product = d_att.astype(F32) * att_ref[:, cols].astype(F32)
            none = jnp.zeros((DOCS, WIDE), BF16)
            for head in range(heads):
                centre = column_sum(product[head_rows(head)])
                do_s[extra_rows(head, width), cols] = parts_rows(-centre, none)

        @pl.loop(0, blocks)
        def _(index):
            attend_block_back(
                rows_of(index), width, key_ref, value_ref, side_ref.at[0], do_s, kt_s, all_t,
                dk_t, dv_t,
            )

            @pl.when((step == 4) & (index == 0))
            def _():
                next_hop(SUMS, sums_s, sums_r, 0)
                inner.add_y(1)
                inner.start_z(1)

            @pl.when((step == 4) & (index == 1))
            def _():
                next_hop(SUMS, sums_s, sums_r, 1)

            @pl.when((step == 4) & (index == 3))
            def _():
                next_hop(SUMS, sums_s, sums_r, 2)
                inner.add_y(0)
                inner.start_z(0)
                outer.add_whole_x()
                outer.y_copy(0).start()

            @pl.when((step == 5) & (index == 0))
            def _():
                next_hop(SUMS, sums_s, sums_r, 3)

            @pl.when((step == 5) & (index == 1))
            def _():
                next_hop(SUMS, sums_s, sums_r, 4)
                inner.send_x()

            @pl.when((step == 5) & (index == 3))
            def _():
                outer.add_y(0)
                outer.start_z(0)

            @pl.when((step == 6) & (index == 1))
            def _():
                gi_res[...] = inner.total()

            @pl.when((step == 6) & (index == 3))
            def _():
                go_res[...] = outer.total_z(0)

            @pl.when((step == 7) & (index == 3))
            def _():
                for reduce in attn:
                    reduce.add_y(1)
                    reduce.start_z(1)

        all_t[width : 2 * width, :] = dk_t[...].astype(BF16)
        all_t[2 * width :, :] = dv_t[...].astype(BF16)
        for_all = dot_nt(jnp.ones((8, length), BF16), all_t[...])[:1]
        for number, bits in enumerate(order):

            @pl.when(step == 4 + number)
            def _(bits=bits):
                late_s[0, pl.ds(partner(place, bits, 4), 1), : 3 * width] = for_all

        for half, cols in enumerate(halves):

            @pl.loop(0, model // (4 * share))
            def _(pair):
                rows = rows_of(pair, 4 * share)
                if half == 0:
                    grads = dot_nt(low_t[rows, :], all_t[: 2 * width, :])
                else:
                    for_value = dot_nt(low_t[rows, :], all_t[2 * width :, :])
                    for_mixer = dot_nt(back_t[rows, :], att_ref[...])
                    grads = jnp.concatenate([for_value, for_mixer], axis=1)
                pieces = grads.astype(BF16).reshape(2, 2, share, model // 2)

                @pl.when(step < 6)
                def _(pieces=pieces):
                    send_a[step - 4, pl.ds(2 * pair, 2), :, :, cols] = pieces

                @pl.when(step >= 6)
                def _(pieces=pieces):
                    held_a[7 - step, pl.ds(2 * pair, 2), :, :, cols] = pieces

            for number, j in ((0, 1), (1, 0)):

                @pl.when(step == 4 + number)
                def _(number=number, j=j):
                    attn[half].core_copy(j, send_a.at[number]).start()

            @pl.when(step == 7)
            def _():
                attn[half].add_core(0)
                attn[half].y_copy(0).start()

        @pl.when(step == 7)
        def _():
            hop(LATE_SUMS, late_s, late_r, 0).start()

        @pl.loop(0, wides)
        def _(index):
            rows = rows_of(index, WIDE)
            transposed = all_t[:, rows].T
            grad_s[rows, :] += dot_nt(transposed, wia_ref[0, :, : 3 * width])

            @pl.when(step == 7)
            def _():
                places = pl.ds(index * (WIDE // part), WIDE // part)
                flow_s[places] = grad_s[rows, :].astype(BF16).reshape(WIDE // part, part, model)

    @pl.when(step == 7)
    def _():
        for bits in (2, 3, 1):
            exchange(TOKEN_GRADS, flow_s, dtok_res, bits, True).start()
        keep_dtok.start()
        next_hop(LATE_SUMS, late_s, late_r, 0)
        for reduce in attn:
            reduce.send_x()
            reduce.add_y(0)
            reduce.start_z(0)
        for number in range(1, len(HOPS)):
            next_hop(LATE_SUMS, late_s, late_r, number)
        sum_res[...] = sums_s[5]
        late_res[...] = late_s[5]
        for reduce, cols in zip(attn, halves):
            ga_res[:, cols] = reduce.total()
        for bits in (1, 2, 3):
            for base, source, target in (
                (OUTPUTS, out_s, out_res), (TOKEN_GRADS, flow_s, dtok_res),
            ):
                exchange(base, source, target, bits, False).wait_recv()
                exchange(base, source, target, bits, True).wait_send()
        keep_out.wait()
        keep_dtok.wait()
        for number in range(len(HOPS)):
            hop(SUMS, sums_s, sums_r, number).wait_send()
            hop(LATE_SUMS, late_s, late_r, number).wait_send()
        for number, j in ((0, 1), (1, 0)):
            outer.core_copy(j, send_o.at[number]).wait_send()
            for reduce in attn:
                reduce.core_copy(j, send_a.at[number]).wait_send()
        inner.wait_sent((0, 1))
        inner.x_copy().wait_send()
        outer.wait_sent((0,))
        outer.whole_x_copy().wait_send()
        for reduce in attn:
            reduce.wait_sent((0, 1))
            reduce.x_copy().wait_send()


VMEM_LIMIT = 62 * 1024 * 1024


def resident(shape):
    return pl.BlockSpec(shape, lambda step: (0,) * len(shape))


def stepped(shape):
    return pl.BlockSpec((1,) + shape[1:], lambda step: (step,) + (0,) * (len(shape) - 1))


def spec_list(pairs):
    return [stepped(shape) if moves else resident(shape) for shape, moves in pairs]


def near_forward(tokens, cotangent, shard_i, w_query, w_key, w_value, w_mixer, w_outer, docs, vectors):
    groups, part, model = tokens.shape
    length = groups * part
    share, width = w_query.shape
    whole = (groups, model // share, share, model)
    sides = (groups, 2 * PAD, length)
    slopes = (groups, length, model)
    flat = (length, model)
    shard = (share, model)
    biases = (groups,) + vectors.shape
    anywhere = pl.BlockSpec(memory_space=pl.ANY)

    def early(shape):
        return pl.BlockSpec(
            (1,) + shape[1:], lambda step: (jnp.minimum(step, 3),) + (0,) * (len(shape) - 1)
        )

    def late(shape):
        return pl.BlockSpec(
            (1,) + shape[1:], lambda step: (jnp.maximum(step - 4, 0),) + (0,) * (len(shape) - 1)
        )

    def vmem(*shape, kind=BF16):
        return pltpu.VMEM(shape, kind)

    kept = [w_query, w_key, w_value, w_mixer, w_outer, docs, vectors]
    return pl.pallas_call(
        forward_kernel,
        grid=(2 * groups,),
        out_shape=[
            jax.ShapeDtypeStruct((2 * groups, length, model), BF16),
            jax.ShapeDtypeStruct(sides, BF16),
            jax.ShapeDtypeStruct(slopes, BF16),
            jax.ShapeDtypeStruct(flat, F32),
            jax.ShapeDtypeStruct(flat, F32),
            jax.ShapeDtypeStruct(flat, BF16),
            jax.ShapeDtypeStruct((model, length), BF16),
            jax.ShapeDtypeStruct(tokens.shape, BF16),
            jax.ShapeDtypeStruct((2,) + whole, BF16),
            jax.ShapeDtypeStruct(whole, BF16),
        ],
        in_specs=[anywhere] * 3 + [resident(each.shape) for each in kept],
        out_specs=[stepped((2 * groups, length, model)), early(sides), late(slopes)]
        + [anywhere] * 7,
        scratch_shapes=[
            vmem(*shard), vmem(*shard), vmem(model, 3 * PAD), vmem(model, PAD),
            vmem(*tokens.shape), vmem(model, length), vmem(*whole), vmem(*whole), vmem(*whole),
            vmem(*biases, kind=F32), vmem(length, PAD // 2), vmem(SEG, length),
            vmem(width // HEAD, HEAD + SEG, length), vmem(length, PAD),
            vmem(*flat, kind=F32), vmem(*flat, kind=F32), vmem(*flat),
            pltpu.SemaphoreType.DMA((FORWARD_WIRES,)),
            pltpu.SemaphoreType.DMA((FORWARD_WIRES,)),
            pltpu.SemaphoreType.DMA((13,)),
        ],
        compiler_params=pltpu.CompilerParams(
            vmem_limit_bytes=VMEM_LIMIT, collective_id=0, has_side_effects=True
        ),
        name="near_forward",
    )(tokens, cotangent, shard_i, *kept)


def attend_plain(x, a_all, biases, qaug, kaug, vaug, b_mixer):
    length, model = x.shape
    groups = a_all.shape[0]
    block = (groups, length, PAD)
    return pl.pallas_call(
        attend_plain_kernel,
        grid=(groups,),
        out_shape=[jax.ShapeDtypeStruct(block, BF16)] * 4 + [jax.ShapeDtypeStruct(x.shape, F32)],
        in_specs=spec_list(
            [
                (x.shape, 0), (a_all.shape, 1), (biases.shape, 1),
                (qaug.shape, 0), (kaug.shape, 0), (vaug.shape, 0), (b_mixer.shape, 0),
            ]
        ),
        out_specs=spec_list([(block, 1)] * 4 + [(x.shape, 0)]),
        scratch_shapes=[pltpu.VMEM((4, model, PAD), BF16)],
        compiler_params=pltpu.CompilerParams(vmem_limit_bytes=VMEM_LIMIT),
        name="attend_plain",
    )(x, a_all, biases, qaug, kaug, vaug, b_mixer)


def dense_both(first_sum, wi, wo, bi, vectors, cotangent):
    length, model = first_sum.shape
    groups, _, hidden = wi.shape
    grad = (groups, model, hidden)
    forth = lambda shape: pl.BlockSpec(
        (1,) + shape[1:], lambda step: (lax.rem(step, groups),) + (0,) * (len(shape) - 1)
    )
    late = lambda shape: pl.BlockSpec(
        (1,) + shape[1:], lambda step: (jnp.maximum(step - groups, 0),) + (0,) * (len(shape) - 1)
    )
    return pl.pallas_call(
        dense_kernel,
        grid=(2 * groups,),
        out_shape=[
            jax.ShapeDtypeStruct((length, model), BF16),
            jax.ShapeDtypeStruct((length, model), F32),
            jax.ShapeDtypeStruct((length, model), BF16),
            jax.ShapeDtypeStruct(grad, BF16),
            jax.ShapeDtypeStruct(grad, BF16),
            jax.ShapeDtypeStruct((groups, 1, hidden), F32),
            jax.ShapeDtypeStruct((8, model), F32),
        ],
        in_specs=[
            pl.BlockSpec(memory_space=pl.ANY), forth(wi.shape), forth(wo.shape), forth(bi.shape),
            resident(vectors.shape), resident(cotangent.shape),
        ],
        out_specs=[
            resident((length, model)), resident((length, model)), resident((length, model)),
            late(grad), late(grad), late((groups, 1, hidden)), resident((8, model)),
        ],
        scratch_shapes=[
            pltpu.VMEM((length, model), F32),
            pltpu.VMEM((length, model), F32),
            pltpu.VMEM((length, model), F32),
            pltpu.VMEM((length, model), F32),
            pltpu.VMEM((groups, length, hidden), BF16),
            pltpu.VMEM((groups, length, hidden), BF16),
            pltpu.VMEM((length, model), BF16),
            pltpu.VMEM((model, length), BF16),
            pltpu.VMEM((model, length), BF16),
            pltpu.VMEM((length, hidden), BF16),
        ],
        compiler_params=pltpu.CompilerParams(vmem_limit_bytes=VMEM_LIMIT),
        name="dense_both",
    )(first_sum, wi, wo, bi, vectors, cotangent)


def attend_backward(x, a_all, d_mixed, d_first, q, k, v, attended):
    length, model = x.shape
    groups = a_all.shape[0]
    sums = (groups, 1, PAD)
    return pl.pallas_call(
        attend_back_kernel,
        grid=(groups,),
        out_shape=[
            jax.ShapeDtypeStruct(x.shape, F32),
            jax.ShapeDtypeStruct(a_all.shape, BF16),
            jax.ShapeDtypeStruct(sums, F32),
            jax.ShapeDtypeStruct(sums, F32),
        ],
        in_specs=spec_list(
            [
                (x.shape, 0), (a_all.shape, 1), (d_mixed.shape, 0), (d_first.shape, 0),
                (q.shape, 1), (k.shape, 1), (v.shape, 1), (attended.shape, 1),
            ]
        ),
        out_specs=spec_list([(x.shape, 0), (a_all.shape, 1), (sums, 1), (sums, 1)]),
        scratch_shapes=[
            pltpu.VMEM((4, model, PAD), BF16),
            pltpu.VMEM((model, length), BF16),
            pltpu.VMEM((model, length), BF16),
            pltpu.VMEM((PAD, length), BF16),
            pltpu.VMEM((PAD, length), F32),
            pltpu.VMEM((length, PAD), F32),
            pltpu.VMEM((length, PAD), F32),
            pltpu.VMEM((length, 3 * PAD), BF16),
        ],
        compiler_params=pltpu.CompilerParams(vmem_limit_bytes=VMEM_LIMIT),
        name="attend_backward",
    )(x, a_all, d_mixed, d_first, q, k, v, attended)


def near_backward(acts, sides, slopes, w_ia, w_o, vectors, second, first, low, xt, cotangent):
    quarters, part, model = cotangent.shape
    length = quarters * part
    share = model // 8
    width = model // 4
    block = (4, 2, share, model)
    anywhere = pl.BlockSpec(memory_space=pl.ANY)

    def ordered(shape, place):
        return pl.BlockSpec(
            (1,) + shape[1:], lambda step: (place(step),) + (0,) * (len(shape) - 1)
        )

    def acts_at(step):
        return jnp.where(step < 4, 4 + slot_at(step), slot_at(step - 4))

    def weights_at(step):
        return jnp.where(step < 4, slot_at(step), 4 + slot_at(step - 4))

    def first_half(step):
        return slot_at(jnp.minimum(step, 3))

    def last_half(step):
        return slot_at(jnp.maximum(step - 4, 0))

    def vmem(*shape, kind=BF16):
        return pltpu.VMEM(shape, kind)

    final = [
        ((share, model), F32), ((share, model), F32), ((share, model), F32), ((16, model), F32),
        ((8, model), F32),
    ]
    return pl.pallas_call(
        backward_kernel,
        grid=(8,),
        out_shape=[jax.ShapeDtypeStruct(cotangent.shape, BF16)] * 2
        + [jax.ShapeDtypeStruct(*each) for each in final],
        in_specs=[
            ordered(acts.shape, acts_at), ordered(sides.shape, last_half),
            ordered(slopes.shape, first_half), ordered(w_ia.shape, weights_at),
            ordered(w_o.shape, first_half), resident(vectors.shape),
        ]
        + [anywhere] * 5,
        out_specs=[anywhere] * 2 + [resident(each[0]) for each in final],
        scratch_shapes=[
            vmem(model, length), vmem(model, length), vmem(length, model), vmem(length, model),
            vmem(*cotangent.shape), vmem(*cotangent.shape), vmem(length, model, kind=F32),
            vmem(2, ROWS, model, kind=F32),
            vmem(width, model), vmem(PAD, length), vmem(width, length), vmem(3 * width, length),
            vmem(width, length, kind=F32), vmem(width, length, kind=F32),
            vmem(6, 16, model, kind=F32), vmem(6, 8, model, kind=F32),
            vmem(5, 16, model, kind=F32), vmem(5, 8, model, kind=F32),
            vmem(2, *block), vmem(2, *block), vmem(2, *block), vmem(2, 4, share, model),
            vmem(2, 3, share, model), vmem(share, model),
            vmem(2, *block), vmem(2, *block), vmem(2, *block), vmem(1, 4, share, model),
            vmem(1, 3, share, model), vmem(*block),
            vmem(2, *block), vmem(2, *block), vmem(2, 4, share, model),
            vmem(2, 3, share, model), vmem(share, model),
            pltpu.SemaphoreType.DMA((BACKWARD_WIRES,)),
            pltpu.SemaphoreType.DMA((BACKWARD_WIRES,)),
            pltpu.SemaphoreType.DMA((8,)),
        ],
        compiler_params=pltpu.CompilerParams(
            vmem_limit_bytes=VMEM_LIMIT, collective_id=1, has_side_effects=True
        ),
        name="near_backward",
    )(acts, sides, slopes, w_ia, w_o, vectors, second, first, low, xt, cotangent)


def augment(labels, width):
    length = labels.shape[0]
    lanes = lax.broadcasted_iota(jnp.int32, (length, PAD), 1)
    in_docs = (lanes >= width) & (lanes < width + DOCS)
    same = (lanes - width) == labels[:, None]
    qaug = jnp.where(in_docs & same, 1.0, 0.0).astype(BF16)
    spare = (lanes >= width + DOCS) & (lanes < width + DOCS + 3 * (width // HEAD))
    kaug = jnp.where(in_docs & ~same, -(2.0**100), jnp.where(spare, 1.0, 0.0)).astype(BF16)
    vaug = jnp.where((lanes[:1] == width) | spare[:1], 1.0, 0.0).astype(BF16)
    return qaug, kaug, vaug


def body(
    tokens, doc_ids, w_query, b_query, w_key, w_value, b_value, w_mixer, b_mixer, gain_one,
    bias_one, w_inner, b_inner, w_outer, b_outer, gain_two, bias_two, cotangent,
):
    groups = lax.axis_size("tensor")
    rings = lax.axis_size("dp")
    place = lax.axis_index("tensor")
    width = w_query.shape[1]
    hidden = w_inner.shape[1]
    length = doc_ids.shape[2]
    model = tokens.shape[3]
    near = groups == 4 and rings == 8 and hidden == model and 4 * width == model

    if near:
        spare = jnp.zeros((PAD - width,), F32)
        vectors = jnp.concatenate(
            [
                b_mixer, gain_one, bias_one, b_outer, gain_two, bias_two, b_inner,
                b_query, spare, b_value, spare, jnp.zeros((PAD,), F32),
            ]
        ).reshape(8, model)
        acts, sides, slopes, first, second, low, xt, cot, w_ia, w_o = near_forward(
            tokens[:, 0], cotangent[:, 0], w_inner, w_query, w_key, w_value, w_mixer, w_outer,
            doc_ids, vectors,
        )
        out, d_tokens, ga, gi, go, tail, late = near_backward(
            acts, sides, slopes, w_ia.reshape(2 * groups, model, model),
            w_o.reshape(groups, model, model), vectors, second, first, low, xt, cot,
        )
        own = lambda whole, start: lax.dynamic_index_in_dim(whole, start + place, 0, False)
        mine = own(late, 0)
        dbq, dbv = mine[:width], mine[2 * width : 3 * width]
        dbi = own(tail, 0)
        tail = tail[2 * groups :]
        out, d_tokens = out[:, None], d_tokens[:, None].astype(F32)
    else:

        def gather(shard):
            whole = lax.all_gather(shard, ("tensor", "dp"), axis=0, tiled=True)
            return whole.reshape(groups, model, shard.shape[1])

        def to_sequence(part):
            return lax.all_to_all(part, "tensor", 0, 2, tiled=True).reshape(length, model)

        def from_sequence(whole):
            return lax.all_to_all(whole.reshape(1, 1, length, model), "tensor", 2, 0, tiled=True)

        def scatter(part):
            flat = part.reshape(-1, part.shape[2])
            total = lax.psum_scatter(flat, ("tensor", "dp"), scatter_dimension=0, tiled=True)
            return total.astype(F32)

        labels = lax.dynamic_index_in_dim(doc_ids[:, 0], place, 0, keepdims=False)
        qaug, kaug, vaug = augment(labels, width)
        shard_a = jnp.concatenate([w_query, w_key, w_value, w_mixer.T], axis=1)
        shard_o = w_outer.T
        spare = jnp.zeros((PAD - width,), F32)
        biases = jnp.concatenate([b_query, spare, b_value, spare, b_inner])[None]
        vectors = jnp.stack([gain_one, bias_one, b_outer, gain_two, bias_two] + [b_outer] * 3)
        x, cot = to_sequence(tokens), to_sequence(cotangent)
        a_all, wi, wo = gather(shard_a), gather(w_inner), gather(shard_o)
        every = lax.all_gather(biases, "tensor", axis=0)
        *saved, first_sum = attend_plain(x, a_all, every, qaug, kaug, vaug, b_mixer[None])
        out, d_first, d_mixed, g_inner, g_outer, dbi, small = dense_both(
            first_sum, wi, wo, every[:, :, 2 * PAD :], vectors, cot
        )
        d_tokens, g_attend, dbq, dbv = attend_backward(x, a_all, d_mixed, d_first, *saved)
        ga, gi, go = scatter(g_attend), scatter(g_inner), scatter(g_outer)
        rows = [dbq[:, 0, :width], dbv[:, 0, :width], dbi[:, 0], small]
        summed = lax.psum(jnp.concatenate([part.reshape(-1) for part in rows]), ("dp", "tensor"))
        own = lambda start, size: lax.dynamic_slice_in_dim(summed, start + place * size, size)
        dbq, dbv, dbi = own(0, width), own(model, width), own(2 * model, hidden)
        tail = summed[-small.size :].reshape(small.shape)
        out, d_tokens = from_sequence(out), from_sequence(d_tokens)
    return (
        out,
        d_tokens,
        ga[:, :width],
        dbq,
        ga[:, width : 2 * width],
        ga[:, 2 * width : 3 * width],
        dbv,
        ga[:, 3 * width :].T,
        tail[3],
        tail[4],
        tail[5],
        gi,
        dbi,
        go.T,
        tail[0],
        tail[1],
        tail[2],
    )


def solution(mesh):
    split = P(None, "dp", "tensor", None)
    both, flipped, part = P("dp", "tensor"), P("tensor", "dp"), P("tensor")
    return jax.shard_map(
        body,
        mesh=mesh,
        in_specs=(
            split, P(None, "dp", None), both, part, both, both, part, flipped, P(), P(), P(),
            both, part, flipped, P(), P(), P(), split,
        ),
        out_specs=(
            split, split, both, part, both, both, part, flipped, P(), P(), P(), both, part,
            flipped, P(), P(), P(),
        ),
        check_vma=False,
    )
```

```python
from functools import partial

import jax
import jax.numpy as jnp
from jax import lax
from jax.experimental import pallas as pl
from jax.experimental.pallas import tpu as pltpu
from jax.sharding import PartitionSpec as P

HEAD = 64
DOCS = 8
PAD = 256
ROWS = 256
LOG2E = 1.4426950408889634
EPS = 1e-12
F32 = jnp.float32
BF16 = jnp.bfloat16


def dot_nn(left, right):
    return lax.dot_general(left, right, (((1,), (0,)), ((), ())), preferred_element_type=F32)


def dot_nt(left, right):
    return lax.dot_general(left, right, (((1,), (1,)), ((), ())), preferred_element_type=F32)


def rows_of(index, size=ROWS):
    return pl.ds(pl.multiple_of(index * size, size), size)


def lane_index(shape):
    return lax.broadcasted_iota(jnp.int32, shape, 1)


def three_parts(values):
    high = values.astype(BF16)
    rest = values - high.astype(F32)
    middle = rest.astype(BF16)
    low = (rest - middle.astype(F32)).astype(BF16)
    return high, middle, low


def head_only(lanes, head):
    return (lanes >= head * HEAD) & (lanes < (head + 1) * HEAD)


def head_and_extra(lanes, head, width):
    extra = width + DOCS + 3 * head
    return (
        head_only(lanes, head)
        | ((lanes >= width) & (lanes < width + DOCS))
        | ((lanes >= extra) & (lanes < extra + 3))
    )


def unpack(block_ref, slot, width):
    part = block_ref[:, slot * width : (slot + 1) * width]
    return jnp.concatenate([part, jnp.zeros((part.shape[0], PAD - width), part.dtype)], axis=1)


def project(x_rows, rows, bq, bv, w_s, qaug_ref, kaug_ref, vaug_ref, q_ref, k_ref, v_ref):
    queries = (dot_nn(x_rows, w_s[0]) + bq).astype(BF16)
    q_ref[rows, :] = queries * jnp.asarray(HEAD**-0.5, BF16) + qaug_ref[rows, :]
    keys = dot_nn(x_rows, w_s[1]).astype(BF16)
    k_ref[rows, :] = keys + kaug_ref[rows, :]
    values = (dot_nn(x_rows, w_s[2]) + bv).astype(BF16)
    v_ref[rows, :] = values + vaug_ref[...]


def attend_rows(rows, width, w_s, q_ref, k_ref, v_ref, att_ref, first_ref):
    lanes = lane_index((ROWS, PAD))
    queries = q_ref[rows, :]
    attended = jnp.zeros((ROWS, PAD), F32)
    extended = queries
    for head in range(width // HEAD):
        masked = jnp.where(head_and_extra(lanes, head, width), queries, 0)
        scores = dot_nt(masked, k_ref[...])
        highest = jnp.max(scores, axis=1, keepdims=True)
        raw = jnp.exp2((scores - highest) * LOG2E).astype(BF16)
        mixed = dot_nn(raw, v_ref[...])
        total = mixed[:, width : width + 1]
        attended = jnp.where(head_only(lanes, head), mixed / total, attended)
        for spot, part in enumerate(three_parts(-(highest + jnp.log(total)))):
            here = lanes == width + DOCS + 3 * head + spot
            extended = jnp.where(here, jnp.broadcast_to(part, (ROWS, PAD)), extended)
    q_ref[rows, :] = extended
    attended = attended.astype(BF16)
    att_ref[rows, :] = attended
    first_ref[rows, :] += dot_nt(attended, w_s[3])


def attend_plain_kernel(
    x_ref, a_ref, bias_ref, qaug_ref, kaug_ref, vaug_ref, bm_ref,
    q_ref, k_ref, v_ref, att_ref, first_ref, w_s,
):
    length, model = x_ref.shape
    width = a_ref.shape[2] // 4
    for slot in range(4):
        w_s[slot] = unpack(a_ref.at[0], slot, width)
    biases = bias_ref[0]

    @pl.when(pl.program_id(0) == 0)
    def _():
        first_ref[...] = x_ref[...].astype(F32) + bm_ref[...]

    @pl.loop(0, length // ROWS)
    def _(index):
        rows = rows_of(index)
        project(
            x_ref[rows, :], rows, biases[:, :PAD], biases[:, PAD : 2 * PAD], w_s, qaug_ref,
            kaug_ref, vaug_ref, q_ref.at[0], k_ref.at[0], v_ref.at[0],
        )

    @pl.loop(0, length // ROWS)
    def _(index):
        refs = (ref.at[0] for ref in (q_ref, k_ref, v_ref, att_ref))
        attend_rows(rows_of(index), width, w_s, *refs, first_ref)


MESH = pl.DeviceIdType.MESH


def partner(index, bits, size):
    flipped = index
    for bit in (1, 2, 4):
        if bits & bit and bit < size:
            flipped = flipped + bit - 2 * bit * lax.rem(lax.div(index, bit), 2)
    return flipped


class Wires:
    def __init__(self, send, recv, place, row):
        self.send, self.recv, self.place, self.row = send, recv, place, row

    def to(self, tensor_bits, dp_bits):
        return (partner(self.row, dp_bits, 8), partner(self.place, tensor_bits, 4))

    def copy(self, number, source, target, tensor_bits=0, dp_bits=0):
        return pltpu.make_async_remote_copy(
            src_ref=source,
            dst_ref=target,
            send_sem=self.send.at[number],
            recv_sem=self.recv.at[number],
            device_id=self.to(tensor_bits, dp_bits),
            device_id_type=MESH,
        )


def greet(wires, peers):
    barrier = pltpu.get_barrier_semaphore()
    for tensor_bits, dp_bits in peers:
        pl.semaphore_signal(
            barrier, inc=1, device_id=wires.to(tensor_bits, dp_bits), device_id_type=MESH
        )
    pl.semaphore_wait(barrier, len(peers))


PEERS = ((1, 0), (2, 0), (3, 0), (0, 1), (0, 2), (0, 4), (0, 6))
TOKENS, COTS, BIASES, KIND_A = 0, 3, 6, 9
SHARD_WIRES, BLOCK_WIRES = 19, 11
KIND_I = KIND_A + SHARD_WIRES
KIND_O = KIND_I + SHARD_WIRES
FORWARD_WIRES = KIND_O + BLOCK_WIRES


class ShardGather:
    def __init__(self, wires, base, shard, whole):
        self.wires, self.base, self.shard, self.whole = wires, base, shard, whole
        z = lax.div(wires.row, 2)
        self.middle = (z == 1) | (z == 2)

    def at(self, slot, dp_bits):
        return self.whole.at[slot, partner(self.wires.row, dp_bits, 8)]

    def own(self, slot):
        return self.shard if slot == 0 else self.at(slot, 0)

    def cross_x(self):
        return self.wires.copy(self.base, self.shard, self.at(2, 0), 2, 0)

    def along_z(self, slot, step):
        number = self.base + 1 + 3 * (slot // 2) + step - 1
        return self.wires.copy(number, self.own(slot), self.at(slot, 0), 0, 2 * step)

    def hand_on(self, slot):
        number = self.base + 17 + slot // 2
        return self.wires.copy(number, self.at(slot, 4), self.at(slot, 4), 0, 2)

    def along_y(self, slot, step):
        source = self.own(slot) if step == 0 else self.at(slot, 2 * step)
        number = self.base + 7 + 4 * (slot // 2) + step
        return self.wires.copy(number, source, self.at(slot, 2 * step), 0, 1)

    def to_core(self, slot):
        number = self.base + 15 + slot // 2
        return self.wires.copy(number, self.whole.at[slot], self.whole.at[slot + 1], 1, 0)

    def start(self, slot):
        self.along_z(slot, 1).start()
        self.along_z(slot, 2).start()

        @pl.when(self.middle)
        def _():
            self.along_z(slot, 3).start()

        self.along_y(slot, 0).start()

    def advance(self, slot):
        self.along_z(slot, 2).wait_recv()

        @pl.when(self.middle)
        def _():
            self.hand_on(slot).start()

        self.along_y(slot, 2).start()
        self.along_z(slot, 1).wait_recv()
        self.along_y(slot, 1).start()

        @pl.when(self.middle)
        def _():
            self.along_z(slot, 3).wait_recv()

        @pl.when(jnp.logical_not(self.middle))
        def _():
            self.hand_on(slot).wait_recv()

        self.along_y(slot, 3).start()

    def wait_y(self, slot):
        for step in range(4):
            self.along_y(slot, step).wait_recv()

    def wait_sent(self, slots):
        self.cross_x().wait_send()
        for slot in slots:
            for step in (1, 2):
                self.along_z(slot, step).wait_send()

            @pl.when(self.middle)
            def _(slot=slot):
                self.along_z(slot, 3).wait_send()
                self.hand_on(slot).wait_send()

            for step in range(4):
                self.along_y(slot, step).wait_send()
        for slot in (0, 2):
            self.to_core(slot).wait_send()


class BlockGather(ShardGather):
    def along_z(self, slot, step):
        return self.wires.copy(
            self.base + step - 1, self.shard, self.at(0, 0), 0, 2 * step
        )

    def hand_on(self, slot):
        return self.wires.copy(self.base + 10, self.at(0, 4), self.at(0, 4), 0, 2)

    def along_y(self, slot, step):
        source = self.own(0) if step == 0 else self.at(0, 2 * step)
        return self.wires.copy(self.base + 3 + step, source, self.at(0, 2 * step), 0, 1)

    def cross_x(self):
        return self.wires.copy(self.base + 7, self.whole.at[0], self.whole.at[2], 2, 0)

    def to_core(self, slot):
        return self.wires.copy(
            self.base + 8 + slot // 2, self.whole.at[slot], self.whole.at[slot + 1], 1, 0
        )


def gelu_parts(values):
    phi = jnp.exp2(values * values * (-0.5 * LOG2E)) * 0.3989422804014327
    total = 0.5 + 0.5 * lax.erf(values * 0.7071067811865476)
    return values * total, total + values * phi


def norm_parts(values):
    average = jnp.mean(values, axis=-1, keepdims=True)
    centred = values - average
    spread = jnp.mean(centred * centred, axis=-1, keepdims=True)
    inverse = lax.rsqrt(spread + EPS)
    return centred * inverse, inverse


def norm_back(grads, gain, unit, inverse):
    scaled = grads * gain
    average = jnp.mean(scaled, axis=-1, keepdims=True)
    along = jnp.mean(scaled * unit, axis=-1, keepdims=True)
    return (scaled - average - unit * along) * inverse


def column_sum(values):
    return jnp.sum(values, axis=0, keepdims=True)


WIDE = 512
SEG = 16


def head_rows(head):
    return slice(head * HEAD, (head + 1) * HEAD)


def extra_rows(head, width):
    return slice(width + head * SEG, width + (head + 1) * SEG)


def place_head(part, extra, head, width):
    count = part.shape[1]
    zeros = lambda rows: [jnp.zeros((rows, count), part.dtype)] if rows else []
    pieces = zeros(head * HEAD) + [part] + zeros(width - (head + 1) * HEAD)
    pieces += zeros(head * SEG) + [extra] + zeros(PAD - width - (head + 1) * SEG)
    return jnp.concatenate(pieces, axis=0)


def parts_rows(values, before):
    parts = [part for part in three_parts(values)]
    rest = jnp.zeros((SEG - DOCS - 3, values.shape[1]), BF16)
    return jnp.concatenate([before] + parts + [rest], axis=0)


def attend_block(cols, width, key_ref, vt_s, side_ref):
    heads = range(width // HEAD)
    docs = side_ref[extra_rows(0, width), cols]

    def score(head):
        queries = place_head(side_ref[head_rows(head), cols], docs, head, width)
        return dot_nn(key_ref[...], queries)

    scores, highest, mixed = [score(0)], [], []
    for head in heads:
        if head + 1 < len(heads):
            scores.append(score(head + 1))
        highest.append(jnp.max(scores[head], axis=0, keepdims=True))
        raw = jnp.exp2((scores[head] - highest[head]) * LOG2E).astype(BF16)
        mixed.append(dot_nn(vt_s[head], raw))
    for head in heads:
        logs = -(highest[head] + jnp.log(mixed[head][HEAD : HEAD + 1]))
        side_ref[extra_rows(head, width), cols] = parts_rows(logs, docs[:DOCS])
    outs = [(each[:HEAD] / each[HEAD : HEAD + 1]).astype(BF16) for each in mixed]
    return jnp.concatenate(outs, axis=0)


def attend_block_back(cols, width, key_ref, value_ref, side_ref, do_s, kt_s, all_t, dk_t, dv_t):
    heads = range(width // HEAD)

    def products(head):
        queries = side_ref[head_rows(head), cols]
        d_att = do_s[head_rows(head), cols]
        extra = extra_rows(head, width)
        scores = dot_nn(key_ref[...], place_head(queries, side_ref[extra, cols], head, width))
        d_chances = dot_nn(value_ref[...], place_head(d_att, do_s[extra, cols], head, width))
        return queries, d_att, scores, d_chances

    ahead = products(0)
    d_queries, d_keys, d_values = [], [], []
    for head in heads:
        queries, d_att, scores, d_chances = ahead
        if head + 1 < len(heads):
            ahead = products(head + 1)
        chances = jnp.exp2(scores * LOG2E)
        d_scores = (chances * d_chances).astype(BF16)
        d_queries.append(dot_nn(kt_s[head_rows(head), :], d_scores) * HEAD**-0.5)
        d_keys.append(dot_nt(queries, d_scores))
        d_values.append(dot_nt(d_att, chances.astype(BF16)))
    for head in heads:
        all_t[head_rows(head), cols] = d_queries[head].astype(BF16)
        dk_t[head_rows(head), :] += d_keys[head]
        dv_t[head_rows(head), :] += d_values[head]


def forward_kernel(
    tok_ref, cot_ref, si_ref, wq_ref, wk_ref, wv_ref, wm_ref, wo_ref, doc_ref, vec_ref,
    acts_ref, side_ref, slope_ref, first_out, second_out, low_out, xt_out, cot_out, wia_out,
    wo_out,
    sa_s, so_s, w_s, wm_s, x_s, xt_s, a_s, i_s, o_s, bias_s, kaug_s, qdoc_s, vt_s, mix_s,
    first_s, second_s, low_s, send_sem, recv_sem, here_sem,
):
    step = pl.program_id(0)
    place = lax.axis_index("tensor")
    row = lax.axis_index("dp")
    quarters, part, model = x_s.shape
    length = quarters * part
    share, width = wq_ref.shape
    heads = width // HEAD
    blocks = length // ROWS
    wides = length // WIDE
    wires = Wires(send_sem, recv_sem, place, row)
    attn = ShardGather(wires, KIND_A, sa_s, a_s)
    inner = ShardGather(wires, KIND_I, si_ref, i_s)
    outer = BlockGather(wires, KIND_O, so_s, o_s)
    b_mixer, gain_one, bias_one, b_outer = (vec_ref[i : i + 1, :] for i in range(4))
    key_ref, value_ref = (acts_ref.at[0, :, i * PAD : (i + 1) * PAD] for i in range(2))

    def exchange(base, source, target, bits, mine):
        other = partner(place, bits, 4)
        return wires.copy(
            base + bits - 1, source.at[other], target.at[place if mine else other], bits, 0
        )

    def bias_copy(bits, mine):
        return wires.copy(BIASES + bits - 1, vec_ref, bias_s.at[bits], bits, 0)

    local = [
        pltpu.make_async_copy(tok_ref.at[place], x_s.at[place], here_sem.at[0]),
        pltpu.make_async_copy(sa_s, a_s.at[0, row], here_sem.at[1]),
        pltpu.make_async_copy(si_ref, i_s.at[0, row], here_sem.at[2]),
        pltpu.make_async_copy(so_s, o_s.at[0, row], here_sem.at[3]),
        pltpu.make_async_copy(vec_ref, bias_s.at[0], here_sem.at[4]),
    ]
    own_cot = pltpu.make_async_copy(cot_ref.at[place], cot_out.at[place], here_sem.at[5])
    keep_x = pltpu.make_async_copy(xt_s, xt_out, here_sem.at[6])
    keep_a = pltpu.make_async_copy(a_s, wia_out.at[1], here_sem.at[7])
    keep_i = pltpu.make_async_copy(i_s, wia_out.at[0], here_sem.at[8])
    keep_o = pltpu.make_async_copy(o_s, wo_out, here_sem.at[9])
    keep_first = pltpu.make_async_copy(first_s, first_out, here_sem.at[10])
    keep_low = pltpu.make_async_copy(low_s, low_out, here_sem.at[11])
    keep_second = pltpu.make_async_copy(second_s, second_out, here_sem.at[12])

    @pl.when(step == 0)
    def _():
        sa_s[...] = jnp.concatenate(
            [wq_ref[...], wk_ref[...], wv_ref[...], wm_ref[...].T], axis=1
        )
        greet(wires, PEERS)
        attn.cross_x().start()
        for bits in (1, 2, 3):
            bias_copy(bits, True).start()
        attn.start(0)
        for bits in (2, 3, 1):
            exchange(TOKENS, tok_ref, x_s, bits, True).start()
        so_s[...] = wo_ref[...].T
        for copy in local:
            copy.start()
        own_cot.start()
        labels = doc_ref[place]
        docs = lax.broadcasted_iota(jnp.int32, (DOCS, length), 0)
        same = docs == labels
        ones = jnp.ones((3, length), F32)
        rest = jnp.zeros((SEG - DOCS - 3, length), F32)
        qdoc_s[...] = jnp.concatenate(
            [jnp.where(same, 1.0, 0.0), jnp.zeros((SEG - DOCS, length), F32)], axis=0
        ).astype(BF16)
        one_head = jnp.concatenate([jnp.where(same, 0.0, -(2.0**100)), ones, rest], axis=0)
        tall = jnp.zeros((width - PAD // 2, length), F32)
        last = jnp.zeros((PAD - width - heads * SEG, length), F32)
        kaug_s[...] = jnp.concatenate([tall] + [one_head] * heads + [last], axis=0).astype(BF16).T
        for head in range(heads):
            vt_s[head, HEAD:, :] = jnp.ones((SEG, length), BF16)
        for copy in local:
            copy.wait()
        attn.cross_x().wait_recv()
        attn.start(2)
        attn.advance(0)
        attn.wait_y(0)
        attn.to_core(0).start()
        inner.cross_x().start()
        for bits in (1, 2, 3):
            exchange(TOKENS, tok_ref, x_s, bits, False).wait_recv()
            bias_copy(bits, False).wait_recv()

        @pl.loop(0, quarters)
        def _(index):
            rows = rows_of(index, part)
            first_s[rows, :] = x_s[index].astype(F32) + b_mixer

    @pl.when(step == 1)
    def _():
        @pl.loop(0, quarters)
        def _(index):
            xt_s[:, rows_of(index, part)] = x_s[index].T

        keep_x.start()

    @pl.when(step == 1)
    def _():
        attn.to_core(0).wait_recv()

    @pl.when(step == 2)
    def _():
        attn.wait_y(2)
        attn.to_core(2).start()

    @pl.when(step == 3)
    def _():
        attn.to_core(2).wait_recv()
        keep_a.start()

    @pl.when(step < 4)
    def _():
        for dp_row in range(a_s.shape[1]):
            packed = a_s[step, dp_row]
            rest = jnp.zeros((share, PAD - width), packed.dtype)
            rows = slice(dp_row * share, (dp_row + 1) * share)
            for slot in range(4):
                piece = packed[:, slot * width : (slot + 1) * width]
                piece = jnp.concatenate([piece, rest], axis=1)
                if slot < 3:
                    w_s[rows, slot * PAD : (slot + 1) * PAD] = piece
                else:
                    wm_s[rows, :] = piece
        bias = bias_s[step][7:8]
        lanes = lax.broadcasted_iota(jnp.int32, (1, PAD), 1) - width
        spare = (lanes >= 0) & (lanes < heads * SEG) & (lax.rem(lanes + SEG, SEG) >= DOCS)
        vaug = jnp.where(spare & (lax.rem(lanes + SEG, SEG) < DOCS + 3), 1.0, 0.0).astype(BF16)

        @pl.loop(0, wides)
        def _(index):
            rows = rows_of(index, WIDE)
            x_rows = x_s[pl.ds(index * (WIDE // part), WIDE // part)].reshape(WIDE, model)
            result = dot_nn(x_rows, w_s[...])
            queries = (result[:, :PAD] + bias[:, :PAD]).astype(BF16)
            queries = (queries * jnp.asarray(HEAD**-0.5, BF16)).T
            side_ref[0, :width, rows] = queries[:width]
            side_ref[0, PAD + width :, rows] = jnp.zeros((PAD - width, WIDE), BF16)
            keys = result[:, PAD : 2 * PAD].astype(BF16)
            key_ref[rows, : PAD // 2] = keys[:, : PAD // 2]
            key_ref[rows, PAD // 2 :] = keys[:, PAD // 2 :] + kaug_s[rows, :]
            values = (result[:, 2 * PAD :] + bias[:, PAD : 2 * PAD]).astype(BF16)
            value_ref[rows, :] = values + vaug
            values_t = values.T
            for head in range(heads):
                vt_s[head, :HEAD, rows] = values_t[head_rows(head)]

        for head in range(heads):
            side_ref[0, extra_rows(head, width), :] = qdoc_s[...]
        side_ref[0, width + heads * SEG : PAD, :] = jnp.zeros(
            (PAD - width - heads * SEG, length), BF16
        )

        @pl.loop(0, blocks)
        def _(index):
            cols = rows_of(index)
            attended = attend_block(cols, width, key_ref, vt_s, side_ref.at[0])
            side_ref[0, PAD : PAD + width, cols] = attended
            rest = jnp.zeros((PAD - width, ROWS), BF16)
            mix_s[cols, :] = jnp.concatenate([attended, rest], axis=0).T

            @pl.when((step == 0) & (index == 0))
            def _():
                outer.start(0)
                for bits in (2, 3, 1):
                    exchange(COTS, cot_ref, cot_out, bits, True).start()

            @pl.when((step == 0) & (index == 1))
            def _():
                attn.advance(2)

            @pl.when((step == 0) & (index == 3))
            def _():
                inner.cross_x().wait_recv()
                inner.start(0)

            @pl.when((step == 1) & (index == 2))
            def _():
                outer.advance(0)
                inner.start(2)

            @pl.when((step == 2) & (index == 3))
            def _():
                inner.advance(0)

            @pl.when((step == 3) & (index == 0))
            def _():
                outer.wait_y(0)
                outer.cross_x().start()
                outer.to_core(0).start()

            @pl.when((step == 3) & (index == 3))
            def _():
                inner.advance(2)

        @pl.loop(0, wides)
        def _(index):
            rows = rows_of(index, WIDE)
            first_s[rows, :] += dot_nt(mix_s[rows, :], wm_s[...])

    @pl.when(step == 4)
    def _():
        keep_first.start()

        @pl.loop(0, blocks)
        def _(index):
            rows = rows_of(index)
            unit, _inverse = norm_parts(first_s[rows, :])
            normed = unit * gain_one + bias_one
            low_s[rows, :] = normed.astype(BF16)
            second_s[rows, :] = normed + b_outer

        keep_low.start()
        inner.wait_y(0)
        inner.to_core(0).start()

    @pl.when(step == 5)
    def _():
        inner.to_core(0).wait_recv()
        outer.to_core(0).wait_recv()

    @pl.when(step == 6)
    def _():
        inner.wait_y(2)
        inner.to_core(2).start()
        outer.cross_x().wait_recv()
        outer.to_core(2).start()

    @pl.when(step == 7)
    def _():
        inner.to_core(2).wait_recv()
        outer.to_core(2).wait_recv()
        keep_i.start()
        keep_o.start()

    @pl.when(step >= 4)
    def _():
        slot = step - 4
        w_inner = i_s[slot].reshape(model, model)
        w_outer = o_s[slot].reshape(model, model)
        b_inner = bias_s[slot][6:7]

        @pl.loop(0, wides)
        def _(index):
            rows = rows_of(index, WIDE)
            value, slope = gelu_parts(dot_nn(low_s[rows, :], w_inner) + b_inner)
            hidden = value.astype(BF16)
            acts_ref[0, rows, :] = hidden
            slope_ref[0, rows, :] = slope.astype(BF16)
            second_s[rows, :] += dot_nt(hidden, w_outer)

    @pl.when(step == 7)
    def _():
        keep_second.start()
        for bits in (1, 2, 3):
            exchange(COTS, cot_ref, cot_out, bits, False).wait_recv()
        attn.wait_sent((0, 2))
        inner.wait_sent((0, 2))
        outer.wait_sent((0,))
        for bits in (1, 2, 3):
            exchange(TOKENS, tok_ref, x_s, bits, True).wait_send()
            exchange(COTS, cot_ref, cot_out, bits, True).wait_send()
            bias_copy(bits, True).wait_send()
        for copy in (
            own_cot, keep_x, keep_a, keep_i, keep_o, keep_first, keep_low, keep_second,
        ):
            copy.wait()


def dense_kernel(
    first_in, wi_ref, wo_ref, bi_ref, vec_ref, cot_ref,
    out_ref, dfirst_ref, dmix_ref, gi_ref, go_ref, dbi_ref, small_ref,
    first_ref, second_ref, normed_s, dsec_s, hidden_s, slope_s, low_s, low_t, back_t, dinner_s,
):
    step = pl.program_id(0)
    count = pl.num_programs(0) // 2
    length, model = first_in.shape
    blocks = length // ROWS
    gain_one, bias_one, b_outer, gain_two, bias_two = (vec_ref[i : i + 1, :] for i in range(5))

    @pl.when(step == 0)
    def _():
        copied = pltpu.sync_copy
        copied(first_in, first_ref)

        @pl.loop(0, blocks)
        def _(index):
            rows = rows_of(index)
            unit, _inverse = norm_parts(first_ref[rows, :])
            normed = unit * gain_one + bias_one
            normed_s[rows, :] = normed
            low_s[rows, :] = normed.astype(BF16)
            low_t[:, rows] = normed.astype(BF16).T
            second_ref[rows, :] = normed + b_outer

    @pl.when(step < count)
    def _():
        @pl.loop(0, blocks)
        def _(index):
            rows = rows_of(index)
            inner = dot_nn(low_s[rows, :], wi_ref[0]) + bi_ref[0]
            value, slope = gelu_parts(inner)
            hidden = value.astype(BF16)
            hidden_s[step, rows, :] = hidden
            slope_s[step, rows, :] = slope.astype(BF16)
            second_ref[rows, :] += dot_nt(hidden, wo_ref[0])

    @pl.when(step == count - 1)
    def _():
        small_ref[...] = jnp.zeros_like(small_ref)

        @pl.loop(0, blocks)
        def _(index):
            rows = rows_of(index)
            unit, inverse = norm_parts(second_ref[rows, :])
            out_ref[rows, :] = (unit * gain_two + bias_two).astype(BF16)
            grads = cot_ref[rows, :].astype(F32)
            d_second = norm_back(grads, gain_two, unit, inverse)
            small_ref[0:1, :] += column_sum(d_second)
            small_ref[1:2, :] += column_sum(grads * unit)
            small_ref[2:3, :] += column_sum(grads)
            dsec_s[rows, :] = d_second
            low = d_second.astype(BF16)
            dmix_ref[rows, :] = low
            back_t[:, rows] = low.T

    @pl.when(step >= count)
    def _():
        place = step - count
        dbi_ref[...] = jnp.zeros_like(dbi_ref)

        @pl.loop(0, blocks)
        def _(index):
            rows = rows_of(index)
            d_hidden = dot_nn(dmix_ref[rows, :], wo_ref[0])
            d_inner = (d_hidden * slope_s[place, rows, :].astype(F32)).astype(BF16)
            dinner_s[rows, :] = d_inner
            dbi_ref[0] += column_sum(d_inner.astype(F32))
            dsec_s[rows, :] += dot_nt(d_inner, wi_ref[0])

        @pl.loop(0, model // ROWS)
        def _(index):
            rows = rows_of(index)
            gi_ref[0, rows, :] = dot_nn(low_t[rows, :], dinner_s[...]).astype(gi_ref.dtype)
            go_ref[0, rows, :] = dot_nn(back_t[rows, :], hidden_s[place]).astype(go_ref.dtype)

    @pl.when(step == 2 * count - 1)
    def _():
        @pl.loop(0, blocks)
        def _(index):
            rows = rows_of(index)
            unit, inverse = norm_parts(first_ref[rows, :])
            grads = dsec_s[rows, :]
            d_first = norm_back(grads, gain_one, unit, inverse)
            small_ref[3:4, :] += column_sum(d_first)
            small_ref[4:5, :] += column_sum(grads * unit)
            small_ref[5:6, :] += column_sum(grads)
            dfirst_ref[rows, :] = d_first
            dmix_ref[rows, :] = d_first.astype(BF16)


def back_rows(rows, width, w_s, dmix_rows, q_ref, k_ref, v_ref, att_ref, kt_s, dq_s, dk_s, dv_s):
    lanes = lane_index((ROWS, PAD))
    queries = q_ref[rows, :]
    d_att = dot_nn(dmix_rows, w_s[3]).astype(BF16)
    product = d_att.astype(F32) * att_ref[rows, :].astype(F32)
    heads = range(width // HEAD)
    extended = d_att
    for head in heads:
        centre = jnp.sum(jnp.where(head_only(lanes, head), product, 0.0), axis=1, keepdims=True)
        for spot, part in enumerate(three_parts(-centre)):
            here = lanes == width + DOCS + 3 * head + spot
            extended = jnp.where(here, jnp.broadcast_to(part, (ROWS, PAD)), extended)
    chances_all = []
    d_scores_all = []
    d_att_all = []
    queries_all = []
    for head in heads:
        wide = head_and_extra(lanes, head, width)
        only = head_only(lanes, head)
        chances = jnp.exp2(dot_nt(k_ref[...], jnp.where(wide, queries, 0)) * LOG2E)
        d_chances = dot_nt(v_ref[...], jnp.where(wide, extended, 0))
        d_scores = (chances * d_chances).astype(BF16)
        chances_all.append(chances.astype(BF16))
        d_scores_all.append(d_scores)
        d_att_all.append(jnp.where(only, d_att, 0))
        queries_all.append(jnp.where(only, queries, 0))
        head_rows = slice(head * HEAD, (head + 1) * HEAD)
        dq_s[head_rows, rows] = dot_nn(kt_s[head_rows, :], d_scores)
    dv_s[...] += dot_nn(jnp.concatenate(chances_all, 1), jnp.concatenate(d_att_all, 0))
    dk_s[...] += dot_nn(jnp.concatenate(d_scores_all, 1), jnp.concatenate(queries_all, 0))


def back_low(rows, width, dq_s, dk_s, dv_s, low_s):
    d_query = (dq_s[:, rows].T * HEAD**-0.5).astype(BF16)
    d_query = jnp.where(lane_index(d_query.shape) < width, d_query, 0)
    d_value = dv_s[rows, :].astype(BF16)
    low_s[rows, :PAD] = d_query
    low_s[rows, PAD : 2 * PAD] = dk_s[rows, :].astype(BF16)
    low_s[rows, 2 * PAD :] = d_value
    return column_sum(d_query.astype(F32)), column_sum(d_value.astype(F32))


def back_tokens(rows, w_s, low_s):
    return sum(dot_nt(low_s[rows, slot * PAD : (slot + 1) * PAD], w_s[slot]) for slot in range(3))


def back_weights(rows, width, slots, xt_s, dmixt_s, low_s, att_ref):
    parts = []
    for slot in slots:
        if slot < 3:
            part = dot_nn(xt_s[rows, :], low_s[:, slot * PAD : (slot + 1) * PAD])
        else:
            part = dot_nn(dmixt_s[rows, :], att_ref[...])
        parts.append(part[:, :width])
    return jnp.concatenate(parts, axis=1).astype(BF16)


def attend_back_kernel(
    x_ref, a_ref, dmix_ref, dfirst_ref, q_ref, k_ref, v_ref, att_ref,
    dtok_ref, ga_ref, dbq_ref, dbv_ref,
    w_s, xt_s, dmixt_s, kt_s, dq_s, dk_s, dv_s, low_s,
):
    length, model = x_ref.shape
    width = a_ref.shape[2] // 4
    blocks = length // ROWS
    for slot in range(4):
        w_s[slot] = unpack(a_ref.at[0], slot, width)

    @pl.when(pl.program_id(0) == 0)
    def _():
        dtok_ref[...] = dfirst_ref[...]

        @pl.loop(0, blocks)
        def _(index):
            rows = rows_of(index)
            xt_s[:, rows] = x_ref[rows, :].T
            dmixt_s[:, rows] = dmix_ref[rows, :].T

    for sums in (dk_s, dv_s, dbq_ref, dbv_ref):
        sums[...] = jnp.zeros_like(sums)

    @pl.loop(0, blocks)
    def _(index):
        rows = rows_of(index)
        kt_s[:, rows] = k_ref[0, rows, :].T

    @pl.loop(0, blocks)
    def _(index):
        rows = rows_of(index)
        dmix_rows = dmix_ref[rows, :]
        refs = (ref.at[0] for ref in (q_ref, k_ref, v_ref, att_ref))
        back_rows(rows, width, w_s, dmix_rows, *refs, kt_s, dq_s, dk_s, dv_s)

    @pl.loop(0, blocks)
    def _(index):
        rows = rows_of(index)
        for_query, for_value = back_low(rows, width, dq_s, dk_s, dv_s, low_s)
        dbq_ref[0] += for_query
        dbv_ref[0] += for_value
        dtok_ref[rows, :] += back_tokens(rows, w_s, low_s)

    @pl.loop(0, model // ROWS)
    def _(index):
        rows = rows_of(index)
        ga_ref[0, rows, :] = back_weights(
            rows, width, range(4), xt_s, dmixt_s, low_s, att_ref.at[0]
        )


def add_into(target, source):
    target[...] = (target[...].astype(F32) + source[...].astype(F32)).astype(target.dtype)


class Reduce:
    COUNT = 11

    def __init__(self, wires, base, held, core, by_y, by_z, by_x, cols=slice(None)):
        self.wires, self.base, self.held, self.core = wires, base, held, core
        self.by_y, self.by_z, self.by_x = by_y, by_z, by_x
        self.cols = cols
        self.z, self.y = lax.div(wires.row, 2), lax.rem(wires.row, 2)

    def part(self, ref, *index):
        return ref.at[index + (slice(None), self.cols)]

    def core_copy(self, j, source):
        everything = (slice(None), slice(None))
        return self.wires.copy(
            self.base + j, self.part(source, *everything), self.part(self.core, j, *everything), 1, 0
        )

    def add_core(self, j):
        self.core_copy(j, self.held.at[j]).wait_recv()
        for z in range(4):
            for y in range(2):
                add_into(self.part(self.held, j, z, y), self.part(self.core, j, z, y))

    def y_copy(self, j):
        source = self.part(self.held, j, slice(None), 1 - self.y)
        return self.wires.copy(
            self.base + 2 + j, source, self.part(self.by_y, j, slice(None)), 0, 1
        )

    def add_y(self, j):
        self.y_copy(j).wait_recv()
        for z in range(4):
            add_into(self.part(self.held, j, z, self.y), self.part(self.by_y, j, z))

    def z_copy(self, j, step):
        other = lax.div(partner(self.wires.row, 2 * step, 8), 2)
        number = self.base + 4 + 3 * j + step - 1
        return self.wires.copy(
            number, self.part(self.held, j, other, self.y), self.part(self.by_z, j, step - 1),
            0, 2 * step,
        )

    def start_z(self, j):
        for step in (1, 2, 3):
            self.z_copy(j, step).start()

    def total_z(self, j):
        total = self.part(self.held, j, self.z, self.y)[...].astype(F32)
        for step in (1, 2, 3):
            self.z_copy(j, step).wait_recv()
            total = total + self.part(self.by_z, j, step - 1)[...].astype(F32)
        return total

    def x_copy(self):
        source = self.part(self.held, 1, self.z, self.y)
        return self.wires.copy(self.base + 10, source, self.part(self.by_x), 2, 0)

    def send_x(self):
        self.part(self.held, 1, self.z, self.y)[...] = self.total_z(1).astype(BF16)
        self.x_copy().start()

    def total(self):
        self.x_copy().wait_recv()
        return self.total_z(0) + self.part(self.by_x)[...].astype(F32)

    def whole_x_copy(self):
        return self.wires.copy(self.base + 10, self.held.at[1], self.by_x, 2, 0)

    def add_whole_x(self):
        self.whole_x_copy().wait_recv()
        for z in range(4):
            for y in range(2):
                add_into(self.held.at[0, z, y], self.by_x.at[z, y])

    def wait_sent(self, j_all):
        for j in j_all:
            self.y_copy(j).wait_send()
            for step in (1, 2, 3):
                self.z_copy(j, step).wait_send()


OUTPUTS, TOKEN_GRADS, SUMS, LATE_SUMS = 0, 3, 6, 16
RED_I = 26
RED_O = RED_I + Reduce.COUNT
RED_A = RED_O + Reduce.COUNT
BACKWARD_WIRES = RED_A + 2 * Reduce.COUNT
BACK_PEERS = PEERS + ((0, 3), (0, 5), (0, 7))


def slot_at(step):
    return jnp.where(step < 2, 3 - 2 * step, 6 - 2 * step)


def backward_kernel(
    acts_ref, side_ref, slope_ref, wia_ref, wo_ref, vec_ref, second_ref, first_ref, low_ref, xt_ref,
    cot_ref,
    out_res, dtok_res, ga_res, gi_res, go_res, sum_res, late_res,
    low_t, back_t, dmix_s, low_s, flow_s, out_s, grad_s, first_s, wmt_s, do_s, kt_s, all_t, dk_t,
    dv_t, sums_s, sums_o, sums_d, late_o, late_t, late_d,
    send_i, held_i, core_i, y_i, z_i, x_i, send_o, held_o, core_o, y_o, z_o, x_o,
    held_a, core_a, y_a, z_a, x_a,
    send_sem, recv_sem, here_sem,
):
    step = pl.program_id(0)
    place = lax.axis_index("tensor")
    row = lax.axis_index("dp")
    length, model = dmix_s.shape
    quarters, part, _ = flow_s.shape
    width = wia_ref.shape[2] // 4
    heads = width // HEAD
    blocks = length // ROWS
    wides = length // WIDE
    share = held_i.shape[3]
    wires = Wires(send_sem, recv_sem, place, row)
    inner = Reduce(wires, RED_I, held_i, core_i, y_i, z_i, x_i)
    outer = Reduce(wires, RED_O, held_o, core_o, y_o, z_o, x_o)
    halves = (slice(0, model // 2), slice(model // 2, model))
    send_a = send_i
    attn = [
        Reduce(wires, RED_A + half * Reduce.COUNT, held_a, core_a, y_a, z_a, x_a, cols)
        for half, cols in enumerate(halves)
    ]
    gain_one, gain_two, bias_two = (vec_ref[i : i + 1, :] for i in (1, 4, 5))
    key_ref, value_ref = (acts_ref.at[0, :, i * PAD : (i + 1) * PAD] for i in range(2))
    att_ref = side_ref.at[0, PAD : PAD + width]

    def exchange(base, source, target, bits, mine):
        other = partner(place, bits, 4)
        return wires.copy(
            base + bits - 1, source.at[other], target.at[place if mine else other], bits, 0
        )

    def by_tensor(bits):
        return wires.copy(
            SUMS + bits - 1, sums_s.at[place], sums_s.at[place], bits, 0
        )

    def by_rows(base, kept, bits):
        return wires.copy(base + 2 + bits, kept.at[row], kept.at[row], 0, bits)

    def late_copy(bits):
        return wires.copy(LATE_SUMS + bits - 1, late_o.at[bits], late_t.at[bits], bits, 0)

    def sum_rows(base, kept):
        for bits in range(1, 8):
            by_rows(base, kept, bits).wait_recv()
        return sum((kept[number] for number in range(1, 8)), kept[0])

    load_second = pltpu.make_async_copy(second_ref, grad_s, here_sem.at[0])
    load_cot = pltpu.make_async_copy(cot_ref, flow_s, here_sem.at[1])
    load_low = pltpu.make_async_copy(low_ref, low_s, here_sem.at[2])
    load_x = pltpu.make_async_copy(xt_ref, low_t, here_sem.at[3])
    keep_out = pltpu.make_async_copy(out_s.at[place], out_res.at[place], here_sem.at[4])
    keep_dtok = pltpu.make_async_copy(flow_s.at[place], dtok_res.at[place], here_sem.at[5])

    def load_first(index):
        return pltpu.make_async_copy(
            first_ref.at[rows_of(index)], first_s.at[index % 2], here_sem.at[6 + index % 2]
        )

    order = (3, 1, 2, 0)

    @pl.when(step == 0)
    def _():
        load_second.start()
        load_cot.start()
        load_low.start()
        sums_s[place] = jnp.zeros_like(sums_s[0])
        for bits in range(4):
            late_o[bits] = jnp.zeros_like(late_o[0])
        greet(wires, BACK_PEERS)
        load_second.wait()
        load_cot.wait()
        load_low.wait()

        @pl.loop(0, quarters)
        def _(index):
            rows = rows_of(index, part)
            low_t[:, rows] = low_s[rows, :].T
            unit, inverse = norm_parts(grad_s[rows, :])
            out_s[index] = (unit * gain_two + bias_two).astype(BF16)
            grads = flow_s[index].astype(F32)
            d_second = norm_back(grads, gain_two, unit, inverse)
            sums_s[place, 8:9, :] += column_sum(d_second)
            sums_s[place, 9:10, :] += column_sum(grads * unit)
            sums_s[place, 10:11, :] += column_sum(grads)
            grad_s[rows, :] = d_second
            lower = d_second.astype(BF16)
            dmix_s[rows, :] = lower
            back_t[:, rows] = lower.T

        for bits in (2, 3, 1):
            exchange(OUTPUTS, out_s, out_res, bits, True).start()
        keep_out.start()

    @pl.when(step < 4)
    def _():
        @pl.loop(0, wides)
        def _(index):
            rows = rows_of(index, WIDE)
            d_hidden = dot_nn(dmix_s[rows, :], wo_ref[0])
            d_inner = (d_hidden * slope_ref[0, rows, :].astype(F32)).astype(BF16)
            low_s[rows, :] = d_inner
            for_inner = column_sum(d_inner.astype(F32))
            for number, bits in enumerate(order):

                @pl.when(step == number)
                def _(bits=bits):
                    sums_s[place, pl.ds(partner(place, bits, 4), 1), :] += for_inner

            grad_s[rows, :] += dot_nt(d_inner, wia_ref[0])

        @pl.loop(0, model // (4 * share))
        def _(pair):
            rows = rows_of(pair, 4 * share)
            for transposed, right, sent, held in (
                (back_t, acts_ref.at[0], send_o, held_o), (low_t, low_s, send_i, held_i),
            ):
                grads = dot_nn(transposed[rows, :], right[...]).astype(BF16)
                pieces = grads.reshape(2, 2, share, model)

                @pl.when(step < 2)
                def _(pieces=pieces, sent=sent):
                    sent[step, pl.ds(2 * pair, 2)] = pieces

                @pl.when(step >= 2)
                def _(pieces=pieces, held=held):
                    held[3 - step, pl.ds(2 * pair, 2)] = pieces

    for number, j in ((0, 1), (1, 0)):

        @pl.when(step == number)
        def _(number=number, j=j):
            outer.core_copy(j, send_o.at[number]).start()
            inner.core_copy(j, send_i.at[number]).start()

    @pl.when(step == 2)
    def _():
        load_first(0).start()
        load_first(1).start()
        outer.add_core(1)
        outer.whole_x_copy().start()
        inner.add_core(1)
        inner.y_copy(1).start()

    @pl.when(step == 3)
    def _():
        inner.add_core(0)
        inner.y_copy(0).start()
        outer.add_core(0)
        load_x.start()
        for index in range(blocks):
            rows = slice(index * ROWS, (index + 1) * ROWS)
            load_first(index).wait()
            unit, inverse = norm_parts(first_s[index % 2])
            if index + 2 < blocks:
                load_first(index + 2).start()
            grads = grad_s[rows, :]
            d_first = norm_back(grads, gain_one, unit, inverse)
            sums_s[place, 11:12, :] += column_sum(d_first)
            sums_s[place, 12:13, :] += column_sum(grads * unit)
            sums_s[place, 13:14, :] += column_sum(grads)
            grad_s[rows, :] = d_first
            lower = d_first.astype(BF16)
            dmix_s[rows, :] = lower
            back_t[:, rows] = lower.T
        load_x.wait()
        for bits in (1, 2, 3):
            by_tensor(bits).start()

    @pl.when(step == 4)
    def _():
        for number, j in ((0, 1), (1, 0)):
            inner.core_copy(j, send_i.at[number]).wait_send()

    @pl.when(step == 7)
    def _():
        for reduce in attn:
            reduce.add_core(1)
            reduce.y_copy(1).start()

    @pl.when(step >= 4)
    def _():
        wmt_s[...] = wia_ref[0, :, 3 * width :].T
        for sums in (dk_t, dv_t):
            sums[...] = jnp.zeros_like(sums)

        @pl.loop(0, wides)
        def _(index):
            cols = rows_of(index, WIDE)
            kt_s[:, cols] = key_ref[cols, :].T[:width]
            d_att = dot_nn(wmt_s[...], back_t[:, cols]).astype(BF16)
            do_s[:width, cols] = d_att
            product = d_att.astype(F32) * att_ref[:, cols].astype(F32)
            none = jnp.zeros((DOCS, WIDE), BF16)
            for head in range(heads):
                centre = column_sum(product[head_rows(head)])
                do_s[extra_rows(head, width), cols] = parts_rows(-centre, none)

        @pl.loop(0, blocks)
        def _(index):
            attend_block_back(
                rows_of(index), width, key_ref, value_ref, side_ref.at[0], do_s, kt_s, all_t,
                dk_t, dv_t,
            )

            @pl.when((step == 4) & (index == 0))
            def _():
                inner.add_y(1)
                inner.start_z(1)

            @pl.when((step == 4) & (index == 3))
            def _():
                inner.add_y(0)
                inner.start_z(0)
                outer.add_whole_x()
                outer.y_copy(0).start()

            @pl.when((step == 5) & (index == 1))
            def _():
                inner.send_x()
                for bits in (1, 2, 3):
                    by_tensor(bits).wait_recv()
                sums_o[...] = sums_s[0] + sums_s[1] + sums_s[2] + sums_s[3]
                sums_d[row, :6, :] = sums_o[8:14, :]
                sums_d[row, 6:7, :] = sums_o[pl.ds(place, 1), :]
                sums_d[row, 7:, :] = jnp.zeros((1, model), F32)
                for bits in range(1, 8):
                    by_rows(SUMS, sums_d, bits).start()

            @pl.when((step == 7) & (index == 1))
            def _():
                sum_res[...] = sum_rows(SUMS, sums_d)

            @pl.when((step == 5) & (index == 3))
            def _():
                outer.add_y(0)
                outer.start_z(0)

            @pl.when((step == 6) & (index == 1))
            def _():
                gi_res[...] = inner.total()

            @pl.when((step == 6) & (index == 3))
            def _():
                go_res[...] = outer.total_z(0)

            @pl.when((step == 7) & (index == 3))
            def _():
                for reduce in attn:
                    reduce.add_y(1)
                    reduce.start_z(1)

        all_t[width : 2 * width, :] = dk_t[...].astype(BF16)
        all_t[2 * width :, :] = dv_t[...].astype(BF16)
        for_all = dot_nt(jnp.ones((8, length), BF16), all_t[...])
        for number, bits in enumerate(order):

            @pl.when(step == 4 + number)
            def _(bits=bits):
                late_o[bits, :, : 3 * width] = for_all
                if bits:
                    late_copy(bits).start()
                    return
                for other in (1, 2, 3):
                    late_copy(other).wait_recv()
                late_d[row] = late_o[0] + late_t[1] + late_t[2] + late_t[3]
                for other in range(1, 8):
                    by_rows(LATE_SUMS, late_d, other).start()

        for half, cols in enumerate(halves):

            @pl.loop(0, model // (4 * share))
            def _(pair):
                rows = rows_of(pair, 4 * share)
                if half == 0:
                    grads = dot_nt(low_t[rows, :], all_t[: 2 * width, :])
                else:
                    for_value = dot_nt(low_t[rows, :], all_t[2 * width :, :])
                    for_mixer = dot_nt(back_t[rows, :], att_ref[...])
                    grads = jnp.concatenate([for_value, for_mixer], axis=1)
                pieces = grads.astype(BF16).reshape(2, 2, share, model // 2)

                @pl.when(step < 6)
                def _(pieces=pieces):
                    send_a[step - 4, pl.ds(2 * pair, 2), :, :, cols] = pieces

                @pl.when(step >= 6)
                def _(pieces=pieces):
                    held_a[7 - step, pl.ds(2 * pair, 2), :, :, cols] = pieces

            for number, j in ((0, 1), (1, 0)):

                @pl.when(step == 4 + number)
                def _(number=number, j=j):
                    attn[half].core_copy(j, send_a.at[number]).start()

            @pl.when(step == 7)
            def _():
                attn[half].add_core(0)
                attn[half].y_copy(0).start()

        @pl.loop(0, wides)
        def _(index):
            rows = rows_of(index, WIDE)
            transposed = all_t[:, rows].T
            grad_s[rows, :] += dot_nt(transposed, wia_ref[0, :, : 3 * width])

            @pl.when(step == 7)
            def _():
                places = pl.ds(index * (WIDE // part), WIDE // part)
                flow_s[places] = grad_s[rows, :].astype(BF16).reshape(WIDE // part, part, model)

    @pl.when(step == 7)
    def _():
        for bits in (2, 3, 1):
            exchange(TOKEN_GRADS, flow_s, dtok_res, bits, True).start()
        keep_dtok.start()
        for reduce in attn:
            reduce.send_x()
        for reduce in attn:
            reduce.add_y(0)
            reduce.start_z(0)
        late_res[...] = sum_rows(LATE_SUMS, late_d)
        for reduce, cols in zip(attn, halves):
            ga_res[:, cols] = reduce.total()
        for bits in (1, 2, 3):
            for base, source, target in (
                (OUTPUTS, out_s, out_res), (TOKEN_GRADS, flow_s, dtok_res),
            ):
                exchange(base, source, target, bits, False).wait_recv()
                exchange(base, source, target, bits, True).wait_send()
        keep_out.wait()
        keep_dtok.wait()
        for bits in (1, 2, 3):
            by_tensor(bits).wait_send()
            late_copy(bits).wait_send()
        for bits in range(1, 8):
            by_rows(SUMS, sums_d, bits).wait_send()
            by_rows(LATE_SUMS, late_d, bits).wait_send()
        for number, j in ((0, 1), (1, 0)):
            outer.core_copy(j, send_o.at[number]).wait_send()
            for reduce in attn:
                reduce.core_copy(j, send_a.at[number]).wait_send()
        inner.wait_sent((0, 1))
        inner.x_copy().wait_send()
        outer.wait_sent((0,))
        outer.whole_x_copy().wait_send()
        for reduce in attn:
            reduce.wait_sent((0, 1))
            reduce.x_copy().wait_send()


VMEM_LIMIT = 62 * 1024 * 1024


def resident(shape):
    return pl.BlockSpec(shape, lambda step: (0,) * len(shape))


def stepped(shape):
    return pl.BlockSpec((1,) + shape[1:], lambda step: (step,) + (0,) * (len(shape) - 1))


def spec_list(pairs):
    return [stepped(shape) if moves else resident(shape) for shape, moves in pairs]


def near_forward(tokens, cotangent, shard_i, w_query, w_key, w_value, w_mixer, w_outer, docs, vectors):
    groups, part, model = tokens.shape
    length = groups * part
    share, width = w_query.shape
    whole = (groups, model // share, share, model)
    sides = (groups, 2 * PAD, length)
    slopes = (groups, length, model)
    flat = (length, model)
    shard = (share, model)
    biases = (groups,) + vectors.shape
    anywhere = pl.BlockSpec(memory_space=pl.ANY)

    def early(shape):
        return pl.BlockSpec(
            (1,) + shape[1:], lambda step: (jnp.minimum(step, 3),) + (0,) * (len(shape) - 1)
        )

    def late(shape):
        return pl.BlockSpec(
            (1,) + shape[1:], lambda step: (jnp.maximum(step - 4, 0),) + (0,) * (len(shape) - 1)
        )

    def vmem(*shape, kind=BF16):
        return pltpu.VMEM(shape, kind)

    kept = [w_query, w_key, w_value, w_mixer, w_outer, docs, vectors]
    return pl.pallas_call(
        forward_kernel,
        grid=(2 * groups,),
        out_shape=[
            jax.ShapeDtypeStruct((2 * groups, length, model), BF16),
            jax.ShapeDtypeStruct(sides, BF16),
            jax.ShapeDtypeStruct(slopes, BF16),
            jax.ShapeDtypeStruct(flat, F32),
            jax.ShapeDtypeStruct(flat, F32),
            jax.ShapeDtypeStruct(flat, BF16),
            jax.ShapeDtypeStruct((model, length), BF16),
            jax.ShapeDtypeStruct(tokens.shape, BF16),
            jax.ShapeDtypeStruct((2,) + whole, BF16),
            jax.ShapeDtypeStruct(whole, BF16),
        ],
        in_specs=[anywhere] * 3 + [resident(each.shape) for each in kept],
        out_specs=[stepped((2 * groups, length, model)), early(sides), late(slopes)]
        + [anywhere] * 7,
        scratch_shapes=[
            vmem(*shard), vmem(*shard), vmem(model, 3 * PAD), vmem(model, PAD),
            vmem(*tokens.shape), vmem(model, length), vmem(*whole), vmem(*whole), vmem(*whole),
            vmem(*biases, kind=F32), vmem(length, PAD // 2), vmem(SEG, length),
            vmem(width // HEAD, HEAD + SEG, length), vmem(length, PAD),
            vmem(*flat, kind=F32), vmem(*flat, kind=F32), vmem(*flat),
            pltpu.SemaphoreType.DMA((FORWARD_WIRES,)),
            pltpu.SemaphoreType.DMA((FORWARD_WIRES,)),
            pltpu.SemaphoreType.DMA((13,)),
        ],
        compiler_params=pltpu.CompilerParams(
            vmem_limit_bytes=VMEM_LIMIT, collective_id=0, has_side_effects=True
        ),
        name="near_forward",
    )(tokens, cotangent, shard_i, *kept)


def attend_plain(x, a_all, biases, qaug, kaug, vaug, b_mixer):
    length, model = x.shape
    groups = a_all.shape[0]
    block = (groups, length, PAD)
    return pl.pallas_call(
        attend_plain_kernel,
        grid=(groups,),
        out_shape=[jax.ShapeDtypeStruct(block, BF16)] * 4 + [jax.ShapeDtypeStruct(x.shape, F32)],
        in_specs=spec_list(
            [
                (x.shape, 0), (a_all.shape, 1), (biases.shape, 1),
                (qaug.shape, 0), (kaug.shape, 0), (vaug.shape, 0), (b_mixer.shape, 0),
            ]
        ),
        out_specs=spec_list([(block, 1)] * 4 + [(x.shape, 0)]),
        scratch_shapes=[pltpu.VMEM((4, model, PAD), BF16)],
        compiler_params=pltpu.CompilerParams(vmem_limit_bytes=VMEM_LIMIT),
        name="attend_plain",
    )(x, a_all, biases, qaug, kaug, vaug, b_mixer)


def dense_both(first_sum, wi, wo, bi, vectors, cotangent):
    length, model = first_sum.shape
    groups, _, hidden = wi.shape
    grad = (groups, model, hidden)
    forth = lambda shape: pl.BlockSpec(
        (1,) + shape[1:], lambda step: (lax.rem(step, groups),) + (0,) * (len(shape) - 1)
    )
    late = lambda shape: pl.BlockSpec(
        (1,) + shape[1:], lambda step: (jnp.maximum(step - groups, 0),) + (0,) * (len(shape) - 1)
    )
    return pl.pallas_call(
        dense_kernel,
        grid=(2 * groups,),
        out_shape=[
            jax.ShapeDtypeStruct((length, model), BF16),
            jax.ShapeDtypeStruct((length, model), F32),
            jax.ShapeDtypeStruct((length, model), BF16),
            jax.ShapeDtypeStruct(grad, BF16),
            jax.ShapeDtypeStruct(grad, BF16),
            jax.ShapeDtypeStruct((groups, 1, hidden), F32),
            jax.ShapeDtypeStruct((8, model), F32),
        ],
        in_specs=[
            pl.BlockSpec(memory_space=pl.ANY), forth(wi.shape), forth(wo.shape), forth(bi.shape),
            resident(vectors.shape), resident(cotangent.shape),
        ],
        out_specs=[
            resident((length, model)), resident((length, model)), resident((length, model)),
            late(grad), late(grad), late((groups, 1, hidden)), resident((8, model)),
        ],
        scratch_shapes=[
            pltpu.VMEM((length, model), F32),
            pltpu.VMEM((length, model), F32),
            pltpu.VMEM((length, model), F32),
            pltpu.VMEM((length, model), F32),
            pltpu.VMEM((groups, length, hidden), BF16),
            pltpu.VMEM((groups, length, hidden), BF16),
            pltpu.VMEM((length, model), BF16),
            pltpu.VMEM((model, length), BF16),
            pltpu.VMEM((model, length), BF16),
            pltpu.VMEM((length, hidden), BF16),
        ],
        compiler_params=pltpu.CompilerParams(vmem_limit_bytes=VMEM_LIMIT),
        name="dense_both",
    )(first_sum, wi, wo, bi, vectors, cotangent)


def attend_backward(x, a_all, d_mixed, d_first, q, k, v, attended):
    length, model = x.shape
    groups = a_all.shape[0]
    sums = (groups, 1, PAD)
    return pl.pallas_call(
        attend_back_kernel,
        grid=(groups,),
        out_shape=[
            jax.ShapeDtypeStruct(x.shape, F32),
            jax.ShapeDtypeStruct(a_all.shape, BF16),
            jax.ShapeDtypeStruct(sums, F32),
            jax.ShapeDtypeStruct(sums, F32),
        ],
        in_specs=spec_list(
            [
                (x.shape, 0), (a_all.shape, 1), (d_mixed.shape, 0), (d_first.shape, 0),
                (q.shape, 1), (k.shape, 1), (v.shape, 1), (attended.shape, 1),
            ]
        ),
        out_specs=spec_list([(x.shape, 0), (a_all.shape, 1), (sums, 1), (sums, 1)]),
        scratch_shapes=[
            pltpu.VMEM((4, model, PAD), BF16),
            pltpu.VMEM((model, length), BF16),
            pltpu.VMEM((model, length), BF16),
            pltpu.VMEM((PAD, length), BF16),
            pltpu.VMEM((PAD, length), F32),
            pltpu.VMEM((length, PAD), F32),
            pltpu.VMEM((length, PAD), F32),
            pltpu.VMEM((length, 3 * PAD), BF16),
        ],
        compiler_params=pltpu.CompilerParams(vmem_limit_bytes=VMEM_LIMIT),
        name="attend_backward",
    )(x, a_all, d_mixed, d_first, q, k, v, attended)


def near_backward(acts, sides, slopes, w_ia, w_o, vectors, second, first, low, xt, cotangent):
    quarters, part, model = cotangent.shape
    length = quarters * part
    share = model // 8
    width = model // 4
    block = (4, 2, share, model)
    anywhere = pl.BlockSpec(memory_space=pl.ANY)

    def ordered(shape, place):
        return pl.BlockSpec(
            (1,) + shape[1:], lambda step: (place(step),) + (0,) * (len(shape) - 1)
        )

    def acts_at(step):
        return jnp.where(step < 4, 4 + slot_at(step), slot_at(step - 4))

    def weights_at(step):
        return jnp.where(step < 4, slot_at(step), 4 + slot_at(step - 4))

    def first_half(step):
        return slot_at(jnp.minimum(step, 3))

    def last_half(step):
        return slot_at(jnp.maximum(step - 4, 0))

    def vmem(*shape, kind=BF16):
        return pltpu.VMEM(shape, kind)

    final = [
        ((share, model), F32), ((share, model), F32), ((share, model), F32), ((8, model), F32),
        ((8, model), F32),
    ]
    return pl.pallas_call(
        backward_kernel,
        grid=(8,),
        out_shape=[jax.ShapeDtypeStruct(cotangent.shape, BF16)] * 2
        + [jax.ShapeDtypeStruct(*each) for each in final],
        in_specs=[
            ordered(acts.shape, acts_at), ordered(sides.shape, last_half),
            ordered(slopes.shape, first_half), ordered(w_ia.shape, weights_at),
            ordered(w_o.shape, first_half), resident(vectors.shape),
        ]
        + [anywhere] * 5,
        out_specs=[anywhere] * 2 + [resident(each[0]) for each in final],
        scratch_shapes=[
            vmem(model, length), vmem(model, length), vmem(length, model), vmem(length, model),
            vmem(*cotangent.shape), vmem(*cotangent.shape), vmem(length, model, kind=F32),
            vmem(2, ROWS, model, kind=F32),
            vmem(width, model), vmem(PAD, length), vmem(width, length), vmem(3 * width, length),
            vmem(width, length, kind=F32), vmem(width, length, kind=F32),
            vmem(4, 16, model, kind=F32), vmem(16, model, kind=F32), vmem(8, 8, model, kind=F32),
            vmem(4, 8, model, kind=F32), vmem(4, 8, model, kind=F32), vmem(8, 8, model, kind=F32),
            vmem(2, *block), vmem(2, *block), vmem(2, *block), vmem(2, 4, share, model),
            vmem(2, 3, share, model), vmem(share, model),
            vmem(2, *block), vmem(2, *block), vmem(2, *block), vmem(1, 4, share, model),
            vmem(1, 3, share, model), vmem(*block),
            vmem(2, *block), vmem(2, *block), vmem(2, 4, share, model),
            vmem(2, 3, share, model), vmem(share, model),
            pltpu.SemaphoreType.DMA((BACKWARD_WIRES,)),
            pltpu.SemaphoreType.DMA((BACKWARD_WIRES,)),
            pltpu.SemaphoreType.DMA((8,)),
        ],
        compiler_params=pltpu.CompilerParams(
            vmem_limit_bytes=VMEM_LIMIT, collective_id=1, has_side_effects=True
        ),
        name="near_backward",
    )(acts, sides, slopes, w_ia, w_o, vectors, second, first, low, xt, cotangent)


def augment(labels, width):
    length = labels.shape[0]
    lanes = lax.broadcasted_iota(jnp.int32, (length, PAD), 1)
    in_docs = (lanes >= width) & (lanes < width + DOCS)
    same = (lanes - width) == labels[:, None]
    qaug = jnp.where(in_docs & same, 1.0, 0.0).astype(BF16)
    spare = (lanes >= width + DOCS) & (lanes < width + DOCS + 3 * (width // HEAD))
    kaug = jnp.where(in_docs & ~same, -(2.0**100), jnp.where(spare, 1.0, 0.0)).astype(BF16)
    vaug = jnp.where((lanes[:1] == width) | spare[:1], 1.0, 0.0).astype(BF16)
    return qaug, kaug, vaug


def body(
    tokens, doc_ids, w_query, b_query, w_key, w_value, b_value, w_mixer, b_mixer, gain_one,
    bias_one, w_inner, b_inner, w_outer, b_outer, gain_two, bias_two, cotangent,
):
    groups = lax.axis_size("tensor")
    rings = lax.axis_size("dp")
    place = lax.axis_index("tensor")
    width = w_query.shape[1]
    hidden = w_inner.shape[1]
    length = doc_ids.shape[2]
    model = tokens.shape[3]
    near = groups == 4 and rings == 8 and hidden == model and 4 * width == model

    if near:
        spare = jnp.zeros((PAD - width,), F32)
        vectors = jnp.concatenate(
            [
                b_mixer, gain_one, bias_one, b_outer, gain_two, bias_two, b_inner,
                b_query, spare, b_value, spare, jnp.zeros((PAD,), F32),
            ]
        ).reshape(8, model)
        acts, sides, slopes, first, second, low, xt, cot, w_ia, w_o = near_forward(
            tokens[:, 0], cotangent[:, 0], w_inner, w_query, w_key, w_value, w_mixer, w_outer,
            doc_ids, vectors,
        )
        out, d_tokens, ga, gi, go, tail, late = near_backward(
            acts, sides, slopes, w_ia.reshape(2 * groups, model, model),
            w_o.reshape(groups, model, model), vectors, second, first, low, xt, cot,
        )
        dbq, dbv = late[0, :width], late[0, 2 * width : 3 * width]
        dbi = tail[6]
        out, d_tokens = out[:, None], d_tokens[:, None].astype(F32)
    else:

        def gather(shard):
            whole = lax.all_gather(shard, ("tensor", "dp"), axis=0, tiled=True)
            return whole.reshape(groups, model, shard.shape[1])

        def to_sequence(part):
            return lax.all_to_all(part, "tensor", 0, 2, tiled=True).reshape(length, model)

        def from_sequence(whole):
            return lax.all_to_all(whole.reshape(1, 1, length, model), "tensor", 2, 0, tiled=True)

        def scatter(part):
            flat = part.reshape(-1, part.shape[2])
            total = lax.psum_scatter(flat, ("tensor", "dp"), scatter_dimension=0, tiled=True)
            return total.astype(F32)

        labels = lax.dynamic_index_in_dim(doc_ids[:, 0], place, 0, keepdims=False)
        qaug, kaug, vaug = augment(labels, width)
        shard_a = jnp.concatenate([w_query, w_key, w_value, w_mixer.T], axis=1)
        shard_o = w_outer.T
        spare = jnp.zeros((PAD - width,), F32)
        biases = jnp.concatenate([b_query, spare, b_value, spare, b_inner])[None]
        vectors = jnp.stack([gain_one, bias_one, b_outer, gain_two, bias_two] + [b_outer] * 3)
        x, cot = to_sequence(tokens), to_sequence(cotangent)
        a_all, wi, wo = gather(shard_a), gather(w_inner), gather(shard_o)
        every = lax.all_gather(biases, "tensor", axis=0)
        *saved, first_sum = attend_plain(x, a_all, every, qaug, kaug, vaug, b_mixer[None])
        out, d_first, d_mixed, g_inner, g_outer, dbi, small = dense_both(
            first_sum, wi, wo, every[:, :, 2 * PAD :], vectors, cot
        )
        d_tokens, g_attend, dbq, dbv = attend_backward(x, a_all, d_mixed, d_first, *saved)
        ga, gi, go = scatter(g_attend), scatter(g_inner), scatter(g_outer)
        rows = [dbq[:, 0, :width], dbv[:, 0, :width], dbi[:, 0], small]
        summed = lax.psum(jnp.concatenate([part.reshape(-1) for part in rows]), ("dp", "tensor"))
        own = lambda start, size: lax.dynamic_slice_in_dim(summed, start + place * size, size)
        dbq, dbv, dbi = own(0, width), own(model, width), own(2 * model, hidden)
        tail = summed[-small.size :].reshape(small.shape)
        out, d_tokens = from_sequence(out), from_sequence(d_tokens)
    return (
        out,
        d_tokens,
        ga[:, :width],
        dbq,
        ga[:, width : 2 * width],
        ga[:, 2 * width : 3 * width],
        dbv,
        ga[:, 3 * width :].T,
        tail[3],
        tail[4],
        tail[5],
        gi,
        dbi,
        go.T,
        tail[0],
        tail[1],
        tail[2],
    )


def solution(mesh):
    split = P(None, "dp", "tensor", None)
    both, flipped, part = P("dp", "tensor"), P("tensor", "dp"), P("tensor")
    return jax.shard_map(
        body,
        mesh=mesh,
        in_specs=(
            split, P(None, "dp", None), both, part, both, both, part, flipped, P(), P(), P(),
            both, part, flipped, P(), P(), P(), split,
        ),
        out_specs=(
            split, split, both, part, both, both, part, flipped, P(), P(), P(), both, part,
            flipped, P(), P(), P(),
        ),
        check_vma=False,
    )
```

```python
from functools import partial

import jax
import jax.numpy as jnp
from jax import lax
from jax.experimental import pallas as pl
from jax.experimental.pallas import tpu as pltpu
from jax.sharding import PartitionSpec as P

HEAD = 64
DOCS = 8
PAD = 256
ROWS = 256
LOG2E = 1.4426950408889634
EPS = 1e-12
F32 = jnp.float32
BF16 = jnp.bfloat16


def dot_nn(left, right):
    return lax.dot_general(left, right, (((1,), (0,)), ((), ())), preferred_element_type=F32)


def dot_nt(left, right):
    return lax.dot_general(left, right, (((1,), (1,)), ((), ())), preferred_element_type=F32)


def rows_of(index, size=ROWS):
    return pl.ds(pl.multiple_of(index * size, size), size)


def lane_index(shape):
    return lax.broadcasted_iota(jnp.int32, shape, 1)


def three_parts(values):
    high = values.astype(BF16)
    rest = values - high.astype(F32)
    middle = rest.astype(BF16)
    low = (rest - middle.astype(F32)).astype(BF16)
    return high, middle, low


def head_only(lanes, head):
    return (lanes >= head * HEAD) & (lanes < (head + 1) * HEAD)


def head_and_extra(lanes, head, width):
    extra = width + DOCS + 3 * head
    return (
        head_only(lanes, head)
        | ((lanes >= width) & (lanes < width + DOCS))
        | ((lanes >= extra) & (lanes < extra + 3))
    )


def unpack(block_ref, slot, width):
    part = block_ref[:, slot * width : (slot + 1) * width]
    return jnp.concatenate([part, jnp.zeros((part.shape[0], PAD - width), part.dtype)], axis=1)


def project(x_rows, rows, bq, bv, w_s, qaug_ref, kaug_ref, vaug_ref, q_ref, k_ref, v_ref):
    queries = (dot_nn(x_rows, w_s[0]) + bq).astype(BF16)
    q_ref[rows, :] = queries * jnp.asarray(HEAD**-0.5, BF16) + qaug_ref[rows, :]
    keys = dot_nn(x_rows, w_s[1]).astype(BF16)
    k_ref[rows, :] = keys + kaug_ref[rows, :]
    values = (dot_nn(x_rows, w_s[2]) + bv).astype(BF16)
    v_ref[rows, :] = values + vaug_ref[...]


def attend_rows(rows, width, w_s, q_ref, k_ref, v_ref, att_ref, first_ref):
    lanes = lane_index((ROWS, PAD))
    queries = q_ref[rows, :]
    attended = jnp.zeros((ROWS, PAD), F32)
    extended = queries
    for head in range(width // HEAD):
        masked = jnp.where(head_and_extra(lanes, head, width), queries, 0)
        scores = dot_nt(masked, k_ref[...])
        highest = jnp.max(scores, axis=1, keepdims=True)
        raw = jnp.exp2((scores - highest) * LOG2E).astype(BF16)
        mixed = dot_nn(raw, v_ref[...])
        total = mixed[:, width : width + 1]
        attended = jnp.where(head_only(lanes, head), mixed / total, attended)
        for spot, part in enumerate(three_parts(-(highest + jnp.log(total)))):
            here = lanes == width + DOCS + 3 * head + spot
            extended = jnp.where(here, jnp.broadcast_to(part, (ROWS, PAD)), extended)
    q_ref[rows, :] = extended
    attended = attended.astype(BF16)
    att_ref[rows, :] = attended
    first_ref[rows, :] += dot_nt(attended, w_s[3])


def attend_plain_kernel(
    x_ref, a_ref, bias_ref, qaug_ref, kaug_ref, vaug_ref, bm_ref,
    q_ref, k_ref, v_ref, att_ref, first_ref, w_s,
):
    length, model = x_ref.shape
    width = a_ref.shape[2] // 4
    for slot in range(4):
        w_s[slot] = unpack(a_ref.at[0], slot, width)
    biases = bias_ref[0]

    @pl.when(pl.program_id(0) == 0)
    def _():
        first_ref[...] = x_ref[...].astype(F32) + bm_ref[...]

    @pl.loop(0, length // ROWS)
    def _(index):
        rows = rows_of(index)
        project(
            x_ref[rows, :], rows, biases[:, :PAD], biases[:, PAD : 2 * PAD], w_s, qaug_ref,
            kaug_ref, vaug_ref, q_ref.at[0], k_ref.at[0], v_ref.at[0],
        )

    @pl.loop(0, length // ROWS)
    def _(index):
        refs = (ref.at[0] for ref in (q_ref, k_ref, v_ref, att_ref))
        attend_rows(rows_of(index), width, w_s, *refs, first_ref)


MESH = pl.DeviceIdType.MESH


def partner(index, bits, size):
    flipped = index
    for bit in (1, 2, 4):
        if bits & bit and bit < size:
            flipped = flipped + bit - 2 * bit * lax.rem(lax.div(index, bit), 2)
    return flipped


class Wires:
    def __init__(self, send, recv, place, row):
        self.send, self.recv, self.place, self.row = send, recv, place, row

    def to(self, tensor_bits, dp_bits):
        return (partner(self.row, dp_bits, 8), partner(self.place, tensor_bits, 4))

    def copy(self, number, source, target, tensor_bits=0, dp_bits=0):
        return pltpu.make_async_remote_copy(
            src_ref=source,
            dst_ref=target,
            send_sem=self.send.at[number],
            recv_sem=self.recv.at[number],
            device_id=self.to(tensor_bits, dp_bits),
            device_id_type=MESH,
        )


def greet(wires, peers):
    barrier = pltpu.get_barrier_semaphore()
    for tensor_bits, dp_bits in peers:
        pl.semaphore_signal(
            barrier, inc=1, device_id=wires.to(tensor_bits, dp_bits), device_id_type=MESH
        )
    pl.semaphore_wait(barrier, len(peers))


PEERS = ((1, 0), (2, 0), (3, 0), (0, 1), (0, 2), (0, 4), (0, 6))
TOKENS, COTS, BIASES, KIND_A = 0, 3, 6, 9
SHARD_WIRES, BLOCK_WIRES = 19, 18
KIND_I = KIND_A + SHARD_WIRES
KIND_O = KIND_I + SHARD_WIRES
FORWARD_WIRES = KIND_O + BLOCK_WIRES


class ShardGather:
    def __init__(self, wires, base, shard, whole, across=False):
        self.wires, self.base, self.shard, self.whole = wires, base, shard, whole
        self.across = across
        z = lax.div(wires.row, 2)
        self.middle = (z == 1) | (z == 2)

    def at(self, slot, dp_bits):
        return self.whole.at[slot, partner(self.wires.row, dp_bits, 8)]

    def own(self, slot):
        return self.shard if slot == 0 else self.at(slot, 0)

    def cross_x(self):
        return self.wires.copy(self.base, self.shard, self.at(2, 0), 2, 0)

    def along_z(self, slot, step):
        number = self.base + 1 + 3 * (slot // 2) + step - 1
        return self.wires.copy(number, self.own(slot), self.at(slot, 0), 0, 2 * step)

    def hand_on(self, slot):
        number = self.base + 17 + slot // 2
        return self.wires.copy(number, self.at(slot, 4), self.at(slot, 4), 0, 2)

    def along_y(self, slot, step):
        number = self.base + 7 + 4 * (slot // 2) + step
        if slot and self.across:
            other = 2 * step + 1
            return self.wires.copy(number, self.at(0, other), self.at(2, other), 2, 0)
        source = self.own(slot) if step == 0 else self.at(slot, 2 * step)
        return self.wires.copy(number, source, self.at(slot, 2 * step), 0, 1)

    def to_core(self, slot):
        number = self.base + 15 + slot // 2
        return self.wires.copy(number, self.whole.at[slot], self.whole.at[slot + 1], 1, 0)

    def start(self, slot):
        self.along_z(slot, 2).start()
        self.along_z(slot, 1).start()

        @pl.when(self.middle)
        def _():
            self.along_z(slot, 3).start()

    def advance(self, slot):
        self.advance_near(slot)
        self.advance_far(slot)

    def advance_near(self, slot):
        self.along_z(slot, 2).wait_recv()

        @pl.when(self.middle)
        def _():
            self.hand_on(slot).start()

        self.pass_y(slot, 2)
        self.along_z(slot, 1).wait_recv()
        self.pass_y(slot, 1)

    def pass_y(self, slot, step):
        if not (slot and self.across):
            self.along_y(slot, step).start()

    def advance_far(self, slot):
        @pl.when(self.middle)
        def _():
            self.along_z(slot, 3).wait_recv()

        @pl.when(jnp.logical_not(self.middle))
        def _():
            self.hand_on(slot).wait_recv()

        self.pass_y(slot, 3)

    def wait_y(self, slot):
        for step in range(4):
            self.along_y(slot, step).wait_recv()

    def wait_sent(self, slots):
        for slot in slots:
            for step in (1, 2):
                self.along_z(slot, step).wait_send()

            @pl.when(self.middle)
            def _(slot=slot):
                self.along_z(slot, 3).wait_send()
                self.hand_on(slot).wait_send()

            for step in range(4):
                self.along_y(slot, step).wait_send()
        for slot in (0, 2):
            self.to_core(slot).wait_send()


class BlockGather(ShardGather):
    def along_z(self, slot, step):
        return self.wires.copy(
            self.base + step - 1, self.shard, self.at(0, 0), 0, 2 * step
        )

    def hand_on(self, slot):
        return self.wires.copy(self.base + 7, self.at(0, 4), self.at(0, 4), 0, 2)

    def along_y(self, slot, step):
        source = self.own(0) if step == 0 else self.at(0, 2 * step)
        return self.wires.copy(self.base + 3 + step, source, self.at(0, 2 * step), 0, 1)

    def cross(self, bits):
        source = self.own(0) if bits == 0 else self.at(0, bits)
        return self.wires.copy(self.base + 8 + bits, source, self.at(2, bits), 2, 0)

    def to_core(self, slot):
        return self.wires.copy(
            self.base + 16 + slot // 2, self.whole.at[slot], self.whole.at[slot + 1], 1, 0
        )

    def advance(self, slot):
        super().advance(slot)
        for bits in (0, 4, 2, 6):
            self.cross(bits).start()

    def wait_y(self, slot):
        super().wait_y(slot)
        for bits in (1, 3, 5, 7):
            self.cross(bits).start()

    def wait_x(self):
        for bits in range(8):
            self.cross(bits).wait_recv()

    def wait_sent(self, slots):
        super().wait_sent(slots)
        for bits in range(8):
            self.cross(bits).wait_send()


def gelu_parts(values):
    phi = jnp.exp2(values * values * (-0.5 * LOG2E)) * 0.3989422804014327
    total = 0.5 + 0.5 * lax.erf(values * 0.7071067811865476)
    return values * total, total + values * phi


def norm_parts(values):
    average = jnp.mean(values, axis=-1, keepdims=True)
    centred = values - average
    spread = jnp.mean(centred * centred, axis=-1, keepdims=True)
    inverse = lax.rsqrt(spread + EPS)
    return centred * inverse, inverse


def norm_back(grads, gain, unit, inverse):
    scaled = grads * gain
    average = jnp.mean(scaled, axis=-1, keepdims=True)
    along = jnp.mean(scaled * unit, axis=-1, keepdims=True)
    return (scaled - average - unit * along) * inverse


def column_sum(values):
    return jnp.sum(values, axis=0, keepdims=True)


WIDE = 512
SEG = 16


def head_rows(head):
    return slice(head * HEAD, (head + 1) * HEAD)


def extra_rows(head, width):
    return slice(width + head * SEG, width + (head + 1) * SEG)


def place_head(part, extra, head, width):
    count = part.shape[1]
    zeros = lambda rows: [jnp.zeros((rows, count), part.dtype)] if rows else []
    pieces = zeros(head * HEAD) + [part] + zeros(width - (head + 1) * HEAD)
    pieces += zeros(head * SEG) + [extra] + zeros(PAD - width - (head + 1) * SEG)
    return jnp.concatenate(pieces, axis=0)


def parts_rows(values, before):
    parts = [part for part in three_parts(values)]
    rest = jnp.zeros((SEG - DOCS - 3, values.shape[1]), BF16)
    return jnp.concatenate([before] + parts + [rest], axis=0)


def attend_block(cols, width, key_ref, vt_s, side_ref):
    heads = range(width // HEAD)
    docs = side_ref[extra_rows(0, width), cols]

    def score(head):
        queries = place_head(side_ref[head_rows(head), cols], docs, head, width)
        return dot_nn(key_ref[...], queries)

    scores, highest, mixed = [score(0)], [], []
    for head in heads:
        if head + 1 < len(heads):
            scores.append(score(head + 1))
        highest.append(jnp.max(scores[head], axis=0, keepdims=True))
        raw = jnp.exp2((scores[head] - highest[head]) * LOG2E).astype(BF16)
        mixed.append(dot_nn(vt_s[head], raw))
    for head in heads:
        logs = -(highest[head] + jnp.log(mixed[head][HEAD : HEAD + 1]))
        side_ref[extra_rows(head, width), cols] = parts_rows(logs, docs[:DOCS])
    outs = [(each[:HEAD] / each[HEAD : HEAD + 1]).astype(BF16) for each in mixed]
    return jnp.concatenate(outs, axis=0)


def attend_block_back(cols, width, key_ref, value_ref, side_ref, do_s, kt_s, all_t, dk_t, dv_t):
    heads = range(width // HEAD)

    def products(head):
        queries = side_ref[head_rows(head), cols]
        d_att = do_s[head_rows(head), cols]
        extra = extra_rows(head, width)
        scores = dot_nn(key_ref[...], place_head(queries, side_ref[extra, cols], head, width))
        d_chances = dot_nn(value_ref[...], place_head(d_att, do_s[extra, cols], head, width))
        return queries, d_att, scores, d_chances

    ahead = products(0)
    d_queries, d_keys, d_values = [], [], []
    for head in heads:
        queries, d_att, scores, d_chances = ahead
        if head + 1 < len(heads):
            ahead = products(head + 1)
        chances = jnp.exp2(scores * LOG2E)
        d_scores = (chances * d_chances).astype(BF16)
        d_queries.append(dot_nn(kt_s[head_rows(head), :], d_scores) * HEAD**-0.5)
        d_keys.append(dot_nt(queries, d_scores))
        d_values.append(dot_nt(d_att, chances.astype(BF16)))
    for head in heads:
        all_t[head_rows(head), cols] = d_queries[head].astype(BF16)
        dk_t[head_rows(head), :] += d_keys[head]
        dv_t[head_rows(head), :] += d_values[head]


def forward_kernel(
    tok_ref, cot_ref, si_ref, wq_ref, wk_ref, wv_ref, wm_ref, wo_ref, doc_ref, vec_ref,
    acts_ref, side_ref, slope_ref, first_out, second_out, low_out, xt_out, cot_out, wia_out,
    wo_out,
    sa_s, so_s, w_s, wm_s, x_s, xt_s, a_s, i_s, o_s, bias_s, kaug_s, qdoc_s, vt_s, mix_s,
    first_s, second_s, low_s, send_sem, recv_sem, here_sem,
):
    step = pl.program_id(0)
    place = lax.axis_index("tensor")
    row = lax.axis_index("dp")
    quarters, part, model = x_s.shape
    length = quarters * part
    share, width = wq_ref.shape
    heads = width // HEAD
    blocks = length // ROWS
    wides = length // WIDE
    wires = Wires(send_sem, recv_sem, place, row)
    attn = ShardGather(wires, KIND_A, sa_s, a_s, True)
    inner = ShardGather(wires, KIND_I, si_ref, i_s)
    outer = BlockGather(wires, KIND_O, so_s, o_s)
    b_mixer, gain_one, bias_one, b_outer = (vec_ref[i : i + 1, :] for i in range(4))
    key_ref, value_ref = (acts_ref.at[0, :, i * PAD : (i + 1) * PAD] for i in range(2))

    def exchange(base, source, target, bits, mine):
        other = partner(place, bits, 4)
        return wires.copy(
            base + bits - 1, source.at[other], target.at[place if mine else other], bits, 0
        )

    def bias_copy(bits, mine):
        return wires.copy(BIASES + bits - 1, vec_ref, bias_s.at[bits], bits, 0)

    local = [
        pltpu.make_async_copy(tok_ref.at[place], x_s.at[place], here_sem.at[0]),
        pltpu.make_async_copy(sa_s, a_s.at[0, row], here_sem.at[1]),
        pltpu.make_async_copy(si_ref, i_s.at[0, row], here_sem.at[2]),
        pltpu.make_async_copy(so_s, o_s.at[0, row], here_sem.at[3]),
        pltpu.make_async_copy(vec_ref, bias_s.at[0], here_sem.at[4]),
    ]
    own_cot = pltpu.make_async_copy(cot_ref.at[place], cot_out.at[place], here_sem.at[5])
    keep_x = pltpu.make_async_copy(xt_s, xt_out, here_sem.at[6])
    keep_a = pltpu.make_async_copy(a_s, wia_out.at[1], here_sem.at[7])
    keep_i = pltpu.make_async_copy(i_s, wia_out.at[0], here_sem.at[8])
    keep_o = pltpu.make_async_copy(o_s, wo_out, here_sem.at[9])
    keep_first = pltpu.make_async_copy(first_s, first_out, here_sem.at[10])
    keep_low = pltpu.make_async_copy(low_s, low_out, here_sem.at[11])
    keep_second = pltpu.make_async_copy(second_s, second_out, here_sem.at[12])

    @pl.when(step == 0)
    def _():
        sa_s[...] = jnp.concatenate(
            [wq_ref[...], wk_ref[...], wv_ref[...], wm_ref[...].T], axis=1
        )
        greet(wires, PEERS)
        attn.start(0)
        attn.along_y(0, 0).start()
        for bits in (2, 3, 1):
            bias_copy(bits, True).start()
            exchange(TOKENS, tok_ref, x_s, bits, True).start()
        so_s[...] = wo_ref[...].T
        for copy in local:
            copy.start()
        own_cot.start()
        labels = doc_ref[place]
        docs = lax.broadcasted_iota(jnp.int32, (DOCS, length), 0)
        same = docs == labels
        ones = jnp.ones((3, length), F32)
        rest = jnp.zeros((SEG - DOCS - 3, length), F32)
        qdoc_s[...] = jnp.concatenate(
            [jnp.where(same, 1.0, 0.0), jnp.zeros((SEG - DOCS, length), F32)], axis=0
        ).astype(BF16)
        one_head = jnp.concatenate([jnp.where(same, 0.0, -(2.0**100)), ones, rest], axis=0)
        tall = jnp.zeros((width - PAD // 2, length), F32)
        last = jnp.zeros((PAD - width - heads * SEG, length), F32)
        kaug_s[...] = jnp.concatenate([tall] + [one_head] * heads + [last], axis=0).astype(BF16).T
        for head in range(heads):
            vt_s[head, HEAD:, :] = jnp.ones((SEG, length), BF16)
        for copy in local:
            copy.wait()
        attn.advance_near(0)
        outer.start(0)
        attn.advance_far(0)
        outer.along_y(0, 0).start()
        inner.along_y(0, 0).start()
        attn.cross_x().start()
        attn.wait_y(0)
        attn.to_core(0).start()
        for number in range(4):
            attn.along_y(2, number).start()
        inner.cross_x().start()
        for bits in (1, 2, 3):
            exchange(TOKENS, tok_ref, x_s, bits, False).wait_recv()
            bias_copy(bits, False).wait_recv()

        @pl.loop(0, quarters)
        def _(index):
            rows = rows_of(index, part)
            first_s[rows, :] = x_s[index].astype(F32) + b_mixer

    @pl.when(step == 1)
    def _():
        @pl.loop(0, quarters)
        def _(index):
            xt_s[:, rows_of(index, part)] = x_s[index].T

        keep_x.start()

    @pl.when(step == 1)
    def _():
        attn.to_core(0).wait_recv()

    @pl.when(step == 2)
    def _():
        attn.wait_y(2)
        attn.to_core(2).start()

    @pl.when(step == 3)
    def _():
        attn.to_core(2).wait_recv()
        keep_a.start()

    @pl.when(step < 4)
    def _():
        for dp_row in range(a_s.shape[1]):
            packed = a_s[step, dp_row]
            rest = jnp.zeros((share, PAD - width), packed.dtype)
            rows = slice(dp_row * share, (dp_row + 1) * share)
            for slot in range(4):
                piece = packed[:, slot * width : (slot + 1) * width]
                piece = jnp.concatenate([piece, rest], axis=1)
                if slot < 3:
                    w_s[rows, slot * PAD : (slot + 1) * PAD] = piece
                else:
                    wm_s[rows, :] = piece
        bias = bias_s[step][7:8]
        lanes = lax.broadcasted_iota(jnp.int32, (1, PAD), 1) - width
        spare = (lanes >= 0) & (lanes < heads * SEG) & (lax.rem(lanes + SEG, SEG) >= DOCS)
        vaug = jnp.where(spare & (lax.rem(lanes + SEG, SEG) < DOCS + 3), 1.0, 0.0).astype(BF16)

        @pl.loop(0, wides)
        def _(index):
            rows = rows_of(index, WIDE)
            x_rows = x_s[pl.ds(index * (WIDE // part), WIDE // part)].reshape(WIDE, model)
            result = dot_nn(x_rows, w_s[...])
            queries = (result[:, :PAD] + bias[:, :PAD]).astype(BF16)
            queries = (queries * jnp.asarray(HEAD**-0.5, BF16)).T
            side_ref[0, :width, rows] = queries[:width]
            side_ref[0, PAD + width :, rows] = jnp.zeros((PAD - width, WIDE), BF16)
            keys = result[:, PAD : 2 * PAD].astype(BF16)
            key_ref[rows, : PAD // 2] = keys[:, : PAD // 2]
            key_ref[rows, PAD // 2 :] = keys[:, PAD // 2 :] + kaug_s[rows, :]
            values = (result[:, 2 * PAD :] + bias[:, PAD : 2 * PAD]).astype(BF16)
            value_ref[rows, :] = values + vaug
            values_t = values.T
            for head in range(heads):
                vt_s[head, :HEAD, rows] = values_t[head_rows(head)]

        for head in range(heads):
            side_ref[0, extra_rows(head, width), :] = qdoc_s[...]
        side_ref[0, width + heads * SEG : PAD, :] = jnp.zeros(
            (PAD - width - heads * SEG, length), BF16
        )

        @pl.when(step == 1)
        def _():
            attn.advance_near(2)
            inner.cross_x().wait_recv()
            inner.start(0)

        @pl.loop(0, blocks)
        def _(index):
            cols = rows_of(index)
            attended = attend_block(cols, width, key_ref, vt_s, side_ref.at[0])
            side_ref[0, PAD : PAD + width, cols] = attended
            rest = jnp.zeros((PAD - width, ROWS), BF16)
            mix_s[cols, :] = jnp.concatenate([attended, rest], axis=0).T

            @pl.when((step == 0) & (index == 0))
            def _():
                attn.cross_x().wait_recv()
                attn.start(2)

            @pl.when((step == 0) & (index == 1))
            def _():
                outer.advance(0)

            @pl.when((step == 1) & (index == 1))
            def _():
                attn.advance_far(2)

            @pl.when((step == 1) & (index == 3))
            def _():
                outer.wait_y(0)
                outer.to_core(0).start()
                inner.start(2)
                inner.along_y(2, 0).start()

            @pl.when((step == 2) & (index == 1))
            def _():
                inner.advance(0)

            @pl.when((step == 3) & (index == 0))
            def _():
                inner.advance(2)
                for bits in (2, 3, 1):
                    exchange(COTS, cot_ref, cot_out, bits, True).start()

        @pl.loop(0, wides)
        def _(index):
            rows = rows_of(index, WIDE)
            first_s[rows, :] += dot_nt(mix_s[rows, :], wm_s[...])

    @pl.when(step == 4)
    def _():
        keep_first.start()

        @pl.loop(0, blocks)
        def _(index):
            rows = rows_of(index)
            unit, _inverse = norm_parts(first_s[rows, :])
            normed = unit * gain_one + bias_one
            low_s[rows, :] = normed.astype(BF16)
            second_s[rows, :] = normed + b_outer

        keep_low.start()
        inner.wait_y(0)
        inner.to_core(0).start()

    @pl.when(step == 5)
    def _():
        inner.to_core(0).wait_recv()
        outer.to_core(0).wait_recv()

    @pl.when(step == 6)
    def _():
        inner.wait_y(2)
        inner.to_core(2).start()
        outer.wait_x()
        outer.to_core(2).start()

    @pl.when(step == 7)
    def _():
        inner.to_core(2).wait_recv()
        outer.to_core(2).wait_recv()
        keep_i.start()
        keep_o.start()

    @pl.when(step >= 4)
    def _():
        slot = step - 4
        w_inner = i_s[slot].reshape(model, model)
        w_outer = o_s[slot].reshape(model, model)
        b_inner = bias_s[slot][6:7]

        @pl.loop(0, wides)
        def _(index):
            rows = rows_of(index, WIDE)
            value, slope = gelu_parts(dot_nn(low_s[rows, :], w_inner) + b_inner)
            hidden = value.astype(BF16)
            acts_ref[0, rows, :] = hidden
            slope_ref[0, rows, :] = slope.astype(BF16)
            second_s[rows, :] += dot_nt(hidden, w_outer)

    @pl.when(step == 7)
    def _():
        keep_second.start()
        for bits in (1, 2, 3):
            exchange(COTS, cot_ref, cot_out, bits, False).wait_recv()
        for gather in (attn, inner):
            gather.cross_x().wait_send()
            gather.wait_sent((0, 2))
        outer.wait_sent((0,))
        for bits in (1, 2, 3):
            exchange(TOKENS, tok_ref, x_s, bits, True).wait_send()
            exchange(COTS, cot_ref, cot_out, bits, True).wait_send()
            bias_copy(bits, True).wait_send()
        for copy in (
            own_cot, keep_x, keep_a, keep_i, keep_o, keep_first, keep_low, keep_second,
        ):
            copy.wait()


def dense_kernel(
    first_in, wi_ref, wo_ref, bi_ref, vec_ref, cot_ref,
    out_ref, dfirst_ref, dmix_ref, gi_ref, go_ref, dbi_ref, small_ref,
    first_ref, second_ref, normed_s, dsec_s, hidden_s, slope_s, low_s, low_t, back_t, dinner_s,
):
    step = pl.program_id(0)
    count = pl.num_programs(0) // 2
    length, model = first_in.shape
    blocks = length // ROWS
    gain_one, bias_one, b_outer, gain_two, bias_two = (vec_ref[i : i + 1, :] for i in range(5))

    @pl.when(step == 0)
    def _():
        copied = pltpu.sync_copy
        copied(first_in, first_ref)

        @pl.loop(0, blocks)
        def _(index):
            rows = rows_of(index)
            unit, _inverse = norm_parts(first_ref[rows, :])
            normed = unit * gain_one + bias_one
            normed_s[rows, :] = normed
            low_s[rows, :] = normed.astype(BF16)
            low_t[:, rows] = normed.astype(BF16).T
            second_ref[rows, :] = normed + b_outer

    @pl.when(step < count)
    def _():
        @pl.loop(0, blocks)
        def _(index):
            rows = rows_of(index)
            inner = dot_nn(low_s[rows, :], wi_ref[0]) + bi_ref[0]
            value, slope = gelu_parts(inner)
            hidden = value.astype(BF16)
            hidden_s[step, rows, :] = hidden
            slope_s[step, rows, :] = slope.astype(BF16)
            second_ref[rows, :] += dot_nt(hidden, wo_ref[0])

    @pl.when(step == count - 1)
    def _():
        small_ref[...] = jnp.zeros_like(small_ref)

        @pl.loop(0, blocks)
        def _(index):
            rows = rows_of(index)
            unit, inverse = norm_parts(second_ref[rows, :])
            out_ref[rows, :] = (unit * gain_two + bias_two).astype(BF16)
            grads = cot_ref[rows, :].astype(F32)
            d_second = norm_back(grads, gain_two, unit, inverse)
            small_ref[0:1, :] += column_sum(d_second)
            small_ref[1:2, :] += column_sum(grads * unit)
            small_ref[2:3, :] += column_sum(grads)
            dsec_s[rows, :] = d_second
            low = d_second.astype(BF16)
            dmix_ref[rows, :] = low
            back_t[:, rows] = low.T

    @pl.when(step >= count)
    def _():
        place = step - count
        dbi_ref[...] = jnp.zeros_like(dbi_ref)

        @pl.loop(0, blocks)
        def _(index):
            rows = rows_of(index)
            d_hidden = dot_nn(dmix_ref[rows, :], wo_ref[0])
            d_inner = (d_hidden * slope_s[place, rows, :].astype(F32)).astype(BF16)
            dinner_s[rows, :] = d_inner
            dbi_ref[0] += column_sum(d_inner.astype(F32))
            dsec_s[rows, :] += dot_nt(d_inner, wi_ref[0])

        @pl.loop(0, model // ROWS)
        def _(index):
            rows = rows_of(index)
            gi_ref[0, rows, :] = dot_nn(low_t[rows, :], dinner_s[...]).astype(gi_ref.dtype)
            go_ref[0, rows, :] = dot_nn(back_t[rows, :], hidden_s[place]).astype(go_ref.dtype)

    @pl.when(step == 2 * count - 1)
    def _():
        @pl.loop(0, blocks)
        def _(index):
            rows = rows_of(index)
            unit, inverse = norm_parts(first_ref[rows, :])
            grads = dsec_s[rows, :]
            d_first = norm_back(grads, gain_one, unit, inverse)
            small_ref[3:4, :] += column_sum(d_first)
            small_ref[4:5, :] += column_sum(grads * unit)
            small_ref[5:6, :] += column_sum(grads)
            dfirst_ref[rows, :] = d_first
            dmix_ref[rows, :] = d_first.astype(BF16)


def back_rows(rows, width, w_s, dmix_rows, q_ref, k_ref, v_ref, att_ref, kt_s, dq_s, dk_s, dv_s):
    lanes = lane_index((ROWS, PAD))
    queries = q_ref[rows, :]
    d_att = dot_nn(dmix_rows, w_s[3]).astype(BF16)
    product = d_att.astype(F32) * att_ref[rows, :].astype(F32)
    heads = range(width // HEAD)
    extended = d_att
    for head in heads:
        centre = jnp.sum(jnp.where(head_only(lanes, head), product, 0.0), axis=1, keepdims=True)
        for spot, part in enumerate(three_parts(-centre)):
            here = lanes == width + DOCS + 3 * head + spot
            extended = jnp.where(here, jnp.broadcast_to(part, (ROWS, PAD)), extended)
    chances_all = []
    d_scores_all = []
    d_att_all = []
    queries_all = []
    for head in heads:
        wide = head_and_extra(lanes, head, width)
        only = head_only(lanes, head)
        chances = jnp.exp2(dot_nt(k_ref[...], jnp.where(wide, queries, 0)) * LOG2E)
        d_chances = dot_nt(v_ref[...], jnp.where(wide, extended, 0))
        d_scores = (chances * d_chances).astype(BF16)
        chances_all.append(chances.astype(BF16))
        d_scores_all.append(d_scores)
        d_att_all.append(jnp.where(only, d_att, 0))
        queries_all.append(jnp.where(only, queries, 0))
        head_rows = slice(head * HEAD, (head + 1) * HEAD)
        dq_s[head_rows, rows] = dot_nn(kt_s[head_rows, :], d_scores)
    dv_s[...] += dot_nn(jnp.concatenate(chances_all, 1), jnp.concatenate(d_att_all, 0))
    dk_s[...] += dot_nn(jnp.concatenate(d_scores_all, 1), jnp.concatenate(queries_all, 0))


def back_low(rows, width, dq_s, dk_s, dv_s, low_s):
    d_query = (dq_s[:, rows].T * HEAD**-0.5).astype(BF16)
    d_query = jnp.where(lane_index(d_query.shape) < width, d_query, 0)
    d_value = dv_s[rows, :].astype(BF16)
    low_s[rows, :PAD] = d_query
    low_s[rows, PAD : 2 * PAD] = dk_s[rows, :].astype(BF16)
    low_s[rows, 2 * PAD :] = d_value
    return column_sum(d_query.astype(F32)), column_sum(d_value.astype(F32))


def back_tokens(rows, w_s, low_s):
    return sum(dot_nt(low_s[rows, slot * PAD : (slot + 1) * PAD], w_s[slot]) for slot in range(3))


def back_weights(rows, width, slots, xt_s, dmixt_s, low_s, att_ref):
    parts = []
    for slot in slots:
        if slot < 3:
            part = dot_nn(xt_s[rows, :], low_s[:, slot * PAD : (slot + 1) * PAD])
        else:
            part = dot_nn(dmixt_s[rows, :], att_ref[...])
        parts.append(part[:, :width])
    return jnp.concatenate(parts, axis=1).astype(BF16)


def attend_back_kernel(
    x_ref, a_ref, dmix_ref, dfirst_ref, q_ref, k_ref, v_ref, att_ref,
    dtok_ref, ga_ref, dbq_ref, dbv_ref,
    w_s, xt_s, dmixt_s, kt_s, dq_s, dk_s, dv_s, low_s,
):
    length, model = x_ref.shape
    width = a_ref.shape[2] // 4
    blocks = length // ROWS
    for slot in range(4):
        w_s[slot] = unpack(a_ref.at[0], slot, width)

    @pl.when(pl.program_id(0) == 0)
    def _():
        dtok_ref[...] = dfirst_ref[...]

        @pl.loop(0, blocks)
        def _(index):
            rows = rows_of(index)
            xt_s[:, rows] = x_ref[rows, :].T
            dmixt_s[:, rows] = dmix_ref[rows, :].T

    for sums in (dk_s, dv_s, dbq_ref, dbv_ref):
        sums[...] = jnp.zeros_like(sums)

    @pl.loop(0, blocks)
    def _(index):
        rows = rows_of(index)
        kt_s[:, rows] = k_ref[0, rows, :].T

    @pl.loop(0, blocks)
    def _(index):
        rows = rows_of(index)
        dmix_rows = dmix_ref[rows, :]
        refs = (ref.at[0] for ref in (q_ref, k_ref, v_ref, att_ref))
        back_rows(rows, width, w_s, dmix_rows, *refs, kt_s, dq_s, dk_s, dv_s)

    @pl.loop(0, blocks)
    def _(index):
        rows = rows_of(index)
        for_query, for_value = back_low(rows, width, dq_s, dk_s, dv_s, low_s)
        dbq_ref[0] += for_query
        dbv_ref[0] += for_value
        dtok_ref[rows, :] += back_tokens(rows, w_s, low_s)

    @pl.loop(0, model // ROWS)
    def _(index):
        rows = rows_of(index)
        ga_ref[0, rows, :] = back_weights(
            rows, width, range(4), xt_s, dmixt_s, low_s, att_ref.at[0]
        )


def add_into(target, source):
    target[...] = (target[...].astype(F32) + source[...].astype(F32)).astype(target.dtype)


class Reduce:
    COUNT = 11

    def __init__(self, wires, base, held, core, by_y, by_z, by_x, cols=slice(None)):
        self.wires, self.base, self.held, self.core = wires, base, held, core
        self.by_y, self.by_z, self.by_x = by_y, by_z, by_x
        self.cols = cols
        self.z, self.y = lax.div(wires.row, 2), lax.rem(wires.row, 2)

    def part(self, ref, *index):
        return ref.at[index + (slice(None), self.cols)]

    def core_copy(self, j, source):
        everything = (slice(None), slice(None))
        return self.wires.copy(
            self.base + j, self.part(source, *everything), self.part(self.core, j, *everything), 1, 0
        )

    def add_core(self, j):
        self.core_copy(j, self.held.at[j]).wait_recv()
        for z in range(4):
            for y in range(2):
                add_into(self.part(self.held, j, z, y), self.part(self.core, j, z, y))

    def y_copy(self, j):
        source = self.part(self.held, j, slice(None), 1 - self.y)
        return self.wires.copy(
            self.base + 2 + j, source, self.part(self.by_y, j, slice(None)), 0, 1
        )

    def add_y(self, j):
        self.y_copy(j).wait_recv()
        for z in range(4):
            add_into(self.part(self.held, j, z, self.y), self.part(self.by_y, j, z))

    def z_copy(self, j, step):
        other = lax.div(partner(self.wires.row, 2 * step, 8), 2)
        number = self.base + 4 + 3 * j + step - 1
        return self.wires.copy(
            number, self.part(self.held, j, other, self.y), self.part(self.by_z, j, step - 1),
            0, 2 * step,
        )

    def start_z(self, j):
        for step in (1, 2, 3):
            self.z_copy(j, step).start()

    def total_z(self, j):
        total = self.part(self.held, j, self.z, self.y)[...].astype(F32)
        for step in (1, 2, 3):
            self.z_copy(j, step).wait_recv()
            total = total + self.part(self.by_z, j, step - 1)[...].astype(F32)
        return total

    def x_copy(self):
        source = self.part(self.held, 1, self.z, self.y)
        return self.wires.copy(self.base + 10, source, self.part(self.by_x), 2, 0)

    def send_x(self):
        self.part(self.held, 1, self.z, self.y)[...] = self.total_z(1).astype(BF16)
        self.x_copy().start()

    def total(self):
        self.x_copy().wait_recv()
        return self.total_z(0) + self.part(self.by_x)[...].astype(F32)

    def whole_x_copy(self):
        return self.wires.copy(self.base + 10, self.held.at[1], self.by_x, 2, 0)

    def add_whole_x(self):
        self.whole_x_copy().wait_recv()
        for z in range(4):
            for y in range(2):
                add_into(self.held.at[0, z, y], self.by_x.at[z, y])

    def wait_sent(self, j_all):
        for j in j_all:
            self.y_copy(j).wait_send()
            for step in (1, 2, 3):
                self.z_copy(j, step).wait_send()


OUTPUTS, TOKEN_GRADS, SUMS, LATE_SUMS = 0, 3, 6, 16
RED_I = 26
RED_O = RED_I + Reduce.COUNT
RED_A = RED_O + Reduce.COUNT
BACKWARD_WIRES = RED_A + 2 * Reduce.COUNT
BACK_PEERS = PEERS + ((0, 3), (0, 5), (0, 7))


def slot_at(step):
    return jnp.where(step < 2, 3 - 2 * step, 6 - 2 * step)


def backward_kernel(
    acts_ref, side_ref, slope_ref, wia_ref, wo_ref, vec_ref, second_ref, first_ref, low_ref, xt_ref,
    cot_ref,
    out_res, dtok_res, ga_res, gi_res, go_res, sum_res, late_res,
    low_t, back_t, dmix_s, low_s, flow_s, out_s, grad_s, first_s, wmt_s, do_s, kt_s, all_t, dk_t,
    dv_t, sums_s, sums_o, sums_d, late_o, late_t, late_d,
    send_i, held_i, core_i, y_i, z_i, x_i, send_o, held_o, core_o, y_o, z_o, x_o,
    held_a, core_a, y_a, z_a, x_a,
    send_sem, recv_sem, here_sem,
):
    step = pl.program_id(0)
    place = lax.axis_index("tensor")
    row = lax.axis_index("dp")
    length, model = dmix_s.shape
    quarters, part, _ = flow_s.shape
    width = wia_ref.shape[2] // 4
    heads = width // HEAD
    blocks = length // ROWS
    wides = length // WIDE
    share = held_i.shape[3]
    wires = Wires(send_sem, recv_sem, place, row)
    inner = Reduce(wires, RED_I, held_i, core_i, y_i, z_i, x_i)
    outer = Reduce(wires, RED_O, held_o, core_o, y_o, z_o, x_o)
    halves = (slice(0, model // 2), slice(model // 2, model))
    send_a = send_i
    attn = [
        Reduce(wires, RED_A + half * Reduce.COUNT, held_a, core_a, y_a, z_a, x_a, cols)
        for half, cols in enumerate(halves)
    ]
    gain_one, gain_two, bias_two = (vec_ref[i : i + 1, :] for i in (1, 4, 5))
    key_ref, value_ref = (acts_ref.at[0, :, i * PAD : (i + 1) * PAD] for i in range(2))
    att_ref = side_ref.at[0, PAD : PAD + width]

    def exchange(base, source, target, bits, mine):
        other = partner(place, bits, 4)
        return wires.copy(
            base + bits - 1, source.at[other], target.at[place if mine else other], bits, 0
        )

    def by_tensor(bits):
        return wires.copy(
            SUMS + bits - 1, sums_s.at[place], sums_s.at[place], bits, 0
        )

    def by_rows(base, kept, bits):
        return wires.copy(base + 2 + bits, kept.at[row], kept.at[row], 0, bits)

    def late_copy(bits):
        return wires.copy(LATE_SUMS + bits - 1, late_o.at[bits], late_t.at[bits], bits, 0)

    def sum_rows(base, kept):
        for bits in range(1, 8):
            by_rows(base, kept, bits).wait_recv()
        return sum((kept[number] for number in range(1, 8)), kept[0])

    load_second = pltpu.make_async_copy(second_ref, grad_s, here_sem.at[0])
    load_cot = pltpu.make_async_copy(cot_ref, flow_s, here_sem.at[1])
    load_low = pltpu.make_async_copy(low_ref, low_s, here_sem.at[2])
    load_x = pltpu.make_async_copy(xt_ref, low_t, here_sem.at[3])
    keep_out = pltpu.make_async_copy(out_s.at[place], out_res.at[place], here_sem.at[4])
    keep_dtok = pltpu.make_async_copy(flow_s.at[place], dtok_res.at[place], here_sem.at[5])

    def load_first(index):
        return pltpu.make_async_copy(
            first_ref.at[rows_of(index)], first_s.at[index % 2], here_sem.at[6 + index % 2]
        )

    order = (3, 1, 2, 0)

    @pl.when(step == 0)
    def _():
        load_second.start()
        load_cot.start()
        load_low.start()
        sums_s[place] = jnp.zeros_like(sums_s[0])
        for bits in range(4):
            late_o[bits] = jnp.zeros_like(late_o[0])
        greet(wires, BACK_PEERS)
        load_second.wait()
        load_cot.wait()
        load_low.wait()

        @pl.loop(0, quarters)
        def _(index):
            rows = rows_of(index, part)
            low_t[:, rows] = low_s[rows, :].T
            unit, inverse = norm_parts(grad_s[rows, :])
            out_s[index] = (unit * gain_two + bias_two).astype(BF16)
            grads = flow_s[index].astype(F32)
            d_second = norm_back(grads, gain_two, unit, inverse)
            sums_s[place, 8:9, :] += column_sum(d_second)
            sums_s[place, 9:10, :] += column_sum(grads * unit)
            sums_s[place, 10:11, :] += column_sum(grads)
            grad_s[rows, :] = d_second
            lower = d_second.astype(BF16)
            dmix_s[rows, :] = lower
            back_t[:, rows] = lower.T

        for bits in (2, 3, 1):
            exchange(OUTPUTS, out_s, out_res, bits, True).start()
        keep_out.start()

    @pl.when(step < 4)
    def _():
        @pl.loop(0, wides)
        def _(index):
            rows = rows_of(index, WIDE)
            d_hidden = dot_nn(dmix_s[rows, :], wo_ref[0])
            d_inner = (d_hidden * slope_ref[0, rows, :].astype(F32)).astype(BF16)
            low_s[rows, :] = d_inner
            for_inner = column_sum(d_inner.astype(F32))
            for number, bits in enumerate(order):

                @pl.when(step == number)
                def _(bits=bits):
                    sums_s[place, pl.ds(partner(place, bits, 4), 1), :] += for_inner

            grad_s[rows, :] += dot_nt(d_inner, wia_ref[0])

        @pl.loop(0, model // (4 * share))
        def _(pair):
            rows = rows_of(pair, 4 * share)
            for transposed, right, sent, held in (
                (back_t, acts_ref.at[0], send_o, held_o), (low_t, low_s, send_i, held_i),
            ):
                grads = dot_nn(transposed[rows, :], right[...]).astype(BF16)
                pieces = grads.reshape(2, 2, share, model)

                @pl.when(step < 2)
                def _(pieces=pieces, sent=sent):
                    sent[step, pl.ds(2 * pair, 2)] = pieces

                @pl.when(step >= 2)
                def _(pieces=pieces, held=held):
                    held[3 - step, pl.ds(2 * pair, 2)] = pieces

    for number, j in ((0, 1), (1, 0)):

        @pl.when(step == number)
        def _(number=number, j=j):
            outer.core_copy(j, send_o.at[number]).start()
            inner.core_copy(j, send_i.at[number]).start()

    @pl.when(step == 2)
    def _():
        load_first(0).start()
        load_first(1).start()
        outer.add_core(1)
        outer.whole_x_copy().start()
        inner.add_core(1)
        inner.y_copy(1).start()

    @pl.when(step == 3)
    def _():
        inner.add_core(0)
        inner.y_copy(0).start()
        outer.add_core(0)
        load_x.start()
        for index in range(blocks):
            rows = slice(index * ROWS, (index + 1) * ROWS)
            load_first(index).wait()
            unit, inverse = norm_parts(first_s[index % 2])
            if index + 2 < blocks:
                load_first(index + 2).start()
            grads = grad_s[rows, :]
            d_first = norm_back(grads, gain_one, unit, inverse)
            sums_s[place, 11:12, :] += column_sum(d_first)
            sums_s[place, 12:13, :] += column_sum(grads * unit)
            sums_s[place, 13:14, :] += column_sum(grads)
            grad_s[rows, :] = d_first
            lower = d_first.astype(BF16)
            dmix_s[rows, :] = lower
            back_t[:, rows] = lower.T
        load_x.wait()
        for bits in (1, 2, 3):
            by_tensor(bits).start()

    @pl.when(step == 4)
    def _():
        for number, j in ((0, 1), (1, 0)):
            inner.core_copy(j, send_i.at[number]).wait_send()

    @pl.when(step == 7)
    def _():
        for reduce in attn:
            reduce.add_core(1)
            reduce.y_copy(1).start()

    @pl.when(step >= 4)
    def _():
        wmt_s[...] = wia_ref[0, :, 3 * width :].T
        for sums in (dk_t, dv_t):
            sums[...] = jnp.zeros_like(sums)

        @pl.loop(0, wides)
        def _(index):
            cols = rows_of(index, WIDE)
            kt_s[:, cols] = key_ref[cols, :].T[:width]
            d_att = dot_nn(wmt_s[...], back_t[:, cols]).astype(BF16)
            do_s[:width, cols] = d_att
            product = d_att.astype(F32) * att_ref[:, cols].astype(F32)
            none = jnp.zeros((DOCS, WIDE), BF16)
            for head in range(heads):
                centre = column_sum(product[head_rows(head)])
                do_s[extra_rows(head, width), cols] = parts_rows(-centre, none)

        @pl.loop(0, blocks)
        def _(index):
            attend_block_back(
                rows_of(index), width, key_ref, value_ref, side_ref.at[0], do_s, kt_s, all_t,
                dk_t, dv_t,
            )

            @pl.when((step == 4) & (index == 0))
            def _():
                inner.add_y(1)
                inner.start_z(1)

            @pl.when((step == 4) & (index == 3))
            def _():
                inner.add_y(0)
                inner.start_z(0)
                outer.add_whole_x()
                outer.y_copy(0).start()

            @pl.when((step == 5) & (index == 1))
            def _():
                inner.send_x()
                for bits in (1, 2, 3):
                    by_tensor(bits).wait_recv()
                sums_o[...] = sums_s[0] + sums_s[1] + sums_s[2] + sums_s[3]
                sums_d[row, :6, :] = sums_o[8:14, :]
                sums_d[row, 6:7, :] = sums_o[pl.ds(place, 1), :]
                sums_d[row, 7:, :] = jnp.zeros((1, model), F32)
                for bits in range(1, 8):
                    by_rows(SUMS, sums_d, bits).start()

            @pl.when((step == 7) & (index == 1))
            def _():
                sum_res[...] = sum_rows(SUMS, sums_d)

            @pl.when((step == 5) & (index == 3))
            def _():
                outer.add_y(0)
                outer.start_z(0)

            @pl.when((step == 6) & (index == 1))
            def _():
                gi_res[...] = inner.total()

            @pl.when((step == 6) & (index == 3))
            def _():
                go_res[...] = outer.total_z(0)

            @pl.when((step == 7) & (index == 3))
            def _():
                for reduce in attn:
                    reduce.add_y(1)
                    reduce.start_z(1)

        all_t[width : 2 * width, :] = dk_t[...].astype(BF16)
        all_t[2 * width :, :] = dv_t[...].astype(BF16)
        for_all = dot_nt(jnp.ones((8, length), BF16), all_t[...])
        for number, bits in enumerate(order):

            @pl.when(step == 4 + number)
            def _(bits=bits):
                late_o[bits, :, : 3 * width] = for_all
                if bits:
                    late_copy(bits).start()
                    return
                for other in (1, 2, 3):
                    late_copy(other).wait_recv()
                late_d[row] = late_o[0] + late_t[1] + late_t[2] + late_t[3]
                for other in range(1, 8):
                    by_rows(LATE_SUMS, late_d, other).start()

        for half, cols in enumerate(halves):

            @pl.loop(0, model // (4 * share))
            def _(pair):
                rows = rows_of(pair, 4 * share)
                if half == 0:
                    grads = dot_nt(low_t[rows, :], all_t[: 2 * width, :])
                else:
                    for_value = dot_nt(low_t[rows, :], all_t[2 * width :, :])
                    for_mixer = dot_nt(back_t[rows, :], att_ref[...])
                    grads = jnp.concatenate([for_value, for_mixer], axis=1)
                pieces = grads.astype(BF16).reshape(2, 2, share, model // 2)

                @pl.when(step < 6)
                def _(pieces=pieces):
                    send_a[step - 4, pl.ds(2 * pair, 2), :, :, cols] = pieces

                @pl.when(step >= 6)
                def _(pieces=pieces):
                    held_a[7 - step, pl.ds(2 * pair, 2), :, :, cols] = pieces

            for number, j in ((0, 1), (1, 0)):

                @pl.when(step == 4 + number)
                def _(number=number, j=j):
                    attn[half].core_copy(j, send_a.at[number]).start()

            @pl.when(step == 7)
            def _():
                attn[half].add_core(0)
                attn[half].y_copy(0).start()

        @pl.loop(0, wides)
        def _(index):
            rows = rows_of(index, WIDE)
            transposed = all_t[:, rows].T
            grad_s[rows, :] += dot_nt(transposed, wia_ref[0, :, : 3 * width])

            @pl.when(step == 7)
            def _():
                places = pl.ds(index * (WIDE // part), WIDE // part)
                flow_s[places] = grad_s[rows, :].astype(BF16).reshape(WIDE // part, part, model)

    @pl.when(step == 7)
    def _():
        for bits in (2, 3, 1):
            exchange(TOKEN_GRADS, flow_s, dtok_res, bits, True).start()
        keep_dtok.start()
        for reduce in attn:
            reduce.send_x()
        for reduce in attn:
            reduce.add_y(0)
            reduce.start_z(0)
        late_res[...] = sum_rows(LATE_SUMS, late_d)
        for reduce, cols in zip(attn, halves):
            ga_res[:, cols] = reduce.total()
        for bits in (1, 2, 3):
            for base, source, target in (
                (OUTPUTS, out_s, out_res), (TOKEN_GRADS, flow_s, dtok_res),
            ):
                exchange(base, source, target, bits, False).wait_recv()
                exchange(base, source, target, bits, True).wait_send()
        keep_out.wait()
        keep_dtok.wait()
        for bits in (1, 2, 3):
            by_tensor(bits).wait_send()
            late_copy(bits).wait_send()
        for bits in range(1, 8):
            by_rows(SUMS, sums_d, bits).wait_send()
            by_rows(LATE_SUMS, late_d, bits).wait_send()
        for number, j in ((0, 1), (1, 0)):
            outer.core_copy(j, send_o.at[number]).wait_send()
            for reduce in attn:
                reduce.core_copy(j, send_a.at[number]).wait_send()
        inner.wait_sent((0, 1))
        inner.x_copy().wait_send()
        outer.wait_sent((0,))
        outer.whole_x_copy().wait_send()
        for reduce in attn:
            reduce.wait_sent((0, 1))
            reduce.x_copy().wait_send()


VMEM_LIMIT = 62 * 1024 * 1024


def resident(shape):
    return pl.BlockSpec(shape, lambda step: (0,) * len(shape))


def stepped(shape):
    return pl.BlockSpec((1,) + shape[1:], lambda step: (step,) + (0,) * (len(shape) - 1))


def spec_list(pairs):
    return [stepped(shape) if moves else resident(shape) for shape, moves in pairs]


def near_forward(tokens, cotangent, shard_i, w_query, w_key, w_value, w_mixer, w_outer, docs, vectors):
    groups, part, model = tokens.shape
    length = groups * part
    share, width = w_query.shape
    whole = (groups, model // share, share, model)
    sides = (groups, 2 * PAD, length)
    slopes = (groups, length, model)
    flat = (length, model)
    shard = (share, model)
    biases = (groups,) + vectors.shape
    anywhere = pl.BlockSpec(memory_space=pl.ANY)

    def early(shape):
        return pl.BlockSpec(
            (1,) + shape[1:], lambda step: (jnp.minimum(step, 3),) + (0,) * (len(shape) - 1)
        )

    def late(shape):
        return pl.BlockSpec(
            (1,) + shape[1:], lambda step: (jnp.maximum(step - 4, 0),) + (0,) * (len(shape) - 1)
        )

    def vmem(*shape, kind=BF16):
        return pltpu.VMEM(shape, kind)

    kept = [w_query, w_key, w_value, w_mixer, w_outer, docs, vectors]
    return pl.pallas_call(
        forward_kernel,
        grid=(2 * groups,),
        out_shape=[
            jax.ShapeDtypeStruct((2 * groups, length, model), BF16),
            jax.ShapeDtypeStruct(sides, BF16),
            jax.ShapeDtypeStruct(slopes, BF16),
            jax.ShapeDtypeStruct(flat, F32),
            jax.ShapeDtypeStruct(flat, F32),
            jax.ShapeDtypeStruct(flat, BF16),
            jax.ShapeDtypeStruct((model, length), BF16),
            jax.ShapeDtypeStruct(tokens.shape, BF16),
            jax.ShapeDtypeStruct((2,) + whole, BF16),
            jax.ShapeDtypeStruct(whole, BF16),
        ],
        in_specs=[anywhere] * 3 + [resident(each.shape) for each in kept],
        out_specs=[stepped((2 * groups, length, model)), early(sides), late(slopes)]
        + [anywhere] * 7,
        scratch_shapes=[
            vmem(*shard), vmem(*shard), vmem(model, 3 * PAD), vmem(model, PAD),
            vmem(*tokens.shape), vmem(model, length), vmem(*whole), vmem(*whole), vmem(*whole),
            vmem(*biases, kind=F32), vmem(length, PAD // 2), vmem(SEG, length),
            vmem(width // HEAD, HEAD + SEG, length), vmem(length, PAD),
            vmem(*flat, kind=F32), vmem(*flat, kind=F32), vmem(*flat),
            pltpu.SemaphoreType.DMA((FORWARD_WIRES,)),
            pltpu.SemaphoreType.DMA((FORWARD_WIRES,)),
            pltpu.SemaphoreType.DMA((13,)),
        ],
        compiler_params=pltpu.CompilerParams(
            vmem_limit_bytes=VMEM_LIMIT, collective_id=0, has_side_effects=True
        ),
        name="near_forward",
    )(tokens, cotangent, shard_i, *kept)


def attend_plain(x, a_all, biases, qaug, kaug, vaug, b_mixer):
    length, model = x.shape
    groups = a_all.shape[0]
    block = (groups, length, PAD)
    return pl.pallas_call(
        attend_plain_kernel,
        grid=(groups,),
        out_shape=[jax.ShapeDtypeStruct(block, BF16)] * 4 + [jax.ShapeDtypeStruct(x.shape, F32)],
        in_specs=spec_list(
            [
                (x.shape, 0), (a_all.shape, 1), (biases.shape, 1),
                (qaug.shape, 0), (kaug.shape, 0), (vaug.shape, 0), (b_mixer.shape, 0),
            ]
        ),
        out_specs=spec_list([(block, 1)] * 4 + [(x.shape, 0)]),
        scratch_shapes=[pltpu.VMEM((4, model, PAD), BF16)],
        compiler_params=pltpu.CompilerParams(vmem_limit_bytes=VMEM_LIMIT),
        name="attend_plain",
    )(x, a_all, biases, qaug, kaug, vaug, b_mixer)


def dense_both(first_sum, wi, wo, bi, vectors, cotangent):
    length, model = first_sum.shape
    groups, _, hidden = wi.shape
    grad = (groups, model, hidden)
    forth = lambda shape: pl.BlockSpec(
        (1,) + shape[1:], lambda step: (lax.rem(step, groups),) + (0,) * (len(shape) - 1)
    )
    late = lambda shape: pl.BlockSpec(
        (1,) + shape[1:], lambda step: (jnp.maximum(step - groups, 0),) + (0,) * (len(shape) - 1)
    )
    return pl.pallas_call(
        dense_kernel,
        grid=(2 * groups,),
        out_shape=[
            jax.ShapeDtypeStruct((length, model), BF16),
            jax.ShapeDtypeStruct((length, model), F32),
            jax.ShapeDtypeStruct((length, model), BF16),
            jax.ShapeDtypeStruct(grad, BF16),
            jax.ShapeDtypeStruct(grad, BF16),
            jax.ShapeDtypeStruct((groups, 1, hidden), F32),
            jax.ShapeDtypeStruct((8, model), F32),
        ],
        in_specs=[
            pl.BlockSpec(memory_space=pl.ANY), forth(wi.shape), forth(wo.shape), forth(bi.shape),
            resident(vectors.shape), resident(cotangent.shape),
        ],
        out_specs=[
            resident((length, model)), resident((length, model)), resident((length, model)),
            late(grad), late(grad), late((groups, 1, hidden)), resident((8, model)),
        ],
        scratch_shapes=[
            pltpu.VMEM((length, model), F32),
            pltpu.VMEM((length, model), F32),
            pltpu.VMEM((length, model), F32),
            pltpu.VMEM((length, model), F32),
            pltpu.VMEM((groups, length, hidden), BF16),
            pltpu.VMEM((groups, length, hidden), BF16),
            pltpu.VMEM((length, model), BF16),
            pltpu.VMEM((model, length), BF16),
            pltpu.VMEM((model, length), BF16),
            pltpu.VMEM((length, hidden), BF16),
        ],
        compiler_params=pltpu.CompilerParams(vmem_limit_bytes=VMEM_LIMIT),
        name="dense_both",
    )(first_sum, wi, wo, bi, vectors, cotangent)


def attend_backward(x, a_all, d_mixed, d_first, q, k, v, attended):
    length, model = x.shape
    groups = a_all.shape[0]
    sums = (groups, 1, PAD)
    return pl.pallas_call(
        attend_back_kernel,
        grid=(groups,),
        out_shape=[
            jax.ShapeDtypeStruct(x.shape, F32),
            jax.ShapeDtypeStruct(a_all.shape, BF16),
            jax.ShapeDtypeStruct(sums, F32),
            jax.ShapeDtypeStruct(sums, F32),
        ],
        in_specs=spec_list(
            [
                (x.shape, 0), (a_all.shape, 1), (d_mixed.shape, 0), (d_first.shape, 0),
                (q.shape, 1), (k.shape, 1), (v.shape, 1), (attended.shape, 1),
            ]
        ),
        out_specs=spec_list([(x.shape, 0), (a_all.shape, 1), (sums, 1), (sums, 1)]),
        scratch_shapes=[
            pltpu.VMEM((4, model, PAD), BF16),
            pltpu.VMEM((model, length), BF16),
            pltpu.VMEM((model, length), BF16),
            pltpu.VMEM((PAD, length), BF16),
            pltpu.VMEM((PAD, length), F32),
            pltpu.VMEM((length, PAD), F32),
            pltpu.VMEM((length, PAD), F32),
            pltpu.VMEM((length, 3 * PAD), BF16),
        ],
        compiler_params=pltpu.CompilerParams(vmem_limit_bytes=VMEM_LIMIT),
        name="attend_backward",
    )(x, a_all, d_mixed, d_first, q, k, v, attended)


def near_backward(acts, sides, slopes, w_ia, w_o, vectors, second, first, low, xt, cotangent):
    quarters, part, model = cotangent.shape
    length = quarters * part
    share = model // 8
    width = model // 4
    block = (4, 2, share, model)
    anywhere = pl.BlockSpec(memory_space=pl.ANY)

    def ordered(shape, place):
        return pl.BlockSpec(
            (1,) + shape[1:], lambda step: (place(step),) + (0,) * (len(shape) - 1)
        )

    def acts_at(step):
        return jnp.where(step < 4, 4 + slot_at(step), slot_at(step - 4))

    def weights_at(step):
        return jnp.where(step < 4, slot_at(step), 4 + slot_at(step - 4))

    def first_half(step):
        return slot_at(jnp.minimum(step, 3))

    def last_half(step):
        return slot_at(jnp.maximum(step - 4, 0))

    def vmem(*shape, kind=BF16):
        return pltpu.VMEM(shape, kind)

    final = [
        ((share, model), F32), ((share, model), F32), ((share, model), F32), ((8, model), F32),
        ((8, model), F32),
    ]
    return pl.pallas_call(
        backward_kernel,
        grid=(8,),
        out_shape=[jax.ShapeDtypeStruct(cotangent.shape, BF16)] * 2
        + [jax.ShapeDtypeStruct(*each) for each in final],
        in_specs=[
            ordered(acts.shape, acts_at), ordered(sides.shape, last_half),
            ordered(slopes.shape, first_half), ordered(w_ia.shape, weights_at),
            ordered(w_o.shape, first_half), resident(vectors.shape),
        ]
        + [anywhere] * 5,
        out_specs=[anywhere] * 2 + [resident(each[0]) for each in final],
        scratch_shapes=[
            vmem(model, length), vmem(model, length), vmem(length, model), vmem(length, model),
            vmem(*cotangent.shape), vmem(*cotangent.shape), vmem(length, model, kind=F32),
            vmem(2, ROWS, model, kind=F32),
            vmem(width, model), vmem(PAD, length), vmem(width, length), vmem(3 * width, length),
            vmem(width, length, kind=F32), vmem(width, length, kind=F32),
            vmem(4, 16, model, kind=F32), vmem(16, model, kind=F32), vmem(8, 8, model, kind=F32),
            vmem(4, 8, model, kind=F32), vmem(4, 8, model, kind=F32), vmem(8, 8, model, kind=F32),
            vmem(2, *block), vmem(2, *block), vmem(2, *block), vmem(2, 4, share, model),
            vmem(2, 3, share, model), vmem(share, model),
            vmem(2, *block), vmem(2, *block), vmem(2, *block), vmem(1, 4, share, model),
            vmem(1, 3, share, model), vmem(*block),
            vmem(2, *block), vmem(2, *block), vmem(2, 4, share, model),
            vmem(2, 3, share, model), vmem(share, model),
            pltpu.SemaphoreType.DMA((BACKWARD_WIRES,)),
            pltpu.SemaphoreType.DMA((BACKWARD_WIRES,)),
            pltpu.SemaphoreType.DMA((8,)),
        ],
        compiler_params=pltpu.CompilerParams(
            vmem_limit_bytes=VMEM_LIMIT, collective_id=1, has_side_effects=True
        ),
        name="near_backward",
    )(acts, sides, slopes, w_ia, w_o, vectors, second, first, low, xt, cotangent)


def augment(labels, width):
    length = labels.shape[0]
    lanes = lax.broadcasted_iota(jnp.int32, (length, PAD), 1)
    in_docs = (lanes >= width) & (lanes < width + DOCS)
    same = (lanes - width) == labels[:, None]
    qaug = jnp.where(in_docs & same, 1.0, 0.0).astype(BF16)
    spare = (lanes >= width + DOCS) & (lanes < width + DOCS + 3 * (width // HEAD))
    kaug = jnp.where(in_docs & ~same, -(2.0**100), jnp.where(spare, 1.0, 0.0)).astype(BF16)
    vaug = jnp.where((lanes[:1] == width) | spare[:1], 1.0, 0.0).astype(BF16)
    return qaug, kaug, vaug


def body(
    tokens, doc_ids, w_query, b_query, w_key, w_value, b_value, w_mixer, b_mixer, gain_one,
    bias_one, w_inner, b_inner, w_outer, b_outer, gain_two, bias_two, cotangent,
):
    groups = lax.axis_size("tensor")
    rings = lax.axis_size("dp")
    place = lax.axis_index("tensor")
    width = w_query.shape[1]
    hidden = w_inner.shape[1]
    length = doc_ids.shape[2]
    model = tokens.shape[3]
    near = groups == 4 and rings == 8 and hidden == model and 4 * width == model

    if near:
        spare = jnp.zeros((PAD - width,), F32)
        vectors = jnp.concatenate(
            [
                b_mixer, gain_one, bias_one, b_outer, gain_two, bias_two, b_inner,
                b_query, spare, b_value, spare, jnp.zeros((PAD,), F32),
            ]
        ).reshape(8, model)
        acts, sides, slopes, first, second, low, xt, cot, w_ia, w_o = near_forward(
            tokens[:, 0], cotangent[:, 0], w_inner, w_query, w_key, w_value, w_mixer, w_outer,
            doc_ids, vectors,
        )
        out, d_tokens, ga, gi, go, tail, late = near_backward(
            acts, sides, slopes, w_ia.reshape(2 * groups, model, model),
            w_o.reshape(groups, model, model), vectors, second, first, low, xt, cot,
        )
        dbq, dbv = late[0, :width], late[0, 2 * width : 3 * width]
        dbi = tail[6]
        out, d_tokens = out[:, None], d_tokens[:, None].astype(F32)
    else:

        def gather(shard):
            whole = lax.all_gather(shard, ("tensor", "dp"), axis=0, tiled=True)
            return whole.reshape(groups, model, shard.shape[1])

        def to_sequence(part):
            return lax.all_to_all(part, "tensor", 0, 2, tiled=True).reshape(length, model)

        def from_sequence(whole):
            return lax.all_to_all(whole.reshape(1, 1, length, model), "tensor", 2, 0, tiled=True)

        def scatter(part):
            flat = part.reshape(-1, part.shape[2])
            total = lax.psum_scatter(flat, ("tensor", "dp"), scatter_dimension=0, tiled=True)
            return total.astype(F32)

        labels = lax.dynamic_index_in_dim(doc_ids[:, 0], place, 0, keepdims=False)
        qaug, kaug, vaug = augment(labels, width)
        shard_a = jnp.concatenate([w_query, w_key, w_value, w_mixer.T], axis=1)
        shard_o = w_outer.T
        spare = jnp.zeros((PAD - width,), F32)
        biases = jnp.concatenate([b_query, spare, b_value, spare, b_inner])[None]
        vectors = jnp.stack([gain_one, bias_one, b_outer, gain_two, bias_two] + [b_outer] * 3)
        x, cot = to_sequence(tokens), to_sequence(cotangent)
        a_all, wi, wo = gather(shard_a), gather(w_inner), gather(shard_o)
        every = lax.all_gather(biases, "tensor", axis=0)
        *saved, first_sum = attend_plain(x, a_all, every, qaug, kaug, vaug, b_mixer[None])
        out, d_first, d_mixed, g_inner, g_outer, dbi, small = dense_both(
            first_sum, wi, wo, every[:, :, 2 * PAD :], vectors, cot
        )
        d_tokens, g_attend, dbq, dbv = attend_backward(x, a_all, d_mixed, d_first, *saved)
        ga, gi, go = scatter(g_attend), scatter(g_inner), scatter(g_outer)
        rows = [dbq[:, 0, :width], dbv[:, 0, :width], dbi[:, 0], small]
        summed = lax.psum(jnp.concatenate([part.reshape(-1) for part in rows]), ("dp", "tensor"))
        own = lambda start, size: lax.dynamic_slice_in_dim(summed, start + place * size, size)
        dbq, dbv, dbi = own(0, width), own(model, width), own(2 * model, hidden)
        tail = summed[-small.size :].reshape(small.shape)
        out, d_tokens = from_sequence(out), from_sequence(d_tokens)
    return (
        out,
        d_tokens,
        ga[:, :width],
        dbq,
        ga[:, width : 2 * width],
        ga[:, 2 * width : 3 * width],
        dbv,
        ga[:, 3 * width :].T,
        tail[3],
        tail[4],
        tail[5],
        gi,
        dbi,
        go.T,
        tail[0],
        tail[1],
        tail[2],
    )


def solution(mesh):
    split = P(None, "dp", "tensor", None)
    both, flipped, part = P("dp", "tensor"), P("tensor", "dp"), P("tensor")
    return jax.shard_map(
        body,
        mesh=mesh,
        in_specs=(
            split, P(None, "dp", None), both, part, both, both, part, flipped, P(), P(), P(),
            both, part, flipped, P(), P(), P(), split,
        ),
        out_specs=(
            split, split, both, part, both, both, part, flipped, P(), P(), P(), both, part,
            flipped, P(), P(), P(),
        ),
        check_vma=False,
    )
```

```python
from functools import partial

import jax
import jax.numpy as jnp
from jax import lax
from jax.experimental import pallas as pl
from jax.experimental.pallas import tpu as pltpu
from jax.sharding import PartitionSpec as P

HEAD = 64
DOCS = 8
PAD = 256
ROWS = 256
LOG2E = 1.4426950408889634
EPS = 1e-12
F32 = jnp.float32
BF16 = jnp.bfloat16


def dot_nn(left, right):
    return lax.dot_general(left, right, (((1,), (0,)), ((), ())), preferred_element_type=F32)


def dot_nt(left, right):
    return lax.dot_general(left, right, (((1,), (1,)), ((), ())), preferred_element_type=F32)


def rows_of(index, size=ROWS):
    return pl.ds(pl.multiple_of(index * size, size), size)


def lane_index(shape):
    return lax.broadcasted_iota(jnp.int32, shape, 1)


def three_parts(values):
    high = values.astype(BF16)
    rest = values - high.astype(F32)
    middle = rest.astype(BF16)
    low = (rest - middle.astype(F32)).astype(BF16)
    return high, middle, low


def head_only(lanes, head):
    return (lanes >= head * HEAD) & (lanes < (head + 1) * HEAD)


def head_and_extra(lanes, head, width):
    extra = width + DOCS + 3 * head
    return (
        head_only(lanes, head)
        | ((lanes >= width) & (lanes < width + DOCS))
        | ((lanes >= extra) & (lanes < extra + 3))
    )


def unpack(block_ref, slot, width):
    part = block_ref[:, slot * width : (slot + 1) * width]
    return jnp.concatenate([part, jnp.zeros((part.shape[0], PAD - width), part.dtype)], axis=1)


def project(x_rows, rows, bq, bv, w_s, qaug_ref, kaug_ref, vaug_ref, q_ref, k_ref, v_ref):
    queries = (dot_nn(x_rows, w_s[0]) + bq).astype(BF16)
    q_ref[rows, :] = queries * jnp.asarray(HEAD**-0.5, BF16) + qaug_ref[rows, :]
    keys = dot_nn(x_rows, w_s[1]).astype(BF16)
    k_ref[rows, :] = keys + kaug_ref[rows, :]
    values = (dot_nn(x_rows, w_s[2]) + bv).astype(BF16)
    v_ref[rows, :] = values + vaug_ref[...]


def attend_rows(rows, width, w_s, q_ref, k_ref, v_ref, att_ref, first_ref):
    lanes = lane_index((ROWS, PAD))
    queries = q_ref[rows, :]
    attended = jnp.zeros((ROWS, PAD), F32)
    extended = queries
    for head in range(width // HEAD):
        masked = jnp.where(head_and_extra(lanes, head, width), queries, 0)
        scores = dot_nt(masked, k_ref[...])
        highest = jnp.max(scores, axis=1, keepdims=True)
        raw = jnp.exp2((scores - highest) * LOG2E).astype(BF16)
        mixed = dot_nn(raw, v_ref[...])
        total = mixed[:, width : width + 1]
        attended = jnp.where(head_only(lanes, head), mixed / total, attended)
        for spot, part in enumerate(three_parts(-(highest + jnp.log(total)))):
            here = lanes == width + DOCS + 3 * head + spot
            extended = jnp.where(here, jnp.broadcast_to(part, (ROWS, PAD)), extended)
    q_ref[rows, :] = extended
    attended = attended.astype(BF16)
    att_ref[rows, :] = attended
    first_ref[rows, :] += dot_nt(attended, w_s[3])


def attend_plain_kernel(
    x_ref, a_ref, bias_ref, qaug_ref, kaug_ref, vaug_ref, bm_ref,
    q_ref, k_ref, v_ref, att_ref, first_ref, w_s,
):
    length, model = x_ref.shape
    width = a_ref.shape[2] // 4
    for slot in range(4):
        w_s[slot] = unpack(a_ref.at[0], slot, width)
    biases = bias_ref[0]

    @pl.when(pl.program_id(0) == 0)
    def _():
        first_ref[...] = x_ref[...].astype(F32) + bm_ref[...]

    @pl.loop(0, length // ROWS)
    def _(index):
        rows = rows_of(index)
        project(
            x_ref[rows, :], rows, biases[:, :PAD], biases[:, PAD : 2 * PAD], w_s, qaug_ref,
            kaug_ref, vaug_ref, q_ref.at[0], k_ref.at[0], v_ref.at[0],
        )

    @pl.loop(0, length // ROWS)
    def _(index):
        refs = (ref.at[0] for ref in (q_ref, k_ref, v_ref, att_ref))
        attend_rows(rows_of(index), width, w_s, *refs, first_ref)


MESH = pl.DeviceIdType.MESH


def partner(index, bits, size):
    flipped = index
    for bit in (1, 2, 4):
        if bits & bit and bit < size:
            flipped = flipped + bit - 2 * bit * lax.rem(lax.div(index, bit), 2)
    return flipped


class Wires:
    def __init__(self, send, recv, place, row):
        self.send, self.recv, self.place, self.row = send, recv, place, row

    def to(self, tensor_bits, dp_bits):
        return (partner(self.row, dp_bits, 8), partner(self.place, tensor_bits, 4))

    def copy(self, number, source, target, tensor_bits=0, dp_bits=0):
        return pltpu.make_async_remote_copy(
            src_ref=source,
            dst_ref=target,
            send_sem=self.send.at[number],
            recv_sem=self.recv.at[number],
            device_id=self.to(tensor_bits, dp_bits),
            device_id_type=MESH,
        )


def greet(wires, peers):
    barrier = pltpu.get_barrier_semaphore()
    for tensor_bits, dp_bits in peers:
        pl.semaphore_signal(
            barrier, inc=1, device_id=wires.to(tensor_bits, dp_bits), device_id_type=MESH
        )
    pl.semaphore_wait(barrier, len(peers))


PEERS = ((1, 0), (2, 0), (3, 0), (0, 1), (0, 2), (0, 4), (0, 6))
TOKENS, COTS, BIASES, KIND_A = 0, 3, 6, 9
SHARD_WIRES, BLOCK_WIRES = 19, 18
KIND_I = KIND_A + SHARD_WIRES
KIND_O = KIND_I + SHARD_WIRES
FORWARD_WIRES = KIND_O + BLOCK_WIRES


class ShardGather:
    def __init__(self, wires, base, shard, whole, across=False):
        self.wires, self.base, self.shard, self.whole = wires, base, shard, whole
        self.across = across
        z = lax.div(wires.row, 2)
        self.middle = (z == 1) | (z == 2)

    def at(self, slot, dp_bits):
        return self.whole.at[slot, partner(self.wires.row, dp_bits, 8)]

    def own(self, slot):
        return self.shard if slot == 0 else self.at(slot, 0)

    def cross_x(self):
        return self.wires.copy(self.base, self.shard, self.at(2, 0), 2, 0)

    def along_z(self, slot, step):
        number = self.base + 1 + 3 * (slot // 2) + step - 1
        return self.wires.copy(number, self.own(slot), self.at(slot, 0), 0, 2 * step)

    def hand_on(self, slot):
        number = self.base + 17 + slot // 2
        return self.wires.copy(number, self.at(slot, 4), self.at(slot, 4), 0, 2)

    def along_y(self, slot, step):
        number = self.base + 7 + 4 * (slot // 2) + step
        if slot and self.across:
            other = 2 * step + 1
            return self.wires.copy(number, self.at(0, other), self.at(2, other), 2, 0)
        source = self.own(slot) if step == 0 else self.at(slot, 2 * step)
        return self.wires.copy(number, source, self.at(slot, 2 * step), 0, 1)

    def to_core(self, slot):
        number = self.base + 15 + slot // 2
        return self.wires.copy(number, self.whole.at[slot], self.whole.at[slot + 1], 1, 0)

    def start(self, slot):
        self.along_z(slot, 2).start()
        self.along_z(slot, 1).start()

        @pl.when(self.middle)
        def _():
            self.along_z(slot, 3).start()

    def advance(self, slot):
        self.advance_near(slot)
        self.advance_far(slot)

    def advance_near(self, slot):
        self.along_z(slot, 2).wait_recv()

        @pl.when(self.middle)
        def _():
            self.hand_on(slot).start()

        self.pass_y(slot, 2)
        self.along_z(slot, 1).wait_recv()
        self.pass_y(slot, 1)

    def pass_y(self, slot, step):
        if not (slot and self.across):
            self.along_y(slot, step).start()

    def advance_far(self, slot):
        @pl.when(self.middle)
        def _():
            self.along_z(slot, 3).wait_recv()

        @pl.when(jnp.logical_not(self.middle))
        def _():
            self.hand_on(slot).wait_recv()

        self.pass_y(slot, 3)

    def wait_y(self, slot):
        for step in range(4):
            self.along_y(slot, step).wait_recv()

    def wait_sent(self, slots):
        for slot in slots:
            for step in (1, 2):
                self.along_z(slot, step).wait_send()

            @pl.when(self.middle)
            def _(slot=slot):
                self.along_z(slot, 3).wait_send()
                self.hand_on(slot).wait_send()

            for step in range(4):
                self.along_y(slot, step).wait_send()
        for slot in (0, 2):
            self.to_core(slot).wait_send()


class BlockGather(ShardGather):
    def along_z(self, slot, step):
        return self.wires.copy(
            self.base + step - 1, self.shard, self.at(0, 0), 0, 2 * step
        )

    def hand_on(self, slot):
        return self.wires.copy(self.base + 7, self.at(0, 4), self.at(0, 4), 0, 2)

    def along_y(self, slot, step):
        source = self.own(0) if step == 0 else self.at(0, 2 * step)
        return self.wires.copy(self.base + 3 + step, source, self.at(0, 2 * step), 0, 1)

    def cross(self, bits):
        source = self.own(0) if bits == 0 else self.at(0, bits)
        return self.wires.copy(self.base + 8 + bits, source, self.at(2, bits), 2, 0)

    def to_core(self, slot):
        return self.wires.copy(
            self.base + 16 + slot // 2, self.whole.at[slot], self.whole.at[slot + 1], 1, 0
        )

    def advance(self, slot):
        super().advance(slot)
        for bits in (0, 4, 2, 6):
            self.cross(bits).start()

    def wait_y(self, slot):
        super().wait_y(slot)
        for bits in (1, 3, 5, 7):
            self.cross(bits).start()

    def wait_x(self):
        for bits in range(8):
            self.cross(bits).wait_recv()

    def wait_sent(self, slots):
        super().wait_sent(slots)
        for bits in range(8):
            self.cross(bits).wait_send()


def gelu_parts(values):
    phi = jnp.exp2(values * values * (-0.5 * LOG2E)) * 0.3989422804014327
    total = 0.5 + 0.5 * lax.erf(values * 0.7071067811865476)
    return values * total, total + values * phi


def norm_parts(values):
    average = jnp.mean(values, axis=-1, keepdims=True)
    centred = values - average
    spread = jnp.mean(centred * centred, axis=-1, keepdims=True)
    inverse = lax.rsqrt(spread + EPS)
    return centred * inverse, inverse


def norm_back(grads, gain, unit, inverse):
    scaled = grads * gain
    average = jnp.mean(scaled, axis=-1, keepdims=True)
    along = jnp.mean(scaled * unit, axis=-1, keepdims=True)
    return (scaled - average - unit * along) * inverse


def column_sum(values):
    return jnp.sum(values, axis=0, keepdims=True)


WIDE = 512
SEG = 16


def head_rows(head):
    return slice(head * HEAD, (head + 1) * HEAD)


def extra_rows(head, width):
    return slice(width + head * SEG, width + (head + 1) * SEG)


def place_head(part, extra, head, width):
    count = part.shape[1]
    zeros = lambda rows: [jnp.zeros((rows, count), part.dtype)] if rows else []
    pieces = zeros(head * HEAD) + [part] + zeros(width - (head + 1) * HEAD)
    pieces += zeros(head * SEG) + [extra] + zeros(PAD - width - (head + 1) * SEG)
    return jnp.concatenate(pieces, axis=0)


def parts_rows(values, before):
    parts = [part for part in three_parts(values)]
    rest = jnp.zeros((SEG - DOCS - 3, values.shape[1]), BF16)
    return jnp.concatenate([before] + parts + [rest], axis=0)


def attend_block(cols, width, key_ref, vt_s, side_ref):
    heads = range(width // HEAD)
    docs = side_ref[extra_rows(0, width), cols]

    def score(head):
        queries = place_head(side_ref[head_rows(head), cols], docs, head, width)
        return dot_nn(key_ref[...], queries)

    scores, highest, mixed = [score(0)], [], []
    for head in heads:
        if head + 1 < len(heads):
            scores.append(score(head + 1))
        highest.append(jnp.max(scores[head], axis=0, keepdims=True))
        raw = jnp.exp2((scores[head] - highest[head]) * LOG2E).astype(BF16)
        mixed.append(dot_nn(vt_s[head], raw))
    for head in heads:
        logs = -(highest[head] + jnp.log(mixed[head][HEAD : HEAD + 1]))
        side_ref[extra_rows(head, width), cols] = parts_rows(logs, docs[:DOCS])
    outs = [(each[:HEAD] / each[HEAD : HEAD + 1]).astype(BF16) for each in mixed]
    return jnp.concatenate(outs, axis=0)


def attend_block_back(cols, width, key_ref, value_ref, side_ref, do_s, kt_s, all_t, dk_t, dv_t):
    heads = range(width // HEAD)

    def products(head):
        queries = side_ref[head_rows(head), cols]
        d_att = do_s[head_rows(head), cols]
        extra = extra_rows(head, width)
        scores = dot_nn(key_ref[...], place_head(queries, side_ref[extra, cols], head, width))
        d_chances = dot_nn(value_ref[...], place_head(d_att, do_s[extra, cols], head, width))
        return queries, d_att, scores, d_chances

    ahead = products(0)
    d_queries, d_keys, d_values = [], [], []
    for head in heads:
        queries, d_att, scores, d_chances = ahead
        if head + 1 < len(heads):
            ahead = products(head + 1)
        chances = jnp.exp2(scores * LOG2E)
        d_scores = (chances * d_chances).astype(BF16)
        d_queries.append(dot_nn(kt_s[head_rows(head), :], d_scores) * HEAD**-0.5)
        d_keys.append(dot_nt(queries, d_scores))
        d_values.append(dot_nt(d_att, chances.astype(BF16)))
    for head in heads:
        all_t[head_rows(head), cols] = d_queries[head].astype(BF16)
        dk_t[head_rows(head), :] += d_keys[head]
        dv_t[head_rows(head), :] += d_values[head]


def forward_kernel(
    tok_ref, cot_ref, si_ref, wq_ref, wk_ref, wv_ref, wm_ref, wo_ref, doc_ref, vec_ref,
    acts_ref, side_ref, slope_ref, first_out, second_out, low_out, xt_out, cot_out, wia_out,
    wo_out,
    sa_s, so_s, w_s, wm_s, x_s, xt_s, a_s, i_s, o_s, bias_s, kaug_s, qdoc_s, vt_s, mix_s,
    first_s, second_s, low_s, send_sem, recv_sem, here_sem,
):
    step = pl.program_id(0)
    place = lax.axis_index("tensor")
    row = lax.axis_index("dp")
    quarters, part, model = x_s.shape
    length = quarters * part
    share, width = wq_ref.shape
    heads = width // HEAD
    blocks = length // ROWS
    wides = length // WIDE
    wires = Wires(send_sem, recv_sem, place, row)
    attn = ShardGather(wires, KIND_A, sa_s, a_s, True)
    inner = ShardGather(wires, KIND_I, si_ref, i_s)
    outer = BlockGather(wires, KIND_O, so_s, o_s)
    b_mixer, gain_one, bias_one, b_outer = (vec_ref[i : i + 1, :] for i in range(4))
    key_ref, value_ref = (acts_ref.at[0, :, i * PAD : (i + 1) * PAD] for i in range(2))

    def exchange(base, source, target, bits, mine):
        other = partner(place, bits, 4)
        return wires.copy(
            base + bits - 1, source.at[other], target.at[place if mine else other], bits, 0
        )

    def bias_copy(bits, mine):
        return wires.copy(BIASES + bits - 1, vec_ref, bias_s.at[bits], bits, 0)

    local = [
        pltpu.make_async_copy(tok_ref.at[place], x_s.at[place], here_sem.at[0]),
        pltpu.make_async_copy(sa_s, a_s.at[0, row], here_sem.at[1]),
        pltpu.make_async_copy(si_ref, i_s.at[0, row], here_sem.at[2]),
        pltpu.make_async_copy(so_s, o_s.at[0, row], here_sem.at[3]),
        pltpu.make_async_copy(vec_ref, bias_s.at[0], here_sem.at[4]),
    ]
    own_cot = pltpu.make_async_copy(cot_ref.at[place], cot_out.at[place], here_sem.at[5])
    keep_x = pltpu.make_async_copy(xt_s, xt_out, here_sem.at[6])
    keep_a = pltpu.make_async_copy(a_s, wia_out.at[1], here_sem.at[7])
    keep_i = pltpu.make_async_copy(i_s, wia_out.at[0], here_sem.at[8])
    keep_o = pltpu.make_async_copy(o_s, wo_out, here_sem.at[9])
    keep_first = pltpu.make_async_copy(first_s, first_out, here_sem.at[10])
    keep_low = pltpu.make_async_copy(low_s, low_out, here_sem.at[11])
    keep_second = pltpu.make_async_copy(second_s, second_out, here_sem.at[12])

    @pl.when(step == 0)
    def _():
        sa_s[...] = jnp.concatenate(
            [wq_ref[...], wk_ref[...], wv_ref[...], wm_ref[...].T], axis=1
        )
        greet(wires, PEERS)
        attn.start(0)
        attn.along_y(0, 0).start()
        for bits in (2, 3, 1):
            bias_copy(bits, True).start()
            exchange(TOKENS, tok_ref, x_s, bits, True).start()
        so_s[...] = wo_ref[...]
        for copy in local:
            copy.start()
        own_cot.start()
        labels = doc_ref[place]
        docs = lax.broadcasted_iota(jnp.int32, (DOCS, length), 0)
        same = docs == labels
        ones = jnp.ones((3, length), F32)
        rest = jnp.zeros((SEG - DOCS - 3, length), F32)
        qdoc_s[...] = jnp.concatenate(
            [jnp.where(same, 1.0, 0.0), jnp.zeros((SEG - DOCS, length), F32)], axis=0
        ).astype(BF16)
        one_head = jnp.concatenate([jnp.where(same, 0.0, -(2.0**100)), ones, rest], axis=0)
        tall = jnp.zeros((width - PAD // 2, length), F32)
        last = jnp.zeros((PAD - width - heads * SEG, length), F32)
        kaug_s[...] = jnp.concatenate([tall] + [one_head] * heads + [last], axis=0).astype(BF16).T
        for head in range(heads):
            vt_s[head, HEAD:, :] = jnp.ones((SEG, length), BF16)
        for copy in local:
            copy.wait()
        attn.advance_near(0)
        outer.start(0)
        attn.advance_far(0)
        outer.along_y(0, 0).start()
        inner.along_y(0, 0).start()
        attn.cross_x().start()
        attn.wait_y(0)
        attn.to_core(0).start()
        for number in range(4):
            attn.along_y(2, number).start()
        inner.cross_x().start()
        for bits in (1, 2, 3):
            exchange(TOKENS, tok_ref, x_s, bits, False).wait_recv()
            bias_copy(bits, False).wait_recv()

        @pl.loop(0, quarters)
        def _(index):
            rows = rows_of(index, part)
            first_s[rows, :] = x_s[index].astype(F32) + b_mixer

    @pl.when(step == 1)
    def _():
        @pl.loop(0, quarters)
        def _(index):
            xt_s[:, rows_of(index, part)] = x_s[index].T

        keep_x.start()

    @pl.when(step == 1)
    def _():
        attn.to_core(0).wait_recv()

    @pl.when(step == 2)
    def _():
        attn.wait_y(2)
        attn.to_core(2).start()

    @pl.when(step == 3)
    def _():
        attn.to_core(2).wait_recv()
        keep_a.start()

    @pl.when(step < 4)
    def _():
        for dp_row in range(a_s.shape[1]):
            packed = a_s[step, dp_row]
            rest = jnp.zeros((share, PAD - width), packed.dtype)
            rows = slice(dp_row * share, (dp_row + 1) * share)
            for slot in range(4):
                piece = packed[:, slot * width : (slot + 1) * width]
                piece = jnp.concatenate([piece, rest], axis=1)
                if slot < 3:
                    w_s[rows, slot * PAD : (slot + 1) * PAD] = piece
                else:
                    wm_s[rows, :] = piece
        bias = bias_s[step][7:8]
        lanes = lax.broadcasted_iota(jnp.int32, (1, PAD), 1) - width
        spare = (lanes >= 0) & (lanes < heads * SEG) & (lax.rem(lanes + SEG, SEG) >= DOCS)
        vaug = jnp.where(spare & (lax.rem(lanes + SEG, SEG) < DOCS + 3), 1.0, 0.0).astype(BF16)

        @pl.loop(0, wides)
        def _(index):
            rows = rows_of(index, WIDE)
            x_rows = x_s[pl.ds(index * (WIDE // part), WIDE // part)].reshape(WIDE, model)
            result = dot_nn(x_rows, w_s[...])
            queries = (result[:, :PAD] + bias[:, :PAD]).astype(BF16)
            queries = (queries * jnp.asarray(HEAD**-0.5, BF16)).T
            side_ref[0, :width, rows] = queries[:width]
            side_ref[0, PAD + width :, rows] = jnp.zeros((PAD - width, WIDE), BF16)
            keys = result[:, PAD : 2 * PAD].astype(BF16)
            key_ref[rows, : PAD // 2] = keys[:, : PAD // 2]
            key_ref[rows, PAD // 2 :] = keys[:, PAD // 2 :] + kaug_s[rows, :]
            values = (result[:, 2 * PAD :] + bias[:, PAD : 2 * PAD]).astype(BF16)
            value_ref[rows, :] = values + vaug
            values_t = values.T
            for head in range(heads):
                vt_s[head, :HEAD, rows] = values_t[head_rows(head)]

        for head in range(heads):
            side_ref[0, extra_rows(head, width), :] = qdoc_s[...]
        side_ref[0, width + heads * SEG : PAD, :] = jnp.zeros(
            (PAD - width - heads * SEG, length), BF16
        )

        @pl.when(step == 1)
        def _():
            attn.advance_near(2)

        @pl.loop(0, blocks)
        def _(index):
            cols = rows_of(index)
            attended = attend_block(cols, width, key_ref, vt_s, side_ref.at[0])
            side_ref[0, PAD : PAD + width, cols] = attended
            rest = jnp.zeros((PAD - width, ROWS), BF16)
            mix_s[cols, :] = jnp.concatenate([attended, rest], axis=0).T

            @pl.when((step == 0) & (index == 0))
            def _():
                attn.cross_x().wait_recv()
                attn.start(2)

            @pl.when((step == 0) & (index == 1))
            def _():
                outer.advance(0)

            @pl.when((step == 0) & (index == 3))
            def _():
                inner.start(0)

            @pl.when((step == 1) & (index == 1))
            def _():
                attn.advance_far(2)

            @pl.when((step == 1) & (index == 3))
            def _():
                outer.wait_y(0)
                outer.to_core(0).start()
                inner.cross_x().wait_recv()
                inner.start(2)
                inner.along_y(2, 0).start()

            @pl.when((step == 2) & (index == 1))
            def _():
                inner.advance(0)

            @pl.when((step == 3) & (index == 2))
            def _():
                inner.advance(2)

            @pl.when((step == 3) & (index == 0))
            def _():
                for bits in (2, 3, 1):
                    exchange(COTS, cot_ref, cot_out, bits, True).start()

        @pl.loop(0, wides)
        def _(index):
            rows = rows_of(index, WIDE)
            first_s[rows, :] += dot_nt(mix_s[rows, :], wm_s[...])

    @pl.when(step == 4)
    def _():
        keep_first.start()

        @pl.loop(0, blocks)
        def _(index):
            rows = rows_of(index)
            unit, _inverse = norm_parts(first_s[rows, :])
            normed = unit * gain_one + bias_one
            low_s[rows, :] = normed.astype(BF16)
            second_s[rows, :] = normed + b_outer

        keep_low.start()
        inner.wait_y(0)
        inner.to_core(0).start()

    @pl.when(step == 5)
    def _():
        inner.to_core(0).wait_recv()
        outer.to_core(0).wait_recv()

    @pl.when(step == 6)
    def _():
        inner.wait_y(2)
        inner.to_core(2).start()
        outer.wait_x()
        outer.to_core(2).start()

    @pl.when(step == 7)
    def _():
        inner.to_core(2).wait_recv()
        outer.to_core(2).wait_recv()
        keep_i.start()
        keep_o.start()

    @pl.when(step >= 4)
    def _():
        slot = step - 4
        w_inner = i_s[slot].reshape(model, model)
        w_outer = o_s[slot].reshape(model, model)
        b_inner = bias_s[slot][6:7]

        @pl.loop(0, wides)
        def _(index):
            rows = rows_of(index, WIDE)
            value, slope = gelu_parts(dot_nn(low_s[rows, :], w_inner) + b_inner)
            hidden = value.astype(BF16)
            acts_ref[0, rows, :] = hidden
            slope_ref[0, rows, :] = slope.astype(BF16)
            second_s[rows, :] += dot_nt(hidden, w_outer)

    @pl.when(step == 7)
    def _():
        keep_second.start()
        for bits in (1, 2, 3):
            exchange(COTS, cot_ref, cot_out, bits, False).wait_recv()
        for gather in (attn, inner):
            gather.cross_x().wait_send()
            gather.wait_sent((0, 2))
        outer.wait_sent((0,))
        for bits in (1, 2, 3):
            exchange(TOKENS, tok_ref, x_s, bits, True).wait_send()
            exchange(COTS, cot_ref, cot_out, bits, True).wait_send()
            bias_copy(bits, True).wait_send()
        for copy in (
            own_cot, keep_x, keep_a, keep_i, keep_o, keep_first, keep_low, keep_second,
        ):
            copy.wait()


def dense_kernel(
    first_in, wi_ref, wo_ref, bi_ref, vec_ref, cot_ref,
    out_ref, dfirst_ref, dmix_ref, gi_ref, go_ref, dbi_ref, small_ref,
    first_ref, second_ref, normed_s, dsec_s, hidden_s, slope_s, low_s, low_t, back_t, dinner_s,
):
    step = pl.program_id(0)
    count = pl.num_programs(0) // 2
    length, model = first_in.shape
    blocks = length // ROWS
    gain_one, bias_one, b_outer, gain_two, bias_two = (vec_ref[i : i + 1, :] for i in range(5))

    @pl.when(step == 0)
    def _():
        copied = pltpu.sync_copy
        copied(first_in, first_ref)

        @pl.loop(0, blocks)
        def _(index):
            rows = rows_of(index)
            unit, _inverse = norm_parts(first_ref[rows, :])
            normed = unit * gain_one + bias_one
            normed_s[rows, :] = normed
            low_s[rows, :] = normed.astype(BF16)
            low_t[:, rows] = normed.astype(BF16).T
            second_ref[rows, :] = normed + b_outer

    @pl.when(step < count)
    def _():
        @pl.loop(0, blocks)
        def _(index):
            rows = rows_of(index)
            inner = dot_nn(low_s[rows, :], wi_ref[0]) + bi_ref[0]
            value, slope = gelu_parts(inner)
            hidden = value.astype(BF16)
            hidden_s[step, rows, :] = hidden
            slope_s[step, rows, :] = slope.astype(BF16)
            second_ref[rows, :] += dot_nt(hidden, wo_ref[0])

    @pl.when(step == count - 1)
    def _():
        small_ref[...] = jnp.zeros_like(small_ref)

        @pl.loop(0, blocks)
        def _(index):
            rows = rows_of(index)
            unit, inverse = norm_parts(second_ref[rows, :])
            out_ref[rows, :] = (unit * gain_two + bias_two).astype(BF16)
            grads = cot_ref[rows, :].astype(F32)
            d_second = norm_back(grads, gain_two, unit, inverse)
            small_ref[0:1, :] += column_sum(d_second)
            small_ref[1:2, :] += column_sum(grads * unit)
            small_ref[2:3, :] += column_sum(grads)
            dsec_s[rows, :] = d_second
            low = d_second.astype(BF16)
            dmix_ref[rows, :] = low
            back_t[:, rows] = low.T

    @pl.when(step >= count)
    def _():
        place = step - count
        dbi_ref[...] = jnp.zeros_like(dbi_ref)

        @pl.loop(0, blocks)
        def _(index):
            rows = rows_of(index)
            d_hidden = dot_nn(dmix_ref[rows, :], wo_ref[0])
            d_inner = (d_hidden * slope_s[place, rows, :].astype(F32)).astype(BF16)
            dinner_s[rows, :] = d_inner
            dbi_ref[0] += column_sum(d_inner.astype(F32))
            dsec_s[rows, :] += dot_nt(d_inner, wi_ref[0])

        @pl.loop(0, model // ROWS)
        def _(index):
            rows = rows_of(index)
            gi_ref[0, rows, :] = dot_nn(low_t[rows, :], dinner_s[...]).astype(gi_ref.dtype)
            go_ref[0, rows, :] = dot_nn(back_t[rows, :], hidden_s[place]).astype(go_ref.dtype)

    @pl.when(step == 2 * count - 1)
    def _():
        @pl.loop(0, blocks)
        def _(index):
            rows = rows_of(index)
            unit, inverse = norm_parts(first_ref[rows, :])
            grads = dsec_s[rows, :]
            d_first = norm_back(grads, gain_one, unit, inverse)
            small_ref[3:4, :] += column_sum(d_first)
            small_ref[4:5, :] += column_sum(grads * unit)
            small_ref[5:6, :] += column_sum(grads)
            dfirst_ref[rows, :] = d_first
            dmix_ref[rows, :] = d_first.astype(BF16)


def back_rows(rows, width, w_s, dmix_rows, q_ref, k_ref, v_ref, att_ref, kt_s, dq_s, dk_s, dv_s):
    lanes = lane_index((ROWS, PAD))
    queries = q_ref[rows, :]
    d_att = dot_nn(dmix_rows, w_s[3]).astype(BF16)
    product = d_att.astype(F32) * att_ref[rows, :].astype(F32)
    heads = range(width // HEAD)
    extended = d_att
    for head in heads:
        centre = jnp.sum(jnp.where(head_only(lanes, head), product, 0.0), axis=1, keepdims=True)
        for spot, part in enumerate(three_parts(-centre)):
            here = lanes == width + DOCS + 3 * head + spot
            extended = jnp.where(here, jnp.broadcast_to(part, (ROWS, PAD)), extended)
    chances_all = []
    d_scores_all = []
    d_att_all = []
    queries_all = []
    for head in heads:
        wide = head_and_extra(lanes, head, width)
        only = head_only(lanes, head)
        chances = jnp.exp2(dot_nt(k_ref[...], jnp.where(wide, queries, 0)) * LOG2E)
        d_chances = dot_nt(v_ref[...], jnp.where(wide, extended, 0))
        d_scores = (chances * d_chances).astype(BF16)
        chances_all.append(chances.astype(BF16))
        d_scores_all.append(d_scores)
        d_att_all.append(jnp.where(only, d_att, 0))
        queries_all.append(jnp.where(only, queries, 0))
        head_rows = slice(head * HEAD, (head + 1) * HEAD)
        dq_s[head_rows, rows] = dot_nn(kt_s[head_rows, :], d_scores)
    dv_s[...] += dot_nn(jnp.concatenate(chances_all, 1), jnp.concatenate(d_att_all, 0))
    dk_s[...] += dot_nn(jnp.concatenate(d_scores_all, 1), jnp.concatenate(queries_all, 0))


def back_low(rows, width, dq_s, dk_s, dv_s, low_s):
    d_query = (dq_s[:, rows].T * HEAD**-0.5).astype(BF16)
    d_query = jnp.where(lane_index(d_query.shape) < width, d_query, 0)
    d_value = dv_s[rows, :].astype(BF16)
    low_s[rows, :PAD] = d_query
    low_s[rows, PAD : 2 * PAD] = dk_s[rows, :].astype(BF16)
    low_s[rows, 2 * PAD :] = d_value
    return column_sum(d_query.astype(F32)), column_sum(d_value.astype(F32))


def back_tokens(rows, w_s, low_s):
    return sum(dot_nt(low_s[rows, slot * PAD : (slot + 1) * PAD], w_s[slot]) for slot in range(3))


def back_weights(rows, width, slots, xt_s, dmixt_s, low_s, att_ref):
    parts = []
    for slot in slots:
        if slot < 3:
            part = dot_nn(xt_s[rows, :], low_s[:, slot * PAD : (slot + 1) * PAD])
        else:
            part = dot_nn(dmixt_s[rows, :], att_ref[...])
        parts.append(part[:, :width])
    return jnp.concatenate(parts, axis=1).astype(BF16)


def attend_back_kernel(
    x_ref, a_ref, dmix_ref, dfirst_ref, q_ref, k_ref, v_ref, att_ref,
    dtok_ref, ga_ref, dbq_ref, dbv_ref,
    w_s, xt_s, dmixt_s, kt_s, dq_s, dk_s, dv_s, low_s,
):
    length, model = x_ref.shape
    width = a_ref.shape[2] // 4
    blocks = length // ROWS
    for slot in range(4):
        w_s[slot] = unpack(a_ref.at[0], slot, width)

    @pl.when(pl.program_id(0) == 0)
    def _():
        dtok_ref[...] = dfirst_ref[...]

        @pl.loop(0, blocks)
        def _(index):
            rows = rows_of(index)
            xt_s[:, rows] = x_ref[rows, :].T
            dmixt_s[:, rows] = dmix_ref[rows, :].T

    for sums in (dk_s, dv_s, dbq_ref, dbv_ref):
        sums[...] = jnp.zeros_like(sums)

    @pl.loop(0, blocks)
    def _(index):
        rows = rows_of(index)
        kt_s[:, rows] = k_ref[0, rows, :].T

    @pl.loop(0, blocks)
    def _(index):
        rows = rows_of(index)
        dmix_rows = dmix_ref[rows, :]
        refs = (ref.at[0] for ref in (q_ref, k_ref, v_ref, att_ref))
        back_rows(rows, width, w_s, dmix_rows, *refs, kt_s, dq_s, dk_s, dv_s)

    @pl.loop(0, blocks)
    def _(index):
        rows = rows_of(index)
        for_query, for_value = back_low(rows, width, dq_s, dk_s, dv_s, low_s)
        dbq_ref[0] += for_query
        dbv_ref[0] += for_value
        dtok_ref[rows, :] += back_tokens(rows, w_s, low_s)

    @pl.loop(0, model // ROWS)
    def _(index):
        rows = rows_of(index)
        ga_ref[0, rows, :] = back_weights(
            rows, width, range(4), xt_s, dmixt_s, low_s, att_ref.at[0]
        )


def add_into(target, source):
    target[...] = (target[...].astype(F32) + source[...].astype(F32)).astype(target.dtype)


class Reduce:
    COUNT = 11

    def __init__(self, wires, base, held, core, by_y, by_z, by_x, cols=slice(None)):
        self.wires, self.base, self.held, self.core = wires, base, held, core
        self.by_y, self.by_z, self.by_x = by_y, by_z, by_x
        self.cols = cols
        self.z, self.y = lax.div(wires.row, 2), lax.rem(wires.row, 2)

    def part(self, ref, *index):
        return ref.at[index + (slice(None), self.cols)]

    def core_copy(self, j, source):
        everything = (slice(None), slice(None))
        return self.wires.copy(
            self.base + j, self.part(source, *everything), self.part(self.core, j, *everything), 1, 0
        )

    def add_core(self, j):
        self.core_copy(j, self.held.at[j]).wait_recv()
        for z in range(4):
            for y in range(2):
                add_into(self.part(self.held, j, z, y), self.part(self.core, j, z, y))

    def y_copy(self, j):
        source = self.part(self.held, j, slice(None), 1 - self.y)
        return self.wires.copy(
            self.base + 2 + j, source, self.part(self.by_y, j, slice(None)), 0, 1
        )

    def add_y(self, j):
        self.y_copy(j).wait_recv()
        for z in range(4):
            add_into(self.part(self.held, j, z, self.y), self.part(self.by_y, j, z))

    def z_copy(self, j, step):
        other = lax.div(partner(self.wires.row, 2 * step, 8), 2)
        number = self.base + 4 + 3 * j + step - 1
        return self.wires.copy(
            number, self.part(self.held, j, other, self.y), self.part(self.by_z, j, step - 1),
            0, 2 * step,
        )

    def start_z(self, j):
        for step in (1, 2, 3):
            self.z_copy(j, step).start()

    def total_z(self, j):
        total = self.part(self.held, j, self.z, self.y)[...].astype(F32)
        for step in (1, 2, 3):
            self.z_copy(j, step).wait_recv()
            total = total + self.part(self.by_z, j, step - 1)[...].astype(F32)
        return total

    def x_copy(self):
        source = self.part(self.held, 1, self.z, self.y)
        return self.wires.copy(self.base + 10, source, self.part(self.by_x), 2, 0)

    def send_x(self):
        self.part(self.held, 1, self.z, self.y)[...] = self.total_z(1).astype(BF16)
        self.x_copy().start()

    def total(self):
        self.x_copy().wait_recv()
        return self.total_z(0) + self.part(self.by_x)[...].astype(F32)

    def whole_x_copy(self):
        return self.wires.copy(self.base + 10, self.held.at[1], self.by_x, 2, 0)

    def add_whole_x(self):
        self.whole_x_copy().wait_recv()
        for z in range(4):
            for y in range(2):
                add_into(self.held.at[0, z, y], self.by_x.at[z, y])

    def wait_sent(self, j_all):
        for j in j_all:
            self.y_copy(j).wait_send()
            for step in (1, 2, 3):
                self.z_copy(j, step).wait_send()


OUTPUTS, TOKEN_GRADS, SUMS, LATE_SUMS = 0, 3, 6, 16
RED_I = 26
RED_O = RED_I + Reduce.COUNT
RED_A = RED_O + Reduce.COUNT
BACKWARD_WIRES = RED_A + 3 * Reduce.COUNT
BACK_PEERS = PEERS + ((0, 3), (0, 5), (0, 7))


def slot_at(step):
    return jnp.where(step < 2, 3 - 2 * step, 6 - 2 * step)


def backward_kernel(
    acts_ref, side_ref, slope_ref, wia_ref, wo_ref, vec_ref, second_ref, first_ref, low_ref, xt_ref,
    cot_ref,
    out_res, dtok_res, ga_res, gi_res, go_res, sum_res, late_res,
    low_t, back_t, dmix_s, low_s, flow_s, out_s, grad_s, first_s, wmt_s, do_s, kt_s, all_t, dk_t,
    dv_t, sums_s, sums_o, sums_d, late_o, late_t, late_d,
    send_i, held_i, core_i, y_i, z_i, x_i, send_o, held_o, core_o, y_o, z_o, x_o,
    held_a, core_a, y_a, z_a, x_a,
    send_sem, recv_sem, here_sem,
):
    step = pl.program_id(0)
    place = lax.axis_index("tensor")
    row = lax.axis_index("dp")
    length, model = dmix_s.shape
    quarters, part, _ = flow_s.shape
    width = wia_ref.shape[2] // 4
    heads = width // HEAD
    blocks = length // ROWS
    wides = length // WIDE
    share = held_i.shape[3]
    wires = Wires(send_sem, recv_sem, place, row)
    inner = Reduce(wires, RED_I, held_i, core_i, y_i, z_i, x_i)
    outer = Reduce(wires, RED_O, held_o, core_o, y_o, z_o, x_o)
    halves = (slice(0, model // 2), slice(model // 2, model))
    send_a = send_i
    thirds = [slice(number * PAD, (number + 1) * PAD) for number in range(model // PAD)]
    attn = [
        Reduce(wires, RED_A + number * Reduce.COUNT, held_a, core_a, y_a, z_a, x_a, cols)
        for number, cols in enumerate(thirds)
    ]
    ready = (attn[:1], attn[1:])
    gain_one, gain_two, bias_two = (vec_ref[i : i + 1, :] for i in (1, 4, 5))
    key_ref, value_ref = (acts_ref.at[0, :, i * PAD : (i + 1) * PAD] for i in range(2))
    att_ref = side_ref.at[0, PAD : PAD + width]

    def exchange(base, source, target, bits, mine):
        other = partner(place, bits, 4)
        return wires.copy(
            base + bits - 1, source.at[other], target.at[place if mine else other], bits, 0
        )

    def by_tensor(bits):
        return wires.copy(
            SUMS + bits - 1, sums_s.at[place], sums_s.at[place], bits, 0
        )

    def by_rows(base, kept, bits):
        return wires.copy(base + 2 + bits, kept.at[row], kept.at[row], 0, bits)

    def late_copy(bits):
        return wires.copy(LATE_SUMS + bits - 1, late_o.at[bits], late_t.at[bits], bits, 0)

    def sum_rows(base, kept):
        for bits in range(1, 8):
            by_rows(base, kept, bits).wait_recv()
        return sum((kept[number] for number in range(1, 8)), kept[0])

    load_second = pltpu.make_async_copy(second_ref, grad_s, here_sem.at[0])
    load_cot = pltpu.make_async_copy(cot_ref, flow_s, here_sem.at[1])
    load_low = pltpu.make_async_copy(low_ref, low_s, here_sem.at[2])
    load_x = pltpu.make_async_copy(xt_ref, low_t, here_sem.at[3])
    keep_out = pltpu.make_async_copy(out_s.at[place], out_res.at[place], here_sem.at[4])
    keep_dtok = pltpu.make_async_copy(flow_s.at[place], dtok_res.at[place], here_sem.at[5])

    def load_first(index):
        return pltpu.make_async_copy(
            first_ref.at[rows_of(index)], first_s.at[index % 2], here_sem.at[6 + index % 2]
        )

    order = (3, 1, 2, 0)

    @pl.when(step == 0)
    def _():
        load_second.start()
        load_cot.start()
        load_low.start()
        sums_s[place] = jnp.zeros_like(sums_s[0])
        for bits in range(4):
            late_o[bits] = jnp.zeros_like(late_o[0])
        greet(wires, BACK_PEERS)
        load_second.wait()
        load_cot.wait()
        load_low.wait()

        @pl.loop(0, quarters)
        def _(index):
            rows = rows_of(index, part)
            low_t[:, rows] = low_s[rows, :].T
            unit, inverse = norm_parts(grad_s[rows, :])
            out_s[index] = (unit * gain_two + bias_two).astype(BF16)
            grads = flow_s[index].astype(F32)
            d_second = norm_back(grads, gain_two, unit, inverse)
            sums_s[place, 8:9, :] += column_sum(d_second)
            sums_s[place, 9:10, :] += column_sum(grads * unit)
            sums_s[place, 10:11, :] += column_sum(grads)
            grad_s[rows, :] = d_second
            lower = d_second.astype(BF16)
            dmix_s[rows, :] = lower
            back_t[:, rows] = lower.T

        for bits in (2, 3, 1):
            exchange(OUTPUTS, out_s, out_res, bits, True).start()
        keep_out.start()

    @pl.when(step < 4)
    def _():
        @pl.loop(0, wides)
        def _(index):
            rows = rows_of(index, WIDE)
            d_hidden = dot_nn(dmix_s[rows, :], wo_ref[0])
            d_inner = (d_hidden * slope_ref[0, rows, :].astype(F32)).astype(BF16)
            low_s[rows, :] = d_inner
            for_inner = column_sum(d_inner.astype(F32))
            for number, bits in enumerate(order):

                @pl.when(step == number)
                def _(bits=bits):
                    sums_s[place, pl.ds(partner(place, bits, 4), 1), :] += for_inner

            grad_s[rows, :] += dot_nt(d_inner, wia_ref[0])

        for transposed, right, sent, held in (
            (back_t, acts_ref.at[0], send_o, held_o), (low_t, low_s, send_i, held_i),
        ):
            grads = dot_nn(transposed[...], right[...]).astype(BF16)
            pieces = grads.reshape(4, 2, share, model)

            @pl.when(step < 2)
            def _(pieces=pieces, sent=sent):
                sent[step] = pieces

            @pl.when(step >= 2)
            def _(pieces=pieces, held=held):
                held[3 - step] = pieces

    for number, j in ((0, 1), (1, 0)):

        @pl.when(step == number)
        def _(number=number, j=j):
            outer.core_copy(j, send_o.at[number]).start()
            inner.core_copy(j, send_i.at[number]).start()

    @pl.when(step == 2)
    def _():
        load_first(0).start()
        load_first(1).start()
        outer.add_core(1)
        outer.whole_x_copy().start()
        inner.add_core(1)
        inner.y_copy(1).start()

    @pl.when(step == 3)
    def _():
        inner.add_core(0)
        inner.y_copy(0).start()
        outer.add_core(0)
        load_x.start()
        for index in range(blocks):
            rows = slice(index * ROWS, (index + 1) * ROWS)
            load_first(index).wait()
            unit, inverse = norm_parts(first_s[index % 2])
            if index + 2 < blocks:
                load_first(index + 2).start()
            grads = grad_s[rows, :]
            d_first = norm_back(grads, gain_one, unit, inverse)
            sums_s[place, 11:12, :] += column_sum(d_first)
            sums_s[place, 12:13, :] += column_sum(grads * unit)
            sums_s[place, 13:14, :] += column_sum(grads)
            grad_s[rows, :] = d_first
            lower = d_first.astype(BF16)
            dmix_s[rows, :] = lower
            back_t[:, rows] = lower.T
        load_x.wait()
        for bits in (1, 2, 3):
            by_tensor(bits).start()

    @pl.when(step == 4)
    def _():
        for number, j in ((0, 1), (1, 0)):
            inner.core_copy(j, send_i.at[number]).wait_send()

    @pl.when(step >= 4)
    def _():
        wmt_s[...] = wia_ref[0, :, 3 * width :].T
        for sums in (dk_t, dv_t):
            sums[...] = jnp.zeros_like(sums)

        @pl.loop(0, wides)
        def _(index):
            cols = rows_of(index, WIDE)
            kt_s[:, cols] = key_ref[cols, :].T[:width]
            d_att = dot_nn(wmt_s[...], back_t[:, cols]).astype(BF16)
            do_s[:width, cols] = d_att
            product = d_att.astype(F32) * att_ref[:, cols].astype(F32)
            none = jnp.zeros((DOCS, WIDE), BF16)
            for head in range(heads):
                centre = column_sum(product[head_rows(head)])
                do_s[extra_rows(head, width), cols] = parts_rows(-centre, none)

        @pl.loop(0, blocks)
        def _(index):
            attend_block_back(
                rows_of(index), width, key_ref, value_ref, side_ref.at[0], do_s, kt_s, all_t,
                dk_t, dv_t,
            )

            @pl.when((step == 4) & (index == 0))
            def _():
                inner.add_y(1)
                inner.start_z(1)

            @pl.when((step == 4) & (index == 3))
            def _():
                inner.add_y(0)
                inner.start_z(0)
                outer.add_whole_x()
                outer.y_copy(0).start()

            @pl.when((step == 5) & (index == 1))
            def _():
                inner.send_x()
                for bits in (1, 2, 3):
                    by_tensor(bits).wait_recv()
                sums_o[...] = sums_s[0] + sums_s[1] + sums_s[2] + sums_s[3]
                sums_d[row, :6, :] = sums_o[8:14, :]
                sums_d[row, 6:7, :] = sums_o[pl.ds(place, 1), :]
                sums_d[row, 7:, :] = jnp.zeros((1, model), F32)
                for bits in range(1, 8):
                    by_rows(SUMS, sums_d, bits).start()

            @pl.when((step == 7) & (index == 1))
            def _():
                sum_res[...] = sum_rows(SUMS, sums_d)

            @pl.when((step == 5) & (index == 3))
            def _():
                outer.add_y(0)
                outer.start_z(0)

            @pl.when((step == 6) & (index == 1))
            def _():
                gi_res[...] = inner.total()

            @pl.when((step == 6) & (index == 3))
            def _():
                go_res[...] = outer.total_z(0)

            for number, reduce in zip((0, 1, 3), attn):

                @pl.when((step == 7) & (index == number))
                def _(reduce=reduce):
                    reduce.add_y(1)
                    reduce.start_z(1)

        all_t[width : 2 * width, :] = dk_t[...].astype(BF16)
        all_t[2 * width :, :] = dv_t[...].astype(BF16)
        for_all = dot_nt(jnp.ones((8, length), BF16), all_t[...])
        for number, bits in enumerate(order):

            @pl.when(step == 4 + number)
            def _(bits=bits):
                late_o[bits, :, : 3 * width] = for_all
                if bits:
                    late_copy(bits).start()
                    return
                for other in (1, 2, 3):
                    late_copy(other).wait_recv()
                late_d[row] = late_o[0] + late_t[1] + late_t[2] + late_t[3]
                for other in range(1, 8):
                    by_rows(LATE_SUMS, late_d, other).start()

        for half, cols in enumerate(halves):

            @pl.loop(0, model // (4 * share))
            def _(pair):
                rows = rows_of(pair, 4 * share)
                if half == 0:
                    grads = dot_nt(low_t[rows, :], all_t[: 2 * width, :])
                else:
                    for_value = dot_nt(low_t[rows, :], all_t[2 * width :, :])
                    for_mixer = dot_nt(back_t[rows, :], att_ref[...])
                    grads = jnp.concatenate([for_value, for_mixer], axis=1)
                pieces = grads.astype(BF16).reshape(2, 2, share, model // 2)

                @pl.when(step < 6)
                def _(pieces=pieces):
                    send_a[step - 4, pl.ds(2 * pair, 2), :, :, cols] = pieces

                @pl.when(step >= 6)
                def _(pieces=pieces):
                    held_a[7 - step, pl.ds(2 * pair, 2), :, :, cols] = pieces

            for number, j in ((0, 1), (1, 0)):

                @pl.when(step == 4 + number)
                def _(number=number, j=j):
                    for reduce in ready[half]:
                        reduce.core_copy(j, send_a.at[number]).start()

            for j in (1, 0):

                @pl.when(step == 7 - j)
                def _(j=j):
                    for reduce in ready[half]:
                        reduce.add_core(j)
                        reduce.y_copy(j).start()

        @pl.loop(0, wides)
        def _(index):
            rows = rows_of(index, WIDE)
            transposed = all_t[:, rows].T
            grad_s[rows, :] += dot_nt(transposed, wia_ref[0, :, : 3 * width])

            @pl.when(step == 7)
            def _():
                places = pl.ds(index * (WIDE // part), WIDE // part)
                flow_s[places] = grad_s[rows, :].astype(BF16).reshape(WIDE // part, part, model)

    @pl.when(step == 7)
    def _():
        for bits in (2, 3, 1):
            exchange(TOKEN_GRADS, flow_s, dtok_res, bits, True).start()
        keep_dtok.start()
        for reduce in attn:
            reduce.add_y(0)
            reduce.start_z(0)
            reduce.send_x()
        late_res[...] = sum_rows(LATE_SUMS, late_d)
        for reduce, cols in zip(attn, thirds):
            ga_res[:, cols] = reduce.total()
        for bits in (1, 2, 3):
            for base, source, target in (
                (OUTPUTS, out_s, out_res), (TOKEN_GRADS, flow_s, dtok_res),
            ):
                exchange(base, source, target, bits, False).wait_recv()
                exchange(base, source, target, bits, True).wait_send()
        keep_out.wait()
        keep_dtok.wait()
        for bits in (1, 2, 3):
            by_tensor(bits).wait_send()
            late_copy(bits).wait_send()
        for bits in range(1, 8):
            by_rows(SUMS, sums_d, bits).wait_send()
            by_rows(LATE_SUMS, late_d, bits).wait_send()
        for number, j in ((0, 1), (1, 0)):
            outer.core_copy(j, send_o.at[number]).wait_send()
            for reduce in attn:
                reduce.core_copy(j, send_a.at[number]).wait_send()
        inner.wait_sent((0, 1))
        inner.x_copy().wait_send()
        outer.wait_sent((0,))
        outer.whole_x_copy().wait_send()
        for reduce in attn:
            reduce.wait_sent((0, 1))
            reduce.x_copy().wait_send()


VMEM_LIMIT = 62 * 1024 * 1024


def resident(shape):
    return pl.BlockSpec(shape, lambda step: (0,) * len(shape))


def stepped(shape):
    return pl.BlockSpec((1,) + shape[1:], lambda step: (step,) + (0,) * (len(shape) - 1))


def spec_list(pairs):
    return [stepped(shape) if moves else resident(shape) for shape, moves in pairs]


def near_forward(tokens, cotangent, shard_i, w_query, w_key, w_value, w_mixer, w_outer, docs, vectors):
    groups, part, model = tokens.shape
    length = groups * part
    share, width = w_query.shape
    whole = (groups, model // share, share, model)
    sides = (groups, 2 * PAD, length)
    slopes = (groups, length, model)
    flat = (length, model)
    shard = (share, model)
    biases = (groups,) + vectors.shape
    anywhere = pl.BlockSpec(memory_space=pl.ANY)

    def early(shape):
        return pl.BlockSpec(
            (1,) + shape[1:], lambda step: (jnp.minimum(step, 3),) + (0,) * (len(shape) - 1)
        )

    def late(shape):
        return pl.BlockSpec(
            (1,) + shape[1:], lambda step: (jnp.maximum(step - 4, 0),) + (0,) * (len(shape) - 1)
        )

    def vmem(*shape, kind=BF16):
        return pltpu.VMEM(shape, kind)

    kept = [w_query, w_key, w_value, w_mixer, w_outer, docs, vectors]
    return pl.pallas_call(
        forward_kernel,
        grid=(2 * groups,),
        out_shape=[
            jax.ShapeDtypeStruct((2 * groups, length, model), BF16),
            jax.ShapeDtypeStruct(sides, BF16),
            jax.ShapeDtypeStruct(slopes, BF16),
            jax.ShapeDtypeStruct(flat, F32),
            jax.ShapeDtypeStruct(flat, F32),
            jax.ShapeDtypeStruct(flat, BF16),
            jax.ShapeDtypeStruct((model, length), BF16),
            jax.ShapeDtypeStruct(tokens.shape, BF16),
            jax.ShapeDtypeStruct((2,) + whole, BF16),
            jax.ShapeDtypeStruct(whole, BF16),
        ],
        in_specs=[anywhere] * 3 + [resident(each.shape) for each in kept],
        out_specs=[stepped((2 * groups, length, model)), early(sides), late(slopes)]
        + [anywhere] * 7,
        scratch_shapes=[
            vmem(*shard), vmem(*shard), vmem(model, 3 * PAD), vmem(model, PAD),
            vmem(*tokens.shape), vmem(model, length), vmem(*whole), vmem(*whole), vmem(*whole),
            vmem(*biases, kind=F32), vmem(length, PAD // 2), vmem(SEG, length),
            vmem(width // HEAD, HEAD + SEG, length), vmem(length, PAD),
            vmem(*flat, kind=F32), vmem(*flat, kind=F32), vmem(*flat),
            pltpu.SemaphoreType.DMA((FORWARD_WIRES,)),
            pltpu.SemaphoreType.DMA((FORWARD_WIRES,)),
            pltpu.SemaphoreType.DMA((13,)),
        ],
        compiler_params=pltpu.CompilerParams(
            vmem_limit_bytes=VMEM_LIMIT, collective_id=0, has_side_effects=True
        ),
        name="near_forward",
    )(tokens, cotangent, shard_i, *kept)


def attend_plain(x, a_all, biases, qaug, kaug, vaug, b_mixer):
    length, model = x.shape
    groups = a_all.shape[0]
    block = (groups, length, PAD)
    return pl.pallas_call(
        attend_plain_kernel,
        grid=(groups,),
        out_shape=[jax.ShapeDtypeStruct(block, BF16)] * 4 + [jax.ShapeDtypeStruct(x.shape, F32)],
        in_specs=spec_list(
            [
                (x.shape, 0), (a_all.shape, 1), (biases.shape, 1),
                (qaug.shape, 0), (kaug.shape, 0), (vaug.shape, 0), (b_mixer.shape, 0),
            ]
        ),
        out_specs=spec_list([(block, 1)] * 4 + [(x.shape, 0)]),
        scratch_shapes=[pltpu.VMEM((4, model, PAD), BF16)],
        compiler_params=pltpu.CompilerParams(vmem_limit_bytes=VMEM_LIMIT),
        name="attend_plain",
    )(x, a_all, biases, qaug, kaug, vaug, b_mixer)


def dense_both(first_sum, wi, wo, bi, vectors, cotangent):
    length, model = first_sum.shape
    groups, _, hidden = wi.shape
    grad = (groups, model, hidden)
    forth = lambda shape: pl.BlockSpec(
        (1,) + shape[1:], lambda step: (lax.rem(step, groups),) + (0,) * (len(shape) - 1)
    )
    late = lambda shape: pl.BlockSpec(
        (1,) + shape[1:], lambda step: (jnp.maximum(step - groups, 0),) + (0,) * (len(shape) - 1)
    )
    return pl.pallas_call(
        dense_kernel,
        grid=(2 * groups,),
        out_shape=[
            jax.ShapeDtypeStruct((length, model), BF16),
            jax.ShapeDtypeStruct((length, model), F32),
            jax.ShapeDtypeStruct((length, model), BF16),
            jax.ShapeDtypeStruct(grad, BF16),
            jax.ShapeDtypeStruct(grad, BF16),
            jax.ShapeDtypeStruct((groups, 1, hidden), F32),
            jax.ShapeDtypeStruct((8, model), F32),
        ],
        in_specs=[
            pl.BlockSpec(memory_space=pl.ANY), forth(wi.shape), forth(wo.shape), forth(bi.shape),
            resident(vectors.shape), resident(cotangent.shape),
        ],
        out_specs=[
            resident((length, model)), resident((length, model)), resident((length, model)),
            late(grad), late(grad), late((groups, 1, hidden)), resident((8, model)),
        ],
        scratch_shapes=[
            pltpu.VMEM((length, model), F32),
            pltpu.VMEM((length, model), F32),
            pltpu.VMEM((length, model), F32),
            pltpu.VMEM((length, model), F32),
            pltpu.VMEM((groups, length, hidden), BF16),
            pltpu.VMEM((groups, length, hidden), BF16),
            pltpu.VMEM((length, model), BF16),
            pltpu.VMEM((model, length), BF16),
            pltpu.VMEM((model, length), BF16),
            pltpu.VMEM((length, hidden), BF16),
        ],
        compiler_params=pltpu.CompilerParams(vmem_limit_bytes=VMEM_LIMIT),
        name="dense_both",
    )(first_sum, wi, wo, bi, vectors, cotangent)


def attend_backward(x, a_all, d_mixed, d_first, q, k, v, attended):
    length, model = x.shape
    groups = a_all.shape[0]
    sums = (groups, 1, PAD)
    return pl.pallas_call(
        attend_back_kernel,
        grid=(groups,),
        out_shape=[
            jax.ShapeDtypeStruct(x.shape, F32),
            jax.ShapeDtypeStruct(a_all.shape, BF16),
            jax.ShapeDtypeStruct(sums, F32),
            jax.ShapeDtypeStruct(sums, F32),
        ],
        in_specs=spec_list(
            [
                (x.shape, 0), (a_all.shape, 1), (d_mixed.shape, 0), (d_first.shape, 0),
                (q.shape, 1), (k.shape, 1), (v.shape, 1), (attended.shape, 1),
            ]
        ),
        out_specs=spec_list([(x.shape, 0), (a_all.shape, 1), (sums, 1), (sums, 1)]),
        scratch_shapes=[
            pltpu.VMEM((4, model, PAD), BF16),
            pltpu.VMEM((model, length), BF16),
            pltpu.VMEM((model, length), BF16),
            pltpu.VMEM((PAD, length), BF16),
            pltpu.VMEM((PAD, length), F32),
            pltpu.VMEM((length, PAD), F32),
            pltpu.VMEM((length, PAD), F32),
            pltpu.VMEM((length, 3 * PAD), BF16),
        ],
        compiler_params=pltpu.CompilerParams(vmem_limit_bytes=VMEM_LIMIT),
        name="attend_backward",
    )(x, a_all, d_mixed, d_first, q, k, v, attended)


def near_backward(acts, sides, slopes, w_ia, w_o, vectors, second, first, low, xt, cotangent):
    quarters, part, model = cotangent.shape
    length = quarters * part
    share = model // 8
    width = model // 4
    block = (4, 2, share, model)
    anywhere = pl.BlockSpec(memory_space=pl.ANY)

    def ordered(shape, place):
        return pl.BlockSpec(
            (1,) + shape[1:], lambda step: (place(step),) + (0,) * (len(shape) - 1)
        )

    def acts_at(step):
        return jnp.where(step < 4, 4 + slot_at(step), slot_at(step - 4))

    def weights_at(step):
        return jnp.where(step < 4, slot_at(step), 4 + slot_at(step - 4))

    def first_half(step):
        return slot_at(jnp.minimum(step, 3))

    def last_half(step):
        return slot_at(jnp.maximum(step - 4, 0))

    def vmem(*shape, kind=BF16):
        return pltpu.VMEM(shape, kind)

    final = [
        ((share, model), F32), ((share, model), F32), ((share, model), F32), ((8, model), F32),
        ((8, model), F32),
    ]
    return pl.pallas_call(
        backward_kernel,
        grid=(8,),
        out_shape=[jax.ShapeDtypeStruct(cotangent.shape, BF16)] * 2
        + [jax.ShapeDtypeStruct(*each) for each in final],
        in_specs=[
            ordered(acts.shape, acts_at), ordered(sides.shape, last_half),
            ordered(slopes.shape, first_half), ordered(w_ia.shape, weights_at),
            ordered(w_o.shape, first_half), resident(vectors.shape),
        ]
        + [anywhere] * 5,
        out_specs=[anywhere] * 2 + [resident(each[0]) for each in final],
        scratch_shapes=[
            vmem(model, length), vmem(model, length), vmem(length, model), vmem(length, model),
            vmem(*cotangent.shape), vmem(*cotangent.shape), vmem(length, model, kind=F32),
            vmem(2, ROWS, model, kind=F32),
            vmem(width, model), vmem(PAD, length), vmem(width, length), vmem(3 * width, length),
            vmem(width, length, kind=F32), vmem(width, length, kind=F32),
            vmem(4, 16, model, kind=F32), vmem(16, model, kind=F32), vmem(8, 8, model, kind=F32),
            vmem(4, 8, model, kind=F32), vmem(4, 8, model, kind=F32), vmem(8, 8, model, kind=F32),
            vmem(2, *block), vmem(2, *block), vmem(2, *block), vmem(2, 4, share, model),
            vmem(2, 3, share, model), vmem(share, model),
            vmem(2, *block), vmem(2, *block), vmem(2, *block), vmem(1, 4, share, model),
            vmem(1, 3, share, model), vmem(*block),
            vmem(2, *block), vmem(2, *block), vmem(2, 4, share, model),
            vmem(2, 3, share, model), vmem(share, model),
            pltpu.SemaphoreType.DMA((BACKWARD_WIRES,)),
            pltpu.SemaphoreType.DMA((BACKWARD_WIRES,)),
            pltpu.SemaphoreType.DMA((8,)),
        ],
        compiler_params=pltpu.CompilerParams(
            vmem_limit_bytes=VMEM_LIMIT, collective_id=1, has_side_effects=True
        ),
        name="near_backward",
    )(acts, sides, slopes, w_ia, w_o, vectors, second, first, low, xt, cotangent)


def augment(labels, width):
    length = labels.shape[0]
    lanes = lax.broadcasted_iota(jnp.int32, (length, PAD), 1)
    in_docs = (lanes >= width) & (lanes < width + DOCS)
    same = (lanes - width) == labels[:, None]
    qaug = jnp.where(in_docs & same, 1.0, 0.0).astype(BF16)
    spare = (lanes >= width + DOCS) & (lanes < width + DOCS + 3 * (width // HEAD))
    kaug = jnp.where(in_docs & ~same, -(2.0**100), jnp.where(spare, 1.0, 0.0)).astype(BF16)
    vaug = jnp.where((lanes[:1] == width) | spare[:1], 1.0, 0.0).astype(BF16)
    return qaug, kaug, vaug


def body(
    tokens, doc_ids, w_query, b_query, w_key, w_value, b_value, w_mixer, b_mixer, gain_one,
    bias_one, w_inner, b_inner, w_outer, b_outer, gain_two, bias_two, cotangent,
):
    groups = lax.axis_size("tensor")
    rings = lax.axis_size("dp")
    place = lax.axis_index("tensor")
    width = w_query.shape[1]
    hidden = w_inner.shape[1]
    length = doc_ids.shape[2]
    model = tokens.shape[3]
    near = groups == 4 and rings == 8 and hidden == model and 4 * width == model

    if near:
        spare = jnp.zeros((PAD - width,), F32)
        vectors = jnp.concatenate(
            [
                b_mixer, gain_one, bias_one, b_outer, gain_two, bias_two, b_inner,
                b_query, spare, b_value, spare, jnp.zeros((PAD,), F32),
            ]
        ).reshape(8, model)
        acts, sides, slopes, first, second, low, xt, cot, w_ia, w_o = near_forward(
            tokens[:, 0], cotangent[:, 0], w_inner, w_query, w_key, w_value, w_mixer, w_outer.T,
            doc_ids, vectors,
        )
        out, d_tokens, ga, gi, go, tail, late = near_backward(
            acts, sides, slopes, w_ia.reshape(2 * groups, model, model),
            w_o.reshape(groups, model, model), vectors, second, first, low, xt, cot,
        )
        dbq, dbv = late[0, :width], late[0, 2 * width : 3 * width]
        dbi = tail[6]
        out, d_tokens = out[:, None], d_tokens[:, None].astype(F32)
    else:

        def gather(shard):
            whole = lax.all_gather(shard, ("tensor", "dp"), axis=0, tiled=True)
            return whole.reshape(groups, model, shard.shape[1])

        def to_sequence(part):
            return lax.all_to_all(part, "tensor", 0, 2, tiled=True).reshape(length, model)

        def from_sequence(whole):
            return lax.all_to_all(whole.reshape(1, 1, length, model), "tensor", 2, 0, tiled=True)

        def scatter(part):
            flat = part.reshape(-1, part.shape[2])
            total = lax.psum_scatter(flat, ("tensor", "dp"), scatter_dimension=0, tiled=True)
            return total.astype(F32)

        labels = lax.dynamic_index_in_dim(doc_ids[:, 0], place, 0, keepdims=False)
        qaug, kaug, vaug = augment(labels, width)
        shard_a = jnp.concatenate([w_query, w_key, w_value, w_mixer.T], axis=1)
        shard_o = w_outer.T
        spare = jnp.zeros((PAD - width,), F32)
        biases = jnp.concatenate([b_query, spare, b_value, spare, b_inner])[None]
        vectors = jnp.stack([gain_one, bias_one, b_outer, gain_two, bias_two] + [b_outer] * 3)
        x, cot = to_sequence(tokens), to_sequence(cotangent)
        a_all, wi, wo = gather(shard_a), gather(w_inner), gather(shard_o)
        every = lax.all_gather(biases, "tensor", axis=0)
        *saved, first_sum = attend_plain(x, a_all, every, qaug, kaug, vaug, b_mixer[None])
        out, d_first, d_mixed, g_inner, g_outer, dbi, small = dense_both(
            first_sum, wi, wo, every[:, :, 2 * PAD :], vectors, cot
        )
        d_tokens, g_attend, dbq, dbv = attend_backward(x, a_all, d_mixed, d_first, *saved)
        ga, gi, go = scatter(g_attend), scatter(g_inner), scatter(g_outer)
        rows = [dbq[:, 0, :width], dbv[:, 0, :width], dbi[:, 0], small]
        summed = lax.psum(jnp.concatenate([part.reshape(-1) for part in rows]), ("dp", "tensor"))
        own = lambda start, size: lax.dynamic_slice_in_dim(summed, start + place * size, size)
        dbq, dbv, dbi = own(0, width), own(model, width), own(2 * model, hidden)
        tail = summed[-small.size :].reshape(small.shape)
        out, d_tokens = from_sequence(out), from_sequence(d_tokens)
    return (
        out,
        d_tokens,
        ga[:, :width],
        dbq,
        ga[:, width : 2 * width],
        ga[:, 2 * width : 3 * width],
        dbv,
        ga[:, 3 * width :].T,
        tail[3],
        tail[4],
        tail[5],
        gi,
        dbi,
        go.T,
        tail[0],
        tail[1],
        tail[2],
    )


def solution(mesh):
    split = P(None, "dp", "tensor", None)
    both, flipped, part = P("dp", "tensor"), P("tensor", "dp"), P("tensor")
    return jax.shard_map(
        body,
        mesh=mesh,
        in_specs=(
            split, P(None, "dp", None), both, part, both, both, part, flipped, P(), P(), P(),
            both, part, flipped, P(), P(), P(), split,
        ),
        out_specs=(
            split, split, both, part, both, both, part, flipped, P(), P(), P(), both, part,
            flipped, P(), P(), P(),
        ),
        check_vma=False,
    )
```

```python
from functools import partial

import jax
import jax.numpy as jnp
from jax import lax
from jax.experimental import pallas as pl
from jax.experimental.pallas import tpu as pltpu
from jax.sharding import PartitionSpec as P

HEAD = 64
DOCS = 8
PAD = 256
ROWS = 256
LOG2E = 1.4426950408889634
EPS = 1e-12
F32 = jnp.float32
BF16 = jnp.bfloat16


def dot_nn(left, right):
    return lax.dot_general(left, right, (((1,), (0,)), ((), ())), preferred_element_type=F32)


def dot_nt(left, right):
    return lax.dot_general(left, right, (((1,), (1,)), ((), ())), preferred_element_type=F32)


def rows_of(index, size=ROWS):
    return pl.ds(pl.multiple_of(index * size, size), size)


def lane_index(shape):
    return lax.broadcasted_iota(jnp.int32, shape, 1)


def three_parts(values):
    high = values.astype(BF16)
    rest = values - high.astype(F32)
    middle = rest.astype(BF16)
    low = (rest - middle.astype(F32)).astype(BF16)
    return high, middle, low


def head_only(lanes, head):
    return (lanes >= head * HEAD) & (lanes < (head + 1) * HEAD)


def head_and_extra(lanes, head, width):
    extra = width + DOCS + 3 * head
    return (
        head_only(lanes, head)
        | ((lanes >= width) & (lanes < width + DOCS))
        | ((lanes >= extra) & (lanes < extra + 3))
    )


def unpack(block_ref, slot, width):
    part = block_ref[:, slot * width : (slot + 1) * width]
    return jnp.concatenate([part, jnp.zeros((part.shape[0], PAD - width), part.dtype)], axis=1)


def project(x_rows, rows, bq, bv, w_s, qaug_ref, kaug_ref, vaug_ref, q_ref, k_ref, v_ref):
    queries = (dot_nn(x_rows, w_s[0]) + bq).astype(BF16)
    q_ref[rows, :] = queries * jnp.asarray(HEAD**-0.5, BF16) + qaug_ref[rows, :]
    keys = dot_nn(x_rows, w_s[1]).astype(BF16)
    k_ref[rows, :] = keys + kaug_ref[rows, :]
    values = (dot_nn(x_rows, w_s[2]) + bv).astype(BF16)
    v_ref[rows, :] = values + vaug_ref[...]


def attend_rows(rows, width, w_s, q_ref, k_ref, v_ref, att_ref, first_ref):
    lanes = lane_index((ROWS, PAD))
    queries = q_ref[rows, :]
    attended = jnp.zeros((ROWS, PAD), F32)
    extended = queries
    for head in range(width // HEAD):
        masked = jnp.where(head_and_extra(lanes, head, width), queries, 0)
        scores = dot_nt(masked, k_ref[...])
        highest = jnp.max(scores, axis=1, keepdims=True)
        raw = jnp.exp2((scores - highest) * LOG2E).astype(BF16)
        mixed = dot_nn(raw, v_ref[...])
        total = mixed[:, width : width + 1]
        attended = jnp.where(head_only(lanes, head), mixed / total, attended)
        for spot, part in enumerate(three_parts(-(highest + jnp.log(total)))):
            here = lanes == width + DOCS + 3 * head + spot
            extended = jnp.where(here, jnp.broadcast_to(part, (ROWS, PAD)), extended)
    q_ref[rows, :] = extended
    attended = attended.astype(BF16)
    att_ref[rows, :] = attended
    first_ref[rows, :] += dot_nt(attended, w_s[3])


def attend_plain_kernel(
    x_ref, a_ref, bias_ref, qaug_ref, kaug_ref, vaug_ref, bm_ref,
    q_ref, k_ref, v_ref, att_ref, first_ref, w_s,
):
    length, model = x_ref.shape
    width = a_ref.shape[2] // 4
    for slot in range(4):
        w_s[slot] = unpack(a_ref.at[0], slot, width)
    biases = bias_ref[0]

    @pl.when(pl.program_id(0) == 0)
    def _():
        first_ref[...] = x_ref[...].astype(F32) + bm_ref[...]

    @pl.loop(0, length // ROWS)
    def _(index):
        rows = rows_of(index)
        project(
            x_ref[rows, :], rows, biases[:, :PAD], biases[:, PAD : 2 * PAD], w_s, qaug_ref,
            kaug_ref, vaug_ref, q_ref.at[0], k_ref.at[0], v_ref.at[0],
        )

    @pl.loop(0, length // ROWS)
    def _(index):
        refs = (ref.at[0] for ref in (q_ref, k_ref, v_ref, att_ref))
        attend_rows(rows_of(index), width, w_s, *refs, first_ref)


MESH = pl.DeviceIdType.MESH


def partner(index, bits, size):
    flipped = index
    for bit in (1, 2, 4):
        if bits & bit and bit < size:
            flipped = flipped + bit - 2 * bit * lax.rem(lax.div(index, bit), 2)
    return flipped


class Wires:
    def __init__(self, send, recv, place, row):
        self.send, self.recv, self.place, self.row = send, recv, place, row

    def to(self, tensor_bits, dp_bits):
        return (partner(self.row, dp_bits, 8), partner(self.place, tensor_bits, 4))

    def copy(self, number, source, target, tensor_bits=0, dp_bits=0):
        return pltpu.make_async_remote_copy(
            src_ref=source,
            dst_ref=target,
            send_sem=self.send.at[number],
            recv_sem=self.recv.at[number],
            device_id=self.to(tensor_bits, dp_bits),
            device_id_type=MESH,
        )


def greet(wires, peers):
    barrier = pltpu.get_barrier_semaphore()
    for tensor_bits, dp_bits in peers:
        pl.semaphore_signal(
            barrier, inc=1, device_id=wires.to(tensor_bits, dp_bits), device_id_type=MESH
        )
    pl.semaphore_wait(barrier, len(peers))


PEERS = ((1, 0), (2, 0), (3, 0), (0, 1), (0, 2), (0, 4), (0, 6))
TOKENS, COTS, BIASES, KIND_A = 0, 3, 6, 9
SHARD_WIRES, BLOCK_WIRES = 19, 18
KIND_I = KIND_A + SHARD_WIRES
KIND_O = KIND_I + SHARD_WIRES
FORWARD_WIRES = KIND_O + BLOCK_WIRES


class ShardGather:
    def __init__(self, wires, base, shard, whole, across=False):
        self.wires, self.base, self.shard, self.whole = wires, base, shard, whole
        self.across = across
        z = lax.div(wires.row, 2)
        self.middle = (z == 1) | (z == 2)

    def at(self, slot, dp_bits):
        return self.whole.at[slot, partner(self.wires.row, dp_bits, 8)]

    def own(self, slot):
        return self.shard if slot == 0 else self.at(slot, 0)

    def cross_x(self):
        return self.wires.copy(self.base, self.shard, self.at(2, 0), 2, 0)

    def along_z(self, slot, step):
        number = self.base + 1 + 3 * (slot // 2) + step - 1
        return self.wires.copy(number, self.own(slot), self.at(slot, 0), 0, 2 * step)

    def hand_on(self, slot):
        number = self.base + 17 + slot // 2
        return self.wires.copy(number, self.at(slot, 4), self.at(slot, 4), 0, 2)

    def along_y(self, slot, step):
        number = self.base + 7 + 4 * (slot // 2) + step
        if slot and self.across:
            other = 2 * step + 1
            return self.wires.copy(number, self.at(0, other), self.at(2, other), 2, 0)
        source = self.own(slot) if step == 0 else self.at(slot, 2 * step)
        return self.wires.copy(number, source, self.at(slot, 2 * step), 0, 1)

    def to_core(self, slot):
        number = self.base + 15 + slot // 2
        return self.wires.copy(number, self.whole.at[slot], self.whole.at[slot + 1], 1, 0)

    def start(self, slot):
        self.along_z(slot, 2).start()
        self.along_z(slot, 1).start()

        @pl.when(self.middle)
        def _():
            self.along_z(slot, 3).start()

    def advance(self, slot):
        self.advance_near(slot)
        self.advance_far(slot)

    def advance_near(self, slot):
        self.along_z(slot, 2).wait_recv()

        @pl.when(self.middle)
        def _():
            self.hand_on(slot).start()

        self.pass_y(slot, 2)
        self.along_z(slot, 1).wait_recv()
        self.pass_y(slot, 1)

    def pass_y(self, slot, step):
        if not (slot and self.across):
            self.along_y(slot, step).start()

    def advance_far(self, slot):
        @pl.when(self.middle)
        def _():
            self.along_z(slot, 3).wait_recv()

        @pl.when(jnp.logical_not(self.middle))
        def _():
            self.hand_on(slot).wait_recv()

        self.pass_y(slot, 3)

    def wait_y(self, slot):
        for step in range(4):
            self.along_y(slot, step).wait_recv()

    def wait_sent(self, slots):
        for slot in slots:
            for step in (1, 2):
                self.along_z(slot, step).wait_send()

            @pl.when(self.middle)
            def _(slot=slot):
                self.along_z(slot, 3).wait_send()
                self.hand_on(slot).wait_send()

            for step in range(4):
                self.along_y(slot, step).wait_send()
        for slot in (0, 2):
            self.to_core(slot).wait_send()


class BlockGather(ShardGather):
    def along_z(self, slot, step):
        return self.wires.copy(
            self.base + step - 1, self.shard, self.at(0, 0), 0, 2 * step
        )

    def hand_on(self, slot):
        return self.wires.copy(self.base + 7, self.at(0, 4), self.at(0, 4), 0, 2)

    def along_y(self, slot, step):
        source = self.own(0) if step == 0 else self.at(0, 2 * step)
        return self.wires.copy(self.base + 3 + step, source, self.at(0, 2 * step), 0, 1)

    def cross(self, bits):
        source = self.own(0) if bits == 0 else self.at(0, bits)
        return self.wires.copy(self.base + 8 + bits, source, self.at(2, bits), 2, 0)

    def to_core(self, slot):
        return self.wires.copy(
            self.base + 16 + slot // 2, self.whole.at[slot], self.whole.at[slot + 1], 1, 0
        )

    def advance(self, slot):
        super().advance(slot)
        for bits in (0, 4, 2, 6):
            self.cross(bits).start()

    def wait_y(self, slot):
        super().wait_y(slot)
        for bits in (1, 3, 5, 7):
            self.cross(bits).start()

    def wait_x(self):
        for bits in range(8):
            self.cross(bits).wait_recv()

    def wait_sent(self, slots):
        super().wait_sent(slots)
        for bits in range(8):
            self.cross(bits).wait_send()


def gelu_parts(values):
    phi = jnp.exp2(values * values * (-0.5 * LOG2E)) * 0.3989422804014327
    total = 0.5 + 0.5 * lax.erf(values * 0.7071067811865476)
    return values * total, total + values * phi


def norm_parts(values):
    average = jnp.mean(values, axis=-1, keepdims=True)
    centred = values - average
    spread = jnp.mean(centred * centred, axis=-1, keepdims=True)
    inverse = lax.rsqrt(spread + EPS)
    return centred * inverse, inverse


def norm_back(grads, gain, unit, inverse):
    scaled = grads * gain
    average = jnp.mean(scaled, axis=-1, keepdims=True)
    along = jnp.mean(scaled * unit, axis=-1, keepdims=True)
    return (scaled - average - unit * along) * inverse


def column_sum(values):
    return jnp.sum(values, axis=0, keepdims=True)


WIDE = 512
SEG = 16


def head_rows(head):
    return slice(head * HEAD, (head + 1) * HEAD)


def extra_rows(head, width):
    return slice(width + head * SEG, width + (head + 1) * SEG)


def place_head(part, extra, head, width):
    count = part.shape[1]
    zeros = lambda rows: [jnp.zeros((rows, count), part.dtype)] if rows else []
    pieces = zeros(head * HEAD) + [part] + zeros(width - (head + 1) * HEAD)
    pieces += zeros(head * SEG) + [extra] + zeros(PAD - width - (head + 1) * SEG)
    return jnp.concatenate(pieces, axis=0)


def parts_rows(values, before):
    parts = [part for part in three_parts(values)]
    rest = jnp.zeros((SEG - DOCS - 3, values.shape[1]), BF16)
    return jnp.concatenate([before] + parts + [rest], axis=0)


def attend_block(cols, width, key_ref, vt_s, side_ref):
    heads = range(width // HEAD)
    docs = side_ref[extra_rows(0, width), cols]

    def score(head):
        queries = place_head(side_ref[head_rows(head), cols], docs, head, width)
        return dot_nn(key_ref[...], queries)

    scores, highest, mixed = [score(0)], [], []
    for head in heads:
        if head + 1 < len(heads):
            scores.append(score(head + 1))
        highest.append(jnp.max(scores[head], axis=0, keepdims=True))
        raw = jnp.exp2((scores[head] - highest[head]) * LOG2E).astype(BF16)
        mixed.append(dot_nn(vt_s[head], raw))
    for head in heads:
        logs = -(highest[head] + jnp.log(mixed[head][HEAD : HEAD + 1]))
        side_ref[extra_rows(head, width), cols] = parts_rows(logs, docs[:DOCS])
    outs = [(each[:HEAD] / each[HEAD : HEAD + 1]).astype(BF16) for each in mixed]
    return jnp.concatenate(outs, axis=0)


def attend_block_back(cols, width, key_ref, value_ref, side_ref, do_s, kt_s, all_t, dk_t, dv_t):
    heads = range(width // HEAD)

    def products(head):
        queries = side_ref[head_rows(head), cols]
        d_att = do_s[head_rows(head), cols]
        extra = extra_rows(head, width)
        scores = dot_nn(key_ref[...], place_head(queries, side_ref[extra, cols], head, width))
        d_chances = dot_nn(value_ref[...], place_head(d_att, do_s[extra, cols], head, width))
        return queries, d_att, scores, d_chances

    ahead = products(0)
    d_queries, d_keys, d_values = [], [], []
    for head in heads:
        queries, d_att, scores, d_chances = ahead
        if head + 1 < len(heads):
            ahead = products(head + 1)
        chances = jnp.exp2(scores * LOG2E)
        d_scores = (chances * d_chances).astype(BF16)
        d_queries.append(dot_nn(kt_s[head_rows(head), :], d_scores) * HEAD**-0.5)
        d_keys.append(dot_nt(queries, d_scores))
        d_values.append(dot_nt(d_att, chances.astype(BF16)))
    for head in heads:
        all_t[head_rows(head), cols] = d_queries[head].astype(BF16)
        dk_t[head_rows(head), :] += d_keys[head]
        dv_t[head_rows(head), :] += d_values[head]


def forward_kernel(
    tok_ref, cot_ref, si_ref, wq_ref, wk_ref, wv_ref, wm_ref, wo_ref, doc_ref, vec_ref,
    acts_ref, side_ref, slope_ref, first_out, second_out, low_out, xt_out, cot_out, wia_out,
    wo_out,
    sa_s, so_s, w_s, wm_s, x_s, xt_s, a_s, i_s, o_s, bias_s, kaug_s, qdoc_s, vt_s, mix_s,
    first_s, second_s, low_s, send_sem, recv_sem, here_sem,
):
    step = pl.program_id(0)
    place = lax.axis_index("tensor")
    row = lax.axis_index("dp")
    quarters, part, model = x_s.shape
    length = quarters * part
    share, width = wq_ref.shape
    heads = width // HEAD
    blocks = length // ROWS
    wides = length // WIDE
    wires = Wires(send_sem, recv_sem, place, row)
    attn = ShardGather(wires, KIND_A, sa_s, a_s, True)
    inner = ShardGather(wires, KIND_I, si_ref, i_s)
    outer = BlockGather(wires, KIND_O, so_s, o_s)
    b_mixer, gain_one, bias_one, b_outer = (vec_ref[i : i + 1, :] for i in range(4))
    key_ref, value_ref = (acts_ref.at[0, :, i * PAD : (i + 1) * PAD] for i in range(2))

    def exchange(base, source, target, bits, mine):
        other = partner(place, bits, 4)
        return wires.copy(
            base + bits - 1, source.at[other], target.at[place if mine else other], bits, 0
        )

    def bias_copy(bits, mine):
        return wires.copy(BIASES + bits - 1, vec_ref, bias_s.at[bits], bits, 0)

    local = [
        pltpu.make_async_copy(tok_ref.at[place], x_s.at[place], here_sem.at[0]),
        pltpu.make_async_copy(sa_s, a_s.at[0, row], here_sem.at[1]),
        pltpu.make_async_copy(si_ref, i_s.at[0, row], here_sem.at[2]),
        pltpu.make_async_copy(so_s, o_s.at[0, row], here_sem.at[3]),
        pltpu.make_async_copy(vec_ref, bias_s.at[0], here_sem.at[4]),
    ]
    own_cot = pltpu.make_async_copy(cot_ref.at[place], cot_out.at[place], here_sem.at[5])
    keep_x = pltpu.make_async_copy(xt_s, xt_out, here_sem.at[6])
    keep_a = pltpu.make_async_copy(a_s, wia_out.at[1], here_sem.at[7])
    keep_i = pltpu.make_async_copy(i_s, wia_out.at[0], here_sem.at[8])
    keep_o = pltpu.make_async_copy(o_s, wo_out, here_sem.at[9])
    keep_first = pltpu.make_async_copy(first_s, first_out, here_sem.at[10])
    keep_low = pltpu.make_async_copy(low_s, low_out, here_sem.at[11])
    keep_second = pltpu.make_async_copy(second_s, second_out, here_sem.at[12])

    @pl.when(step == 0)
    def _():
        sa_s[...] = jnp.concatenate(
            [wq_ref[...], wk_ref[...], wv_ref[...], wm_ref[...].T], axis=1
        )
        greet(wires, PEERS)
        attn.start(0)
        attn.along_y(0, 0).start()
        for bits in (2, 3, 1):
            bias_copy(bits, True).start()
            exchange(TOKENS, tok_ref, x_s, bits, True).start()
        so_s[...] = wo_ref[...]
        for copy in local:
            copy.start()
        own_cot.start()
        labels = doc_ref[place]
        docs = lax.broadcasted_iota(jnp.int32, (DOCS, length), 0)
        same = docs == labels
        ones = jnp.ones((3, length), F32)
        rest = jnp.zeros((SEG - DOCS - 3, length), F32)
        qdoc_s[...] = jnp.concatenate(
            [jnp.where(same, 1.0, 0.0), jnp.zeros((SEG - DOCS, length), F32)], axis=0
        ).astype(BF16)
        one_head = jnp.concatenate([jnp.where(same, 0.0, -(2.0**100)), ones, rest], axis=0)
        tall = jnp.zeros((width - PAD // 2, length), F32)
        last = jnp.zeros((PAD - width - heads * SEG, length), F32)
        kaug_s[...] = jnp.concatenate([tall] + [one_head] * heads + [last], axis=0).astype(BF16).T
        for head in range(heads):
            vt_s[head, HEAD:, :] = jnp.ones((SEG, length), BF16)
        for copy in local:
            copy.wait()
        attn.advance_near(0)
        outer.start(0)
        attn.advance_far(0)
        outer.along_y(0, 0).start()
        inner.along_y(0, 0).start()
        attn.cross_x().start()
        attn.wait_y(0)
        attn.to_core(0).start()
        for number in range(4):
            attn.along_y(2, number).start()
        inner.cross_x().start()
        for bits in (1, 2, 3):
            exchange(TOKENS, tok_ref, x_s, bits, False).wait_recv()
            bias_copy(bits, False).wait_recv()

        @pl.loop(0, quarters)
        def _(index):
            rows = rows_of(index, part)
            first_s[rows, :] = x_s[index].astype(F32) + b_mixer

    @pl.when(step == 1)
    def _():
        @pl.loop(0, quarters)
        def _(index):
            xt_s[:, rows_of(index, part)] = x_s[index].T

        keep_x.start()

    @pl.when(step == 1)
    def _():
        attn.to_core(0).wait_recv()

    @pl.when(step == 2)
    def _():
        attn.wait_y(2)
        attn.to_core(2).start()

    @pl.when(step == 3)
    def _():
        attn.to_core(2).wait_recv()
        keep_a.start()

    @pl.when(step < 4)
    def _():
        for dp_row in range(a_s.shape[1]):
            packed = a_s[step, dp_row]
            rest = jnp.zeros((share, PAD - width), packed.dtype)
            rows = slice(dp_row * share, (dp_row + 1) * share)
            for slot in range(4):
                piece = packed[:, slot * width : (slot + 1) * width]
                piece = jnp.concatenate([piece, rest], axis=1)
                if slot < 3:
                    w_s[rows, slot * PAD : (slot + 1) * PAD] = piece
                else:
                    wm_s[rows, :] = piece
        bias = bias_s[step][7:8]
        lanes = lax.broadcasted_iota(jnp.int32, (1, PAD), 1) - width
        spare = (lanes >= 0) & (lanes < heads * SEG) & (lax.rem(lanes + SEG, SEG) >= DOCS)
        vaug = jnp.where(spare & (lax.rem(lanes + SEG, SEG) < DOCS + 3), 1.0, 0.0).astype(BF16)

        @pl.loop(0, wides)
        def _(index):
            rows = rows_of(index, WIDE)
            x_rows = x_s[pl.ds(index * (WIDE // part), WIDE // part)].reshape(WIDE, model)
            result = dot_nn(x_rows, w_s[...])
            queries = (result[:, :PAD] + bias[:, :PAD]).astype(BF16)
            queries = (queries * jnp.asarray(HEAD**-0.5, BF16)).T
            side_ref[0, :width, rows] = queries[:width]
            side_ref[0, PAD + width :, rows] = jnp.zeros((PAD - width, WIDE), BF16)
            keys = result[:, PAD : 2 * PAD].astype(BF16)
            key_ref[rows, : PAD // 2] = keys[:, : PAD // 2]
            key_ref[rows, PAD // 2 :] = keys[:, PAD // 2 :] + kaug_s[rows, :]
            values = (result[:, 2 * PAD :] + bias[:, PAD : 2 * PAD]).astype(BF16)
            value_ref[rows, :] = values + vaug
            values_t = values.T
            for head in range(heads):
                vt_s[head, :HEAD, rows] = values_t[head_rows(head)]

        for head in range(heads):
            side_ref[0, extra_rows(head, width), :] = qdoc_s[...]
        side_ref[0, width + heads * SEG : PAD, :] = jnp.zeros(
            (PAD - width - heads * SEG, length), BF16
        )

        @pl.when(step == 1)
        def _():
            attn.advance_near(2)

        @pl.loop(0, blocks)
        def _(index):
            cols = rows_of(index)
            attended = attend_block(cols, width, key_ref, vt_s, side_ref.at[0])
            side_ref[0, PAD : PAD + width, cols] = attended
            rest = jnp.zeros((PAD - width, ROWS), BF16)
            mix_s[cols, :] = jnp.concatenate([attended, rest], axis=0).T

            @pl.when((step == 0) & (index == 0))
            def _():
                attn.cross_x().wait_recv()
                attn.start(2)

            @pl.when((step == 0) & (index == 1))
            def _():
                outer.advance(0)

            @pl.when((step == 0) & (index == 3))
            def _():
                inner.start(0)

            @pl.when((step == 1) & (index == 1))
            def _():
                attn.advance_far(2)

            @pl.when((step == 1) & (index == 3))
            def _():
                outer.wait_y(0)
                outer.to_core(0).start()
                inner.cross_x().wait_recv()
                inner.start(2)
                inner.along_y(2, 0).start()

            @pl.when((step == 2) & (index == 1))
            def _():
                inner.advance(0)

            @pl.when((step == 3) & (index == 2))
            def _():
                inner.advance(2)

            @pl.when((step == 3) & (index == 0))
            def _():
                for bits in (2, 3, 1):
                    exchange(COTS, cot_ref, cot_out, bits, True).start()

        @pl.loop(0, wides)
        def _(index):
            rows = rows_of(index, WIDE)
            first_s[rows, :] += dot_nt(mix_s[rows, :], wm_s[...])

    @pl.when(step == 4)
    def _():
        keep_first.start()

        @pl.loop(0, blocks)
        def _(index):
            rows = rows_of(index)
            unit, _inverse = norm_parts(first_s[rows, :])
            normed = unit * gain_one + bias_one
            low_s[rows, :] = normed.astype(BF16)
            second_s[rows, :] = normed + b_outer

        keep_low.start()
        inner.wait_y(0)
        inner.to_core(0).start()

    @pl.when(step == 5)
    def _():
        inner.to_core(0).wait_recv()
        outer.to_core(0).wait_recv()

    @pl.when(step == 6)
    def _():
        inner.wait_y(2)
        inner.to_core(2).start()
        outer.wait_x()
        outer.to_core(2).start()

    @pl.when(step == 7)
    def _():
        inner.to_core(2).wait_recv()
        outer.to_core(2).wait_recv()
        keep_i.start()
        keep_o.start()

    @pl.when(step >= 4)
    def _():
        slot = step - 4
        w_inner = i_s[slot].reshape(model, model)
        w_outer = o_s[slot].reshape(model, model)
        b_inner = bias_s[slot][6:7]

        @pl.loop(0, wides)
        def _(index):
            rows = rows_of(index, WIDE)
            value, slope = gelu_parts(dot_nn(low_s[rows, :], w_inner) + b_inner)
            hidden = value.astype(BF16)
            acts_ref[0, rows, :] = hidden
            slope_ref[0, rows, :] = slope.astype(BF16)
            second_s[rows, :] += dot_nt(hidden, w_outer)

    @pl.when(step == 7)
    def _():
        keep_second.start()
        for bits in (1, 2, 3):
            exchange(COTS, cot_ref, cot_out, bits, False).wait_recv()
        for gather in (attn, inner):
            gather.cross_x().wait_send()
            gather.wait_sent((0, 2))
        outer.wait_sent((0,))
        for bits in (1, 2, 3):
            exchange(TOKENS, tok_ref, x_s, bits, True).wait_send()
            exchange(COTS, cot_ref, cot_out, bits, True).wait_send()
            bias_copy(bits, True).wait_send()
        for copy in (
            own_cot, keep_x, keep_a, keep_i, keep_o, keep_first, keep_low, keep_second,
        ):
            copy.wait()


def dense_kernel(
    first_in, wi_ref, wo_ref, bi_ref, vec_ref, cot_ref,
    out_ref, dfirst_ref, dmix_ref, gi_ref, go_ref, dbi_ref, small_ref,
    first_ref, second_ref, normed_s, dsec_s, hidden_s, slope_s, low_s, low_t, back_t, dinner_s,
):
    step = pl.program_id(0)
    count = pl.num_programs(0) // 2
    length, model = first_in.shape
    blocks = length // ROWS
    gain_one, bias_one, b_outer, gain_two, bias_two = (vec_ref[i : i + 1, :] for i in range(5))

    @pl.when(step == 0)
    def _():
        copied = pltpu.sync_copy
        copied(first_in, first_ref)

        @pl.loop(0, blocks)
        def _(index):
            rows = rows_of(index)
            unit, _inverse = norm_parts(first_ref[rows, :])
            normed = unit * gain_one + bias_one
            normed_s[rows, :] = normed
            low_s[rows, :] = normed.astype(BF16)
            low_t[:, rows] = normed.astype(BF16).T
            second_ref[rows, :] = normed + b_outer

    @pl.when(step < count)
    def _():
        @pl.loop(0, blocks)
        def _(index):
            rows = rows_of(index)
            inner = dot_nn(low_s[rows, :], wi_ref[0]) + bi_ref[0]
            value, slope = gelu_parts(inner)
            hidden = value.astype(BF16)
            hidden_s[step, rows, :] = hidden
            slope_s[step, rows, :] = slope.astype(BF16)
            second_ref[rows, :] += dot_nt(hidden, wo_ref[0])

    @pl.when(step == count - 1)
    def _():
        small_ref[...] = jnp.zeros_like(small_ref)

        @pl.loop(0, blocks)
        def _(index):
            rows = rows_of(index)
            unit, inverse = norm_parts(second_ref[rows, :])
            out_ref[rows, :] = (unit * gain_two + bias_two).astype(BF16)
            grads = cot_ref[rows, :].astype(F32)
            d_second = norm_back(grads, gain_two, unit, inverse)
            small_ref[0:1, :] += column_sum(d_second)
            small_ref[1:2, :] += column_sum(grads * unit)
            small_ref[2:3, :] += column_sum(grads)
            dsec_s[rows, :] = d_second
            low = d_second.astype(BF16)
            dmix_ref[rows, :] = low
            back_t[:, rows] = low.T

    @pl.when(step >= count)
    def _():
        place = step - count
        dbi_ref[...] = jnp.zeros_like(dbi_ref)

        @pl.loop(0, blocks)
        def _(index):
            rows = rows_of(index)
            d_hidden = dot_nn(dmix_ref[rows, :], wo_ref[0])
            d_inner = (d_hidden * slope_s[place, rows, :].astype(F32)).astype(BF16)
            dinner_s[rows, :] = d_inner
            dbi_ref[0] += column_sum(d_inner.astype(F32))
            dsec_s[rows, :] += dot_nt(d_inner, wi_ref[0])

        @pl.loop(0, model // ROWS)
        def _(index):
            rows = rows_of(index)
            gi_ref[0, rows, :] = dot_nn(low_t[rows, :], dinner_s[...]).astype(gi_ref.dtype)
            go_ref[0, rows, :] = dot_nn(back_t[rows, :], hidden_s[place]).astype(go_ref.dtype)

    @pl.when(step == 2 * count - 1)
    def _():
        @pl.loop(0, blocks)
        def _(index):
            rows = rows_of(index)
            unit, inverse = norm_parts(first_ref[rows, :])
            grads = dsec_s[rows, :]
            d_first = norm_back(grads, gain_one, unit, inverse)
            small_ref[3:4, :] += column_sum(d_first)
            small_ref[4:5, :] += column_sum(grads * unit)
            small_ref[5:6, :] += column_sum(grads)
            dfirst_ref[rows, :] = d_first
            dmix_ref[rows, :] = d_first.astype(BF16)


def back_rows(rows, width, w_s, dmix_rows, q_ref, k_ref, v_ref, att_ref, kt_s, dq_s, dk_s, dv_s):
    lanes = lane_index((ROWS, PAD))
    queries = q_ref[rows, :]
    d_att = dot_nn(dmix_rows, w_s[3]).astype(BF16)
    product = d_att.astype(F32) * att_ref[rows, :].astype(F32)
    heads = range(width // HEAD)
    extended = d_att
    for head in heads:
        centre = jnp.sum(jnp.where(head_only(lanes, head), product, 0.0), axis=1, keepdims=True)
        for spot, part in enumerate(three_parts(-centre)):
            here = lanes == width + DOCS + 3 * head + spot
            extended = jnp.where(here, jnp.broadcast_to(part, (ROWS, PAD)), extended)
    chances_all = []
    d_scores_all = []
    d_att_all = []
    queries_all = []
    for head in heads:
        wide = head_and_extra(lanes, head, width)
        only = head_only(lanes, head)
        chances = jnp.exp2(dot_nt(k_ref[...], jnp.where(wide, queries, 0)) * LOG2E)
        d_chances = dot_nt(v_ref[...], jnp.where(wide, extended, 0))
        d_scores = (chances * d_chances).astype(BF16)
        chances_all.append(chances.astype(BF16))
        d_scores_all.append(d_scores)
        d_att_all.append(jnp.where(only, d_att, 0))
        queries_all.append(jnp.where(only, queries, 0))
        head_rows = slice(head * HEAD, (head + 1) * HEAD)
        dq_s[head_rows, rows] = dot_nn(kt_s[head_rows, :], d_scores)
    dv_s[...] += dot_nn(jnp.concatenate(chances_all, 1), jnp.concatenate(d_att_all, 0))
    dk_s[...] += dot_nn(jnp.concatenate(d_scores_all, 1), jnp.concatenate(queries_all, 0))


def back_low(rows, width, dq_s, dk_s, dv_s, low_s):
    d_query = (dq_s[:, rows].T * HEAD**-0.5).astype(BF16)
    d_query = jnp.where(lane_index(d_query.shape) < width, d_query, 0)
    d_value = dv_s[rows, :].astype(BF16)
    low_s[rows, :PAD] = d_query
    low_s[rows, PAD : 2 * PAD] = dk_s[rows, :].astype(BF16)
    low_s[rows, 2 * PAD :] = d_value
    return column_sum(d_query.astype(F32)), column_sum(d_value.astype(F32))


def back_tokens(rows, w_s, low_s):
    return sum(dot_nt(low_s[rows, slot * PAD : (slot + 1) * PAD], w_s[slot]) for slot in range(3))


def back_weights(rows, width, slots, xt_s, dmixt_s, low_s, att_ref):
    parts = []
    for slot in slots:
        if slot < 3:
            part = dot_nn(xt_s[rows, :], low_s[:, slot * PAD : (slot + 1) * PAD])
        else:
            part = dot_nn(dmixt_s[rows, :], att_ref[...])
        parts.append(part[:, :width])
    return jnp.concatenate(parts, axis=1).astype(BF16)


def attend_back_kernel(
    x_ref, a_ref, dmix_ref, dfirst_ref, q_ref, k_ref, v_ref, att_ref,
    dtok_ref, ga_ref, dbq_ref, dbv_ref,
    w_s, xt_s, dmixt_s, kt_s, dq_s, dk_s, dv_s, low_s,
):
    length, model = x_ref.shape
    width = a_ref.shape[2] // 4
    blocks = length // ROWS
    for slot in range(4):
        w_s[slot] = unpack(a_ref.at[0], slot, width)

    @pl.when(pl.program_id(0) == 0)
    def _():
        dtok_ref[...] = dfirst_ref[...]

        @pl.loop(0, blocks)
        def _(index):
            rows = rows_of(index)
            xt_s[:, rows] = x_ref[rows, :].T
            dmixt_s[:, rows] = dmix_ref[rows, :].T

    for sums in (dk_s, dv_s, dbq_ref, dbv_ref):
        sums[...] = jnp.zeros_like(sums)

    @pl.loop(0, blocks)
    def _(index):
        rows = rows_of(index)
        kt_s[:, rows] = k_ref[0, rows, :].T

    @pl.loop(0, blocks)
    def _(index):
        rows = rows_of(index)
        dmix_rows = dmix_ref[rows, :]
        refs = (ref.at[0] for ref in (q_ref, k_ref, v_ref, att_ref))
        back_rows(rows, width, w_s, dmix_rows, *refs, kt_s, dq_s, dk_s, dv_s)

    @pl.loop(0, blocks)
    def _(index):
        rows = rows_of(index)
        for_query, for_value = back_low(rows, width, dq_s, dk_s, dv_s, low_s)
        dbq_ref[0] += for_query
        dbv_ref[0] += for_value
        dtok_ref[rows, :] += back_tokens(rows, w_s, low_s)

    @pl.loop(0, model // ROWS)
    def _(index):
        rows = rows_of(index)
        ga_ref[0, rows, :] = back_weights(
            rows, width, range(4), xt_s, dmixt_s, low_s, att_ref.at[0]
        )


def add_into(target, source):
    target[...] = (target[...].astype(F32) + source[...].astype(F32)).astype(target.dtype)


class Reduce:
    COUNT = 11

    def __init__(self, wires, base, held, core, by_y, by_z, by_x, cols=slice(None)):
        self.wires, self.base, self.held, self.core = wires, base, held, core
        self.by_y, self.by_z, self.by_x = by_y, by_z, by_x
        self.cols = cols
        self.z, self.y = lax.div(wires.row, 2), lax.rem(wires.row, 2)

    def part(self, ref, *index):
        return ref.at[index + (slice(None), self.cols)]

    def core_copy(self, j, source):
        everything = (slice(None), slice(None))
        return self.wires.copy(
            self.base + j, self.part(source, *everything), self.part(self.core, j, *everything), 1, 0
        )

    def add_core(self, j):
        self.core_copy(j, self.held.at[j]).wait_recv()
        for z in range(4):
            for y in range(2):
                add_into(self.part(self.held, j, z, y), self.part(self.core, j, z, y))

    def y_copy(self, j):
        source = self.part(self.held, j, slice(None), 1 - self.y)
        return self.wires.copy(
            self.base + 2 + j, source, self.part(self.by_y, j, slice(None)), 0, 1
        )

    def add_y(self, j):
        self.y_copy(j).wait_recv()
        for z in range(4):
            add_into(self.part(self.held, j, z, self.y), self.part(self.by_y, j, z))

    def z_copy(self, j, step):
        other = lax.div(partner(self.wires.row, 2 * step, 8), 2)
        number = self.base + 4 + 3 * j + step - 1
        return self.wires.copy(
            number, self.part(self.held, j, other, self.y), self.part(self.by_z, j, step - 1),
            0, 2 * step,
        )

    def start_z(self, j):
        for step in (1, 2, 3):
            self.z_copy(j, step).start()

    def total_z(self, j):
        total = self.part(self.held, j, self.z, self.y)[...].astype(F32)
        for step in (1, 2, 3):
            self.z_copy(j, step).wait_recv()
            total = total + self.part(self.by_z, j, step - 1)[...].astype(F32)
        return total

    def x_copy(self):
        source = self.part(self.held, 1, self.z, self.y)
        return self.wires.copy(self.base + 10, source, self.part(self.by_x), 2, 0)

    def send_x(self):
        self.part(self.held, 1, self.z, self.y)[...] = self.total_z(1).astype(BF16)
        self.x_copy().start()

    def total(self):
        self.x_copy().wait_recv()
        return self.total_z(0) + self.part(self.by_x)[...].astype(F32)

    def whole_x_copy(self):
        return self.wires.copy(self.base + 10, self.held.at[1], self.by_x, 2, 0)

    def add_whole_x(self):
        self.whole_x_copy().wait_recv()
        for z in range(4):
            for y in range(2):
                add_into(self.held.at[0, z, y], self.by_x.at[z, y])

    def wait_sent(self, j_all):
        for j in j_all:
            self.y_copy(j).wait_send()
            for step in (1, 2, 3):
                self.z_copy(j, step).wait_send()


OUTPUTS, TOKEN_GRADS, SUMS, LATE_SUMS = 0, 3, 6, 16
RED_I = 26
RED_O = RED_I + Reduce.COUNT
RED_A = RED_O + Reduce.COUNT
BACKWARD_WIRES = RED_A + 3 * Reduce.COUNT
BACK_PEERS = PEERS + ((0, 3), (0, 5), (0, 7))


def slot_at(step):
    return jnp.where(step < 2, 3 - 2 * step, 6 - 2 * step)


def backward_kernel(
    acts_ref, side_ref, slope_ref, wia_ref, wo_ref, vec_ref, second_ref, first_ref, low_ref, xt_ref,
    cot_ref,
    out_res, dtok_res, ga_res, gi_res, go_res, sum_res, late_res,
    low_t, back_t, dmix_s, low_s, flow_s, out_s, grad_s, first_s, wmt_s, do_s, kt_s, all_t, dk_t,
    dv_t, sums_s, sums_o, sums_d, late_o, late_t, late_d,
    send_i, held_i, core_i, y_i, z_i, x_i, send_o, held_o, core_o, y_o, z_o, x_o,
    held_a, core_a, y_a, z_a, x_a,
    send_sem, recv_sem, here_sem,
):
    step = pl.program_id(0)
    place = lax.axis_index("tensor")
    row = lax.axis_index("dp")
    length, model = dmix_s.shape
    quarters, part, _ = flow_s.shape
    width = wia_ref.shape[2] // 4
    heads = width // HEAD
    blocks = length // ROWS
    wides = length // WIDE
    share = held_i.shape[3]
    wires = Wires(send_sem, recv_sem, place, row)
    inner = Reduce(wires, RED_I, held_i, core_i, y_i, z_i, x_i)
    outer = Reduce(wires, RED_O, held_o, core_o, y_o, z_o, x_o)
    halves = (slice(0, model // 2), slice(model // 2, model))
    send_a = send_i
    thirds = [slice(number * PAD, (number + 1) * PAD) for number in range(model // PAD)]
    attn = [
        Reduce(wires, RED_A + number * Reduce.COUNT, held_a, core_a, y_a, z_a, x_a, cols)
        for number, cols in enumerate(thirds)
    ]
    ready = (attn[:1], attn[1:])
    gain_one, gain_two, bias_two = (vec_ref[i : i + 1, :] for i in (1, 4, 5))
    key_ref, value_ref = (acts_ref.at[0, :, i * PAD : (i + 1) * PAD] for i in range(2))
    att_ref = side_ref.at[0, PAD : PAD + width]

    def exchange(base, source, target, bits, mine):
        other = partner(place, bits, 4)
        return wires.copy(
            base + bits - 1, source.at[other], target.at[place if mine else other], bits, 0
        )

    def by_tensor(bits):
        return wires.copy(
            SUMS + bits - 1, sums_s.at[place], sums_s.at[place], bits, 0
        )

    def by_rows(base, kept, bits):
        return wires.copy(base + 2 + bits, kept.at[row], kept.at[row], 0, bits)

    def late_copy(bits):
        return wires.copy(LATE_SUMS + bits - 1, late_o.at[bits], late_t.at[bits], bits, 0)

    def sum_rows(base, kept):
        for bits in range(1, 8):
            by_rows(base, kept, bits).wait_recv()
        return sum((kept[number] for number in range(1, 8)), kept[0])

    load_second = pltpu.make_async_copy(second_ref, grad_s, here_sem.at[0])
    load_cot = pltpu.make_async_copy(cot_ref, flow_s, here_sem.at[1])
    load_low = pltpu.make_async_copy(low_ref, low_s, here_sem.at[2])
    load_x = pltpu.make_async_copy(xt_ref, low_t, here_sem.at[3])
    keep_out = pltpu.make_async_copy(out_s.at[place], out_res.at[place], here_sem.at[4])
    keep_dtok = pltpu.make_async_copy(flow_s.at[place], dtok_res.at[place], here_sem.at[5])

    def load_first(index):
        return pltpu.make_async_copy(
            first_ref.at[rows_of(index)], first_s.at[index % 2], here_sem.at[6 + index % 2]
        )

    order = (3, 1, 2, 0)

    @pl.when(step == 0)
    def _():
        load_second.start()
        load_cot.start()
        load_low.start()
        sums_s[place] = jnp.zeros_like(sums_s[0])
        for bits in range(4):
            late_o[bits] = jnp.zeros_like(late_o[0])
        greet(wires, BACK_PEERS)
        load_second.wait()
        load_cot.wait()
        load_low.wait()

        @pl.loop(0, quarters)
        def _(index):
            rows = rows_of(index, part)
            low_t[:, rows] = low_s[rows, :].T
            unit, inverse = norm_parts(grad_s[rows, :])
            out_s[index] = (unit * gain_two + bias_two).astype(BF16)
            grads = flow_s[index].astype(F32)
            d_second = norm_back(grads, gain_two, unit, inverse)
            sums_s[place, 8:9, :] += column_sum(d_second)
            sums_s[place, 9:10, :] += column_sum(grads * unit)
            sums_s[place, 10:11, :] += column_sum(grads)
            grad_s[rows, :] = d_second
            lower = d_second.astype(BF16)
            dmix_s[rows, :] = lower
            back_t[:, rows] = lower.T

        for bits in (2, 3, 1):
            exchange(OUTPUTS, out_s, out_res, bits, True).start()
        keep_out.start()

    @pl.when(step < 4)
    def _():
        @pl.loop(0, wides)
        def _(index):
            rows = rows_of(index, WIDE)
            d_hidden = dot_nn(dmix_s[rows, :], wo_ref[0])
            d_inner = (d_hidden * slope_ref[0, rows, :].astype(F32)).astype(BF16)
            low_s[rows, :] = d_inner
            for_inner = column_sum(d_inner.astype(F32))
            for number, bits in enumerate(order):

                @pl.when(step == number)
                def _(bits=bits):
                    sums_s[place, pl.ds(partner(place, bits, 4), 1), :] += for_inner

            grad_s[rows, :] += dot_nt(d_inner, wia_ref[0])

        for transposed, right, sent, held in (
            (back_t, acts_ref.at[0], send_o, held_o), (low_t, low_s, send_i, held_i),
        ):
            grads = dot_nn(transposed[...], right[...]).astype(BF16)
            pieces = grads.reshape(4, 2, share, model)

            @pl.when(step < 2)
            def _(pieces=pieces, sent=sent):
                sent[step] = pieces

            @pl.when(step >= 2)
            def _(pieces=pieces, held=held):
                held[3 - step] = pieces

    for number, j in ((0, 1), (1, 0)):

        @pl.when(step == number)
        def _(number=number, j=j):
            outer.core_copy(j, send_o.at[number]).start()
            inner.core_copy(j, send_i.at[number]).start()

    @pl.when(step == 2)
    def _():
        load_first(0).start()
        load_first(1).start()
        outer.add_core(1)
        outer.whole_x_copy().start()
        inner.add_core(1)
        inner.y_copy(1).start()

    @pl.when(step == 3)
    def _():
        inner.add_core(0)
        inner.y_copy(0).start()
        outer.add_core(0)
        load_x.start()
        for index in range(blocks):
            rows = slice(index * ROWS, (index + 1) * ROWS)
            load_first(index).wait()
            unit, inverse = norm_parts(first_s[index % 2])
            if index + 2 < blocks:
                load_first(index + 2).start()
            grads = grad_s[rows, :]
            d_first = norm_back(grads, gain_one, unit, inverse)
            sums_s[place, 11:12, :] += column_sum(d_first)
            sums_s[place, 12:13, :] += column_sum(grads * unit)
            sums_s[place, 13:14, :] += column_sum(grads)
            grad_s[rows, :] = d_first
            lower = d_first.astype(BF16)
            dmix_s[rows, :] = lower
            back_t[:, rows] = lower.T
        load_x.wait()
        for bits in (1, 2, 3):
            by_tensor(bits).start()

    @pl.when(step == 4)
    def _():
        for number, j in ((0, 1), (1, 0)):
            inner.core_copy(j, send_i.at[number]).wait_send()

    @pl.when(step >= 4)
    def _():
        wmt_s[...] = wia_ref[0, :, 3 * width :].T
        for sums in (dk_t, dv_t):
            sums[...] = jnp.zeros_like(sums)

        @pl.loop(0, wides)
        def _(index):
            cols = rows_of(index, WIDE)
            kt_s[:, cols] = key_ref[cols, :].T[:width]
            d_att = dot_nn(wmt_s[...], back_t[:, cols]).astype(BF16)
            do_s[:width, cols] = d_att
            product = d_att.astype(F32) * att_ref[:, cols].astype(F32)
            none = jnp.zeros((DOCS, WIDE), BF16)
            for head in range(heads):
                centre = column_sum(product[head_rows(head)])
                do_s[extra_rows(head, width), cols] = parts_rows(-centre, none)

        @pl.loop(0, blocks)
        def _(index):
            attend_block_back(
                rows_of(index), width, key_ref, value_ref, side_ref.at[0], do_s, kt_s, all_t,
                dk_t, dv_t,
            )

            @pl.when((step == 4) & (index == 0))
            def _():
                inner.add_y(1)
                inner.start_z(1)

            @pl.when((step == 5) & (index == 0))
            def _():
                inner.add_y(0)
                inner.start_z(0)
                outer.add_whole_x()
                outer.y_copy(0).start()

            @pl.when((step == 5) & (index == 1))
            def _():
                inner.send_x()
                for bits in (1, 2, 3):
                    by_tensor(bits).wait_recv()
                sums_o[...] = sums_s[0] + sums_s[1] + sums_s[2] + sums_s[3]
                sums_d[row, :6, :] = sums_o[8:14, :]
                sums_d[row, 6:7, :] = sums_o[pl.ds(place, 1), :]
                sums_d[row, 7:, :] = jnp.zeros((1, model), F32)
                for bits in range(1, 8):
                    by_rows(SUMS, sums_d, bits).start()

            @pl.when((step == 7) & (index == 1))
            def _():
                sum_res[...] = sum_rows(SUMS, sums_d)

            @pl.when((step == 6) & (index == 1))
            def _():
                outer.add_y(0)
                outer.start_z(0)

            @pl.when((step == 6) & (index == 1))
            def _():
                gi_res[...] = inner.total()

            @pl.when((step == 7) & (index == 2))
            def _():
                go_res[...] = outer.total_z(0)

            for number, reduce in zip((0, 1, 3), attn):

                @pl.when((step == 7) & (index == number))
                def _(reduce=reduce):
                    reduce.add_y(1)
                    reduce.start_z(1)

        all_t[width : 2 * width, :] = dk_t[...].astype(BF16)
        all_t[2 * width :, :] = dv_t[...].astype(BF16)
        for_all = dot_nt(jnp.ones((8, length), BF16), all_t[...])
        for number, bits in enumerate(order):

            @pl.when(step == 4 + number)
            def _(bits=bits):
                late_o[bits, :, : 3 * width] = for_all
                if bits:
                    late_copy(bits).start()
                    return
                for other in (1, 2, 3):
                    late_copy(other).wait_recv()
                late_d[row] = late_o[0] + late_t[1] + late_t[2] + late_t[3]
                for other in range(1, 8):
                    by_rows(LATE_SUMS, late_d, other).start()

        for half, cols in enumerate(halves):

            @pl.loop(0, model // (4 * share))
            def _(pair):
                rows = rows_of(pair, 4 * share)
                if half == 0:
                    grads = dot_nt(low_t[rows, :], all_t[: 2 * width, :])
                else:
                    for_value = dot_nt(low_t[rows, :], all_t[2 * width :, :])
                    for_mixer = dot_nt(back_t[rows, :], att_ref[...])
                    grads = jnp.concatenate([for_value, for_mixer], axis=1)
                pieces = grads.astype(BF16).reshape(2, 2, share, model // 2)

                @pl.when(step < 6)
                def _(pieces=pieces):
                    send_a[step - 4, pl.ds(2 * pair, 2), :, :, cols] = pieces

                @pl.when(step >= 6)
                def _(pieces=pieces):
                    held_a[7 - step, pl.ds(2 * pair, 2), :, :, cols] = pieces

            for number, j in ((0, 1), (1, 0)):

                @pl.when(step == 4 + number)
                def _(number=number, j=j):
                    for reduce in ready[half]:
                        reduce.core_copy(j, send_a.at[number]).start()

            for j in (1, 0):

                @pl.when(step == 7 - j)
                def _(j=j):
                    for reduce in ready[half]:
                        reduce.add_core(j)
                        reduce.y_copy(j).start()

            if half == 0:

                @pl.loop(0, wides)
                def _(index):
                    rows = rows_of(index, WIDE)
                    transposed = all_t[:, rows].T
                    grad_s[rows, :] += dot_nt(transposed, wia_ref[0, :, : 3 * width])

                    @pl.when(step == 7)
                    def _():
                        places = pl.ds(index * (WIDE // part), WIDE // part)
                        flow_s[places] = grad_s[rows, :].astype(BF16).reshape(WIDE // part, part, model)

                @pl.when(step == 7)
                def _():
                    for bits in (2, 3, 1):
                        exchange(TOKEN_GRADS, flow_s, dtok_res, bits, True).start()
                    keep_dtok.start()


    @pl.when(step == 7)
    def _():
        for reduce in attn:
            reduce.add_y(0)
            reduce.start_z(0)
            reduce.send_x()
        late_res[...] = sum_rows(LATE_SUMS, late_d)
        for reduce, cols in zip(attn, thirds):
            ga_res[:, cols] = reduce.total()
        for bits in (1, 2, 3):
            for base, source, target in (
                (OUTPUTS, out_s, out_res), (TOKEN_GRADS, flow_s, dtok_res),
            ):
                exchange(base, source, target, bits, False).wait_recv()
                exchange(base, source, target, bits, True).wait_send()
        keep_out.wait()
        keep_dtok.wait()
        for bits in (1, 2, 3):
            by_tensor(bits).wait_send()
            late_copy(bits).wait_send()
        for bits in range(1, 8):
            by_rows(SUMS, sums_d, bits).wait_send()
            by_rows(LATE_SUMS, late_d, bits).wait_send()
        for number, j in ((0, 1), (1, 0)):
            outer.core_copy(j, send_o.at[number]).wait_send()
            for reduce in attn:
                reduce.core_copy(j, send_a.at[number]).wait_send()
        inner.wait_sent((0, 1))
        inner.x_copy().wait_send()
        outer.wait_sent((0,))
        outer.whole_x_copy().wait_send()
        for reduce in attn:
            reduce.wait_sent((0, 1))
            reduce.x_copy().wait_send()


VMEM_LIMIT = 62 * 1024 * 1024


def resident(shape):
    return pl.BlockSpec(shape, lambda step: (0,) * len(shape))


def stepped(shape):
    return pl.BlockSpec((1,) + shape[1:], lambda step: (step,) + (0,) * (len(shape) - 1))


def spec_list(pairs):
    return [stepped(shape) if moves else resident(shape) for shape, moves in pairs]


def near_forward(tokens, cotangent, shard_i, w_query, w_key, w_value, w_mixer, w_outer, docs, vectors):
    groups, part, model = tokens.shape
    length = groups * part
    share, width = w_query.shape
    whole = (groups, model // share, share, model)
    sides = (groups, 2 * PAD, length)
    slopes = (groups, length, model)
    flat = (length, model)
    shard = (share, model)
    biases = (groups,) + vectors.shape
    anywhere = pl.BlockSpec(memory_space=pl.ANY)

    def early(shape):
        return pl.BlockSpec(
            (1,) + shape[1:], lambda step: (jnp.minimum(step, 3),) + (0,) * (len(shape) - 1)
        )

    def late(shape):
        return pl.BlockSpec(
            (1,) + shape[1:], lambda step: (jnp.maximum(step - 4, 0),) + (0,) * (len(shape) - 1)
        )

    def vmem(*shape, kind=BF16):
        return pltpu.VMEM(shape, kind)

    kept = [w_query, w_key, w_value, w_mixer, w_outer, docs, vectors]
    return pl.pallas_call(
        forward_kernel,
        grid=(2 * groups,),
        out_shape=[
            jax.ShapeDtypeStruct((2 * groups, length, model), BF16),
            jax.ShapeDtypeStruct(sides, BF16),
            jax.ShapeDtypeStruct(slopes, BF16),
            jax.ShapeDtypeStruct(flat, F32),
            jax.ShapeDtypeStruct(flat, F32),
            jax.ShapeDtypeStruct(flat, BF16),
            jax.ShapeDtypeStruct((model, length), BF16),
            jax.ShapeDtypeStruct(tokens.shape, BF16),
            jax.ShapeDtypeStruct((2,) + whole, BF16),
            jax.ShapeDtypeStruct(whole, BF16),
        ],
        in_specs=[anywhere] * 3 + [resident(each.shape) for each in kept],
        out_specs=[stepped((2 * groups, length, model)), early(sides), late(slopes)]
        + [anywhere] * 7,
        scratch_shapes=[
            vmem(*shard), vmem(*shard), vmem(model, 3 * PAD), vmem(model, PAD),
            vmem(*tokens.shape), vmem(model, length), vmem(*whole), vmem(*whole), vmem(*whole),
            vmem(*biases, kind=F32), vmem(length, PAD // 2), vmem(SEG, length),
            vmem(width // HEAD, HEAD + SEG, length), vmem(length, PAD),
            vmem(*flat, kind=F32), vmem(*flat, kind=F32), vmem(*flat),
            pltpu.SemaphoreType.DMA((FORWARD_WIRES,)),
            pltpu.SemaphoreType.DMA((FORWARD_WIRES,)),
            pltpu.SemaphoreType.DMA((13,)),
        ],
        compiler_params=pltpu.CompilerParams(
            vmem_limit_bytes=VMEM_LIMIT, collective_id=0, has_side_effects=True
        ),
        name="near_forward",
    )(tokens, cotangent, shard_i, *kept)


def attend_plain(x, a_all, biases, qaug, kaug, vaug, b_mixer):
    length, model = x.shape
    groups = a_all.shape[0]
    block = (groups, length, PAD)
    return pl.pallas_call(
        attend_plain_kernel,
        grid=(groups,),
        out_shape=[jax.ShapeDtypeStruct(block, BF16)] * 4 + [jax.ShapeDtypeStruct(x.shape, F32)],
        in_specs=spec_list(
            [
                (x.shape, 0), (a_all.shape, 1), (biases.shape, 1),
                (qaug.shape, 0), (kaug.shape, 0), (vaug.shape, 0), (b_mixer.shape, 0),
            ]
        ),
        out_specs=spec_list([(block, 1)] * 4 + [(x.shape, 0)]),
        scratch_shapes=[pltpu.VMEM((4, model, PAD), BF16)],
        compiler_params=pltpu.CompilerParams(vmem_limit_bytes=VMEM_LIMIT),
        name="attend_plain",
    )(x, a_all, biases, qaug, kaug, vaug, b_mixer)


def dense_both(first_sum, wi, wo, bi, vectors, cotangent):
    length, model = first_sum.shape
    groups, _, hidden = wi.shape
    grad = (groups, model, hidden)
    forth = lambda shape: pl.BlockSpec(
        (1,) + shape[1:], lambda step: (lax.rem(step, groups),) + (0,) * (len(shape) - 1)
    )
    late = lambda shape: pl.BlockSpec(
        (1,) + shape[1:], lambda step: (jnp.maximum(step - groups, 0),) + (0,) * (len(shape) - 1)
    )
    return pl.pallas_call(
        dense_kernel,
        grid=(2 * groups,),
        out_shape=[
            jax.ShapeDtypeStruct((length, model), BF16),
            jax.ShapeDtypeStruct((length, model), F32),
            jax.ShapeDtypeStruct((length, model), BF16),
            jax.ShapeDtypeStruct(grad, BF16),
            jax.ShapeDtypeStruct(grad, BF16),
            jax.ShapeDtypeStruct((groups, 1, hidden), F32),
            jax.ShapeDtypeStruct((8, model), F32),
        ],
        in_specs=[
            pl.BlockSpec(memory_space=pl.ANY), forth(wi.shape), forth(wo.shape), forth(bi.shape),
            resident(vectors.shape), resident(cotangent.shape),
        ],
        out_specs=[
            resident((length, model)), resident((length, model)), resident((length, model)),
            late(grad), late(grad), late((groups, 1, hidden)), resident((8, model)),
        ],
        scratch_shapes=[
            pltpu.VMEM((length, model), F32),
            pltpu.VMEM((length, model), F32),
            pltpu.VMEM((length, model), F32),
            pltpu.VMEM((length, model), F32),
            pltpu.VMEM((groups, length, hidden), BF16),
            pltpu.VMEM((groups, length, hidden), BF16),
            pltpu.VMEM((length, model), BF16),
            pltpu.VMEM((model, length), BF16),
            pltpu.VMEM((model, length), BF16),
            pltpu.VMEM((length, hidden), BF16),
        ],
        compiler_params=pltpu.CompilerParams(vmem_limit_bytes=VMEM_LIMIT),
        name="dense_both",
    )(first_sum, wi, wo, bi, vectors, cotangent)


def attend_backward(x, a_all, d_mixed, d_first, q, k, v, attended):
    length, model = x.shape
    groups = a_all.shape[0]
    sums = (groups, 1, PAD)
    return pl.pallas_call(
        attend_back_kernel,
        grid=(groups,),
        out_shape=[
            jax.ShapeDtypeStruct(x.shape, F32),
            jax.ShapeDtypeStruct(a_all.shape, BF16),
            jax.ShapeDtypeStruct(sums, F32),
            jax.ShapeDtypeStruct(sums, F32),
        ],
        in_specs=spec_list(
            [
                (x.shape, 0), (a_all.shape, 1), (d_mixed.shape, 0), (d_first.shape, 0),
                (q.shape, 1), (k.shape, 1), (v.shape, 1), (attended.shape, 1),
            ]
        ),
        out_specs=spec_list([(x.shape, 0), (a_all.shape, 1), (sums, 1), (sums, 1)]),
        scratch_shapes=[
            pltpu.VMEM((4, model, PAD), BF16),
            pltpu.VMEM((model, length), BF16),
            pltpu.VMEM((model, length), BF16),
            pltpu.VMEM((PAD, length), BF16),
            pltpu.VMEM((PAD, length), F32),
            pltpu.VMEM((length, PAD), F32),
            pltpu.VMEM((length, PAD), F32),
            pltpu.VMEM((length, 3 * PAD), BF16),
        ],
        compiler_params=pltpu.CompilerParams(vmem_limit_bytes=VMEM_LIMIT),
        name="attend_backward",
    )(x, a_all, d_mixed, d_first, q, k, v, attended)


def near_backward(acts, sides, slopes, w_ia, w_o, vectors, second, first, low, xt, cotangent):
    quarters, part, model = cotangent.shape
    length = quarters * part
    share = model // 8
    width = model // 4
    block = (4, 2, share, model)
    anywhere = pl.BlockSpec(memory_space=pl.ANY)

    def ordered(shape, place):
        return pl.BlockSpec(
            (1,) + shape[1:], lambda step: (place(step),) + (0,) * (len(shape) - 1)
        )

    def acts_at(step):
        return jnp.where(step < 4, 4 + slot_at(step), slot_at(step - 4))

    def weights_at(step):
        return jnp.where(step < 4, slot_at(step), 4 + slot_at(step - 4))

    def first_half(step):
        return slot_at(jnp.minimum(step, 3))

    def last_half(step):
        return slot_at(jnp.maximum(step - 4, 0))

    def vmem(*shape, kind=BF16):
        return pltpu.VMEM(shape, kind)

    final = [
        ((share, model), F32), ((share, model), F32), ((share, model), F32), ((8, model), F32),
        ((8, model), F32),
    ]
    return pl.pallas_call(
        backward_kernel,
        grid=(8,),
        out_shape=[jax.ShapeDtypeStruct(cotangent.shape, BF16)] * 2
        + [jax.ShapeDtypeStruct(*each) for each in final],
        in_specs=[
            ordered(acts.shape, acts_at), ordered(sides.shape, last_half),
            ordered(slopes.shape, first_half), ordered(w_ia.shape, weights_at),
            ordered(w_o.shape, first_half), resident(vectors.shape),
        ]
        + [anywhere] * 5,
        out_specs=[anywhere] * 2 + [resident(each[0]) for each in final],
        scratch_shapes=[
            vmem(model, length), vmem(model, length), vmem(length, model), vmem(length, model),
            vmem(*cotangent.shape), vmem(*cotangent.shape), vmem(length, model, kind=F32),
            vmem(2, ROWS, model, kind=F32),
            vmem(width, model), vmem(PAD, length), vmem(width, length), vmem(3 * width, length),
            vmem(width, length, kind=F32), vmem(width, length, kind=F32),
            vmem(4, 16, model, kind=F32), vmem(16, model, kind=F32), vmem(8, 8, model, kind=F32),
            vmem(4, 8, model, kind=F32), vmem(4, 8, model, kind=F32), vmem(8, 8, model, kind=F32),
            vmem(2, *block), vmem(2, *block), vmem(2, *block), vmem(2, 4, share, model),
            vmem(2, 3, share, model), vmem(share, model),
            vmem(2, *block), vmem(2, *block), vmem(2, *block), vmem(1, 4, share, model),
            vmem(1, 3, share, model), vmem(*block),
            vmem(2, *block), vmem(2, *block), vmem(2, 4, share, model),
            vmem(2, 3, share, model), vmem(share, model),
            pltpu.SemaphoreType.DMA((BACKWARD_WIRES,)),
            pltpu.SemaphoreType.DMA((BACKWARD_WIRES,)),
            pltpu.SemaphoreType.DMA((8,)),
        ],
        compiler_params=pltpu.CompilerParams(
            vmem_limit_bytes=VMEM_LIMIT, collective_id=1, has_side_effects=True
        ),
        name="near_backward",
    )(acts, sides, slopes, w_ia, w_o, vectors, second, first, low, xt, cotangent)


def augment(labels, width):
    length = labels.shape[0]
    lanes = lax.broadcasted_iota(jnp.int32, (length, PAD), 1)
    in_docs = (lanes >= width) & (lanes < width + DOCS)
    same = (lanes - width) == labels[:, None]
    qaug = jnp.where(in_docs & same, 1.0, 0.0).astype(BF16)
    spare = (lanes >= width + DOCS) & (lanes < width + DOCS + 3 * (width // HEAD))
    kaug = jnp.where(in_docs & ~same, -(2.0**100), jnp.where(spare, 1.0, 0.0)).astype(BF16)
    vaug = jnp.where((lanes[:1] == width) | spare[:1], 1.0, 0.0).astype(BF16)
    return qaug, kaug, vaug


def body(
    tokens, doc_ids, w_query, b_query, w_key, w_value, b_value, w_mixer, b_mixer, gain_one,
    bias_one, w_inner, b_inner, w_outer, b_outer, gain_two, bias_two, cotangent,
):
    groups = lax.axis_size("tensor")
    rings = lax.axis_size("dp")
    place = lax.axis_index("tensor")
    width = w_query.shape[1]
    hidden = w_inner.shape[1]
    length = doc_ids.shape[2]
    model = tokens.shape[3]
    near = groups == 4 and rings == 8 and hidden == model and 4 * width == model

    if near:
        spare = jnp.zeros((PAD - width,), F32)
        vectors = jnp.concatenate(
            [
                b_mixer, gain_one, bias_one, b_outer, gain_two, bias_two, b_inner,
                b_query, spare, b_value, spare, jnp.zeros((PAD,), F32),
            ]
        ).reshape(8, model)
        acts, sides, slopes, first, second, low, xt, cot, w_ia, w_o = near_forward(
            tokens[:, 0], cotangent[:, 0], w_inner, w_query, w_key, w_value, w_mixer, w_outer.T,
            doc_ids, vectors,
        )
        out, d_tokens, ga, gi, go, tail, late = near_backward(
            acts, sides, slopes, w_ia.reshape(2 * groups, model, model),
            w_o.reshape(groups, model, model), vectors, second, first, low, xt, cot,
        )
        dbq, dbv = late[0, :width], late[0, 2 * width : 3 * width]
        dbi = tail[6]
        out, d_tokens = out[:, None], d_tokens[:, None].astype(F32)
    else:

        def gather(shard):
            whole = lax.all_gather(shard, ("tensor", "dp"), axis=0, tiled=True)
            return whole.reshape(groups, model, shard.shape[1])

        def to_sequence(part):
            return lax.all_to_all(part, "tensor", 0, 2, tiled=True).reshape(length, model)

        def from_sequence(whole):
            return lax.all_to_all(whole.reshape(1, 1, length, model), "tensor", 2, 0, tiled=True)

        def scatter(part):
            flat = part.reshape(-1, part.shape[2])
            total = lax.psum_scatter(flat, ("tensor", "dp"), scatter_dimension=0, tiled=True)
            return total.astype(F32)

        labels = lax.dynamic_index_in_dim(doc_ids[:, 0], place, 0, keepdims=False)
        qaug, kaug, vaug = augment(labels, width)
        shard_a = jnp.concatenate([w_query, w_key, w_value, w_mixer.T], axis=1)
        shard_o = w_outer.T
        spare = jnp.zeros((PAD - width,), F32)
        biases = jnp.concatenate([b_query, spare, b_value, spare, b_inner])[None]
        vectors = jnp.stack([gain_one, bias_one, b_outer, gain_two, bias_two] + [b_outer] * 3)
        x, cot = to_sequence(tokens), to_sequence(cotangent)
        a_all, wi, wo = gather(shard_a), gather(w_inner), gather(shard_o)
        every = lax.all_gather(biases, "tensor", axis=0)
        *saved, first_sum = attend_plain(x, a_all, every, qaug, kaug, vaug, b_mixer[None])
        out, d_first, d_mixed, g_inner, g_outer, dbi, small = dense_both(
            first_sum, wi, wo, every[:, :, 2 * PAD :], vectors, cot
        )
        d_tokens, g_attend, dbq, dbv = attend_backward(x, a_all, d_mixed, d_first, *saved)
        ga, gi, go = scatter(g_attend), scatter(g_inner), scatter(g_outer)
        rows = [dbq[:, 0, :width], dbv[:, 0, :width], dbi[:, 0], small]
        summed = lax.psum(jnp.concatenate([part.reshape(-1) for part in rows]), ("dp", "tensor"))
        own = lambda start, size: lax.dynamic_slice_in_dim(summed, start + place * size, size)
        dbq, dbv, dbi = own(0, width), own(model, width), own(2 * model, hidden)
        tail = summed[-small.size :].reshape(small.shape)
        out, d_tokens = from_sequence(out), from_sequence(d_tokens)
    return (
        out,
        d_tokens,
        ga[:, :width],
        dbq,
        ga[:, width : 2 * width],
        ga[:, 2 * width : 3 * width],
        dbv,
        ga[:, 3 * width :].T,
        tail[3],
        tail[4],
        tail[5],
        gi,
        dbi,
        go.T,
        tail[0],
        tail[1],
        tail[2],
    )


def solution(mesh):
    split = P(None, "dp", "tensor", None)
    both, flipped, part = P("dp", "tensor"), P("tensor", "dp"), P("tensor")
    return jax.shard_map(
        body,
        mesh=mesh,
        in_specs=(
            split, P(None, "dp", None), both, part, both, both, part, flipped, P(), P(), P(),
            both, part, flipped, P(), P(), P(), split,
        ),
        out_specs=(
            split, split, both, part, both, both, part, flipped, P(), P(), P(), both, part,
            flipped, P(), P(), P(),
        ),
        check_vma=False,
    )
```

```python
from functools import partial

import jax
import jax.numpy as jnp
from jax import lax
from jax.experimental import pallas as pl
from jax.experimental.pallas import tpu as pltpu
from jax.sharding import PartitionSpec as P

HEAD = 64
DOCS = 8
PAD = 256
ROWS = 256
LOG2E = 1.4426950408889634
EPS = 1e-12
F32 = jnp.float32
BF16 = jnp.bfloat16


def dot_nn(left, right):
    return lax.dot_general(left, right, (((1,), (0,)), ((), ())), preferred_element_type=F32)


def dot_nt(left, right):
    return lax.dot_general(left, right, (((1,), (1,)), ((), ())), preferred_element_type=F32)


def rows_of(index, size=ROWS):
    return pl.ds(pl.multiple_of(index * size, size), size)


def lane_index(shape):
    return lax.broadcasted_iota(jnp.int32, shape, 1)


def three_parts(values):
    high = values.astype(BF16)
    rest = values - high.astype(F32)
    middle = rest.astype(BF16)
    low = (rest - middle.astype(F32)).astype(BF16)
    return high, middle, low


def head_only(lanes, head):
    return (lanes >= head * HEAD) & (lanes < (head + 1) * HEAD)


def head_and_extra(lanes, head, width):
    extra = width + DOCS + 3 * head
    return (
        head_only(lanes, head)
        | ((lanes >= width) & (lanes < width + DOCS))
        | ((lanes >= extra) & (lanes < extra + 3))
    )


def unpack(block_ref, slot, width):
    part = block_ref[:, slot * width : (slot + 1) * width]
    return jnp.concatenate([part, jnp.zeros((part.shape[0], PAD - width), part.dtype)], axis=1)


def project(x_rows, rows, bq, bv, w_s, qaug_ref, kaug_ref, vaug_ref, q_ref, k_ref, v_ref):
    queries = (dot_nn(x_rows, w_s[0]) + bq).astype(BF16)
    q_ref[rows, :] = queries * jnp.asarray(HEAD**-0.5, BF16) + qaug_ref[rows, :]
    keys = dot_nn(x_rows, w_s[1]).astype(BF16)
    k_ref[rows, :] = keys + kaug_ref[rows, :]
    values = (dot_nn(x_rows, w_s[2]) + bv).astype(BF16)
    v_ref[rows, :] = values + vaug_ref[...]


def attend_rows(rows, width, w_s, q_ref, k_ref, v_ref, att_ref, first_ref):
    lanes = lane_index((ROWS, PAD))
    queries = q_ref[rows, :]
    attended = jnp.zeros((ROWS, PAD), F32)
    extended = queries
    for head in range(width // HEAD):
        masked = jnp.where(head_and_extra(lanes, head, width), queries, 0)
        scores = dot_nt(masked, k_ref[...])
        highest = jnp.max(scores, axis=1, keepdims=True)
        raw = jnp.exp2((scores - highest) * LOG2E).astype(BF16)
        mixed = dot_nn(raw, v_ref[...])
        total = mixed[:, width : width + 1]
        attended = jnp.where(head_only(lanes, head), mixed / total, attended)
        for spot, part in enumerate(three_parts(-(highest + jnp.log(total)))):
            here = lanes == width + DOCS + 3 * head + spot
            extended = jnp.where(here, jnp.broadcast_to(part, (ROWS, PAD)), extended)
    q_ref[rows, :] = extended
    attended = attended.astype(BF16)
    att_ref[rows, :] = attended
    first_ref[rows, :] += dot_nt(attended, w_s[3])


def attend_plain_kernel(
    x_ref, a_ref, bias_ref, qaug_ref, kaug_ref, vaug_ref, bm_ref,
    q_ref, k_ref, v_ref, att_ref, first_ref, w_s,
):
    length, model = x_ref.shape
    width = a_ref.shape[2] // 4
    for slot in range(4):
        w_s[slot] = unpack(a_ref.at[0], slot, width)
    biases = bias_ref[0]

    @pl.when(pl.program_id(0) == 0)
    def _():
        first_ref[...] = x_ref[...].astype(F32) + bm_ref[...]

    @pl.loop(0, length // ROWS)
    def _(index):
        rows = rows_of(index)
        project(
            x_ref[rows, :], rows, biases[:, :PAD], biases[:, PAD : 2 * PAD], w_s, qaug_ref,
            kaug_ref, vaug_ref, q_ref.at[0], k_ref.at[0], v_ref.at[0],
        )

    @pl.loop(0, length // ROWS)
    def _(index):
        refs = (ref.at[0] for ref in (q_ref, k_ref, v_ref, att_ref))
        attend_rows(rows_of(index), width, w_s, *refs, first_ref)


MESH = pl.DeviceIdType.MESH


def partner(index, bits, size):
    flipped = index
    for bit in (1, 2, 4):
        if bits & bit and bit < size:
            flipped = flipped + bit - 2 * bit * lax.rem(lax.div(index, bit), 2)
    return flipped


class Wires:
    def __init__(self, send, recv, place, row):
        self.send, self.recv, self.place, self.row = send, recv, place, row

    def to(self, tensor_bits, dp_bits):
        return (partner(self.row, dp_bits, 8), partner(self.place, tensor_bits, 4))

    def copy(self, number, source, target, tensor_bits=0, dp_bits=0):
        return pltpu.make_async_remote_copy(
            src_ref=source,
            dst_ref=target,
            send_sem=self.send.at[number],
            recv_sem=self.recv.at[number],
            device_id=self.to(tensor_bits, dp_bits),
            device_id_type=MESH,
        )


def greet(wires, peers):
    barrier = pltpu.get_barrier_semaphore()
    for tensor_bits, dp_bits in peers:
        pl.semaphore_signal(
            barrier, inc=1, device_id=wires.to(tensor_bits, dp_bits), device_id_type=MESH
        )
    pl.semaphore_wait(barrier, len(peers))


PEERS = ((1, 0), (2, 0), (3, 0), (0, 1), (0, 2), (0, 4), (0, 6))
TOKENS, COTS, BIASES, KIND_A = 0, 3, 6, 9
SHARD_WIRES, BLOCK_WIRES = 19, 18
KIND_I = KIND_A + SHARD_WIRES
KIND_O = KIND_I + SHARD_WIRES
FORWARD_WIRES = KIND_O + BLOCK_WIRES


class ShardGather:
    def __init__(self, wires, base, shard, whole, across=False):
        self.wires, self.base, self.shard, self.whole = wires, base, shard, whole
        self.across = across
        z = lax.div(wires.row, 2)
        self.middle = (z == 1) | (z == 2)

    def at(self, slot, dp_bits):
        return self.whole.at[slot, partner(self.wires.row, dp_bits, 8)]

    def own(self, slot):
        return self.shard if slot == 0 else self.at(slot, 0)

    def cross_x(self):
        return self.wires.copy(self.base, self.shard, self.at(2, 0), 2, 0)

    def along_z(self, slot, step):
        number = self.base + 1 + 3 * (slot // 2) + step - 1
        return self.wires.copy(number, self.own(slot), self.at(slot, 0), 0, 2 * step)

    def hand_on(self, slot):
        number = self.base + 17 + slot // 2
        return self.wires.copy(number, self.at(slot, 4), self.at(slot, 4), 0, 2)

    def along_y(self, slot, step):
        number = self.base + 7 + 4 * (slot // 2) + step
        if slot and self.across:
            other = 2 * step + 1
            return self.wires.copy(number, self.at(0, other), self.at(2, other), 2, 0)
        source = self.own(slot) if step == 0 else self.at(slot, 2 * step)
        return self.wires.copy(number, source, self.at(slot, 2 * step), 0, 1)

    def to_core(self, slot):
        number = self.base + 15 + slot // 2
        return self.wires.copy(number, self.whole.at[slot], self.whole.at[slot + 1], 1, 0)

    def start(self, slot):
        self.along_z(slot, 2).start()
        self.along_z(slot, 1).start()

        @pl.when(self.middle)
        def _():
            self.along_z(slot, 3).start()

    def advance(self, slot):
        self.advance_near(slot)
        self.advance_far(slot)

    def advance_near(self, slot):
        self.along_z(slot, 2).wait_recv()

        @pl.when(self.middle)
        def _():
            self.hand_on(slot).start()

        self.pass_y(slot, 2)
        self.along_z(slot, 1).wait_recv()
        self.pass_y(slot, 1)

    def pass_y(self, slot, step):
        if not (slot and self.across):
            self.along_y(slot, step).start()

    def advance_far(self, slot):
        @pl.when(self.middle)
        def _():
            self.along_z(slot, 3).wait_recv()

        @pl.when(jnp.logical_not(self.middle))
        def _():
            self.hand_on(slot).wait_recv()

        self.pass_y(slot, 3)

    def wait_y(self, slot):
        for step in range(4):
            self.along_y(slot, step).wait_recv()

    def wait_sent(self, slots):
        for slot in slots:
            for step in (1, 2):
                self.along_z(slot, step).wait_send()

            @pl.when(self.middle)
            def _(slot=slot):
                self.along_z(slot, 3).wait_send()
                self.hand_on(slot).wait_send()

            for step in range(4):
                self.along_y(slot, step).wait_send()
        for slot in (0, 2):
            self.to_core(slot).wait_send()


class BlockGather(ShardGather):
    def along_z(self, slot, step):
        return self.wires.copy(
            self.base + step - 1, self.shard, self.at(0, 0), 0, 2 * step
        )

    def hand_on(self, slot):
        return self.wires.copy(self.base + 7, self.at(0, 4), self.at(0, 4), 0, 2)

    def along_y(self, slot, step):
        source = self.own(0) if step == 0 else self.at(0, 2 * step)
        return self.wires.copy(self.base + 3 + step, source, self.at(0, 2 * step), 0, 1)

    def cross(self, bits):
        source = self.own(0) if bits == 0 else self.at(0, bits)
        return self.wires.copy(self.base + 8 + bits, source, self.at(2, bits), 2, 0)

    def to_core(self, slot):
        return self.wires.copy(
            self.base + 16 + slot // 2, self.whole.at[slot], self.whole.at[slot + 1], 1, 0
        )

    def advance(self, slot):
        super().advance(slot)
        for bits in (0, 4, 2, 6):
            self.cross(bits).start()

    def wait_y(self, slot):
        super().wait_y(slot)
        for bits in (1, 3, 5, 7):
            self.cross(bits).start()

    def wait_x(self):
        for bits in range(8):
            self.cross(bits).wait_recv()

    def wait_sent(self, slots):
        super().wait_sent(slots)
        for bits in range(8):
            self.cross(bits).wait_send()


def gelu_parts(values):
    phi = jnp.exp2(values * values * (-0.5 * LOG2E)) * 0.3989422804014327
    total = 0.5 + 0.5 * lax.erf(values * 0.7071067811865476)
    return values * total, total + values * phi


def norm_parts(values):
    average = jnp.mean(values, axis=-1, keepdims=True)
    centred = values - average
    spread = jnp.mean(centred * centred, axis=-1, keepdims=True)
    inverse = lax.rsqrt(spread + EPS)
    return centred * inverse, inverse


def norm_back(grads, gain, unit, inverse):
    scaled = grads * gain
    average = jnp.mean(scaled, axis=-1, keepdims=True)
    along = jnp.mean(scaled * unit, axis=-1, keepdims=True)
    return (scaled - average - unit * along) * inverse


def column_sum(values):
    return jnp.sum(values, axis=0, keepdims=True)


WIDE = 512
SEG = 16


def head_rows(head):
    return slice(head * HEAD, (head + 1) * HEAD)


def extra_rows(head, width):
    return slice(width + head * SEG, width + (head + 1) * SEG)


def place_head(part, extra, head, width):
    count = part.shape[1]
    zeros = lambda rows: [jnp.zeros((rows, count), part.dtype)] if rows else []
    pieces = zeros(head * HEAD) + [part] + zeros(width - (head + 1) * HEAD)
    pieces += zeros(head * SEG) + [extra] + zeros(PAD - width - (head + 1) * SEG)
    return jnp.concatenate(pieces, axis=0)


def parts_rows(values, before):
    parts = [part for part in three_parts(values)]
    rest = jnp.zeros((SEG - DOCS - 3, values.shape[1]), BF16)
    return jnp.concatenate([before] + parts + [rest], axis=0)


def attend_block(cols, width, key_ref, vt_s, side_ref):
    heads = range(width // HEAD)
    docs = side_ref[extra_rows(0, width), cols]

    def score(head):
        queries = place_head(side_ref[head_rows(head), cols], docs, head, width)
        return dot_nn(key_ref[...], queries)

    scores, highest, mixed = [score(0)], [], []
    for head in heads:
        if head + 1 < len(heads):
            scores.append(score(head + 1))
        highest.append(jnp.max(scores[head], axis=0, keepdims=True))
        raw = jnp.exp2((scores[head] - highest[head]) * LOG2E).astype(BF16)
        mixed.append(dot_nn(vt_s[head], raw))
    for head in heads:
        logs = -(highest[head] + jnp.log(mixed[head][HEAD : HEAD + 1]))
        side_ref[extra_rows(head, width), cols] = parts_rows(logs, docs[:DOCS])
    outs = [(each[:HEAD] / each[HEAD : HEAD + 1]).astype(BF16) for each in mixed]
    return jnp.concatenate(outs, axis=0)


def attend_block_back(cols, width, key_ref, value_ref, side_ref, do_s, kt_s, all_t, dk_t, dv_t):
    heads = range(width // HEAD)

    def products(head):
        queries = side_ref[head_rows(head), cols]
        d_att = do_s[head_rows(head), cols]
        extra = extra_rows(head, width)
        scores = dot_nn(key_ref[...], place_head(queries, side_ref[extra, cols], head, width))
        d_chances = dot_nn(value_ref[...], place_head(d_att, do_s[extra, cols], head, width))
        return queries, d_att, scores, d_chances

    ahead = products(0)
    d_queries, d_keys, d_values = [], [], []
    for head in heads:
        queries, d_att, scores, d_chances = ahead
        if head + 1 < len(heads):
            ahead = products(head + 1)
        chances = jnp.exp2(scores * LOG2E)
        d_scores = (chances * d_chances).astype(BF16)
        d_queries.append(dot_nn(kt_s[head_rows(head), :], d_scores) * HEAD**-0.5)
        d_keys.append(dot_nt(queries, d_scores))
        d_values.append(dot_nt(d_att, chances.astype(BF16)))
    for head in heads:
        all_t[head_rows(head), cols] = d_queries[head].astype(BF16)
        dk_t[head_rows(head), :] += d_keys[head]
        dv_t[head_rows(head), :] += d_values[head]


def forward_kernel(
    tok_ref, cot_ref, si_ref, wq_ref, wk_ref, wv_ref, wm_ref, wo_ref, doc_ref, vec_ref,
    acts_ref, side_ref, slope_ref, first_out, second_out, low_out, xt_out, cot_out, wia_out,
    wo_out,
    sa_s, so_s, w_s, wm_s, x_s, xt_s, a_s, i_s, o_s, bias_s, kaug_s, qdoc_s, vt_s, mix_s,
    first_s, second_s, low_s, send_sem, recv_sem, here_sem,
):
    step = pl.program_id(0)
    place = lax.axis_index("tensor")
    row = lax.axis_index("dp")
    quarters, part, model = x_s.shape
    length = quarters * part
    share, width = wq_ref.shape
    heads = width // HEAD
    blocks = length // ROWS
    wides = length // WIDE
    wires = Wires(send_sem, recv_sem, place, row)
    attn = ShardGather(wires, KIND_A, sa_s, a_s, True)
    inner = ShardGather(wires, KIND_I, si_ref, i_s)
    outer = BlockGather(wires, KIND_O, so_s, o_s)
    b_mixer, gain_one, bias_one, b_outer = (vec_ref[i : i + 1, :] for i in range(4))
    key_ref, value_ref = (acts_ref.at[0, :, i * PAD : (i + 1) * PAD] for i in range(2))

    def exchange(base, source, target, bits, mine):
        other = partner(place, bits, 4)
        return wires.copy(
            base + bits - 1, source.at[other], target.at[place if mine else other], bits, 0
        )

    def bias_copy(bits, mine):
        return wires.copy(BIASES + bits - 1, vec_ref, bias_s.at[bits], bits, 0)

    local = [
        pltpu.make_async_copy(tok_ref.at[place], x_s.at[place], here_sem.at[0]),
        pltpu.make_async_copy(sa_s, a_s.at[0, row], here_sem.at[1]),
        pltpu.make_async_copy(si_ref, i_s.at[0, row], here_sem.at[2]),
        pltpu.make_async_copy(so_s, o_s.at[0, row], here_sem.at[3]),
        pltpu.make_async_copy(vec_ref, bias_s.at[0], here_sem.at[4]),
    ]
    own_cot = pltpu.make_async_copy(cot_ref.at[place], cot_out.at[place], here_sem.at[5])
    keep_x = pltpu.make_async_copy(xt_s, xt_out, here_sem.at[6])
    keep_a = pltpu.make_async_copy(a_s, wia_out.at[1], here_sem.at[7])
    keep_i = pltpu.make_async_copy(i_s, wia_out.at[0], here_sem.at[8])
    keep_o = pltpu.make_async_copy(o_s, wo_out, here_sem.at[9])
    keep_first = pltpu.make_async_copy(first_s, first_out, here_sem.at[10])
    keep_low = pltpu.make_async_copy(low_s, low_out, here_sem.at[11])
    keep_second = pltpu.make_async_copy(second_s, second_out, here_sem.at[12])

    @pl.when(step == 0)
    def _():
        sa_s[...] = jnp.concatenate(
            [wq_ref[...], wk_ref[...], wv_ref[...], wm_ref[...].T], axis=1
        )
        greet(wires, PEERS)
        attn.start(0)
        attn.along_y(0, 0).start()
        for bits in (2, 3, 1):
            bias_copy(bits, True).start()
            exchange(TOKENS, tok_ref, x_s, bits, True).start()
        so_s[...] = wo_ref[...]
        for copy in local:
            copy.start()
        own_cot.start()
        labels = doc_ref[place]
        docs = lax.broadcasted_iota(jnp.int32, (DOCS, length), 0)
        same = docs == labels
        ones = jnp.ones((3, length), F32)
        rest = jnp.zeros((SEG - DOCS - 3, length), F32)
        qdoc_s[...] = jnp.concatenate(
            [jnp.where(same, 1.0, 0.0), jnp.zeros((SEG - DOCS, length), F32)], axis=0
        ).astype(BF16)
        one_head = jnp.concatenate([jnp.where(same, 0.0, -(2.0**100)), ones, rest], axis=0)
        tall = jnp.zeros((width - PAD // 2, length), F32)
        last = jnp.zeros((PAD - width - heads * SEG, length), F32)
        kaug_s[...] = jnp.concatenate([tall] + [one_head] * heads + [last], axis=0).astype(BF16).T
        for head in range(heads):
            vt_s[head, HEAD:, :] = jnp.ones((SEG, length), BF16)
        for copy in local:
            copy.wait()
        attn.advance_near(0)
        outer.start(0)
        attn.advance_far(0)
        outer.along_y(0, 0).start()
        inner.along_y(0, 0).start()
        attn.cross_x().start()
        attn.wait_y(0)
        attn.to_core(0).start()
        for number in range(4):
            attn.along_y(2, number).start()
        inner.cross_x().start()
        for bits in (1, 2, 3):
            exchange(TOKENS, tok_ref, x_s, bits, False).wait_recv()
            bias_copy(bits, False).wait_recv()

        @pl.loop(0, quarters)
        def _(index):
            rows = rows_of(index, part)
            first_s[rows, :] = x_s[index].astype(F32) + b_mixer

    @pl.when(step == 1)
    def _():
        @pl.loop(0, quarters)
        def _(index):
            xt_s[:, rows_of(index, part)] = x_s[index].T

        keep_x.start()

    @pl.when(step == 1)
    def _():
        attn.to_core(0).wait_recv()

    @pl.when(step == 2)
    def _():
        attn.wait_y(2)
        attn.to_core(2).start()

    @pl.when(step == 3)
    def _():
        attn.to_core(2).wait_recv()
        keep_a.start()

    @pl.when(step < 4)
    def _():
        for dp_row in range(a_s.shape[1]):
            packed = a_s[step, dp_row]
            rest = jnp.zeros((share, PAD - width), packed.dtype)
            rows = slice(dp_row * share, (dp_row + 1) * share)
            for slot in range(4):
                piece = packed[:, slot * width : (slot + 1) * width]
                piece = jnp.concatenate([piece, rest], axis=1)
                if slot < 3:
                    w_s[rows, slot * PAD : (slot + 1) * PAD] = piece
                else:
                    wm_s[rows, :] = piece
        bias = bias_s[step][7:8]
        lanes = lax.broadcasted_iota(jnp.int32, (1, PAD), 1) - width
        spare = (lanes >= 0) & (lanes < heads * SEG) & (lax.rem(lanes + SEG, SEG) >= DOCS)
        vaug = jnp.where(spare & (lax.rem(lanes + SEG, SEG) < DOCS + 3), 1.0, 0.0).astype(BF16)

        @pl.loop(0, wides)
        def _(index):
            rows = rows_of(index, WIDE)
            x_rows = x_s[pl.ds(index * (WIDE // part), WIDE // part)].reshape(WIDE, model)
            result = dot_nn(x_rows, w_s[...])
            queries = (result[:, :PAD] + bias[:, :PAD]).astype(BF16)
            queries = (queries * jnp.asarray(HEAD**-0.5, BF16)).T
            side_ref[0, :width, rows] = queries[:width]
            side_ref[0, PAD + width :, rows] = jnp.zeros((PAD - width, WIDE), BF16)
            keys = result[:, PAD : 2 * PAD].astype(BF16)
            key_ref[rows, : PAD // 2] = keys[:, : PAD // 2]
            key_ref[rows, PAD // 2 :] = keys[:, PAD // 2 :] + kaug_s[rows, :]
            values = (result[:, 2 * PAD :] + bias[:, PAD : 2 * PAD]).astype(BF16)
            value_ref[rows, :] = values + vaug
            values_t = values.T
            for head in range(heads):
                vt_s[head, :HEAD, rows] = values_t[head_rows(head)]

        for head in range(heads):
            side_ref[0, extra_rows(head, width), :] = qdoc_s[...]
        side_ref[0, width + heads * SEG : PAD, :] = jnp.zeros(
            (PAD - width - heads * SEG, length), BF16
        )

        @pl.when(step == 1)
        def _():
            attn.advance_near(2)

        @pl.loop(0, blocks)
        def _(index):
            cols = rows_of(index)
            attended = attend_block(cols, width, key_ref, vt_s, side_ref.at[0])
            side_ref[0, PAD : PAD + width, cols] = attended
            rest = jnp.zeros((PAD - width, ROWS), BF16)
            mix_s[cols, :] = jnp.concatenate([attended, rest], axis=0).T

            @pl.when((step == 0) & (index == 0))
            def _():
                attn.cross_x().wait_recv()
                attn.start(2)

            @pl.when((step == 0) & (index == 1))
            def _():
                outer.advance(0)

            @pl.when((step == 0) & (index == 3))
            def _():
                inner.start(0)

            @pl.when((step == 1) & (index == 1))
            def _():
                attn.advance_far(2)

            @pl.when((step == 1) & (index == 3))
            def _():
                outer.wait_y(0)
                outer.to_core(0).start()
                inner.cross_x().wait_recv()
                inner.start(2)
                inner.along_y(2, 0).start()

            @pl.when((step == 2) & (index == 1))
            def _():
                inner.advance(0)

            @pl.when((step == 3) & (index == 2))
            def _():
                inner.advance(2)

            @pl.when((step == 3) & (index == 0))
            def _():
                for bits in (2, 3, 1):
                    exchange(COTS, cot_ref, cot_out, bits, True).start()

        @pl.loop(0, wides)
        def _(index):
            rows = rows_of(index, WIDE)
            first_s[rows, :] += dot_nt(mix_s[rows, :], wm_s[...])

    @pl.when(step == 4)
    def _():
        keep_first.start()

        @pl.loop(0, blocks)
        def _(index):
            rows = rows_of(index)
            unit, _inverse = norm_parts(first_s[rows, :])
            normed = unit * gain_one + bias_one
            low_s[rows, :] = normed.astype(BF16)
            second_s[rows, :] = normed + b_outer

        keep_low.start()
        inner.wait_y(0)
        inner.to_core(0).start()

    @pl.when(step == 5)
    def _():
        inner.to_core(0).wait_recv()
        outer.to_core(0).wait_recv()

    @pl.when(step == 6)
    def _():
        inner.wait_y(2)
        inner.to_core(2).start()
        outer.wait_x()
        outer.to_core(2).start()

    @pl.when(step == 7)
    def _():
        inner.to_core(2).wait_recv()
        outer.to_core(2).wait_recv()
        keep_i.start()
        keep_o.start()

    @pl.when(step >= 4)
    def _():
        slot = step - 4
        w_inner = i_s[slot].reshape(model, model)
        w_outer = o_s[slot].reshape(model, model)
        b_inner = bias_s[slot][6:7]

        @pl.loop(0, wides)
        def _(index):
            rows = rows_of(index, WIDE)
            value, slope = gelu_parts(dot_nn(low_s[rows, :], w_inner) + b_inner)
            hidden = value.astype(BF16)
            acts_ref[0, rows, :] = hidden
            slope_ref[0, rows, :] = slope.astype(BF16)
            second_s[rows, :] += dot_nt(hidden, w_outer)

    @pl.when(step == 7)
    def _():
        keep_second.start()
        for bits in (1, 2, 3):
            exchange(COTS, cot_ref, cot_out, bits, False).wait_recv()
        for gather in (attn, inner):
            gather.cross_x().wait_send()
            gather.wait_sent((0, 2))
        outer.wait_sent((0,))
        for bits in (1, 2, 3):
            exchange(TOKENS, tok_ref, x_s, bits, True).wait_send()
            exchange(COTS, cot_ref, cot_out, bits, True).wait_send()
            bias_copy(bits, True).wait_send()
        for copy in (
            own_cot, keep_x, keep_a, keep_i, keep_o, keep_first, keep_low, keep_second,
        ):
            copy.wait()


def dense_kernel(
    first_in, wi_ref, wo_ref, bi_ref, vec_ref, cot_ref,
    out_ref, dfirst_ref, dmix_ref, gi_ref, go_ref, dbi_ref, small_ref,
    first_ref, second_ref, normed_s, dsec_s, hidden_s, slope_s, low_s, low_t, back_t, dinner_s,
):
    step = pl.program_id(0)
    count = pl.num_programs(0) // 2
    length, model = first_in.shape
    blocks = length // ROWS
    gain_one, bias_one, b_outer, gain_two, bias_two = (vec_ref[i : i + 1, :] for i in range(5))

    @pl.when(step == 0)
    def _():
        copied = pltpu.sync_copy
        copied(first_in, first_ref)

        @pl.loop(0, blocks)
        def _(index):
            rows = rows_of(index)
            unit, _inverse = norm_parts(first_ref[rows, :])
            normed = unit * gain_one + bias_one
            normed_s[rows, :] = normed
            low_s[rows, :] = normed.astype(BF16)
            low_t[:, rows] = normed.astype(BF16).T
            second_ref[rows, :] = normed + b_outer

    @pl.when(step < count)
    def _():
        @pl.loop(0, blocks)
        def _(index):
            rows = rows_of(index)
            inner = dot_nn(low_s[rows, :], wi_ref[0]) + bi_ref[0]
            value, slope = gelu_parts(inner)
            hidden = value.astype(BF16)
            hidden_s[step, rows, :] = hidden
            slope_s[step, rows, :] = slope.astype(BF16)
            second_ref[rows, :] += dot_nt(hidden, wo_ref[0])

    @pl.when(step == count - 1)
    def _():
        small_ref[...] = jnp.zeros_like(small_ref)

        @pl.loop(0, blocks)
        def _(index):
            rows = rows_of(index)
            unit, inverse = norm_parts(second_ref[rows, :])
            out_ref[rows, :] = (unit * gain_two + bias_two).astype(BF16)
            grads = cot_ref[rows, :].astype(F32)
            d_second = norm_back(grads, gain_two, unit, inverse)
            small_ref[0:1, :] += column_sum(d_second)
            small_ref[1:2, :] += column_sum(grads * unit)
            small_ref[2:3, :] += column_sum(grads)
            dsec_s[rows, :] = d_second
            low = d_second.astype(BF16)
            dmix_ref[rows, :] = low
            back_t[:, rows] = low.T

    @pl.when(step >= count)
    def _():
        place = step - count
        dbi_ref[...] = jnp.zeros_like(dbi_ref)

        @pl.loop(0, blocks)
        def _(index):
            rows = rows_of(index)
            d_hidden = dot_nn(dmix_ref[rows, :], wo_ref[0])
            d_inner = (d_hidden * slope_s[place, rows, :].astype(F32)).astype(BF16)
            dinner_s[rows, :] = d_inner
            dbi_ref[0] += column_sum(d_inner.astype(F32))
            dsec_s[rows, :] += dot_nt(d_inner, wi_ref[0])

        @pl.loop(0, model // ROWS)
        def _(index):
            rows = rows_of(index)
            gi_ref[0, rows, :] = dot_nn(low_t[rows, :], dinner_s[...]).astype(gi_ref.dtype)
            go_ref[0, rows, :] = dot_nn(back_t[rows, :], hidden_s[place]).astype(go_ref.dtype)

    @pl.when(step == 2 * count - 1)
    def _():
        @pl.loop(0, blocks)
        def _(index):
            rows = rows_of(index)
            unit, inverse = norm_parts(first_ref[rows, :])
            grads = dsec_s[rows, :]
            d_first = norm_back(grads, gain_one, unit, inverse)
            small_ref[3:4, :] += column_sum(d_first)
            small_ref[4:5, :] += column_sum(grads * unit)
            small_ref[5:6, :] += column_sum(grads)
            dfirst_ref[rows, :] = d_first
            dmix_ref[rows, :] = d_first.astype(BF16)


def back_rows(rows, width, w_s, dmix_rows, q_ref, k_ref, v_ref, att_ref, kt_s, dq_s, dk_s, dv_s):
    lanes = lane_index((ROWS, PAD))
    queries = q_ref[rows, :]
    d_att = dot_nn(dmix_rows, w_s[3]).astype(BF16)
    product = d_att.astype(F32) * att_ref[rows, :].astype(F32)
    heads = range(width // HEAD)
    extended = d_att
    for head in heads:
        centre = jnp.sum(jnp.where(head_only(lanes, head), product, 0.0), axis=1, keepdims=True)
        for spot, part in enumerate(three_parts(-centre)):
            here = lanes == width + DOCS + 3 * head + spot
            extended = jnp.where(here, jnp.broadcast_to(part, (ROWS, PAD)), extended)
    chances_all = []
    d_scores_all = []
    d_att_all = []
    queries_all = []
    for head in heads:
        wide = head_and_extra(lanes, head, width)
        only = head_only(lanes, head)
        chances = jnp.exp2(dot_nt(k_ref[...], jnp.where(wide, queries, 0)) * LOG2E)
        d_chances = dot_nt(v_ref[...], jnp.where(wide, extended, 0))
        d_scores = (chances * d_chances).astype(BF16)
        chances_all.append(chances.astype(BF16))
        d_scores_all.append(d_scores)
        d_att_all.append(jnp.where(only, d_att, 0))
        queries_all.append(jnp.where(only, queries, 0))
        head_rows = slice(head * HEAD, (head + 1) * HEAD)
        dq_s[head_rows, rows] = dot_nn(kt_s[head_rows, :], d_scores)
    dv_s[...] += dot_nn(jnp.concatenate(chances_all, 1), jnp.concatenate(d_att_all, 0))
    dk_s[...] += dot_nn(jnp.concatenate(d_scores_all, 1), jnp.concatenate(queries_all, 0))


def back_low(rows, width, dq_s, dk_s, dv_s, low_s):
    d_query = (dq_s[:, rows].T * HEAD**-0.5).astype(BF16)
    d_query = jnp.where(lane_index(d_query.shape) < width, d_query, 0)
    d_value = dv_s[rows, :].astype(BF16)
    low_s[rows, :PAD] = d_query
    low_s[rows, PAD : 2 * PAD] = dk_s[rows, :].astype(BF16)
    low_s[rows, 2 * PAD :] = d_value
    return column_sum(d_query.astype(F32)), column_sum(d_value.astype(F32))


def back_tokens(rows, w_s, low_s):
    return sum(dot_nt(low_s[rows, slot * PAD : (slot + 1) * PAD], w_s[slot]) for slot in range(3))


def back_weights(rows, width, slots, xt_s, dmixt_s, low_s, att_ref):
    parts = []
    for slot in slots:
        if slot < 3:
            part = dot_nn(xt_s[rows, :], low_s[:, slot * PAD : (slot + 1) * PAD])
        else:
            part = dot_nn(dmixt_s[rows, :], att_ref[...])
        parts.append(part[:, :width])
    return jnp.concatenate(parts, axis=1).astype(BF16)


def attend_back_kernel(
    x_ref, a_ref, dmix_ref, dfirst_ref, q_ref, k_ref, v_ref, att_ref,
    dtok_ref, ga_ref, dbq_ref, dbv_ref,
    w_s, xt_s, dmixt_s, kt_s, dq_s, dk_s, dv_s, low_s,
):
    length, model = x_ref.shape
    width = a_ref.shape[2] // 4
    blocks = length // ROWS
    for slot in range(4):
        w_s[slot] = unpack(a_ref.at[0], slot, width)

    @pl.when(pl.program_id(0) == 0)
    def _():
        dtok_ref[...] = dfirst_ref[...]

        @pl.loop(0, blocks)
        def _(index):
            rows = rows_of(index)
            xt_s[:, rows] = x_ref[rows, :].T
            dmixt_s[:, rows] = dmix_ref[rows, :].T

    for sums in (dk_s, dv_s, dbq_ref, dbv_ref):
        sums[...] = jnp.zeros_like(sums)

    @pl.loop(0, blocks)
    def _(index):
        rows = rows_of(index)
        kt_s[:, rows] = k_ref[0, rows, :].T

    @pl.loop(0, blocks)
    def _(index):
        rows = rows_of(index)
        dmix_rows = dmix_ref[rows, :]
        refs = (ref.at[0] for ref in (q_ref, k_ref, v_ref, att_ref))
        back_rows(rows, width, w_s, dmix_rows, *refs, kt_s, dq_s, dk_s, dv_s)

    @pl.loop(0, blocks)
    def _(index):
        rows = rows_of(index)
        for_query, for_value = back_low(rows, width, dq_s, dk_s, dv_s, low_s)
        dbq_ref[0] += for_query
        dbv_ref[0] += for_value
        dtok_ref[rows, :] += back_tokens(rows, w_s, low_s)

    @pl.loop(0, model // ROWS)
    def _(index):
        rows = rows_of(index)
        ga_ref[0, rows, :] = back_weights(
            rows, width, range(4), xt_s, dmixt_s, low_s, att_ref.at[0]
        )


def add_into(target, source):
    target[...] = (target[...].astype(F32) + source[...].astype(F32)).astype(target.dtype)


class Reduce:
    COUNT = 11

    def __init__(self, wires, base, held, core, by_y, by_z, by_x, cols=slice(None)):
        self.wires, self.base, self.held, self.core = wires, base, held, core
        self.by_y, self.by_z, self.by_x = by_y, by_z, by_x
        self.cols = cols
        self.z, self.y = lax.div(wires.row, 2), lax.rem(wires.row, 2)

    def part(self, ref, *index):
        return ref.at[index + (slice(None), self.cols)]

    def core_copy(self, j, source):
        everything = (slice(None), slice(None))
        return self.wires.copy(
            self.base + j, self.part(source, *everything), self.part(self.core, j, *everything), 1, 0
        )

    def add_core(self, j):
        self.core_copy(j, self.held.at[j]).wait_recv()
        for z in range(4):
            for y in range(2):
                add_into(self.part(self.held, j, z, y), self.part(self.core, j, z, y))

    def y_copy(self, j):
        source = self.part(self.held, j, slice(None), 1 - self.y)
        return self.wires.copy(
            self.base + 2 + j, source, self.part(self.by_y, j, slice(None)), 0, 1
        )

    def add_y(self, j):
        self.y_copy(j).wait_recv()
        for z in range(4):
            add_into(self.part(self.held, j, z, self.y), self.part(self.by_y, j, z))

    def z_copy(self, j, step):
        other = lax.div(partner(self.wires.row, 2 * step, 8), 2)
        number = self.base + 4 + 3 * j + step - 1
        return self.wires.copy(
            number, self.part(self.held, j, other, self.y), self.part(self.by_z, j, step - 1),
            0, 2 * step,
        )

    def start_z(self, j):
        for step in (1, 2, 3):
            self.z_copy(j, step).start()

    def total_z(self, j):
        total = self.part(self.held, j, self.z, self.y)[...].astype(F32)
        for step in (1, 2, 3):
            self.z_copy(j, step).wait_recv()
            total = total + self.part(self.by_z, j, step - 1)[...].astype(F32)
        return total

    def x_copy(self):
        source = self.part(self.held, 1, self.z, self.y)
        return self.wires.copy(self.base + 10, source, self.part(self.by_x), 2, 0)

    def send_x(self):
        self.part(self.held, 1, self.z, self.y)[...] = self.total_z(1).astype(BF16)
        self.x_copy().start()

    def total(self):
        self.x_copy().wait_recv()
        return self.total_z(0) + self.part(self.by_x)[...].astype(F32)

    def whole_x_copy(self):
        return self.wires.copy(self.base + 10, self.held.at[1], self.by_x, 2, 0)

    def add_whole_x(self):
        self.whole_x_copy().wait_recv()
        for z in range(4):
            for y in range(2):
                add_into(self.held.at[0, z, y], self.by_x.at[z, y])

    def wait_sent(self, j_all):
        for j in j_all:
            self.y_copy(j).wait_send()
            for step in (1, 2, 3):
                self.z_copy(j, step).wait_send()


OUTPUTS, TOKEN_GRADS, SUMS, LATE_SUMS = 0, 3, 6, 16
RED_I = 26
RED_O = RED_I + Reduce.COUNT
RED_A = RED_O + Reduce.COUNT
BACKWARD_WIRES = RED_A + 3 * Reduce.COUNT
BACK_PEERS = PEERS + ((0, 3), (0, 5), (0, 7))


def slot_at(step):
    return jnp.where(step < 2, 3 - 2 * step, 6 - 2 * step)


def backward_kernel(
    acts_ref, side_ref, slope_ref, wia_ref, wo_ref, vec_ref, second_ref, first_ref, low_ref, xt_ref,
    cot_ref,
    out_res, dtok_res, ga_res, gi_res, go_res, sum_res, late_res,
    low_t, back_t, dmix_s, low_s, flow_s, out_s, grad_s, first_s, wmt_s, do_s, kt_s, all_t, dk_t,
    dv_t, sums_s, sums_o, sums_d, late_o, late_t, late_d,
    send_i, held_i, core_i, y_i, z_i, x_i, send_o, held_o, core_o, y_o, z_o, x_o,
    held_a, core_a, y_a, z_a, x_a,
    send_sem, recv_sem, here_sem,
):
    step = pl.program_id(0)
    place = lax.axis_index("tensor")
    row = lax.axis_index("dp")
    length, model = dmix_s.shape
    quarters, part, _ = flow_s.shape
    width = wia_ref.shape[2] // 4
    heads = width // HEAD
    blocks = length // ROWS
    wides = length // WIDE
    share = held_i.shape[3]
    wires = Wires(send_sem, recv_sem, place, row)
    inner = Reduce(wires, RED_I, held_i, core_i, y_i, z_i, x_i)
    outer = Reduce(wires, RED_O, held_o, core_o, y_o, z_o, x_o)
    halves = (slice(0, model // 2), slice(model // 2, model))
    send_a = send_i
    thirds = [slice(number * PAD, (number + 1) * PAD) for number in range(model // PAD)]
    attn = [
        Reduce(wires, RED_A + number * Reduce.COUNT, held_a, core_a, y_a, z_a, x_a, cols)
        for number, cols in enumerate(thirds)
    ]
    ready = (attn[:1], attn[1:])
    gain_one, gain_two, bias_two = (vec_ref[i : i + 1, :] for i in (1, 4, 5))
    key_ref, value_ref = (acts_ref.at[0, :, i * PAD : (i + 1) * PAD] for i in range(2))
    att_ref = side_ref.at[0, PAD : PAD + width]

    def exchange(base, source, target, bits, mine):
        other = partner(place, bits, 4)
        return wires.copy(
            base + bits - 1, source.at[other], target.at[place if mine else other], bits, 0
        )

    def by_tensor(bits):
        return wires.copy(
            SUMS + bits - 1, sums_s.at[place], sums_s.at[place], bits, 0
        )

    def by_rows(base, kept, bits):
        return wires.copy(base + 2 + bits, kept.at[row], kept.at[row], 0, bits)

    def late_copy(bits):
        return wires.copy(LATE_SUMS + bits - 1, late_o.at[bits], late_t.at[bits], bits, 0)

    def sum_rows(base, kept):
        for bits in range(1, 8):
            by_rows(base, kept, bits).wait_recv()
        return sum((kept[number] for number in range(1, 8)), kept[0])

    load_second = pltpu.make_async_copy(second_ref, grad_s, here_sem.at[0])
    load_cot = pltpu.make_async_copy(cot_ref, flow_s, here_sem.at[1])
    load_low = pltpu.make_async_copy(low_ref, low_s, here_sem.at[2])
    load_x = pltpu.make_async_copy(xt_ref, low_t, here_sem.at[3])
    keep_out = pltpu.make_async_copy(out_s.at[place], out_res.at[place], here_sem.at[4])
    keep_dtok = pltpu.make_async_copy(flow_s.at[place], dtok_res.at[place], here_sem.at[5])

    def load_first(index):
        return pltpu.make_async_copy(
            first_ref.at[rows_of(index)], first_s.at[index % 2], here_sem.at[6 + index % 2]
        )

    order = (3, 1, 2, 0)

    @pl.when(step == 0)
    def _():
        load_second.start()
        load_cot.start()
        load_low.start()
        sums_s[place] = jnp.zeros_like(sums_s[0])
        for bits in range(4):
            late_o[bits] = jnp.zeros_like(late_o[0])
        greet(wires, BACK_PEERS)
        load_second.wait()
        load_cot.wait()
        load_low.wait()

        @pl.loop(0, quarters)
        def _(index):
            rows = rows_of(index, part)
            low_t[:, rows] = low_s[rows, :].T
            unit, inverse = norm_parts(grad_s[rows, :])
            out_s[index] = (unit * gain_two + bias_two).astype(BF16)
            grads = flow_s[index].astype(F32)
            d_second = norm_back(grads, gain_two, unit, inverse)
            sums_s[place, 8:9, :] += column_sum(d_second)
            sums_s[place, 9:10, :] += column_sum(grads * unit)
            sums_s[place, 10:11, :] += column_sum(grads)
            grad_s[rows, :] = d_second
            lower = d_second.astype(BF16)
            dmix_s[rows, :] = lower
            back_t[:, rows] = lower.T

        for bits in (2, 3, 1):
            exchange(OUTPUTS, out_s, out_res, bits, True).start()
        keep_out.start()

    @pl.when(step < 4)
    def _():
        @pl.loop(0, 1)
        def _(index):
            rows = rows_of(index, length)
            d_hidden = dot_nn(dmix_s[rows, :], wo_ref[0])
            d_inner = (d_hidden * slope_ref[0, rows, :].astype(F32)).astype(BF16)
            low_s[rows, :] = d_inner
            for_inner = column_sum(d_inner.astype(F32))
            for number, bits in enumerate(order):

                @pl.when(step == number)
                def _(bits=bits):
                    sums_s[place, pl.ds(partner(place, bits, 4), 1), :] += for_inner

            grad_s[rows, :] += dot_nt(d_inner, wia_ref[0])

        for transposed, right, sent, held in (
            (back_t, acts_ref.at[0], send_o, held_o), (low_t, low_s, send_i, held_i),
        ):
            grads = dot_nn(transposed[...], right[...]).astype(BF16)
            pieces = grads.reshape(4, 2, share, model)

            @pl.when(step < 2)
            def _(pieces=pieces, sent=sent):
                sent[step] = pieces

            @pl.when(step >= 2)
            def _(pieces=pieces, held=held):
                held[3 - step] = pieces

    for number, j in ((0, 1), (1, 0)):

        @pl.when(step == number)
        def _(number=number, j=j):
            outer.core_copy(j, send_o.at[number]).start()
            inner.core_copy(j, send_i.at[number]).start()

    @pl.when(step == 2)
    def _():
        load_first(0).start()
        load_first(1).start()
        outer.add_core(1)
        outer.whole_x_copy().start()
        inner.add_core(1)
        inner.y_copy(1).start()

    @pl.when(step == 3)
    def _():
        inner.add_core(0)
        inner.y_copy(0).start()
        outer.add_core(0)
        load_x.start()
        for index in range(blocks):
            rows = slice(index * ROWS, (index + 1) * ROWS)
            load_first(index).wait()
            unit, inverse = norm_parts(first_s[index % 2])
            if index + 2 < blocks:
                load_first(index + 2).start()
            grads = grad_s[rows, :]
            d_first = norm_back(grads, gain_one, unit, inverse)
            sums_s[place, 11:12, :] += column_sum(d_first)
            sums_s[place, 12:13, :] += column_sum(grads * unit)
            sums_s[place, 13:14, :] += column_sum(grads)
            grad_s[rows, :] = d_first
            lower = d_first.astype(BF16)
            dmix_s[rows, :] = lower
            back_t[:, rows] = lower.T
        load_x.wait()
        for bits in (1, 2, 3):
            by_tensor(bits).start()

    @pl.when(step == 4)
    def _():
        for number, j in ((0, 1), (1, 0)):
            inner.core_copy(j, send_i.at[number]).wait_send()

    @pl.when(step >= 4)
    def _():
        wmt_s[...] = wia_ref[0, :, 3 * width :].T
        for sums in (dk_t, dv_t):
            sums[...] = jnp.zeros_like(sums)

        @pl.loop(0, wides)
        def _(index):
            cols = rows_of(index, WIDE)
            kt_s[:, cols] = key_ref[cols, :].T[:width]
            d_att = dot_nn(wmt_s[...], back_t[:, cols]).astype(BF16)
            do_s[:width, cols] = d_att
            product = d_att.astype(F32) * att_ref[:, cols].astype(F32)
            none = jnp.zeros((DOCS, WIDE), BF16)
            for head in range(heads):
                centre = column_sum(product[head_rows(head)])
                do_s[extra_rows(head, width), cols] = parts_rows(-centre, none)

        @pl.loop(0, blocks)
        def _(index):
            attend_block_back(
                rows_of(index), width, key_ref, value_ref, side_ref.at[0], do_s, kt_s, all_t,
                dk_t, dv_t,
            )

            @pl.when((step == 4) & (index == 0))
            def _():
                inner.add_y(1)
                inner.start_z(1)

            @pl.when((step == 5) & (index == 0))
            def _():
                inner.add_y(0)
                inner.start_z(0)
                outer.add_whole_x()
                outer.y_copy(0).start()

            @pl.when((step == 5) & (index == 1))
            def _():
                inner.send_x()
                for bits in (1, 2, 3):
                    by_tensor(bits).wait_recv()
                sums_o[...] = sums_s[0] + sums_s[1] + sums_s[2] + sums_s[3]
                sums_d[row, :6, :] = sums_o[8:14, :]
                sums_d[row, 6:7, :] = sums_o[pl.ds(place, 1), :]
                sums_d[row, 7:, :] = jnp.zeros((1, model), F32)
                for bits in range(1, 8):
                    by_rows(SUMS, sums_d, bits).start()

            @pl.when((step == 7) & (index == 1))
            def _():
                sum_res[...] = sum_rows(SUMS, sums_d)

            @pl.when((step == 6) & (index == 1))
            def _():
                outer.add_y(0)
                outer.start_z(0)

            @pl.when((step == 6) & (index == 1))
            def _():
                gi_res[...] = inner.total()

            @pl.when((step == 7) & (index == 2))
            def _():
                go_res[...] = outer.total_z(0)

            for number, reduce in zip((0, 1, 3), attn):

                @pl.when((step == 7) & (index == number))
                def _(reduce=reduce):
                    reduce.add_y(1)
                    reduce.start_z(1)

        all_t[width : 2 * width, :] = dk_t[...].astype(BF16)
        all_t[2 * width :, :] = dv_t[...].astype(BF16)
        for_all = dot_nt(jnp.ones((8, length), BF16), all_t[...])
        for number, bits in enumerate(order):

            @pl.when(step == 4 + number)
            def _(bits=bits):
                late_o[bits, :, : 3 * width] = for_all
                if bits:
                    late_copy(bits).start()
                    return
                for other in (1, 2, 3):
                    late_copy(other).wait_recv()
                late_d[row] = late_o[0] + late_t[1] + late_t[2] + late_t[3]
                for other in range(1, 8):
                    by_rows(LATE_SUMS, late_d, other).start()

        for half, cols in enumerate(halves):

            @pl.loop(0, model // (4 * share))
            def _(pair):
                rows = rows_of(pair, 4 * share)
                if half == 0:
                    grads = dot_nt(low_t[rows, :], all_t[: 2 * width, :])
                else:
                    for_value = dot_nt(low_t[rows, :], all_t[2 * width :, :])
                    for_mixer = dot_nt(back_t[rows, :], att_ref[...])
                    grads = jnp.concatenate([for_value, for_mixer], axis=1)
                pieces = grads.astype(BF16).reshape(2, 2, share, model // 2)

                @pl.when(step < 6)
                def _(pieces=pieces):
                    send_a[step - 4, pl.ds(2 * pair, 2), :, :, cols] = pieces

                @pl.when(step >= 6)
                def _(pieces=pieces):
                    held_a[7 - step, pl.ds(2 * pair, 2), :, :, cols] = pieces

            for number, j in ((0, 1), (1, 0)):

                @pl.when(step == 4 + number)
                def _(number=number, j=j):
                    for reduce in ready[half]:
                        reduce.core_copy(j, send_a.at[number]).start()

            for j in (1, 0):

                @pl.when(step == 7 - j)
                def _(j=j):
                    for reduce in ready[half]:
                        reduce.add_core(j)
                        reduce.y_copy(j).start()

            if half == 0:

                @pl.loop(0, 1)
                def _(index):
                    rows = rows_of(index, length)
                    transposed = all_t[:, rows].T
                    grad_s[rows, :] += dot_nt(transposed, wia_ref[0, :, : 3 * width])

                    @pl.when(step == 7)
                    def _():
                        places = pl.ds(0, quarters)
                        flow_s[places] = grad_s[rows, :].astype(BF16).reshape(quarters, part, model)

                @pl.when(step == 7)
                def _():
                    for bits in (2, 3, 1):
                        exchange(TOKEN_GRADS, flow_s, dtok_res, bits, True).start()
                    keep_dtok.start()


    @pl.when(step == 7)
    def _():
        for reduce in attn:
            reduce.add_y(0)
            reduce.start_z(0)
            reduce.send_x()
        late_res[...] = sum_rows(LATE_SUMS, late_d)
        for reduce, cols in zip(attn, thirds):
            ga_res[:, cols] = reduce.total()
        for bits in (1, 2, 3):
            for base, source, target in (
                (OUTPUTS, out_s, out_res), (TOKEN_GRADS, flow_s, dtok_res),
            ):
                exchange(base, source, target, bits, False).wait_recv()
                exchange(base, source, target, bits, True).wait_send()
        keep_out.wait()
        keep_dtok.wait()
        for bits in (1, 2, 3):
            by_tensor(bits).wait_send()
            late_copy(bits).wait_send()
        for bits in range(1, 8):
            by_rows(SUMS, sums_d, bits).wait_send()
            by_rows(LATE_SUMS, late_d, bits).wait_send()
        for number, j in ((0, 1), (1, 0)):
            outer.core_copy(j, send_o.at[number]).wait_send()
            for reduce in attn:
                reduce.core_copy(j, send_a.at[number]).wait_send()
        inner.wait_sent((0, 1))
        inner.x_copy().wait_send()
        outer.wait_sent((0,))
        outer.whole_x_copy().wait_send()
        for reduce in attn:
            reduce.wait_sent((0, 1))
            reduce.x_copy().wait_send()


VMEM_LIMIT = 62 * 1024 * 1024


def resident(shape):
    return pl.BlockSpec(shape, lambda step: (0,) * len(shape))


def stepped(shape):
    return pl.BlockSpec((1,) + shape[1:], lambda step: (step,) + (0,) * (len(shape) - 1))


def spec_list(pairs):
    return [stepped(shape) if moves else resident(shape) for shape, moves in pairs]


def near_forward(tokens, cotangent, shard_i, w_query, w_key, w_value, w_mixer, w_outer, docs, vectors):
    groups, part, model = tokens.shape
    length = groups * part
    share, width = w_query.shape
    whole = (groups, model // share, share, model)
    sides = (groups, 2 * PAD, length)
    slopes = (groups, length, model)
    flat = (length, model)
    shard = (share, model)
    biases = (groups,) + vectors.shape
    anywhere = pl.BlockSpec(memory_space=pl.ANY)

    def early(shape):
        return pl.BlockSpec(
            (1,) + shape[1:], lambda step: (jnp.minimum(step, 3),) + (0,) * (len(shape) - 1)
        )

    def late(shape):
        return pl.BlockSpec(
            (1,) + shape[1:], lambda step: (jnp.maximum(step - 4, 0),) + (0,) * (len(shape) - 1)
        )

    def vmem(*shape, kind=BF16):
        return pltpu.VMEM(shape, kind)

    kept = [w_query, w_key, w_value, w_mixer, w_outer, docs, vectors]
    return pl.pallas_call(
        forward_kernel,
        grid=(2 * groups,),
        out_shape=[
            jax.ShapeDtypeStruct((2 * groups, length, model), BF16),
            jax.ShapeDtypeStruct(sides, BF16),
            jax.ShapeDtypeStruct(slopes, BF16),
            jax.ShapeDtypeStruct(flat, F32),
            jax.ShapeDtypeStruct(flat, F32),
            jax.ShapeDtypeStruct(flat, BF16),
            jax.ShapeDtypeStruct((model, length), BF16),
            jax.ShapeDtypeStruct(tokens.shape, BF16),
            jax.ShapeDtypeStruct((2,) + whole, BF16),
            jax.ShapeDtypeStruct(whole, BF16),
        ],
        in_specs=[anywhere] * 3 + [resident(each.shape) for each in kept],
        out_specs=[stepped((2 * groups, length, model)), early(sides), late(slopes)]
        + [anywhere] * 7,
        scratch_shapes=[
            vmem(*shard), vmem(*shard), vmem(model, 3 * PAD), vmem(model, PAD),
            vmem(*tokens.shape), vmem(model, length), vmem(*whole), vmem(*whole), vmem(*whole),
            vmem(*biases, kind=F32), vmem(length, PAD // 2), vmem(SEG, length),
            vmem(width // HEAD, HEAD + SEG, length), vmem(length, PAD),
            vmem(*flat, kind=F32), vmem(*flat, kind=F32), vmem(*flat),
            pltpu.SemaphoreType.DMA((FORWARD_WIRES,)),
            pltpu.SemaphoreType.DMA((FORWARD_WIRES,)),
            pltpu.SemaphoreType.DMA((13,)),
        ],
        compiler_params=pltpu.CompilerParams(
            vmem_limit_bytes=VMEM_LIMIT, collective_id=0, has_side_effects=True
        ),
        name="near_forward",
    )(tokens, cotangent, shard_i, *kept)


def attend_plain(x, a_all, biases, qaug, kaug, vaug, b_mixer):
    length, model = x.shape
    groups = a_all.shape[0]
    block = (groups, length, PAD)
    return pl.pallas_call(
        attend_plain_kernel,
        grid=(groups,),
        out_shape=[jax.ShapeDtypeStruct(block, BF16)] * 4 + [jax.ShapeDtypeStruct(x.shape, F32)],
        in_specs=spec_list(
            [
                (x.shape, 0), (a_all.shape, 1), (biases.shape, 1),
                (qaug.shape, 0), (kaug.shape, 0), (vaug.shape, 0), (b_mixer.shape, 0),
            ]
        ),
        out_specs=spec_list([(block, 1)] * 4 + [(x.shape, 0)]),
        scratch_shapes=[pltpu.VMEM((4, model, PAD), BF16)],
        compiler_params=pltpu.CompilerParams(vmem_limit_bytes=VMEM_LIMIT),
        name="attend_plain",
    )(x, a_all, biases, qaug, kaug, vaug, b_mixer)


def dense_both(first_sum, wi, wo, bi, vectors, cotangent):
    length, model = first_sum.shape
    groups, _, hidden = wi.shape
    grad = (groups, model, hidden)
    forth = lambda shape: pl.BlockSpec(
        (1,) + shape[1:], lambda step: (lax.rem(step, groups),) + (0,) * (len(shape) - 1)
    )
    late = lambda shape: pl.BlockSpec(
        (1,) + shape[1:], lambda step: (jnp.maximum(step - groups, 0),) + (0,) * (len(shape) - 1)
    )
    return pl.pallas_call(
        dense_kernel,
        grid=(2 * groups,),
        out_shape=[
            jax.ShapeDtypeStruct((length, model), BF16),
            jax.ShapeDtypeStruct((length, model), F32),
            jax.ShapeDtypeStruct((length, model), BF16),
            jax.ShapeDtypeStruct(grad, BF16),
            jax.ShapeDtypeStruct(grad, BF16),
            jax.ShapeDtypeStruct((groups, 1, hidden), F32),
            jax.ShapeDtypeStruct((8, model), F32),
        ],
        in_specs=[
            pl.BlockSpec(memory_space=pl.ANY), forth(wi.shape), forth(wo.shape), forth(bi.shape),
            resident(vectors.shape), resident(cotangent.shape),
        ],
        out_specs=[
            resident((length, model)), resident((length, model)), resident((length, model)),
            late(grad), late(grad), late((groups, 1, hidden)), resident((8, model)),
        ],
        scratch_shapes=[
            pltpu.VMEM((length, model), F32),
            pltpu.VMEM((length, model), F32),
            pltpu.VMEM((length, model), F32),
            pltpu.VMEM((length, model), F32),
            pltpu.VMEM((groups, length, hidden), BF16),
            pltpu.VMEM((groups, length, hidden), BF16),
            pltpu.VMEM((length, model), BF16),
            pltpu.VMEM((model, length), BF16),
            pltpu.VMEM((model, length), BF16),
            pltpu.VMEM((length, hidden), BF16),
        ],
        compiler_params=pltpu.CompilerParams(vmem_limit_bytes=VMEM_LIMIT),
        name="dense_both",
    )(first_sum, wi, wo, bi, vectors, cotangent)


def attend_backward(x, a_all, d_mixed, d_first, q, k, v, attended):
    length, model = x.shape
    groups = a_all.shape[0]
    sums = (groups, 1, PAD)
    return pl.pallas_call(
        attend_back_kernel,
        grid=(groups,),
        out_shape=[
            jax.ShapeDtypeStruct(x.shape, F32),
            jax.ShapeDtypeStruct(a_all.shape, BF16),
            jax.ShapeDtypeStruct(sums, F32),
            jax.ShapeDtypeStruct(sums, F32),
        ],
        in_specs=spec_list(
            [
                (x.shape, 0), (a_all.shape, 1), (d_mixed.shape, 0), (d_first.shape, 0),
                (q.shape, 1), (k.shape, 1), (v.shape, 1), (attended.shape, 1),
            ]
        ),
        out_specs=spec_list([(x.shape, 0), (a_all.shape, 1), (sums, 1), (sums, 1)]),
        scratch_shapes=[
            pltpu.VMEM((4, model, PAD), BF16),
            pltpu.VMEM((model, length), BF16),
            pltpu.VMEM((model, length), BF16),
            pltpu.VMEM((PAD, length), BF16),
            pltpu.VMEM((PAD, length), F32),
            pltpu.VMEM((length, PAD), F32),
            pltpu.VMEM((length, PAD), F32),
            pltpu.VMEM((length, 3 * PAD), BF16),
        ],
        compiler_params=pltpu.CompilerParams(vmem_limit_bytes=VMEM_LIMIT),
        name="attend_backward",
    )(x, a_all, d_mixed, d_first, q, k, v, attended)


def near_backward(acts, sides, slopes, w_ia, w_o, vectors, second, first, low, xt, cotangent):
    quarters, part, model = cotangent.shape
    length = quarters * part
    share = model // 8
    width = model // 4
    block = (4, 2, share, model)
    anywhere = pl.BlockSpec(memory_space=pl.ANY)

    def ordered(shape, place):
        return pl.BlockSpec(
            (1,) + shape[1:], lambda step: (place(step),) + (0,) * (len(shape) - 1)
        )

    def acts_at(step):
        return jnp.where(step < 4, 4 + slot_at(step), slot_at(step - 4))

    def weights_at(step):
        return jnp.where(step < 4, slot_at(step), 4 + slot_at(step - 4))

    def first_half(step):
        return slot_at(jnp.minimum(step, 3))

    def last_half(step):
        return slot_at(jnp.maximum(step - 4, 0))

    def vmem(*shape, kind=BF16):
        return pltpu.VMEM(shape, kind)

    final = [
        ((share, model), F32), ((share, model), F32), ((share, model), F32), ((8, model), F32),
        ((8, model), F32),
    ]
    return pl.pallas_call(
        backward_kernel,
        grid=(8,),
        out_shape=[jax.ShapeDtypeStruct(cotangent.shape, BF16)] * 2
        + [jax.ShapeDtypeStruct(*each) for each in final],
        in_specs=[
            ordered(acts.shape, acts_at), ordered(sides.shape, last_half),
            ordered(slopes.shape, first_half), ordered(w_ia.shape, weights_at),
            ordered(w_o.shape, first_half), resident(vectors.shape),
        ]
        + [anywhere] * 5,
        out_specs=[anywhere] * 2 + [resident(each[0]) for each in final],
        scratch_shapes=[
            vmem(model, length), vmem(model, length), vmem(length, model), vmem(length, model),
            vmem(*cotangent.shape), vmem(*cotangent.shape), vmem(length, model, kind=F32),
            vmem(2, ROWS, model, kind=F32),
            vmem(width, model), vmem(PAD, length), vmem(width, length), vmem(3 * width, length),
            vmem(width, length, kind=F32), vmem(width, length, kind=F32),
            vmem(4, 16, model, kind=F32), vmem(16, model, kind=F32), vmem(8, 8, model, kind=F32),
            vmem(4, 8, model, kind=F32), vmem(4, 8, model, kind=F32), vmem(8, 8, model, kind=F32),
            vmem(2, *block), vmem(2, *block), vmem(2, *block), vmem(2, 4, share, model),
            vmem(2, 3, share, model), vmem(share, model),
            vmem(2, *block), vmem(2, *block), vmem(2, *block), vmem(1, 4, share, model),
            vmem(1, 3, share, model), vmem(*block),
            vmem(2, *block), vmem(2, *block), vmem(2, 4, share, model),
            vmem(2, 3, share, model), vmem(share, model),
            pltpu.SemaphoreType.DMA((BACKWARD_WIRES,)),
            pltpu.SemaphoreType.DMA((BACKWARD_WIRES,)),
            pltpu.SemaphoreType.DMA((8,)),
        ],
        compiler_params=pltpu.CompilerParams(
            vmem_limit_bytes=VMEM_LIMIT, collective_id=1, has_side_effects=True
        ),
        name="near_backward",
    )(acts, sides, slopes, w_ia, w_o, vectors, second, first, low, xt, cotangent)


def augment(labels, width):
    length = labels.shape[0]
    lanes = lax.broadcasted_iota(jnp.int32, (length, PAD), 1)
    in_docs = (lanes >= width) & (lanes < width + DOCS)
    same = (lanes - width) == labels[:, None]
    qaug = jnp.where(in_docs & same, 1.0, 0.0).astype(BF16)
    spare = (lanes >= width + DOCS) & (lanes < width + DOCS + 3 * (width // HEAD))
    kaug = jnp.where(in_docs & ~same, -(2.0**100), jnp.where(spare, 1.0, 0.0)).astype(BF16)
    vaug = jnp.where((lanes[:1] == width) | spare[:1], 1.0, 0.0).astype(BF16)
    return qaug, kaug, vaug


def body(
    tokens, doc_ids, w_query, b_query, w_key, w_value, b_value, w_mixer, b_mixer, gain_one,
    bias_one, w_inner, b_inner, w_outer, b_outer, gain_two, bias_two, cotangent,
):
    groups = lax.axis_size("tensor")
    rings = lax.axis_size("dp")
    place = lax.axis_index("tensor")
    width = w_query.shape[1]
    hidden = w_inner.shape[1]
    length = doc_ids.shape[2]
    model = tokens.shape[3]
    near = groups == 4 and rings == 8 and hidden == model and 4 * width == model

    if near:
        spare = jnp.zeros((PAD - width,), F32)
        vectors = jnp.concatenate(
            [
                b_mixer, gain_one, bias_one, b_outer, gain_two, bias_two, b_inner,
                b_query, spare, b_value, spare, jnp.zeros((PAD,), F32),
            ]
        ).reshape(8, model)
        acts, sides, slopes, first, second, low, xt, cot, w_ia, w_o = near_forward(
            tokens[:, 0], cotangent[:, 0], w_inner, w_query, w_key, w_value, w_mixer, w_outer.T,
            doc_ids, vectors,
        )
        out, d_tokens, ga, gi, go, tail, late = near_backward(
            acts, sides, slopes, w_ia.reshape(2 * groups, model, model),
            w_o.reshape(groups, model, model), vectors, second, first, low, xt, cot,
        )
        dbq, dbv = late[0, :width], late[0, 2 * width : 3 * width]
        dbi = tail[6]
        out, d_tokens = out[:, None], d_tokens[:, None].astype(F32)
    else:

        def gather(shard):
            whole = lax.all_gather(shard, ("tensor", "dp"), axis=0, tiled=True)
            return whole.reshape(groups, model, shard.shape[1])

        def to_sequence(part):
            return lax.all_to_all(part, "tensor", 0, 2, tiled=True).reshape(length, model)

        def from_sequence(whole):
            return lax.all_to_all(whole.reshape(1, 1, length, model), "tensor", 2, 0, tiled=True)

        def scatter(part):
            flat = part.reshape(-1, part.shape[2])
            total = lax.psum_scatter(flat, ("tensor", "dp"), scatter_dimension=0, tiled=True)
            return total.astype(F32)

        labels = lax.dynamic_index_in_dim(doc_ids[:, 0], place, 0, keepdims=False)
        qaug, kaug, vaug = augment(labels, width)
        shard_a = jnp.concatenate([w_query, w_key, w_value, w_mixer.T], axis=1)
        shard_o = w_outer.T
        spare = jnp.zeros((PAD - width,), F32)
        biases = jnp.concatenate([b_query, spare, b_value, spare, b_inner])[None]
        vectors = jnp.stack([gain_one, bias_one, b_outer, gain_two, bias_two] + [b_outer] * 3)
        x, cot = to_sequence(tokens), to_sequence(cotangent)
        a_all, wi, wo = gather(shard_a), gather(w_inner), gather(shard_o)
        every = lax.all_gather(biases, "tensor", axis=0)
        *saved, first_sum = attend_plain(x, a_all, every, qaug, kaug, vaug, b_mixer[None])
        out, d_first, d_mixed, g_inner, g_outer, dbi, small = dense_both(
            first_sum, wi, wo, every[:, :, 2 * PAD :], vectors, cot
        )
        d_tokens, g_attend, dbq, dbv = attend_backward(x, a_all, d_mixed, d_first, *saved)
        ga, gi, go = scatter(g_attend), scatter(g_inner), scatter(g_outer)
        rows = [dbq[:, 0, :width], dbv[:, 0, :width], dbi[:, 0], small]
        summed = lax.psum(jnp.concatenate([part.reshape(-1) for part in rows]), ("dp", "tensor"))
        own = lambda start, size: lax.dynamic_slice_in_dim(summed, start + place * size, size)
        dbq, dbv, dbi = own(0, width), own(model, width), own(2 * model, hidden)
        tail = summed[-small.size :].reshape(small.shape)
        out, d_tokens = from_sequence(out), from_sequence(d_tokens)
    return (
        out,
        d_tokens,
        ga[:, :width],
        dbq,
        ga[:, width : 2 * width],
        ga[:, 2 * width : 3 * width],
        dbv,
        ga[:, 3 * width :].T,
        tail[3],
        tail[4],
        tail[5],
        gi,
        dbi,
        go.T,
        tail[0],
        tail[1],
        tail[2],
    )


def solution(mesh):
    split = P(None, "dp", "tensor", None)
    both, flipped, part = P("dp", "tensor"), P("tensor", "dp"), P("tensor")
    return jax.shard_map(
        body,
        mesh=mesh,
        in_specs=(
            split, P(None, "dp", None), both, part, both, both, part, flipped, P(), P(), P(),
            both, part, flipped, P(), P(), P(), split,
        ),
        out_specs=(
            split, split, both, part, both, both, part, flipped, P(), P(), P(), both, part,
            flipped, P(), P(), P(),
        ),
        check_vma=False,
    )
```
